32 devices in a mesh: row: 4 (over x, core), long: 8 (over z, y).
Axes of the slice: x: 2, y: 2, z: 4, core: 2. Of those that a mesh axis runs over, the one named last changes fastest.
Arguments:
- slip: float32 [32, 16, 768], P('long'), may hold values from -6 to 6
- vertices: float32 [3, 4488], P(None, 'long'), may hold values from -2.5 to 258.5
- triangles: int32 [3, 8192], P(None, 'long'), may hold values from 0 to 4487, as said below
- elem_map: int32 [32, 256], P('long'), may hold values from 0 to 1023, as said below
- near_pairs: int32 [2, 640], P(None, ('row', 'long')), may hold values from 0 to 31, as said below
- near_count: int32 [32], P(('row', 'long')), may hold values from 1 to 20, as said below
- far_pairs: int32 [2, 512], P(None, ('row', 'long')), may hold values from 0 to 31, as said below
- far_coef: bfloat16 [512, 1024], P(('row', 'long')), may hold values from -1 to 1
- basis: bfloat16 [32, 32, 768], P('long'), may hold values from -0.21875 to 0.21875
Outputs:
- traction: float32 [32, 16, 768], P('long')
The draws below stay inside these ranges and needn't reach their ends.
Inputs may be any that keep to these rules, and one draw needn't show every extreme that they name: `triangles`: each element's three vertices belong to its owner's block of 561 vertices (owner = element // 1024). `elem_map`: the 4 clusters of one owner name each of its 1024 elements exactly once. `near_pairs`: in device block b the first cluster is owned by long index b % 8 and the second is the first plus 0 to 2; dead slots hold pairs of the same kind. `near_count`: some device has all 20 slots live. `far_pairs`: the second cluster of a far pair is owned by a long index more than 1 away from the first cluster's owner in both directions around the axis.
All inputs are finite; a program needn't handle non-finite values.
Results may differ from the reference program's by a relative error of at most 0.0041.
Values may be sent and summed in bfloat16 or wider, within the bound.
No kernel may reach another device: no remote copies, remote signals or barrier semaphores. Data moves between devices by JAX's collectives and lax.ppermute only.
A program may use at most 64 MiB of HBM per device.

```python
import jax
import jax.numpy as jnp
from jax import lax

CL = 4
CSIZE = 256
NRHS = 16
PD = 20
RANK = 32
NEARC = 2
REACH = 1
UNK = 768
GY = 16
NC = 32
ELEM_DEV = 1024
NE = 8192
VERT_DEV = 561
NV = 4488
NPAIR = 640
NFAR = 512


def element_order(key):
    long_count = NC // CL
    key_list = jax.random.split(jax.random.fold_in(key, 101), long_count)
    return jax.vmap(lambda one_key: jax.random.permutation(one_key, ELEM_DEV))(key_list).astype(jnp.int32)


def draw_triangles(key, part):
    placing = element_order(key)
    natural = placing.reshape(-1)
    device_id = jnp.arange(NE, dtype=jnp.int32) // ELEM_DEV
    local_cluster = natural // CSIZE
    within = natural % CSIZE
    cell_id = within // 2
    halves = within % 2
    column = local_cluster * 8 + cell_id // GY
    across = cell_id % GY

    def vertex_id(col_pos, row_pos):
        return device_id * VERT_DEV + col_pos * (GY + 1) + row_pos
    corner_one = vertex_id(column, across)
    corner_two = jnp.where(halves == 0, vertex_id(column + 1, across), vertex_id(column + 1, across + 1))
    corner_three = jnp.where(halves == 0, vertex_id(column + 1, across + 1), vertex_id(column, across + 1))
    return jnp.stack([corner_one, corner_two, corner_three]).astype(jnp.int32)


def draw_elem_map(key, part):
    placing = element_order(key)
    key = jax.random.fold_in(key, 5)
    inverse = jnp.argsort(placing, axis=1).astype(jnp.int32)
    key_list = jax.random.split(key, NC)
    slot_perm = jax.vmap(lambda one_key: jax.random.permutation(one_key, CSIZE))(key_list).astype(jnp.int32)
    cluster_ids = jnp.arange(NC, dtype=jnp.int32)
    owner = cluster_ids // CL
    natural = (cluster_ids % CL)[:, None] * CSIZE + slot_perm
    return inverse[owner[:, None], natural].astype(jnp.int32)


def draw_vertices(key, part):
    key = jax.random.fold_in(key, 7)
    key_x, key_y, key_z = jax.random.split(key, 3)
    index = jnp.arange(NV, dtype=jnp.int32)
    device_id = index // VERT_DEV
    local_id = index % VERT_DEV
    column = (device_id * 8 * CL + local_id // (GY + 1)).astype(jnp.float32)
    across = (local_id % (GY + 1)).astype(jnp.float32)
    coord_x = column + jax.random.uniform(key_x, (NV,), jnp.float32, -0.2, 0.2)
    coord_y = across + jax.random.uniform(key_y, (NV,), jnp.float32, -0.2, 0.2)
    coord_z = jax.random.uniform(key_z, (NV,), jnp.float32, -0.3, 0.3)
    return jnp.stack([coord_x, coord_y, coord_z]).astype(jnp.float32)


def draw_near_pairs(key, part):
    key = jax.random.fold_in(key, 9)
    key_one, key_two = jax.random.split(key, 2)
    long_count = NC // CL
    slot_ids = jnp.arange(NPAIR, dtype=jnp.int32)
    owner = slot_ids // PD % long_count
    cluster_a = owner * CL + jax.random.randint(key_one, (NPAIR,), 0, CL, jnp.int32)
    stride = jax.random.randint(key_two, (NPAIR,), 0, NEARC + 1, jnp.int32)
    cluster_b = jnp.minimum(cluster_a + stride, NC - 1)
    return jnp.stack([cluster_a, cluster_b]).astype(jnp.int32)


def draw_near_count(key, part):
    key = jax.random.fold_in(key, 13)
    key_one, key_two, key_three = jax.random.split(key, 3)
    blocks = NPAIR // PD
    busy = jax.random.randint(key_one, (blocks,), 0, 8, jnp.int32) == 0
    lower = jax.random.randint(key_two, (blocks,), max(PD // 6, 1), PD // 2 + 1, jnp.int32)
    counts = jnp.where(busy, PD, lower)
    forced = jax.random.randint(key_three, (), 0, blocks, jnp.int32)
    return jnp.where(jnp.arange(blocks, dtype=jnp.int32) == forced, PD, counts).astype(jnp.int32)


def draw_far_pairs(key, part):
    key = jax.random.fold_in(key, 17)
    key_one, key_two, key_three, key_four = jax.random.split(key, 4)
    long_count = NC // CL
    owner = jax.random.randint(key_four, (NFAR,), 0, long_count, jnp.int32)
    cluster_a = owner * CL + jax.random.randint(key_one, (NFAR,), 0, CL, jnp.int32)
    offset = jax.random.randint(key_two, (NFAR,), REACH + 1, long_count - REACH, jnp.int32)
    cluster_b = (owner + offset) % long_count * CL + jax.random.randint(key_three, (NFAR,), 0, CL, jnp.int32)
    return jnp.stack([cluster_a, cluster_b]).astype(jnp.int32)


def block_levels(rng, dims, cuts, low, high):
    gain = 1.0
    for position, shards_of in cuts:
        steps = jax.random.uniform(jax.random.fold_in(jax.random.fold_in(rng, 6), position), (shards_of,), jnp.float32, low / len(cuts), high / len(cuts))
        gain = gain * jnp.repeat(jnp.exp(steps), dims[position] // shards_of).reshape((-1,) + (1,) * (len(dims) - 1 - position))
    return gain


def scatter_about(rng, dims, spread, reach, shards=(), kind=jnp.bfloat16):
    array = spread * jax.random.normal(rng, dims, jnp.float32)
    if shards:
        array = array * block_levels(rng, dims, shards, -0.22, 0.18)
    return jnp.clip(array, -reach, reach).astype(kind)


def setup_inputs(seed: int = 0) -> dict:
    arg_keys = jax.random.split(jax.random.key(seed), 10)
    slip = scatter_about(arg_keys[0], (NC, NRHS, UNK), 1.0, 6.0, ((0, 8),), jnp.float32)
    vertices = draw_vertices(jax.random.fold_in(arg_keys[9], 71), 0)
    triangles = draw_triangles(jax.random.fold_in(arg_keys[9], 71), 0)
    elem_map = draw_elem_map(jax.random.fold_in(arg_keys[9], 71), 0)
    near_pairs = draw_near_pairs(jax.random.fold_in(arg_keys[9], 71), 0)
    near_count = draw_near_count(jax.random.fold_in(arg_keys[9], 71), 0)
    far_pairs = draw_far_pairs(jax.random.fold_in(arg_keys[9], 71), 0)
    far_coef = scatter_about(arg_keys[7], (NFAR, RANK * RANK), RANK ** -0.5, 1.0, ((0, 32),))
    basis = scatter_about(arg_keys[8], (NC, RANK, UNK), UNK ** -0.5, 0.21875, ((0, 8),))
    return {"slip": slip, "vertices": vertices, "triangles": triangles, "elem_map": elem_map, "near_pairs": near_pairs, "near_count": near_count, "far_pairs": far_pairs, "far_coef": far_coef, "basis": basis}


soften = 0.25

def widen(value):
    return lax.optimization_barrier(value).astype(jnp.float32)

def element_geometry(vertices, triangles):
    corner_one = vertices[:, triangles[0]]
    corner_two = vertices[:, triangles[1]]
    corner_three = vertices[:, triangles[2]]
    centre = (corner_one + corner_two + corner_three) / 3.0
    edge_one = corner_two - corner_one
    edge_two = corner_three - corner_one
    normal = jnp.stack([edge_one[1] * edge_two[2] - edge_one[2] * edge_two[1], edge_one[2] * edge_two[0] - edge_one[0] * edge_two[2], edge_one[0] * edge_two[1] - edge_one[1] * edge_two[0]])
    element_area = 0.5 * jnp.sqrt(lax.optimization_barrier(jnp.sum(normal * normal, axis=0)))
    return jnp.concatenate([centre, element_area[None]], axis=0)

def near_block(geom_left, geom_right):
    offsets = [geom_left[axis_id][:, None] - geom_right[axis_id][None, :] for axis_id in range(3)]
    radius_sq = offsets[0] * offsets[0] + offsets[1] * offsets[1] + offsets[2] * offsets[2]
    inverse = lax.rsqrt(radius_sq + soften)
    cubed = inverse * inverse * inverse
    weight = geom_left[3][:, None] * geom_right[3][None, :]
    blocks = []
    for row_id in range(3):
        pieces = []
        for col_id in range(3):
            term = offsets[row_id] * offsets[col_id] * cubed
            if row_id == col_id:
                term = term + inverse
            pieces.append(weight * term)
        blocks.append(jnp.concatenate(pieces, axis=1))
    return jnp.concatenate(blocks, axis=0).astype(jnp.bfloat16)

def reference(slip, vertices, triangles, elem_map, near_pairs, near_count, far_pairs, far_coef, basis):
    geometry = element_geometry(vertices, triangles)
    owners = jnp.arange(NC, dtype=jnp.int32) // CL
    element_index = (owners[:, None] * ELEM_DEV + elem_map).astype(jnp.int32)
    cluster_geom = jnp.transpose(geometry[:, element_index], (1, 0, 2))
    slip_wide = widen(slip.astype(jnp.bfloat16))
    slot_ids = jnp.arange(NPAIR, dtype=jnp.int32)
    live_mask = (slot_ids % PD < near_count[slot_ids // PD]).astype(jnp.float32)

    def visit_slot(running, item):
        cluster_a, cluster_b, weight_live = item
        block = widen(near_block(cluster_geom[cluster_a], cluster_geom[cluster_b]))
        into_a = jnp.dot(slip_wide[cluster_b], block.T)
        into_b = jnp.dot(slip_wide[cluster_a], block)
        other = weight_live * (cluster_a != cluster_b).astype(jnp.float32)
        running = running.at[cluster_a].add(weight_live * into_a)
        running = running.at[cluster_b].add(other * into_b)
        return (running, None)
    near_total, unused_out = lax.scan(visit_slot, jnp.zeros((NC, NRHS, UNK), jnp.float32), (near_pairs[0], near_pairs[1], live_mask))
    basis_wide = basis.astype(jnp.float32)
    coeffs = widen(jnp.einsum('cna,cka->cnk', slip_wide, basis_wide).astype(jnp.bfloat16))
    coupling = far_coef.astype(jnp.float32).reshape(NFAR, RANK, RANK)
    to_first = jnp.einsum('fnm,fkm->fnk', coeffs[far_pairs[1]], coupling)
    to_second = jnp.einsum('fnk,fkm->fnm', coeffs[far_pairs[0]], coupling)
    far_sum = jnp.zeros((NC, NRHS, RANK), jnp.float32).at[far_pairs[0]].add(to_first).at[far_pairs[1]].add(to_second)
    far_field = jnp.einsum('cnk,cka->cna', widen(far_sum.astype(jnp.bfloat16)), basis_wide)
    return near_total + far_field
```

```python
import functools

import jax
import jax.numpy as jnp
from jax import lax
from jax.experimental import pallas as pl
from jax.experimental.pallas import tpu as pltpu
from jax.sharding import PartitionSpec as P

NEARC = 2
LANES = 128
ROWS = 16
PIECES = 3

soften = 0.25

VMEM = pl.BlockSpec(memory_space=pltpu.VMEM)
SMEM = pl.BlockSpec(memory_space=pltpu.SMEM)


def shifted(block, axis, distance):
    devices = range(lax.axis_size(axis))
    route = [(i - distance, i) for i in devices if i - distance in devices]
    return lax.ppermute(block, axis, route)


def lane_gather(table, index):
    length = table.shape[1]
    lane = index & (LANES - 1)
    chunk = index // LANES
    found = jnp.zeros(index.shape, table.dtype)
    for piece_id in range(-(-length // LANES)):
        piece = table[:, piece_id * LANES : min(length, (piece_id + 1) * LANES)]
        missing = LANES - piece.shape[1]
        if missing:
            piece = jnp.concatenate([piece, jnp.zeros((1, missing), table.dtype)], axis=1)
        picked = jnp.take_along_axis(jnp.broadcast_to(piece, index.shape), lane, axis=1)
        found = jnp.where(chunk == piece_id, picked, found)
    return found


def split_three(value):
    high = value.astype(jnp.bfloat16).astype(jnp.float32)
    rest = value - high
    middle = rest.astype(jnp.bfloat16).astype(jnp.float32)
    return [high, middle, rest - middle]


def prepare_kernel(
    slip_ref, basis_ref, vertices_ref, triangles_ref, map_ref, pairs_ref, count_ref, place_ref,
    pay_ref, xs_ref, to_next_ref, to_prev_ref, geom_ref,
):
    clusters, rhs_count, unknowns = slip_ref.shape
    rank_size = basis_ref.shape[1]
    row_index = place_ref[0]
    long_index = place_ref[1]
    xs_ref[...] = slip_ref[...].astype(jnp.bfloat16)

    mine = row_index % clusters
    wide = jnp.concatenate([basis_ref[mine]] * (LANES // rank_size), axis=0)
    coeffs = lax.dot_general(
        xs_ref[mine], wide, (((1,), (1,)), ((), ())), preferred_element_type=jnp.float32
    )
    first = pairs_ref[0:1, :]
    kind = (first - long_index * clusters) * (NEARC + 1) + pairs_ref[1:2, :] - first
    slots = lax.broadcasted_iota(jnp.int32, (rhs_count, kind.shape[1]), 1)
    kinds = lax.broadcasted_iota(jnp.int32, (rhs_count, kind.shape[1]), 0)
    hits = jnp.where((slots < count_ref[0]) & (kinds == kind), 1.0, 0.0)
    counts = jnp.sum(hits, axis=1, keepdims=True)
    lane_id = lax.broadcasted_iota(jnp.int32, (rhs_count, LANES), 1)
    pay = jnp.where(lane_id < LANES - rank_size, coeffs, counts).astype(jnp.bfloat16)
    for target in range(pay_ref.shape[0]):
        pay_ref[target] = pay

    half = map_ref.shape[1] // LANES
    slot_map = map_ref[...]
    index = jnp.concatenate(
        [slot_map[:, part * LANES : (part + 1) * LANES] for part in range(half)], axis=0
    )
    vertex_base = long_index * vertices_ref.shape[1]
    corners = []
    for corner_id in range(3):
        vertex = lane_gather(triangles_ref[corner_id : corner_id + 1, :], index) - vertex_base
        corners.append(
            [lane_gather(vertices_ref[axis_id : axis_id + 1, :], vertex) for axis_id in range(3)]
        )
    one, two, three = corners
    centre = [(one[a] + two[a] + three[a]) / 3.0 for a in range(3)]
    edge_one = [two[a] - one[a] for a in range(3)]
    edge_two = [three[a] - one[a] for a in range(3)]
    normal = [
        edge_one[1] * edge_two[2] - edge_one[2] * edge_two[1],
        edge_one[2] * edge_two[0] - edge_one[0] * edge_two[2],
        edge_one[0] * edge_two[1] - edge_one[1] * edge_two[0],
    ]
    area = 0.5 * jnp.sqrt(normal[0] * normal[0] + normal[1] * normal[1] + normal[2] * normal[2])
    geometry = []
    for part_id, value in enumerate(centre + [area]):
        whole = jnp.concatenate(
            [value[part * clusters : (part + 1) * clusters] for part in range(half)], axis=1
        )
        geom_ref[part_id] = whole
        geometry.extend(split_three(whole))

    size = map_ref.shape[1]
    for out_ref, start in ((to_next_ref, clusters - NEARC), (to_prev_ref, 0)):
        for turn in range(NEARC):
            cluster = start + turn
            rows = [piece[cluster : cluster + 1, :] for piece in geometry]
            rows.append(jnp.zeros((ROWS - len(rows), size), jnp.float32))
            out_ref[turn, 0:rhs_count, :] = xs_ref[cluster]
            out_ref[turn, rhs_count : rhs_count + ROWS, 0:size] = jnp.concatenate(
                rows, axis=0
            ).astype(jnp.bfloat16)
            out_ref[turn, rhs_count : rhs_count + ROWS, size:unknowns] = jnp.zeros(
                (ROWS, unknowns - size), jnp.bfloat16
            )


def near_kernel(xs_ref, geom_ref, prev_ref, next_ref, out_ref, cols_ref, block_ref):
    clusters, rhs_count, unknowns = xs_ref.shape
    size = geom_ref.shape[2]
    window = clusters + 2 * NEARC
    step_rows = ROWS

    def halo_geometry(ref, turn):
        pieces = ref[turn, rhs_count : rhs_count + ROWS, 0:size].astype(jnp.float32)
        return [
            (pieces[3 * p + 2 : 3 * p + 3] + pieces[3 * p + 1 : 3 * p + 2]) + pieces[3 * p : 3 * p + 1]
            for p in range(4)
        ]

    rows = []
    for place in range(window):
        if place < NEARC:
            rows += halo_geometry(prev_ref, place)
        elif place < NEARC + clusters:
            rows += [geom_ref[p, place - NEARC : place - NEARC + 1, :] for p in range(4)]
        else:
            rows += halo_geometry(next_ref, place - NEARC - clusters)
    if len(rows) < LANES:
        rows.append(jnp.zeros((LANES - len(rows), size), jnp.float32))
    cols_ref[...] = jnp.concatenate(rows, axis=0).T

    def slip_of(place):
        if place < NEARC:
            return prev_ref[place, 0:rhs_count, :]
        if place < NEARC + clusters:
            return xs_ref[place - NEARC]
        return next_ref[place - NEARC - clusters, 0:rhs_count, :]

    parts = [(0, 0), (1, 1), (2, 2), (0, 1), (0, 2), (1, 2)]
    for place in range(window):
        targets = [a for a in range(clusters) if abs(a - (place - NEARC)) <= NEARC]

        def fill(step, carry):
            begin = pl.multiple_of(step * step_rows, step_rows)
            here = pl.ds(begin, step_rows)
            column = cols_ref[here, :]
            left = [
                jnp.broadcast_to(column[:, 4 * place + p : 4 * place + p + 1], (step_rows, size))
                for p in range(4)
            ]
            for target in targets:
                right = [geom_ref[p, target : target + 1, :] for p in range(4)]
                offset = [left[p] - right[p] for p in range(3)]
                radius_sq = offset[0] * offset[0] + offset[1] * offset[1] + offset[2] * offset[2]
                inverse = lax.rsqrt(radius_sq + soften)
                weight = left[3] * right[3]
                flat = weight * inverse
                cubed = flat * (inverse * inverse)
                scaled = [offset[p] * cubed for p in range(3)]
                for part_id, (i, j) in enumerate(parts):
                    term = offset[i] * scaled[j]
                    if i == j:
                        term = term + flat
                    block_ref[target, part_id, here, :] = term.astype(jnp.bfloat16)
            return carry

        lax.fori_loop(0, size // step_rows, fill, 0)
        slip = slip_of(place)
        pieces = [slip[:, p * size : (p + 1) * size] for p in range(3)]
        for target in targets:
            sums = [
                jnp.dot(pieces[p], block_ref[target, p], preferred_element_type=jnp.float32)
                for p in range(3)
            ]
            for part_id in range(3, 6):
                i, j = parts[part_id]
                both = jnp.dot(
                    jnp.concatenate([pieces[j], pieces[i]], axis=0),
                    block_ref[target, part_id],
                    preferred_element_type=jnp.float32,
                )
                sums[i] = sums[i] + both[0:rhs_count]
                sums[j] = sums[j] + both[rhs_count : 2 * rhs_count]
            for p in range(3):
                out_ref[target, place - target, :, p * size : (p + 1) * size] = sums[p]


def far_kernel(pairs_ref, coeff_ref, coupling_ref, out_ref, total_ref, *, clusters):
    long_count = total_ref.shape[0]
    rhs_count = coeff_ref.shape[1]
    rank_size = coupling_ref.shape[1]
    groups = LANES // rank_size
    group_id = lax.broadcasted_iota(jnp.int32, (rhs_count, LANES), 1) // rank_size
    total_ref[...] = jnp.zeros(total_ref.shape, jnp.float32)
    results = []
    for pair_id in range(pairs_ref.shape[1]):
        first = pairs_ref[0, pair_id]
        second = pairs_ref[1, pair_id]
        coupling = coupling_ref[pair_id]
        coeff_first = coeff_ref[(first % clusters) * long_count + first // clusters]
        coeff_second = coeff_ref[(second % clusters) * long_count + second // clusters]
        to_first = lax.dot_general(
            coeff_second[:, 0:rank_size],
            jnp.concatenate([coupling] * groups, axis=0),
            (((1,), (1,)), ((), ())),
            preferred_element_type=jnp.float32,
        )
        to_second = jnp.dot(
            coeff_first[:, 0:rank_size],
            jnp.concatenate([coupling] * groups, axis=1),
            preferred_element_type=jnp.float32,
        )
        results.append((first, to_first))
        results.append((second, to_second))
    for cluster, value in results:
        owner = cluster // clusters
        total_ref[owner] += jnp.where(group_id == cluster % clusters, value, 0.0)
    sent = total_ref[...].astype(jnp.bfloat16)
    for copy_id in range(out_ref.shape[0] // long_count):
        out_ref[copy_id * long_count : (copy_id + 1) * long_count] = sent


def finish_kernel(near_ref, pay_ref, far_ref, basis_ref, place_ref, out_ref, *, long_count):
    clusters, rank_size, unknowns = basis_ref.shape
    rhs_count = near_ref.shape[2]
    rows = pay_ref.shape[0] // long_count
    long_index = place_ref[1]
    before = jnp.maximum(long_index - 1, 0)
    own = jnp.zeros(pay_ref.shape[1:], jnp.float32)
    other = jnp.zeros(pay_ref.shape[1:], jnp.float32)
    for row in range(rows):
        own = own + pay_ref[row * long_count + long_index].astype(jnp.float32)
        other = other + pay_ref[row * long_count + before].astype(jnp.float32)
    total = jnp.sum(far_ref[...].astype(jnp.float32), axis=0)
    group_id = lax.broadcasted_iota(jnp.int32, total.shape, 1) // rank_size
    flat_basis = basis_ref[...].reshape(clusters * rank_size, unknowns)
    for cluster in range(clusters):
        picked = jnp.where(group_id == cluster, total, 0.0).astype(jnp.bfloat16)
        result = jnp.dot(picked, flat_basis, preferred_element_type=jnp.float32)
        for turn in range(2 * NEARC + 1):
            reach = turn - NEARC
            if reach >= 0:
                kind, source = cluster * (NEARC + 1) + reach, own
            elif cluster + reach >= 0:
                kind, source = (cluster + reach) * (NEARC + 1) - reach, own
            else:
                kind, source = (cluster + reach + clusters) * (NEARC + 1) - reach, other
            count = source[kind : kind + 1, LANES - 1 : LANES]
            result = result + count * near_ref[cluster, turn]
        out_ref[cluster] = result


def shards(slip, vertices, triangles, elem_map, near_pairs, near_count, far_pairs, far_coef, basis):
    clusters, rhs_count, unknowns = slip.shape
    rank_size = basis.shape[1]
    size = elem_map.shape[1]
    row_count = lax.axis_size("row")
    long_count = lax.axis_size("long")
    devices = row_count * long_count
    place = jnp.stack([lax.axis_index("row"), lax.axis_index("long")]).astype(jnp.int32)
    coupling = far_coef.reshape(-1, rank_size, rank_size)

    halo = jax.ShapeDtypeStruct((NEARC, rhs_count + ROWS, unknowns), jnp.bfloat16)
    pay, xs, to_next, to_prev, geometry = pl.pallas_call(
        prepare_kernel,
        out_shape=[
            jax.ShapeDtypeStruct((devices, rhs_count, LANES), jnp.bfloat16),
            jax.ShapeDtypeStruct(slip.shape, jnp.bfloat16),
            halo,
            halo,
            jax.ShapeDtypeStruct((4, clusters, size), jnp.float32),
        ],
        in_specs=[VMEM] * 6 + [SMEM] * 2,
        out_specs=[VMEM] * 5,
        compiler_params=pltpu.CompilerParams(vmem_limit_bytes=16 << 20),
        name="prepare",
    )(slip, basis, vertices, triangles, elem_map, near_pairs, near_count, place)

    everyone = lax.all_to_all(pay, ("row", "long"), 0, 0, tiled=True)
    from_prev = shifted(to_next, "long", 1)
    from_next = shifted(to_prev, "long", -1)

    near = pl.pallas_call(
        near_kernel,
        out_shape=jax.ShapeDtypeStruct((clusters, 2 * NEARC + 1, rhs_count, unknowns), jnp.float32),
        in_specs=[VMEM] * 4,
        out_specs=VMEM,
        scratch_shapes=[
            pltpu.VMEM((size, LANES), jnp.float32),
            pltpu.VMEM((clusters, 6, size, size), jnp.bfloat16),
        ],
        compiler_params=pltpu.CompilerParams(vmem_limit_bytes=24 << 20),
        cost_estimate=pl.CostEstimate(flops=40_000_000, bytes_accessed=2_000_000, transcendentals=1_300_000),
        name="near",
    )(xs, geometry, from_prev, from_next)

    far = pl.pallas_call(
        functools.partial(far_kernel, clusters=clusters),
        out_shape=jax.ShapeDtypeStruct((devices, rhs_count, clusters * rank_size), jnp.bfloat16),
        in_specs=[SMEM, VMEM, VMEM],
        out_specs=VMEM,
        scratch_shapes=[pltpu.VMEM((long_count, rhs_count, clusters * rank_size), jnp.float32)],
        compiler_params=pltpu.CompilerParams(vmem_limit_bytes=16 << 20),
        name="far",
    )(far_pairs, everyone, coupling)
    far_terms = lax.all_to_all(far, ("row", "long"), 0, 0, tiled=True)

    return pl.pallas_call(
        functools.partial(finish_kernel, long_count=long_count),
        out_shape=jax.ShapeDtypeStruct(slip.shape, jnp.float32),
        in_specs=[VMEM] * 4 + [SMEM],
        out_specs=VMEM,
        compiler_params=pltpu.CompilerParams(vmem_limit_bytes=16 << 20),
        name="finish",
    )(near, everyone, far_terms, basis, place)


def solution(mesh):
    placed = (
        P("long", None, None),
        P(None, "long"),
        P(None, "long"),
        P("long", None),
        P(None, ("row", "long")),
        P(("row", "long")),
        P(None, ("row", "long")),
        P(("row", "long"), None),
        P("long", None, None),
    )
    return jax.shard_map(
        shards, mesh=mesh, in_specs=placed, out_specs=P("long", None, None), check_vma=False
    )
```

```python
import functools

import jax
import jax.numpy as jnp
from jax import lax
from jax.experimental import pallas as pl
from jax.experimental.pallas import tpu as pltpu
from jax.sharding import PartitionSpec as P

NEARC = 2
LANES = 128
ROWS = 16
PIECES = 3

soften = 0.25

VMEM = pl.BlockSpec(memory_space=pltpu.VMEM)
SMEM = pl.BlockSpec(memory_space=pltpu.SMEM)
HBM = pl.BlockSpec(memory_space=pltpu.HBM)


def lane_gather(table, index):
    length = table.shape[1]
    lane = index & (LANES - 1)
    chunk = index // LANES
    found = jnp.zeros(index.shape, table.dtype)
    for piece_id in range(-(-length // LANES)):
        piece = table[:, piece_id * LANES : min(length, (piece_id + 1) * LANES)]
        missing = LANES - piece.shape[1]
        if missing:
            piece = jnp.concatenate([piece, jnp.zeros((1, missing), table.dtype)], axis=1)
        picked = jnp.take_along_axis(jnp.broadcast_to(piece, index.shape), lane, axis=1)
        found = jnp.where(chunk == piece_id, picked, found)
    return found


def split_three(value):
    high = value.astype(jnp.bfloat16).astype(jnp.float32)
    rest = value - high
    middle = rest.astype(jnp.bfloat16).astype(jnp.float32)
    return [high, middle, rest - middle]


def prepare_kernel(
    slip_hbm, basis_hbm, vertices_hbm, triangles_hbm, map_hbm, pairs_hbm, count_ref,
    pay_ref, xs_ref, halo_ref, geom_ref,
    slip_ref, basis_ref, vertices_ref, triangles_ref, map_ref, pairs_ref, sems,
):
    sources = (slip_hbm, basis_hbm, vertices_hbm, triangles_hbm, map_hbm, pairs_hbm)
    targets = (slip_ref, basis_ref, vertices_ref, triangles_ref, map_ref, pairs_ref)
    copies = [
        pltpu.make_async_copy(source, target, sems.at[place])
        for place, (source, target) in enumerate(zip(sources, targets))
    ]
    for copy in copies:
        copy.start()
    clusters, rhs_count, unknowns = slip_ref.shape
    rank_size = basis_ref.shape[1]
    row_index = lax.axis_index("row")
    long_index = lax.axis_index("long")
    mine = row_index % clusters
    for copy in copies:
        copy.wait()

    size = map_ref.shape[1]
    half = size // LANES
    slot_map = map_ref[...]
    index = jnp.concatenate(
        [slot_map[:, part * LANES : (part + 1) * LANES] for part in range(half)], axis=0
    )
    vertex_base = long_index * vertices_ref.shape[1]
    corners = []
    for corner_id in range(3):
        vertex = lane_gather(triangles_ref[corner_id : corner_id + 1, :], index) - vertex_base
        corners.append(
            [lane_gather(vertices_ref[axis_id : axis_id + 1, :], vertex) for axis_id in range(3)]
        )
    one, two, three = corners
    centre = [(one[a] + two[a] + three[a]) / 3.0 for a in range(3)]
    edge_one = [two[a] - one[a] for a in range(3)]
    edge_two = [three[a] - one[a] for a in range(3)]
    normal = [
        edge_one[1] * edge_two[2] - edge_one[2] * edge_two[1],
        edge_one[2] * edge_two[0] - edge_one[0] * edge_two[2],
        edge_one[0] * edge_two[1] - edge_one[1] * edge_two[0],
    ]
    area = 0.5 * jnp.sqrt(normal[0] * normal[0] + normal[1] * normal[1] + normal[2] * normal[2])
    geometry = []
    for value in centre + [area]:
        geometry.append(
            jnp.concatenate(
                [value[part * clusters : (part + 1) * clusters] for part in range(half)], axis=1
            )
        )
    for cluster in range(clusters):
        geom_ref[cluster] = jnp.concatenate(
            [whole[cluster : cluster + 1, :] for whole in geometry], axis=0
        )

    xs_ref[...] = slip_ref[...].astype(jnp.bfloat16)
    wide = jnp.concatenate([basis_ref[mine]] * (LANES // rank_size), axis=0)
    coeffs = lax.dot_general(
        xs_ref[mine], wide, (((1,), (1,)), ((), ())), preferred_element_type=jnp.float32
    )
    first = pairs_ref[0:1, :]
    kind = (first - long_index * clusters) * (NEARC + 1) + pairs_ref[1:2, :] - first
    slots = lax.broadcasted_iota(jnp.int32, (rhs_count, kind.shape[1]), 1)
    kinds = lax.broadcasted_iota(jnp.int32, (rhs_count, kind.shape[1]), 0)
    hits = jnp.where((slots < count_ref[0]) & (kinds == kind), 1.0, 0.0)
    counts = jnp.sum(hits, axis=1, keepdims=True)
    lane_id = lax.broadcasted_iota(jnp.int32, (rhs_count, LANES), 1)
    pay = jnp.where(lane_id < LANES - rank_size, coeffs, counts).astype(jnp.bfloat16)
    for target in range(pay_ref.shape[0]):
        pay_ref[target] = pay

    upward = mine < NEARC
    start = jnp.where(upward, clusters - NEARC, 0)
    pieces = [piece for whole in geometry for piece in split_three(whole)]
    for turn in range(NEARC):
        last = clusters - NEARC + turn
        rows = [
            jnp.where(upward, piece[last : last + 1, :], piece[turn : turn + 1, :])
            for piece in pieces
        ]
        rows.append(jnp.zeros((ROWS - len(rows), size), jnp.float32))
        halo_ref[turn, 0:rhs_count, :] = xs_ref[start + turn]
        halo_ref[turn, rhs_count : rhs_count + ROWS, 0:size] = jnp.concatenate(
            rows, axis=0
        ).astype(jnp.bfloat16)
        halo_ref[turn, rhs_count : rhs_count + ROWS, size:unknowns] = jnp.zeros(
            (ROWS, unknowns - size), jnp.bfloat16
        )


def near_kernel(xs_ref, geom_ref, halo_ref, out_ref, slip_ref, place_ref, cols_ref, block_ref):
    clusters, rhs_count, unknowns = xs_ref.shape
    size = geom_ref.shape[2]
    slots = clusters + NEARC
    mine = lax.axis_index("row") % clusters
    reaches = 2 * NEARC + 1
    where_at = [(mine - NEARC + turn + slots) % slots for turn in range(reaches)]

    slip_ref[0:clusters] = xs_ref[...]
    place_ref[0:clusters] = geom_ref[...]
    for turn in range(NEARC):
        slip_ref[clusters + turn] = halo_ref[turn, 0:rhs_count, :]
        pieces = halo_ref[turn, rhs_count : rhs_count + ROWS, 0:size].astype(jnp.float32)
        place_ref[clusters + turn] = jnp.concatenate(
            [
                (pieces[3 * p + 2 : 3 * p + 3] + pieces[3 * p + 1 : 3 * p + 2])
                + pieces[3 * p : 3 * p + 1]
                for p in range(4)
            ],
            axis=0,
        )
    rows = [place_ref[at] for at in where_at]
    rows.append(jnp.zeros((LANES - 4 * reaches, size), jnp.float32))
    cols_ref[...] = jnp.concatenate(rows, axis=0).T
    parts = [(0, 0), (1, 1), (2, 2), (0, 1), (0, 2), (1, 2)]

    def fill(step, carry):
        here = pl.ds(pl.multiple_of(step * ROWS, ROWS), ROWS)
        column = cols_ref[here, :]
        right = [place_ref[mine, p : p + 1, :] for p in range(4)]
        for turn in range(reaches):
            left = [
                jnp.broadcast_to(column[:, 4 * turn + p : 4 * turn + p + 1], (ROWS, size))
                for p in range(4)
            ]
            offset = [left[p] - right[p] for p in range(3)]
            radius_sq = offset[0] * offset[0] + offset[1] * offset[1] + offset[2] * offset[2]
            inverse = lax.rsqrt(radius_sq + soften)
            flat = (left[3] * right[3]) * inverse
            cubed = flat * (inverse * inverse)
            scaled = [offset[p] * cubed for p in range(3)]
            for part_id, (i, j) in enumerate(parts):
                term = offset[i] * scaled[j]
                if i == j:
                    term = term + flat
                block_ref[turn, part_id, here, :] = term.astype(jnp.bfloat16)
        return carry

    lax.fori_loop(0, size // ROWS, fill, 0)
    for turn in range(reaches):
        slip = slip_ref[where_at[turn]]
        pieces = [slip[:, p * size : (p + 1) * size] for p in range(3)]
        sums = [
            jnp.dot(pieces[p], block_ref[turn, p], preferred_element_type=jnp.float32)
            for p in range(3)
        ]
        for part_id in range(3, 6):
            i, j = parts[part_id]
            both = jnp.dot(
                jnp.concatenate([pieces[j], pieces[i]], axis=0),
                block_ref[turn, part_id],
                preferred_element_type=jnp.float32,
            )
            sums[i] = sums[i] + both[0:rhs_count]
            sums[j] = sums[j] + both[rhs_count : 2 * rhs_count]
        for p in range(3):
            out_ref[turn, :, p * size : (p + 1) * size] = sums[p]


def far_kernel(pairs_ref, coeff_ref, coupling_ref, near_ref, out_ref, own_ref, total_ref, *, clusters):
    long_count = total_ref.shape[0]
    rhs_count = coeff_ref.shape[1]
    rank_size = coupling_ref.shape[1]
    groups = LANES // rank_size
    group_id = lax.broadcasted_iota(jnp.int32, (rhs_count, LANES), 1) // rank_size
    total_ref[...] = jnp.zeros(total_ref.shape, jnp.float32)
    results = []
    for pair_id in range(pairs_ref.shape[1]):
        first = pairs_ref[0, pair_id]
        second = pairs_ref[1, pair_id]
        coupling = coupling_ref[pair_id]
        coeff_first = coeff_ref[(first % clusters) * long_count + first // clusters]
        coeff_second = coeff_ref[(second % clusters) * long_count + second // clusters]
        to_first = lax.dot_general(
            coeff_second[:, 0:rank_size],
            jnp.concatenate([coupling] * groups, axis=0),
            (((1,), (1,)), ((), ())),
            preferred_element_type=jnp.float32,
        )
        to_second = jnp.dot(
            coeff_first[:, 0:rank_size],
            jnp.concatenate([coupling] * groups, axis=1),
            preferred_element_type=jnp.float32,
        )
        results.append((first, to_first))
        results.append((second, to_second))
    for cluster, value in results:
        owner = cluster // clusters
        total_ref[owner] += jnp.where(group_id == cluster % clusters, value, 0.0)
    sent = total_ref[...].astype(jnp.bfloat16)
    for copy_id in range(out_ref.shape[0] // long_count):
        out_ref[copy_id * long_count : (copy_id + 1) * long_count] = sent

    long_index = lax.axis_index("long")
    mine = lax.axis_index("row") % clusters
    before = jnp.maximum(long_index - 1, 0)
    own = jnp.zeros(coeff_ref.shape[1:], jnp.float32)
    other = jnp.zeros(coeff_ref.shape[1:], jnp.float32)
    for row in range(coeff_ref.shape[0] // long_count):
        own = own + coeff_ref[row * long_count + long_index].astype(jnp.float32)
        other = other + coeff_ref[row * long_count + before].astype(jnp.float32)
    kinds = lax.broadcasted_iota(jnp.int32, own.shape, 0)
    result = jnp.zeros(own_ref.shape[1:], jnp.float32)
    for turn in range(near_ref.shape[0]):
        reach = turn - NEARC
        lower = mine + min(reach, 0)
        inside = lower >= 0
        kind = jnp.where(inside, lower, lower + clusters) * (NEARC + 1) + abs(reach)
        source = jnp.where(kinds == kind, jnp.where(inside, own, other), 0.0)
        count = jnp.sum(source, axis=0, keepdims=True)[:, LANES - 1 : LANES]
        result = result + count * near_ref[turn]
    result = result.astype(own_ref.dtype)
    for target in range(own_ref.shape[0]):
        own_ref[target] = result


def finish_kernel(near_ref, far_ref, basis_ref, out_ref):
    clusters, rank_size, unknowns = basis_ref.shape
    total = jnp.sum(far_ref[...].astype(jnp.float32), axis=0)
    group_id = lax.broadcasted_iota(jnp.int32, total.shape, 1) // rank_size
    flat_basis = basis_ref[...].reshape(clusters * rank_size, unknowns)
    for cluster in range(clusters):
        picked = jnp.where(group_id == cluster, total, 0.0).astype(jnp.bfloat16)
        result = jnp.dot(picked, flat_basis, preferred_element_type=jnp.float32)
        out_ref[cluster] = result + near_ref[cluster].astype(jnp.float32)


def shards(slip, vertices, triangles, elem_map, near_pairs, near_count, far_pairs, far_coef, basis):
    clusters, rhs_count, unknowns = slip.shape
    rank_size = basis.shape[1]
    size = elem_map.shape[1]
    row_count = lax.axis_size("row")
    long_count = lax.axis_size("long")
    devices = row_count * long_count
    coupling = far_coef.reshape(-1, rank_size, rank_size)
    reaches = 2 * NEARC + 1

    pay, xs, to_neighbour, geometry = pl.pallas_call(
        prepare_kernel,
        out_shape=[
            jax.ShapeDtypeStruct((devices, rhs_count, LANES), jnp.bfloat16),
            jax.ShapeDtypeStruct(slip.shape, jnp.bfloat16),
            jax.ShapeDtypeStruct((NEARC, rhs_count + ROWS, unknowns), jnp.bfloat16),
            jax.ShapeDtypeStruct((clusters, 4, size), jnp.float32),
        ],
        in_specs=[HBM] * 6 + [SMEM],
        out_specs=[VMEM] * 4,
        scratch_shapes=[
            pltpu.VMEM(slip.shape, slip.dtype),
            pltpu.VMEM(basis.shape, basis.dtype),
            pltpu.VMEM(vertices.shape, vertices.dtype),
            pltpu.VMEM(triangles.shape, triangles.dtype),
            pltpu.VMEM(elem_map.shape, elem_map.dtype),
            pltpu.VMEM(near_pairs.shape, near_pairs.dtype),
            pltpu.SemaphoreType.DMA((6,)),
        ],
        compiler_params=pltpu.CompilerParams(vmem_limit_bytes=16 << 20),
        name="prepare",
    )(
        *[
            pltpu.with_memory_space_constraint(array, pltpu.HBM)
            for array in (slip, basis, vertices, triangles, elem_map, near_pairs)
        ],
        near_count,
    )

    everyone = lax.all_to_all(pay, ("row", "long"), 0, 0, tiled=True)
    route = []
    for row in range(row_count):
        step = 1 if row % clusters < NEARC else -1
        for owner in range(long_count):
            if 0 <= owner - step < long_count:
                route.append((row * long_count + owner - step, row * long_count + owner))
    halo = lax.ppermute(to_neighbour, ("row", "long"), route)

    near = pl.pallas_call(
        near_kernel,
        out_shape=jax.ShapeDtypeStruct((reaches, rhs_count, unknowns), jnp.float32),
        in_specs=[VMEM] * 3,
        out_specs=VMEM,
        scratch_shapes=[
            pltpu.VMEM((clusters + NEARC, rhs_count, unknowns), jnp.bfloat16),
            pltpu.VMEM((clusters + NEARC, 4, size), jnp.float32),
            pltpu.VMEM((size, LANES), jnp.float32),
            pltpu.VMEM((reaches, 6, size, size), jnp.bfloat16),
        ],
        compiler_params=pltpu.CompilerParams(vmem_limit_bytes=24 << 20),
        cost_estimate=pl.CostEstimate(
            flops=500_000_000, bytes_accessed=1_000_000, transcendentals=330_000
        ),
        name="near",
    )(xs, geometry, halo)

    far, own = pl.pallas_call(
        functools.partial(far_kernel, clusters=clusters),
        out_shape=[
            jax.ShapeDtypeStruct((devices, rhs_count, clusters * rank_size), jnp.bfloat16),
            jax.ShapeDtypeStruct((row_count, rhs_count, unknowns), jnp.float32),
        ],
        in_specs=[SMEM, VMEM, VMEM, VMEM],
        out_specs=[VMEM] * 2,
        scratch_shapes=[pltpu.VMEM((long_count, rhs_count, clusters * rank_size), jnp.float32)],
        compiler_params=pltpu.CompilerParams(vmem_limit_bytes=16 << 20),
        name="far",
    )(far_pairs, everyone, coupling, near)
    far_terms = lax.all_to_all(far, ("row", "long"), 0, 0, tiled=True)
    near_rows = lax.all_to_all(own, "row", 0, 0, tiled=True)

    return pl.pallas_call(
        finish_kernel,
        out_shape=jax.ShapeDtypeStruct(slip.shape, jnp.float32),
        in_specs=[VMEM] * 3,
        out_specs=VMEM,
        compiler_params=pltpu.CompilerParams(vmem_limit_bytes=16 << 20),
        name="finish",
    )(near_rows, far_terms, basis)


def solution(mesh):
    placed = (
        P("long", None, None),
        P(None, "long"),
        P(None, "long"),
        P("long", None),
        P(None, ("row", "long")),
        P(("row", "long")),
        P(None, ("row", "long")),
        P(("row", "long"), None),
        P("long", None, None),
    )
    return jax.shard_map(
        shards, mesh=mesh, in_specs=placed, out_specs=P("long", None, None), check_vma=False
    )
```

```python
import functools

import jax
import jax.numpy as jnp
from jax import lax
from jax.experimental import pallas as pl
from jax.experimental.pallas import tpu as pltpu
from jax.sharding import PartitionSpec as P

NEARC = 2
LANES = 128
ROWS = 16
COUNT_ROWS = 8

soften = 0.25

VMEM = pl.BlockSpec(memory_space=pltpu.VMEM)
SMEM = pl.BlockSpec(memory_space=pltpu.SMEM)
HBM = pl.BlockSpec(memory_space=pltpu.HBM)


def lane_gather(table, index):
    length = table.shape[1]
    lane = index & (LANES - 1)
    chunk = index // LANES
    found = jnp.zeros(index.shape, table.dtype)
    for piece_id in range(-(-length // LANES)):
        piece = table[:, piece_id * LANES : min(length, (piece_id + 1) * LANES)]
        missing = LANES - piece.shape[1]
        if missing:
            piece = jnp.concatenate([piece, jnp.zeros((1, missing), table.dtype)], axis=1)
        picked = jnp.take_along_axis(jnp.broadcast_to(piece, index.shape), lane, axis=1)
        found = jnp.where(chunk == piece_id, picked, found)
    return found


def split_three(value):
    high = value.astype(jnp.bfloat16).astype(jnp.float32)
    rest = value - high
    middle = rest.astype(jnp.bfloat16).astype(jnp.float32)
    return [high, middle, rest - middle]


def prepare_kernel(
    slip_hbm, basis_hbm, vertices_hbm, triangles_hbm, map_hbm,
    pay_ref, xs_ref, halo_ref, geom_ref,
    slip_ref, basis_ref, vertices_ref, triangles_ref, map_ref, sems,
):
    sources = (slip_hbm, basis_hbm, vertices_hbm, triangles_hbm, map_hbm)
    targets = (slip_ref, basis_ref, vertices_ref, triangles_ref, map_ref)
    copies = [
        pltpu.make_async_copy(source, target, sems.at[place])
        for place, (source, target) in enumerate(zip(sources, targets))
    ]
    for copy in copies:
        copy.start()
    clusters, rhs_count, unknowns = slip_ref.shape
    long_index = lax.axis_index("long")
    for copy in copies:
        copy.wait()

    size = map_ref.shape[1]
    half = size // LANES
    slot_map = map_ref[...]
    index = jnp.concatenate(
        [slot_map[:, part * LANES : (part + 1) * LANES] for part in range(half)], axis=0
    )
    vertex_base = long_index * vertices_ref.shape[1]
    corners = []
    for corner_id in range(3):
        vertex = lane_gather(triangles_ref[corner_id : corner_id + 1, :], index) - vertex_base
        corners.append(
            [lane_gather(vertices_ref[axis_id : axis_id + 1, :], vertex) for axis_id in range(3)]
        )
    one, two, three = corners
    centre = [(one[a] + two[a] + three[a]) / 3.0 for a in range(3)]
    edge_one = [two[a] - one[a] for a in range(3)]
    edge_two = [three[a] - one[a] for a in range(3)]
    normal = [
        edge_one[1] * edge_two[2] - edge_one[2] * edge_two[1],
        edge_one[2] * edge_two[0] - edge_one[0] * edge_two[2],
        edge_one[0] * edge_two[1] - edge_one[1] * edge_two[0],
    ]
    area = 0.5 * jnp.sqrt(normal[0] * normal[0] + normal[1] * normal[1] + normal[2] * normal[2])
    geometry = []
    for value in centre + [area]:
        geometry.append(
            jnp.concatenate(
                [value[part * clusters : (part + 1) * clusters] for part in range(half)], axis=1
            )
        )
    for cluster in range(clusters):
        geom_ref[cluster] = jnp.concatenate(
            [whole[cluster : cluster + 1, :] for whole in geometry], axis=0
        )

    xs_ref[...] = slip_ref[...].astype(jnp.bfloat16)
    coeffs = jnp.concatenate(
        [
            lax.dot_general(
                xs_ref[cluster],
                basis_ref[cluster],
                (((1,), (1,)), ((), ())),
                preferred_element_type=jnp.float32,
            )
            for cluster in range(clusters)
        ],
        axis=1,
    ).astype(jnp.bfloat16)
    for target in range(pay_ref.shape[0]):
        pay_ref[target] = coeffs

    upward = lax.axis_index("row") % 2 == 0
    start = jnp.where(upward, clusters - NEARC, 0)
    pieces = [piece for whole in geometry for piece in split_three(whole)]
    for turn in range(NEARC):
        last = clusters - NEARC + turn
        rows = [
            jnp.where(upward, piece[last : last + 1, :], piece[turn : turn + 1, :])
            for piece in pieces
        ]
        rows.append(jnp.zeros((ROWS - len(rows), size), jnp.float32))
        halo_ref[turn, 0:rhs_count, :] = xs_ref[start + turn]
        halo_ref[turn, rhs_count : rhs_count + ROWS, 0:size] = jnp.concatenate(
            rows, axis=0
        ).astype(jnp.bfloat16)
        halo_ref[turn, rhs_count : rhs_count + ROWS, size:unknowns] = jnp.zeros(
            (ROWS, unknowns - size), jnp.bfloat16
        )


def near_kernel(
    xs_ref, geom_ref, halo_ref, out_ref, slip_ref, place_ref, cols_ref, even_ref, odd_ref
):
    clusters, rhs_count, unknowns = xs_ref.shape
    size = geom_ref.shape[2]
    slots = clusters + NEARC
    begin = (lax.axis_index("row") % 2) * NEARC

    def slot_of(place):
        return (begin - NEARC + place + slots) % slots

    slip_ref[0:clusters] = xs_ref[...]
    place_ref[0:clusters] = geom_ref[...]
    for turn in range(NEARC):
        slip_ref[clusters + turn] = halo_ref[turn, 0:rhs_count, :]
        pieces = halo_ref[turn, rhs_count : rhs_count + ROWS, 0:size].astype(jnp.float32)
        place_ref[clusters + turn] = jnp.concatenate(
            [
                (pieces[3 * p + 2 : 3 * p + 3] + pieces[3 * p + 1 : 3 * p + 2])
                + pieces[3 * p : 3 * p + 1]
                for p in range(4)
            ],
            axis=0,
        )
    for place in range(slots):
        rows = jnp.concatenate([place_ref[slot_of(place)], jnp.zeros((4, size), jnp.float32)], axis=0)
        cols_ref[place] = rows.T
    right = [[place_ref[begin + u, p : p + 1, :] for p in range(4)] for u in range(NEARC)]
    parts = [(0, 0), (1, 1), (2, 2), (0, 1), (0, 2), (1, 2)]

    def fill(place, targets, block_ref):
        for step in range(size // ROWS):
            here = pl.ds(step * ROWS, ROWS)
            column = cols_ref[place, here, :]
            left = [jnp.broadcast_to(column[:, p : p + 1], (ROWS, size)) for p in range(4)]
            for u in targets:
                offset = [left[p] - right[u][p] for p in range(3)]
                radius_sq = offset[0] * offset[0] + offset[1] * offset[1] + offset[2] * offset[2]
                inverse = lax.rsqrt(radius_sq + soften)
                flat = (left[3] * right[u][3]) * inverse
                cubed = flat * (inverse * inverse)
                scaled = [offset[p] * cubed for p in range(3)]
                for part_id, (i, j) in enumerate(parts):
                    term = offset[i] * scaled[j]
                    if i == j:
                        term = term + flat
                    block_ref[u, part_id, here, :] = term.astype(jnp.bfloat16)

    def apply(place, targets, block_ref):
        slip = slip_ref[slot_of(place)]
        pieces = [slip[:, p * size : (p + 1) * size] for p in range(3)]
        for u in targets:
            sums = [
                jnp.dot(pieces[p], block_ref[u, p], preferred_element_type=jnp.float32)
                for p in range(3)
            ]
            for part_id in range(3, 6):
                i, j = parts[part_id]
                both = jnp.dot(
                    jnp.concatenate([pieces[j], pieces[i]], axis=0),
                    block_ref[u, part_id],
                    preferred_element_type=jnp.float32,
                )
                sums[i] = sums[i] + both[0:rhs_count]
                sums[j] = sums[j] + both[rhs_count : 2 * rhs_count]
            for p in range(3):
                out_ref[place, u, :, p * size : (p + 1) * size] = sums[p].astype(jnp.bfloat16)

    every = list(range(NEARC))
    fill(0, [0], even_ref)
    even_ref[1] = jnp.zeros(even_ref.shape[1:], jnp.bfloat16)

    def two_places(turn, carry):
        place = 2 * turn
        fill(place + 1, every, odd_ref)
        apply(place, every, even_ref)
        fill(place + 2, every, even_ref)
        apply(place + 1, every, odd_ref)
        return carry

    lax.fori_loop(0, (slots - 2) // 2, two_places, 0)
    fill(slots - 1, [NEARC - 1], odd_ref)
    apply(slots - 2, every, even_ref)
    apply(slots - 1, [NEARC - 1], odd_ref)
    out_ref[slots - 1, 0] = jnp.zeros(out_ref.shape[2:], jnp.bfloat16)


def far_kernel(
    pairs_ref, count_ref, coeff_ref, coupling_ref, near_pairs_ref, out_ref, total_ref, *, clusters
):
    long_count = total_ref.shape[0]
    rhs_count = coeff_ref.shape[1]
    rank_size = coupling_ref.shape[1]
    groups = LANES // rank_size
    lane_id = lax.broadcasted_iota(jnp.int32, (rhs_count, LANES), 1)
    group_id = lane_id // rank_size
    total_ref[...] = jnp.zeros(total_ref.shape, jnp.float32)

    def coeff_of(cluster):
        whole = coeff_ref[cluster // clusters].astype(jnp.float32)
        turned = pltpu.roll(whole, (LANES - rank_size * (cluster % clusters)) % LANES, 1)
        return turned[:, 0:rank_size].astype(jnp.bfloat16)

    results = []
    for pair_id in range(pairs_ref.shape[1]):
        first = pairs_ref[0, pair_id]
        second = pairs_ref[1, pair_id]
        coupling = coupling_ref[pair_id]
        to_first = lax.dot_general(
            coeff_of(second),
            jnp.concatenate([coupling] * groups, axis=0),
            (((1,), (1,)), ((), ())),
            preferred_element_type=jnp.float32,
        )
        to_second = jnp.dot(
            coeff_of(first),
            jnp.concatenate([coupling] * groups, axis=1),
            preferred_element_type=jnp.float32,
        )
        results.append((first, to_first))
        results.append((second, to_second))
    for cluster, value in results:
        owner = cluster // clusters
        total_ref[owner] += jnp.where(group_id == cluster % clusters, value, 0.0)

    long_index = lax.axis_index("long")
    first = near_pairs_ref[0:1, :]
    kind = (first - long_index * clusters) * (NEARC + 1) + near_pairs_ref[1:2, :] - first
    kinds = lax.broadcasted_iota(jnp.int32, (COUNT_ROWS, kind.shape[1]), 0)
    live = lax.broadcasted_iota(jnp.int32, kinds.shape, 1) < count_ref[0]
    low = jnp.sum(jnp.where(live & (kinds == kind), 1.0, 0.0), axis=1, keepdims=True)
    high = jnp.sum(jnp.where(live & (kinds + COUNT_ROWS == kind), 1.0, 0.0), axis=1, keepdims=True)
    group = lax.broadcasted_iota(jnp.int32, (COUNT_ROWS, LANES), 1) // (LANES // 4)
    counts = jnp.where(group % 2 == 0, low, high)
    for owner in range(long_count):
        use = jnp.where(
            group < 2, (long_index == owner).astype(jnp.int32), (long_index + 1 == owner).astype(jnp.int32)
        )
        sent = jnp.concatenate([total_ref[owner], jnp.where(use > 0, counts, 0.0)], axis=0).astype(
            jnp.bfloat16
        )
        for copy_id in range(out_ref.shape[0] // long_count):
            out_ref[copy_id * long_count + owner] = sent


def finish_kernel(own_ref, other_ref, far_ref, basis_ref, out_ref):
    clusters, rank_size, unknowns = basis_ref.shape
    rhs_count = out_ref.shape[1]
    whole = jnp.sum(far_ref[...].astype(jnp.float32), axis=0)
    total = whole[0:rhs_count]
    counts = whole[rhs_count : rhs_count + COUNT_ROWS]
    group_id = lax.broadcasted_iota(jnp.int32, total.shape, 1) // rank_size
    flat_basis = basis_ref[...].reshape(clusters * rank_size, unknowns)
    even = lax.axis_index("row") % 2 == 0
    for cluster in range(clusters):
        picked = jnp.where(group_id == cluster, total, 0.0).astype(jnp.bfloat16)
        result = jnp.dot(picked, flat_basis, preferred_element_type=jnp.float32)
        u = cluster % NEARC
        for turn in range(2 * NEARC + 1):
            reach = turn - NEARC
            lower = cluster + min(reach, 0)
            source = 0 if lower >= 0 else 2
            kind = (lower if lower >= 0 else lower + clusters) * (NEARC + 1) + abs(reach)
            lane = (source + kind // COUNT_ROWS) * (LANES // 4)
            count = counts[kind % COUNT_ROWS : kind % COUNT_ROWS + 1, lane : lane + 1]
            mine, theirs = own_ref[u + turn, u], other_ref[u + turn, u]
            here = even if cluster < NEARC else jnp.logical_not(even)
            result = result + count * jnp.where(here, mine, theirs).astype(jnp.float32)
        out_ref[cluster] = result


def shards(slip, vertices, triangles, elem_map, near_pairs, near_count, far_pairs, far_coef, basis):
    clusters, rhs_count, unknowns = slip.shape
    rank_size = basis.shape[1]
    size = elem_map.shape[1]
    row_count = lax.axis_size("row")
    long_count = lax.axis_size("long")
    devices = row_count * long_count
    coupling = far_coef.reshape(-1, rank_size, rank_size)
    slots = clusters + NEARC

    pay, xs, to_neighbour, geometry = pl.pallas_call(
        prepare_kernel,
        out_shape=[
            jax.ShapeDtypeStruct((long_count, rhs_count, clusters * rank_size), jnp.bfloat16),
            jax.ShapeDtypeStruct(slip.shape, jnp.bfloat16),
            jax.ShapeDtypeStruct((NEARC, rhs_count + ROWS, unknowns), jnp.bfloat16),
            jax.ShapeDtypeStruct((clusters, 4, size), jnp.float32),
        ],
        in_specs=[HBM] * 5,
        out_specs=[VMEM] * 4,
        scratch_shapes=[
            pltpu.VMEM(slip.shape, slip.dtype),
            pltpu.VMEM(basis.shape, basis.dtype),
            pltpu.VMEM(vertices.shape, vertices.dtype),
            pltpu.VMEM(triangles.shape, triangles.dtype),
            pltpu.VMEM(elem_map.shape, elem_map.dtype),
            pltpu.SemaphoreType.DMA((5,)),
        ],
        compiler_params=pltpu.CompilerParams(vmem_limit_bytes=16 << 20),
        name="prepare",
    )(
        *[
            pltpu.with_memory_space_constraint(array, pltpu.HBM)
            for array in (slip, basis, vertices, triangles, elem_map)
        ]
    )

    coeffs = lax.all_to_all(pay, "long", 0, 0, tiled=True)
    route = []
    for row in range(row_count):
        step = 1 if row % 2 == 0 else -1
        for owner in range(long_count):
            if 0 <= owner - step < long_count:
                route.append((row * long_count + owner - step, row * long_count + owner))
    halo = lax.ppermute(to_neighbour, ("row", "long"), route)

    far = pl.pallas_call(
        functools.partial(far_kernel, clusters=clusters),
        out_shape=jax.ShapeDtypeStruct((devices, rhs_count + COUNT_ROWS, LANES), jnp.bfloat16),
        in_specs=[SMEM, SMEM, VMEM, VMEM, VMEM],
        out_specs=VMEM,
        scratch_shapes=[pltpu.VMEM((long_count, rhs_count, LANES), jnp.float32)],
        compiler_params=pltpu.CompilerParams(vmem_limit_bytes=16 << 20),
        name="far",
    )(far_pairs, near_count, coeffs, coupling, near_pairs)
    far_terms = lax.all_to_all(far, ("row", "long"), 0, 0, tiled=True)

    near = pl.pallas_call(
        near_kernel,
        out_shape=jax.ShapeDtypeStruct((slots, NEARC, rhs_count, unknowns), jnp.bfloat16),
        in_specs=[VMEM] * 3,
        out_specs=VMEM,
        scratch_shapes=[
            pltpu.VMEM((slots, rhs_count, unknowns), jnp.bfloat16),
            pltpu.VMEM((slots, 4, size), jnp.float32),
            pltpu.VMEM((slots, size, 8), jnp.float32),
            pltpu.VMEM((NEARC, 6, size, size), jnp.bfloat16),
            pltpu.VMEM((NEARC, 6, size, size), jnp.bfloat16),
        ],
        compiler_params=pltpu.CompilerParams(vmem_limit_bytes=24 << 20),
        cost_estimate=pl.CostEstimate(
            flops=1_000_000_000, bytes_accessed=1_000_000, transcendentals=660_000
        ),
        name="near",
    )(xs, geometry, halo)
    partner = [(row, row ^ 1) for row in range(row_count)]
    other = lax.ppermute(near, "row", partner)

    return pl.pallas_call(
        finish_kernel,
        out_shape=jax.ShapeDtypeStruct(slip.shape, jnp.float32),
        in_specs=[VMEM] * 4,
        out_specs=VMEM,
        compiler_params=pltpu.CompilerParams(vmem_limit_bytes=16 << 20),
        name="finish",
    )(near, other, far_terms, basis)


def solution(mesh):
    placed = (
        P("long", None, None),
        P(None, "long"),
        P(None, "long"),
        P("long", None),
        P(None, ("row", "long")),
        P(("row", "long")),
        P(None, ("row", "long")),
        P(("row", "long"), None),
        P("long", None, None),
    )
    return jax.shard_map(
        shards, mesh=mesh, in_specs=placed, out_specs=P("long", None, None), check_vma=False
    )
```

```python
import functools

import jax
import jax.numpy as jnp
from jax import lax
from jax.experimental import pallas as pl
from jax.experimental.pallas import tpu as pltpu
from jax.sharding import PartitionSpec as P

NEARC = 2
LANES = 128
ROWS = 16
COUNT_ROWS = 8

soften = 0.25

VMEM = pl.BlockSpec(memory_space=pltpu.VMEM)
SMEM = pl.BlockSpec(memory_space=pltpu.SMEM)
HBM = pl.BlockSpec(memory_space=pltpu.HBM)


def lane_gather(table, index):
    length = table.shape[1]
    lane = index & (LANES - 1)
    chunk = index // LANES
    found = jnp.zeros(index.shape, table.dtype)
    for piece_id in range(-(-length // LANES)):
        piece = table[:, piece_id * LANES : min(length, (piece_id + 1) * LANES)]
        missing = LANES - piece.shape[1]
        if missing:
            piece = jnp.concatenate([piece, jnp.zeros((1, missing), table.dtype)], axis=1)
        picked = jnp.take_along_axis(jnp.broadcast_to(piece, index.shape), lane, axis=1)
        found = jnp.where(chunk == piece_id, picked, found)
    return found


def split_three(value):
    high = value.astype(jnp.bfloat16).astype(jnp.float32)
    rest = value - high
    middle = rest.astype(jnp.bfloat16).astype(jnp.float32)
    return [high, middle, rest - middle]


def coeffs_kernel(slip_hbm, basis_hbm, pay_ref, xs_ref, slip_ref, basis_ref, sems):
    copies = [
        pltpu.make_async_copy(slip_hbm, slip_ref, sems.at[0]),
        pltpu.make_async_copy(basis_hbm, basis_ref, sems.at[1]),
    ]
    for copy in copies:
        copy.start()
    for copy in copies:
        copy.wait()
    xs_ref[...] = slip_ref[...].astype(jnp.bfloat16)
    coeffs = jnp.concatenate(
        [
            lax.dot_general(
                xs_ref[cluster],
                basis_ref[cluster],
                (((1,), (1,)), ((), ())),
                preferred_element_type=jnp.float32,
            )
            for cluster in range(slip_ref.shape[0])
        ],
        axis=1,
    ).astype(jnp.bfloat16)
    for target in range(pay_ref.shape[0]):
        pay_ref[target] = coeffs


def geometry_kernel(xs_ref, vertices_ref, triangles_ref, map_ref, halo_ref, geom_ref):
    clusters, rhs_count, unknowns = xs_ref.shape
    long_index = lax.axis_index("long")

    size = map_ref.shape[1]
    half = size // LANES
    slot_map = map_ref[...]
    index = jnp.concatenate(
        [slot_map[:, part * LANES : (part + 1) * LANES] for part in range(half)], axis=0
    )
    vertex_base = long_index * vertices_ref.shape[1]
    corners = []
    for corner_id in range(3):
        vertex = lane_gather(triangles_ref[corner_id : corner_id + 1, :], index) - vertex_base
        corners.append(
            [lane_gather(vertices_ref[axis_id : axis_id + 1, :], vertex) for axis_id in range(3)]
        )
    one, two, three = corners
    centre = [(one[a] + two[a] + three[a]) / 3.0 for a in range(3)]
    edge_one = [two[a] - one[a] for a in range(3)]
    edge_two = [three[a] - one[a] for a in range(3)]
    normal = [
        edge_one[1] * edge_two[2] - edge_one[2] * edge_two[1],
        edge_one[2] * edge_two[0] - edge_one[0] * edge_two[2],
        edge_one[0] * edge_two[1] - edge_one[1] * edge_two[0],
    ]
    area = 0.5 * jnp.sqrt(normal[0] * normal[0] + normal[1] * normal[1] + normal[2] * normal[2])
    geometry = []
    for value in centre + [area]:
        geometry.append(
            jnp.concatenate(
                [value[part * clusters : (part + 1) * clusters] for part in range(half)], axis=1
            )
        )
    for cluster in range(clusters):
        geom_ref[cluster] = jnp.concatenate(
            [whole[cluster : cluster + 1, :] for whole in geometry], axis=0
        )

    upward = lax.axis_index("row") % 2 == 0
    start = jnp.where(upward, clusters - NEARC, 0)
    pieces = [piece for whole in geometry for piece in split_three(whole)]
    for turn in range(NEARC):
        last = clusters - NEARC + turn
        rows = [
            jnp.where(upward, piece[last : last + 1, :], piece[turn : turn + 1, :])
            for piece in pieces
        ]
        rows.append(jnp.zeros((ROWS - len(rows), size), jnp.float32))
        halo_ref[turn, 0:rhs_count, :] = xs_ref[start + turn]
        halo_ref[turn, rhs_count : rhs_count + ROWS, 0:size] = jnp.concatenate(
            rows, axis=0
        ).astype(jnp.bfloat16)
        halo_ref[turn, rhs_count : rhs_count + ROWS, size:unknowns] = jnp.zeros(
            (ROWS, unknowns - size), jnp.bfloat16
        )


def near_kernel(
    xs_ref, geom_ref, halo_ref, out_ref, slip_ref, place_ref, cols_ref, even_ref, odd_ref
):
    clusters, rhs_count, unknowns = xs_ref.shape
    size = geom_ref.shape[2]
    slots = clusters + NEARC
    begin = (lax.axis_index("row") % 2) * NEARC

    def slot_of(place):
        return (begin - NEARC + place + slots) % slots

    slip_ref[0:clusters] = xs_ref[...]
    place_ref[0:clusters] = geom_ref[...]
    for turn in range(NEARC):
        slip_ref[clusters + turn] = halo_ref[turn, 0:rhs_count, :]
        pieces = halo_ref[turn, rhs_count : rhs_count + ROWS, 0:size].astype(jnp.float32)
        place_ref[clusters + turn] = jnp.concatenate(
            [
                (pieces[3 * p + 2 : 3 * p + 3] + pieces[3 * p + 1 : 3 * p + 2])
                + pieces[3 * p : 3 * p + 1]
                for p in range(4)
            ],
            axis=0,
        )
    for place in range(slots):
        rows = jnp.concatenate([place_ref[slot_of(place)], jnp.zeros((4, size), jnp.float32)], axis=0)
        cols_ref[place] = rows.T
    right = [[place_ref[begin + u, p : p + 1, :] for p in range(4)] for u in range(NEARC)]
    parts = [(0, 0), (1, 1), (2, 2), (0, 1), (0, 2), (1, 2)]

    def fill(place, targets, block_ref):
        for step in range(size // ROWS):
            here = pl.ds(step * ROWS, ROWS)
            column = cols_ref[place, here, :]
            left = [jnp.broadcast_to(column[:, p : p + 1], (ROWS, size)) for p in range(4)]
            for u in targets:
                offset = [left[p] - right[u][p] for p in range(3)]
                radius_sq = offset[0] * offset[0] + offset[1] * offset[1] + offset[2] * offset[2]
                inverse = lax.rsqrt(radius_sq + soften)
                flat = (left[3] * right[u][3]) * inverse
                cubed = flat * (inverse * inverse)
                scaled = [offset[p] * cubed for p in range(3)]
                for part_id, (i, j) in enumerate(parts):
                    term = offset[i] * scaled[j]
                    if i == j:
                        term = term + flat
                    block_ref[u, part_id, here, :] = term.astype(jnp.bfloat16)

    def apply(place, targets, block_ref):
        slip = slip_ref[slot_of(place)]
        pieces = [slip[:, p * size : (p + 1) * size] for p in range(3)]
        for u in targets:
            sums = [
                jnp.dot(pieces[p], block_ref[u, p], preferred_element_type=jnp.float32)
                for p in range(3)
            ]
            for part_id in range(3, 6):
                i, j = parts[part_id]
                both = jnp.dot(
                    jnp.concatenate([pieces[j], pieces[i]], axis=0),
                    block_ref[u, part_id],
                    preferred_element_type=jnp.float32,
                )
                sums[i] = sums[i] + both[0:rhs_count]
                sums[j] = sums[j] + both[rhs_count : 2 * rhs_count]
            for p in range(3):
                out_ref[place, u, :, p * size : (p + 1) * size] = sums[p].astype(jnp.bfloat16)

    every = list(range(NEARC))
    fill(0, [0], even_ref)
    even_ref[1] = jnp.zeros(even_ref.shape[1:], jnp.bfloat16)

    def two_places(turn, carry):
        place = 2 * turn
        fill(place + 1, every, odd_ref)
        apply(place, every, even_ref)
        fill(place + 2, every, even_ref)
        apply(place + 1, every, odd_ref)
        return carry

    lax.fori_loop(0, (slots - 2) // 2, two_places, 0)
    fill(slots - 1, [NEARC - 1], odd_ref)
    apply(slots - 2, every, even_ref)
    apply(slots - 1, [NEARC - 1], odd_ref)
    out_ref[slots - 1, 0] = jnp.zeros(out_ref.shape[2:], jnp.bfloat16)


def far_kernel(
    pairs_ref, count_ref, coeff_ref, coupling_ref, near_pairs_ref, out_ref, total_ref, *, clusters
):
    long_count = total_ref.shape[0]
    rhs_count = coeff_ref.shape[1]
    rank_size = coupling_ref.shape[1]
    groups = LANES // rank_size
    lane_id = lax.broadcasted_iota(jnp.int32, (rhs_count, LANES), 1)
    group_id = lane_id // rank_size
    total_ref[...] = jnp.zeros(total_ref.shape, jnp.float32)

    def coeff_of(cluster):
        whole = coeff_ref[cluster // clusters].astype(jnp.float32)
        turned = pltpu.roll(whole, (LANES - rank_size * (cluster % clusters)) % LANES, 1)
        return turned[:, 0:rank_size].astype(jnp.bfloat16)

    results = []
    for pair_id in range(pairs_ref.shape[1]):
        first = pairs_ref[0, pair_id]
        second = pairs_ref[1, pair_id]
        coupling = coupling_ref[pair_id]
        to_first = lax.dot_general(
            coeff_of(second),
            jnp.concatenate([coupling] * groups, axis=0),
            (((1,), (1,)), ((), ())),
            preferred_element_type=jnp.float32,
        )
        to_second = jnp.dot(
            coeff_of(first),
            jnp.concatenate([coupling] * groups, axis=1),
            preferred_element_type=jnp.float32,
        )
        results.append((first, to_first))
        results.append((second, to_second))
    for cluster, value in results:
        owner = cluster // clusters
        total_ref[owner] += jnp.where(group_id == cluster % clusters, value, 0.0)

    long_index = lax.axis_index("long")
    first = near_pairs_ref[0:1, :]
    kind = (first - long_index * clusters) * (NEARC + 1) + near_pairs_ref[1:2, :] - first
    kinds = lax.broadcasted_iota(jnp.int32, (COUNT_ROWS, kind.shape[1]), 0)
    live = lax.broadcasted_iota(jnp.int32, kinds.shape, 1) < count_ref[0]
    low = jnp.sum(jnp.where(live & (kinds == kind), 1.0, 0.0), axis=1, keepdims=True)
    high = jnp.sum(jnp.where(live & (kinds + COUNT_ROWS == kind), 1.0, 0.0), axis=1, keepdims=True)
    group = lax.broadcasted_iota(jnp.int32, (COUNT_ROWS, LANES), 1) // (LANES // 4)
    counts = jnp.where(group % 2 == 0, low, high)
    for owner in range(long_count):
        use = jnp.where(
            group < 2, (long_index == owner).astype(jnp.int32), (long_index + 1 == owner).astype(jnp.int32)
        )
        sent = jnp.concatenate([total_ref[owner], jnp.where(use > 0, counts, 0.0)], axis=0).astype(
            jnp.bfloat16
        )
        for copy_id in range(out_ref.shape[0] // long_count):
            out_ref[copy_id * long_count + owner] = sent


def finish_kernel(own_ref, other_ref, far_ref, basis_ref, out_ref):
    clusters, rank_size, unknowns = basis_ref.shape
    rhs_count = out_ref.shape[1]
    whole = jnp.sum(far_ref[...].astype(jnp.float32), axis=0)
    total = whole[0:rhs_count]
    counts = whole[rhs_count : rhs_count + COUNT_ROWS]
    group_id = lax.broadcasted_iota(jnp.int32, total.shape, 1) // rank_size
    flat_basis = basis_ref[...].reshape(clusters * rank_size, unknowns)
    even = lax.axis_index("row") % 2 == 0
    for cluster in range(clusters):
        picked = jnp.where(group_id == cluster, total, 0.0).astype(jnp.bfloat16)
        result = jnp.dot(picked, flat_basis, preferred_element_type=jnp.float32)
        u = cluster % NEARC
        for turn in range(2 * NEARC + 1):
            reach = turn - NEARC
            lower = cluster + min(reach, 0)
            source = 0 if lower >= 0 else 2
            kind = (lower if lower >= 0 else lower + clusters) * (NEARC + 1) + abs(reach)
            lane = (source + kind // COUNT_ROWS) * (LANES // 4)
            count = counts[kind % COUNT_ROWS : kind % COUNT_ROWS + 1, lane : lane + 1]
            mine, theirs = own_ref[u + turn, u], other_ref[u + turn, u]
            here = even if cluster < NEARC else jnp.logical_not(even)
            result = result + count * jnp.where(here, mine, theirs).astype(jnp.float32)
        out_ref[cluster] = result


def shards(slip, vertices, triangles, elem_map, near_pairs, near_count, far_pairs, far_coef, basis):
    clusters, rhs_count, unknowns = slip.shape
    rank_size = basis.shape[1]
    size = elem_map.shape[1]
    row_count = lax.axis_size("row")
    long_count = lax.axis_size("long")
    devices = row_count * long_count
    coupling = far_coef.reshape(-1, rank_size, rank_size)
    slots = clusters + NEARC

    pay, xs = pl.pallas_call(
        coeffs_kernel,
        out_shape=[
            jax.ShapeDtypeStruct((long_count, rhs_count, clusters * rank_size), jnp.bfloat16),
            jax.ShapeDtypeStruct(slip.shape, jnp.bfloat16),
        ],
        in_specs=[HBM] * 2,
        out_specs=[VMEM] * 2,
        scratch_shapes=[
            pltpu.VMEM(slip.shape, slip.dtype),
            pltpu.VMEM(basis.shape, basis.dtype),
            pltpu.SemaphoreType.DMA((2,)),
        ],
        compiler_params=pltpu.CompilerParams(vmem_limit_bytes=16 << 20),
        name="coeffs",
    )(*[pltpu.with_memory_space_constraint(array, pltpu.HBM) for array in (slip, basis)])

    coeffs = lax.all_to_all(pay, "long", 0, 0, tiled=True)
    to_neighbour, geometry = pl.pallas_call(
        geometry_kernel,
        out_shape=[
            jax.ShapeDtypeStruct((NEARC, rhs_count + ROWS, unknowns), jnp.bfloat16),
            jax.ShapeDtypeStruct((clusters, 4, size), jnp.float32),
        ],
        in_specs=[VMEM] * 4,
        out_specs=[VMEM] * 2,
        compiler_params=pltpu.CompilerParams(vmem_limit_bytes=16 << 20),
        cost_estimate=pl.CostEstimate(
            flops=2_000_000, bytes_accessed=1_000_000, transcendentals=1_000
        ),
        name="geometry",
    )(xs, vertices, triangles, elem_map)
    route = []
    for row in range(row_count):
        step = 1 if row % 2 == 0 else -1
        for owner in range(long_count):
            if 0 <= owner - step < long_count:
                route.append((row * long_count + owner - step, row * long_count + owner))
    halo = lax.ppermute(to_neighbour, ("row", "long"), route)

    far = pl.pallas_call(
        functools.partial(far_kernel, clusters=clusters),
        out_shape=jax.ShapeDtypeStruct((devices, rhs_count + COUNT_ROWS, LANES), jnp.bfloat16),
        in_specs=[SMEM, SMEM, VMEM, VMEM, VMEM],
        out_specs=VMEM,
        scratch_shapes=[pltpu.VMEM((long_count, rhs_count, LANES), jnp.float32)],
        compiler_params=pltpu.CompilerParams(vmem_limit_bytes=16 << 20),
        name="far",
    )(far_pairs, near_count, coeffs, coupling, near_pairs)
    far_terms = lax.all_to_all(far, ("row", "long"), 0, 0, tiled=True)

    near = pl.pallas_call(
        near_kernel,
        out_shape=jax.ShapeDtypeStruct((slots, NEARC, rhs_count, unknowns), jnp.bfloat16),
        in_specs=[VMEM] * 3,
        out_specs=VMEM,
        scratch_shapes=[
            pltpu.VMEM((slots, rhs_count, unknowns), jnp.bfloat16),
            pltpu.VMEM((slots, 4, size), jnp.float32),
            pltpu.VMEM((slots, size, 8), jnp.float32),
            pltpu.VMEM((NEARC, 6, size, size), jnp.bfloat16),
            pltpu.VMEM((NEARC, 6, size, size), jnp.bfloat16),
        ],
        compiler_params=pltpu.CompilerParams(vmem_limit_bytes=24 << 20),
        cost_estimate=pl.CostEstimate(
            flops=1_000_000_000, bytes_accessed=1_000_000, transcendentals=660_000
        ),
        name="near",
    )(xs, geometry, halo)
    partner = [(row, row ^ 1) for row in range(row_count)]
    other = lax.ppermute(near, "row", partner)

    return pl.pallas_call(
        finish_kernel,
        out_shape=jax.ShapeDtypeStruct(slip.shape, jnp.float32),
        in_specs=[VMEM] * 4,
        out_specs=VMEM,
        compiler_params=pltpu.CompilerParams(vmem_limit_bytes=16 << 20),
        name="finish",
    )(near, other, far_terms, basis)


def solution(mesh):
    placed = (
        P("long", None, None),
        P(None, "long"),
        P(None, "long"),
        P("long", None),
        P(None, ("row", "long")),
        P(("row", "long")),
        P(None, ("row", "long")),
        P(("row", "long"), None),
        P("long", None, None),
    )
    return jax.shard_map(
        shards, mesh=mesh, in_specs=placed, out_specs=P("long", None, None), check_vma=False
    )
```

```python
import functools

import jax
import jax.numpy as jnp
from jax import lax
from jax.experimental import pallas as pl
from jax.experimental.pallas import tpu as pltpu
from jax.sharding import PartitionSpec as P

NEARC = 2
LANES = 128
ROWS = 16

soften = 0.25

VMEM = pl.BlockSpec(memory_space=pltpu.VMEM)
SMEM = pl.BlockSpec(memory_space=pltpu.SMEM)
HBM = pl.BlockSpec(memory_space=pltpu.HBM)
ANY = pl.BlockSpec(memory_space=pl.ANY)


def lane_gather(table, index):
    length = table.shape[1]
    lane = index & (LANES - 1)
    chunk = index // LANES
    found = jnp.zeros(index.shape, table.dtype)
    for piece_id in range(-(-length // LANES)):
        piece = table[:, piece_id * LANES : min(length, (piece_id + 1) * LANES)]
        missing = LANES - piece.shape[1]
        if missing:
            piece = jnp.concatenate([piece, jnp.zeros((1, missing), table.dtype)], axis=1)
        picked = jnp.take_along_axis(jnp.broadcast_to(piece, index.shape), lane, axis=1)
        found = jnp.where(chunk == piece_id, picked, found)
    return found


def split_three(value):
    high = value.astype(jnp.bfloat16).astype(jnp.float32)
    rest = value - high
    middle = rest.astype(jnp.bfloat16).astype(jnp.float32)
    return [high, middle, rest - middle]


def coeffs_kernel(
    slip_hbm, basis_hbm, pairs_hbm, count_ref, pay_ref, slip_ref, basis_ref, pairs_ref, sems
):
    clusters = slip_hbm.shape[0]
    rhs_count = slip_ref.shape[0]
    rank_size = basis_ref.shape[0]
    mine = lax.axis_index("row") % clusters
    copies = [
        pltpu.make_async_copy(slip_hbm.at[mine], slip_ref, sems.at[0]),
        pltpu.make_async_copy(basis_hbm.at[mine], basis_ref, sems.at[1]),
        pltpu.make_async_copy(pairs_hbm, pairs_ref, sems.at[2]),
    ]
    for copy in copies:
        copy.start()
    for copy in copies:
        copy.wait()
    half = rhs_count // 2
    wide = jnp.concatenate([basis_ref[...]] * (LANES // rank_size), axis=0)
    coeffs = lax.dot_general(
        slip_ref[...].astype(jnp.bfloat16),
        wide,
        (((1,), (1,)), ((), ())),
        preferred_element_type=jnp.float32,
    )
    first = pairs_ref[0:1, :]
    kind = (first - lax.axis_index("long") * clusters) * (NEARC + 1) + pairs_ref[1:2, :] - first
    kinds = lax.broadcasted_iota(jnp.int32, (half, kind.shape[1]), 0)
    live = lax.broadcasted_iota(jnp.int32, kinds.shape, 1) < count_ref[0]
    low = jnp.sum(jnp.where(live & (kinds == kind), 1.0, 0.0), axis=1, keepdims=True)
    high = jnp.sum(jnp.where(live & (kinds + half == kind), 1.0, 0.0), axis=1, keepdims=True)
    group = lax.broadcasted_iota(jnp.int32, (half, LANES), 1) // rank_size
    pay = jnp.where(
        group == 0, coeffs[0:half], jnp.where(group == 1, coeffs[half:], jnp.where(group == 2, low, high))
    ).astype(jnp.bfloat16)
    for target in range(pay_ref.shape[0]):
        pay_ref[target] = pay


def geometry_kernel(
    slip_ref, vertices_ref, triangles_ref, map_ref, after_ref, xs_ref, halo_ref, geom_ref
):
    clusters, rhs_count, unknowns = slip_ref.shape
    xs_ref[...] = slip_ref[...].astype(jnp.bfloat16)
    long_index = lax.axis_index("long")

    size = map_ref.shape[1]
    half = size // LANES
    slot_map = map_ref[...]
    index = jnp.concatenate(
        [slot_map[:, part * LANES : (part + 1) * LANES] for part in range(half)], axis=0
    )
    vertex_base = long_index * vertices_ref.shape[1]
    corners = []
    for corner_id in range(3):
        vertex = lane_gather(triangles_ref[corner_id : corner_id + 1, :], index) - vertex_base
        corners.append(
            [lane_gather(vertices_ref[axis_id : axis_id + 1, :], vertex) for axis_id in range(3)]
        )
    one, two, three = corners
    centre = [(one[a] + two[a] + three[a]) / 3.0 for a in range(3)]
    edge_one = [two[a] - one[a] for a in range(3)]
    edge_two = [three[a] - one[a] for a in range(3)]
    normal = [
        edge_one[1] * edge_two[2] - edge_one[2] * edge_two[1],
        edge_one[2] * edge_two[0] - edge_one[0] * edge_two[2],
        edge_one[0] * edge_two[1] - edge_one[1] * edge_two[0],
    ]
    area = 0.5 * jnp.sqrt(normal[0] * normal[0] + normal[1] * normal[1] + normal[2] * normal[2])
    geometry = []
    for value in centre + [area]:
        geometry.append(
            jnp.concatenate(
                [value[part * clusters : (part + 1) * clusters] for part in range(half)], axis=1
            )
        )
    for cluster in range(clusters):
        geom_ref[cluster] = jnp.concatenate(
            [whole[cluster : cluster + 1, :] for whole in geometry], axis=0
        )

    upward = lax.axis_index("row") % 2 == 0
    start = jnp.where(upward, clusters - NEARC, 0)
    pieces = [piece for whole in geometry for piece in split_three(whole)]
    for turn in range(NEARC):
        last = clusters - NEARC + turn
        rows = [
            jnp.where(upward, piece[last : last + 1, :], piece[turn : turn + 1, :])
            for piece in pieces
        ]
        rows.append(jnp.zeros((ROWS - len(rows), size), jnp.float32))
        halo_ref[turn, 0:rhs_count, :] = xs_ref[start + turn]
        halo_ref[turn, rhs_count : rhs_count + ROWS, 0:size] = jnp.concatenate(
            rows, axis=0
        ).astype(jnp.bfloat16)
        halo_ref[turn, rhs_count : rhs_count + ROWS, size:unknowns] = jnp.zeros(
            (ROWS, unknowns - size), jnp.bfloat16
        )


def window_kernel(xs_ref, geom_ref, halo_ref, slip_ref, place_ref):
    clusters, rhs_count, unknowns = xs_ref.shape
    size = geom_ref.shape[2]
    slots = clusters + NEARC
    odd = lax.axis_index("row") % 2

    def place_of(cluster):
        return (cluster + NEARC * (1 - odd) + slots) % slots

    for cluster in range(clusters):
        slip_ref[place_of(cluster)] = xs_ref[cluster]
        place_ref[place_of(cluster)] = geom_ref[cluster]
    for turn in range(NEARC):
        at = place_of(clusters + turn)
        slip_ref[at] = halo_ref[turn, 0:rhs_count, :]
        pieces = halo_ref[turn, rhs_count : rhs_count + ROWS, 0:size].astype(jnp.float32)
        place_ref[at] = jnp.concatenate(
            [
                (pieces[3 * p + 2 : 3 * p + 3] + pieces[3 * p + 1 : 3 * p + 2])
                + pieces[3 * p : 3 * p + 1]
                for p in range(4)
            ],
            axis=0,
        )


def near_kernel(slip_ref, place_ref, after_ref, out_ref, cols_ref, even_ref, odd_ref):
    slots, rhs_count, unknowns = slip_ref.shape
    size = place_ref.shape[2]
    for place in range(slots):
        rows = jnp.concatenate([place_ref[place], jnp.zeros((4, size), jnp.float32)], axis=0)
        cols_ref[place] = rows.T
    right = [[place_ref[NEARC + u, p : p + 1, :] for p in range(4)] for u in range(NEARC)]
    parts = [(0, 0), (1, 1), (2, 2), (0, 1), (0, 2), (1, 2)]

    def fill(place, targets, block_ref):
        for step in range(size // ROWS):
            here = pl.ds(step * ROWS, ROWS)
            column = cols_ref[place, here, :]
            left = [jnp.broadcast_to(column[:, p : p + 1], (ROWS, size)) for p in range(4)]
            for u in targets:
                offset = [left[p] - right[u][p] for p in range(3)]
                radius_sq = offset[0] * offset[0] + offset[1] * offset[1] + offset[2] * offset[2]
                inverse = lax.rsqrt(radius_sq + soften)
                flat = (left[3] * right[u][3]) * inverse
                cubed = flat * (inverse * inverse)
                scaled = [offset[p] * cubed for p in range(3)]
                for part_id, (i, j) in enumerate(parts):
                    term = offset[i] * scaled[j]
                    if i == j:
                        term = term + flat
                    block_ref[u, part_id, here, :] = term.astype(jnp.bfloat16)

    def apply(place, targets, block_ref):
        slip = slip_ref[place]
        pieces = [slip[:, p * size : (p + 1) * size] for p in range(3)]
        for u in targets:
            sums = [
                jnp.dot(pieces[p], block_ref[u, p], preferred_element_type=jnp.float32)
                for p in range(3)
            ]
            for part_id in range(3, 6):
                i, j = parts[part_id]
                both = jnp.dot(
                    jnp.concatenate([pieces[j], pieces[i]], axis=0),
                    block_ref[u, part_id],
                    preferred_element_type=jnp.float32,
                )
                sums[i] = sums[i] + both[0:rhs_count]
                sums[j] = sums[j] + both[rhs_count : 2 * rhs_count]
            for p in range(3):
                out_ref[place, u, :, p * size : (p + 1) * size] = sums[p].astype(jnp.bfloat16)

    every = list(range(NEARC))
    fill(0, [0], even_ref)
    even_ref[1] = jnp.zeros(even_ref.shape[1:], jnp.bfloat16)

    def two_places(turn, carry):
        place = 2 * turn
        fill(place + 1, every, odd_ref)
        apply(place, every, even_ref)
        fill(place + 2, every, even_ref)
        apply(place + 1, every, odd_ref)
        return carry

    lax.fori_loop(0, (slots - 2) // 2, two_places, 0)
    fill(slots - 1, [NEARC - 1], odd_ref)
    apply(slots - 2, every, even_ref)
    apply(slots - 1, [NEARC - 1], odd_ref)
    out_ref[slots - 1, 0] = jnp.zeros(out_ref.shape[2:], jnp.bfloat16)


def far_kernel(pairs_ref, coeff_ref, coupling_ref, after_ref, out_ref, total_ref, *, clusters):
    long_count, rhs_count, _ = total_ref.shape
    rank_size = coupling_ref.shape[1]
    groups = LANES // rank_size
    group_id = lax.broadcasted_iota(jnp.int32, (rhs_count, LANES), 1) // rank_size
    total_ref[...] = jnp.zeros(total_ref.shape, jnp.float32)

    def coeff_of(cluster):
        whole = coeff_ref[(cluster % clusters) * long_count + cluster // clusters]
        whole = whole.astype(jnp.float32)
        return jnp.concatenate(
            [whole[:, 0:rank_size], whole[:, rank_size : 2 * rank_size]], axis=0
        ).astype(jnp.bfloat16)

    results = []
    for pair_id in range(pairs_ref.shape[1]):
        first = pairs_ref[0, pair_id]
        second = pairs_ref[1, pair_id]
        coupling = coupling_ref[pair_id]
        to_first = lax.dot_general(
            coeff_of(second),
            jnp.concatenate([coupling] * groups, axis=0),
            (((1,), (1,)), ((), ())),
            preferred_element_type=jnp.float32,
        )
        to_second = jnp.dot(
            coeff_of(first),
            jnp.concatenate([coupling] * groups, axis=1),
            preferred_element_type=jnp.float32,
        )
        results.append((first, to_first))
        results.append((second, to_second))
    for cluster, value in results:
        owner = cluster // clusters
        total_ref[owner] += jnp.where(group_id == cluster % clusters, value, 0.0)

    sent = total_ref[...].astype(jnp.bfloat16)
    for copy_id in range(out_ref.shape[0] // long_count):
        out_ref[copy_id * long_count : (copy_id + 1) * long_count] = sent


def finish_kernel(own_ref, other_ref, pay_ref, far_ref, basis_ref, out_ref, *, long_count):
    clusters, rank_size, unknowns = basis_ref.shape
    long_index = lax.axis_index("long")
    before = jnp.maximum(long_index - 1, 0)
    half = pay_ref.shape[1]
    counts = [jnp.zeros(pay_ref.shape[1:], jnp.float32) for _ in range(2)]
    for row in range(pay_ref.shape[0] // long_count):
        for source, owner in enumerate((long_index, before)):
            counts[source] += pay_ref[row * long_count + owner].astype(jnp.float32)
    total = jnp.sum(far_ref[...].astype(jnp.float32), axis=0)
    group_id = lax.broadcasted_iota(jnp.int32, total.shape, 1) // rank_size
    flat_basis = basis_ref[...].reshape(clusters * rank_size, unknowns)
    even = lax.axis_index("row") % 2 == 0
    for cluster in range(clusters):
        picked = jnp.where(group_id == cluster, total, 0.0).astype(jnp.bfloat16)
        result = jnp.dot(picked, flat_basis, preferred_element_type=jnp.float32)
        u = cluster % NEARC
        for turn in range(2 * NEARC + 1):
            reach = turn - NEARC
            lower = cluster + min(reach, 0)
            source = 0 if lower >= 0 else 1
            kind = (lower if lower >= 0 else lower + clusters) * (NEARC + 1) + abs(reach)
            lane = (2 + kind // half) * rank_size
            count = counts[source][kind % half : kind % half + 1, lane : lane + 1]
            mine, theirs = own_ref[u + turn, u], other_ref[u + turn, u]
            here = even if cluster < NEARC else jnp.logical_not(even)
            result = result + count * jnp.where(here, mine, theirs).astype(jnp.float32)
        out_ref[cluster] = result


def shards(slip, vertices, triangles, elem_map, near_pairs, near_count, far_pairs, far_coef, basis):
    clusters, rhs_count, unknowns = slip.shape
    rank_size = basis.shape[1]
    size = elem_map.shape[1]
    row_count = lax.axis_size("row")
    long_count = lax.axis_size("long")
    devices = row_count * long_count
    coupling = far_coef.reshape(-1, rank_size, rank_size)
    slots = clusters + NEARC

    pay = pl.pallas_call(
        coeffs_kernel,
        out_shape=jax.ShapeDtypeStruct((devices, rhs_count // 2, LANES), jnp.bfloat16),
        in_specs=[HBM] * 3 + [SMEM],
        out_specs=VMEM,
        scratch_shapes=[
            pltpu.VMEM(slip.shape[1:], slip.dtype),
            pltpu.VMEM(basis.shape[1:], basis.dtype),
            pltpu.VMEM(near_pairs.shape, near_pairs.dtype),
            pltpu.SemaphoreType.DMA((3,)),
        ],
        compiler_params=pltpu.CompilerParams(vmem_limit_bytes=16 << 20),
        name="coeffs",
    )(
        *[
            pltpu.with_memory_space_constraint(array, pltpu.HBM)
            for array in (slip, basis, near_pairs)
        ],
        near_count,
    )
    everyone = lax.all_to_all(pay, ("row", "long"), 0, 0, tiled=True)

    xs, to_neighbour, geometry = pl.pallas_call(
        geometry_kernel,
        out_shape=[
            jax.ShapeDtypeStruct(slip.shape, jnp.bfloat16),
            jax.ShapeDtypeStruct((NEARC, rhs_count + ROWS, unknowns), jnp.bfloat16),
            jax.ShapeDtypeStruct((clusters, 4, size), jnp.float32),
        ],
        in_specs=[VMEM] * 4 + [ANY],
        out_specs=[VMEM] * 3,
        compiler_params=pltpu.CompilerParams(vmem_limit_bytes=16 << 20),
        cost_estimate=pl.CostEstimate(
            flops=2_000_000, bytes_accessed=1_000_000, transcendentals=1_000
        ),
        name="geometry",
    )(slip, vertices, triangles, elem_map, pay)
    route = []
    for row in range(row_count):
        step = 1 if row % 2 == 0 else -1
        for owner in range(long_count):
            if 0 <= owner - step < long_count:
                route.append((row * long_count + owner - step, row * long_count + owner))
    halo = lax.ppermute(to_neighbour, ("row", "long"), route)

    window, places = pl.pallas_call(
        window_kernel,
        out_shape=[
            jax.ShapeDtypeStruct((slots, rhs_count, unknowns), jnp.bfloat16),
            jax.ShapeDtypeStruct((slots, 4, size), jnp.float32),
        ],
        in_specs=[VMEM] * 3,
        out_specs=[VMEM] * 2,
        compiler_params=pltpu.CompilerParams(vmem_limit_bytes=16 << 20),
        cost_estimate=pl.CostEstimate(
            flops=500_000_000, bytes_accessed=1_000_000, transcendentals=300_000
        ),
        name="window",
    )(xs, geometry, halo)

    far = pl.pallas_call(
        functools.partial(far_kernel, clusters=clusters),
        out_shape=jax.ShapeDtypeStruct((devices, rhs_count, clusters * rank_size), jnp.bfloat16),
        in_specs=[SMEM, VMEM, VMEM, ANY],
        out_specs=VMEM,
        scratch_shapes=[pltpu.VMEM((long_count, rhs_count, clusters * rank_size), jnp.float32)],
        compiler_params=pltpu.CompilerParams(vmem_limit_bytes=16 << 20),
        name="far",
    )(far_pairs, everyone, coupling, places)
    far_terms = lax.all_to_all(far, ("row", "long"), 0, 0, tiled=True)

    near = pl.pallas_call(
        near_kernel,
        out_shape=jax.ShapeDtypeStruct((slots, NEARC, rhs_count, unknowns), jnp.bfloat16),
        in_specs=[VMEM] * 2 + [ANY],
        out_specs=VMEM,
        scratch_shapes=[
            pltpu.VMEM((slots, size, 8), jnp.float32),
            pltpu.VMEM((NEARC, 6, size, size), jnp.bfloat16),
            pltpu.VMEM((NEARC, 6, size, size), jnp.bfloat16),
        ],
        compiler_params=pltpu.CompilerParams(vmem_limit_bytes=24 << 20),
        cost_estimate=pl.CostEstimate(
            flops=1_000_000_000, bytes_accessed=1_000_000, transcendentals=660_000
        ),
        name="near",
    )(window, places, far)
    partner = [(row, row ^ 1) for row in range(row_count)]
    other = lax.ppermute(near, "row", partner)

    return pl.pallas_call(
        functools.partial(finish_kernel, long_count=long_count),
        out_shape=jax.ShapeDtypeStruct(slip.shape, jnp.float32),
        in_specs=[VMEM] * 5,
        out_specs=VMEM,
        compiler_params=pltpu.CompilerParams(vmem_limit_bytes=16 << 20),
        name="finish",
    )(near, other, everyone, far_terms, basis)


def solution(mesh):
    placed = (
        P("long", None, None),
        P(None, "long"),
        P(None, "long"),
        P("long", None),
        P(None, ("row", "long")),
        P(("row", "long")),
        P(None, ("row", "long")),
        P(("row", "long"), None),
        P("long", None, None),
    )
    return jax.shard_map(
        shards, mesh=mesh, in_specs=placed, out_specs=P("long", None, None), check_vma=False
    )
```

```python
import functools

import jax
import jax.numpy as jnp
from jax import lax
from jax.experimental import pallas as pl
from jax.experimental.pallas import tpu as pltpu
from jax.sharding import PartitionSpec as P

NEARC = 2
LANES = 128
ROWS = 16

soften = 0.25

VMEM = pl.BlockSpec(memory_space=pltpu.VMEM)
SMEM = pl.BlockSpec(memory_space=pltpu.SMEM)
HBM = pl.BlockSpec(memory_space=pltpu.HBM)
ANY = pl.BlockSpec(memory_space=pl.ANY)


def lane_gather(table, index):
    length = table.shape[1]
    lane = index & (LANES - 1)
    chunk = index // LANES
    found = jnp.zeros(index.shape, table.dtype)
    for piece_id in range(-(-length // LANES)):
        piece = table[:, piece_id * LANES : min(length, (piece_id + 1) * LANES)]
        missing = LANES - piece.shape[1]
        if missing:
            piece = jnp.concatenate([piece, jnp.zeros((1, missing), table.dtype)], axis=1)
        picked = jnp.take_along_axis(jnp.broadcast_to(piece, index.shape), lane, axis=1)
        found = jnp.where(chunk == piece_id, picked, found)
    return found


def split_three(value):
    high = value.astype(jnp.bfloat16).astype(jnp.float32)
    rest = value - high
    middle = rest.astype(jnp.bfloat16).astype(jnp.float32)
    return [high, middle, rest - middle]


def coeffs_kernel(
    slip_hbm, basis_hbm, pairs_hbm, count_ref, pay_ref, slip_ref, basis_ref, pairs_ref, sems
):
    clusters = slip_hbm.shape[0]
    rhs_count = slip_ref.shape[0]
    rank_size = basis_ref.shape[0]
    mine = lax.axis_index("row") % clusters
    copies = [
        pltpu.make_async_copy(slip_hbm.at[mine], slip_ref, sems.at[0]),
        pltpu.make_async_copy(basis_hbm.at[mine], basis_ref, sems.at[1]),
        pltpu.make_async_copy(pairs_hbm, pairs_ref, sems.at[2]),
    ]
    for copy in copies:
        copy.start()
    for copy in copies:
        copy.wait()
    wide = jnp.concatenate([basis_ref[...]] * (LANES // rank_size), axis=0)
    coeffs = lax.dot_general(
        slip_ref[...].astype(jnp.bfloat16),
        wide,
        (((1,), (1,)), ((), ())),
        preferred_element_type=jnp.float32,
    )
    first = pairs_ref[0:1, :]
    kind = (first - lax.axis_index("long") * clusters) * (NEARC + 1) + pairs_ref[1:2, :] - first
    kinds = lax.broadcasted_iota(jnp.int32, (rhs_count, kind.shape[1]), 0)
    live = lax.broadcasted_iota(jnp.int32, kinds.shape, 1) < count_ref[0]
    counts = jnp.sum(jnp.where(live & (kinds == kind), 1.0, 0.0), axis=1, keepdims=True)
    lane_id = lax.broadcasted_iota(jnp.int32, coeffs.shape, 1)
    pay = jnp.where(lane_id < rank_size, coeffs, counts).astype(jnp.bfloat16)
    for target in range(pay_ref.shape[0]):
        pay_ref[target] = pay


def geometry_kernel(
    slip_ref, vertices_ref, triangles_ref, map_ref, after_ref, xs_ref, halo_ref, geom_ref
):
    clusters, rhs_count, unknowns = slip_ref.shape
    xs_ref[...] = slip_ref[...].astype(jnp.bfloat16)
    long_index = lax.axis_index("long")

    size = map_ref.shape[1]
    half = size // LANES
    slot_map = map_ref[...]
    index = jnp.concatenate(
        [slot_map[:, part * LANES : (part + 1) * LANES] for part in range(half)], axis=0
    )
    vertex_base = long_index * vertices_ref.shape[1]
    corners = []
    for corner_id in range(3):
        vertex = lane_gather(triangles_ref[corner_id : corner_id + 1, :], index) - vertex_base
        corners.append(
            [lane_gather(vertices_ref[axis_id : axis_id + 1, :], vertex) for axis_id in range(3)]
        )
    one, two, three = corners
    centre = [(one[a] + two[a] + three[a]) / 3.0 for a in range(3)]
    edge_one = [two[a] - one[a] for a in range(3)]
    edge_two = [three[a] - one[a] for a in range(3)]
    normal = [
        edge_one[1] * edge_two[2] - edge_one[2] * edge_two[1],
        edge_one[2] * edge_two[0] - edge_one[0] * edge_two[2],
        edge_one[0] * edge_two[1] - edge_one[1] * edge_two[0],
    ]
    area = 0.5 * jnp.sqrt(normal[0] * normal[0] + normal[1] * normal[1] + normal[2] * normal[2])
    geometry = []
    for value in centre + [area]:
        geometry.append(
            jnp.concatenate(
                [value[part * clusters : (part + 1) * clusters] for part in range(half)], axis=1
            )
        )
    for cluster in range(clusters):
        geom_ref[cluster] = jnp.concatenate(
            [whole[cluster : cluster + 1, :] for whole in geometry], axis=0
        )

    upward = lax.axis_index("row") % 2 == 0
    start = jnp.where(upward, clusters - NEARC, 0)
    pieces = [piece for whole in geometry for piece in split_three(whole)]
    for turn in range(NEARC):
        last = clusters - NEARC + turn
        rows = [
            jnp.where(upward, piece[last : last + 1, :], piece[turn : turn + 1, :])
            for piece in pieces
        ]
        rows.append(jnp.zeros((rhs_count - len(rows), size), jnp.float32))
        halo_ref[turn, :, 0:unknowns] = xs_ref[start + turn]
        halo_ref[turn, :, unknowns : unknowns + size] = jnp.concatenate(rows, axis=0).astype(
            jnp.bfloat16
        )


def window_kernel(xs_ref, geom_ref, halo_ref, slip_ref, place_ref):
    clusters, rhs_count, unknowns = xs_ref.shape
    size = geom_ref.shape[2]
    slots = clusters + NEARC
    odd = lax.axis_index("row") % 2

    def place_of(cluster):
        return (cluster + NEARC * (1 - odd) + slots) % slots

    for cluster in range(clusters):
        slip_ref[place_of(cluster)] = xs_ref[cluster]
        place_ref[place_of(cluster)] = geom_ref[cluster]
    for turn in range(NEARC):
        at = place_of(clusters + turn)
        slip_ref[at] = halo_ref[turn, :, 0:unknowns]
        pieces = halo_ref[turn, :, unknowns : unknowns + size].astype(jnp.float32)
        place_ref[at] = jnp.concatenate(
            [
                (pieces[3 * p + 2 : 3 * p + 3] + pieces[3 * p + 1 : 3 * p + 2])
                + pieces[3 * p : 3 * p + 1]
                for p in range(4)
            ],
            axis=0,
        )


def near_kernel(slip_ref, place_ref, out_ref, cols_ref, even_ref, odd_ref):
    slots, rhs_count, unknowns = slip_ref.shape
    size = place_ref.shape[2]
    for place in range(slots):
        rows = jnp.concatenate([place_ref[place], jnp.zeros((4, size), jnp.float32)], axis=0)
        cols_ref[place] = rows.T
    right = [[place_ref[NEARC + u, p : p + 1, :] for p in range(4)] for u in range(NEARC)]
    parts = [(0, 0), (1, 1), (2, 2), (0, 1), (0, 2), (1, 2)]

    def fill(place, targets, block_ref):
        for step in range(size // ROWS):
            here = pl.ds(step * ROWS, ROWS)
            column = cols_ref[place, here, :]
            left = [jnp.broadcast_to(column[:, p : p + 1], (ROWS, size)) for p in range(4)]
            for u in targets:
                offset = [left[p] - right[u][p] for p in range(3)]
                radius_sq = offset[0] * offset[0] + offset[1] * offset[1] + offset[2] * offset[2]
                inverse = lax.rsqrt(radius_sq + soften)
                flat = (left[3] * right[u][3]) * inverse
                cubed = flat * (inverse * inverse)
                scaled = [offset[p] * cubed for p in range(3)]
                for part_id, (i, j) in enumerate(parts):
                    term = offset[i] * scaled[j]
                    if i == j:
                        term = term + flat
                    block_ref[u, part_id, here, :] = term.astype(jnp.bfloat16)

    def apply(place, targets, block_ref):
        slip = slip_ref[place]
        pieces = [slip[:, p * size : (p + 1) * size] for p in range(3)]
        for u in targets:
            sums = [
                jnp.dot(pieces[p], block_ref[u, p], preferred_element_type=jnp.float32)
                for p in range(3)
            ]
            for part_id in range(3, 6):
                i, j = parts[part_id]
                both = jnp.dot(
                    jnp.concatenate([pieces[j], pieces[i]], axis=0),
                    block_ref[u, part_id],
                    preferred_element_type=jnp.float32,
                )
                sums[i] = sums[i] + both[0:rhs_count]
                sums[j] = sums[j] + both[rhs_count : 2 * rhs_count]
            for p in range(3):
                out_ref[place, u, :, p * size : (p + 1) * size] = sums[p].astype(jnp.bfloat16)

    every = list(range(NEARC))
    fill(0, [0], even_ref)
    even_ref[1] = jnp.zeros(even_ref.shape[1:], jnp.bfloat16)

    def two_places(turn, carry):
        place = 2 * turn
        fill(place + 1, every, odd_ref)
        apply(place, every, even_ref)
        fill(place + 2, every, even_ref)
        apply(place + 1, every, odd_ref)
        return carry

    lax.fori_loop(0, (slots - 2) // 2, two_places, 0)
    fill(slots - 1, [NEARC - 1], odd_ref)
    apply(slots - 2, every, even_ref)
    apply(slots - 1, [NEARC - 1], odd_ref)
    out_ref[slots - 1, 0] = jnp.zeros(out_ref.shape[2:], jnp.bfloat16)


def far_kernel(pairs_ref, coeff_ref, coupling_ref, after_ref, out_ref, total_ref, *, clusters):
    long_count, rhs_count, _ = total_ref.shape
    rank_size = coupling_ref.shape[1]
    groups = LANES // rank_size
    group_id = lax.broadcasted_iota(jnp.int32, (rhs_count, LANES), 1) // rank_size
    total_ref[...] = jnp.zeros(total_ref.shape, jnp.float32)

    def coeff_of(cluster):
        at = (cluster % clusters) * long_count + cluster // clusters
        return coeff_ref[at][:, 0:rank_size]

    results = []
    for pair_id in range(pairs_ref.shape[1]):
        first = pairs_ref[0, pair_id]
        second = pairs_ref[1, pair_id]
        coupling = coupling_ref[pair_id]
        to_first = lax.dot_general(
            coeff_of(second),
            jnp.concatenate([coupling] * groups, axis=0),
            (((1,), (1,)), ((), ())),
            preferred_element_type=jnp.float32,
        )
        to_second = jnp.dot(
            coeff_of(first),
            jnp.concatenate([coupling] * groups, axis=1),
            preferred_element_type=jnp.float32,
        )
        results.append((first, to_first))
        results.append((second, to_second))
    for cluster, value in results:
        owner = cluster // clusters
        total_ref[owner] += jnp.where(group_id == cluster % clusters, value, 0.0)

    sent = total_ref[...].astype(jnp.bfloat16)
    for copy_id in range(out_ref.shape[0] // long_count):
        out_ref[copy_id * long_count : (copy_id + 1) * long_count] = sent


def finish_kernel(own_ref, other_ref, pay_ref, far_ref, basis_ref, out_ref, *, long_count):
    clusters, rank_size, unknowns = basis_ref.shape
    long_index = lax.axis_index("long")
    before = jnp.maximum(long_index - 1, 0)
    counts = [jnp.zeros(pay_ref.shape[1:], jnp.float32) for _ in range(2)]
    for row in range(pay_ref.shape[0] // long_count):
        for source, owner in enumerate((long_index, before)):
            counts[source] += pay_ref[row * long_count + owner].astype(jnp.float32)
    total = jnp.sum(far_ref[...].astype(jnp.float32), axis=0)
    group_id = lax.broadcasted_iota(jnp.int32, total.shape, 1) // rank_size
    flat_basis = basis_ref[...].reshape(clusters * rank_size, unknowns)
    even = lax.axis_index("row") % 2 == 0
    for cluster in range(clusters):
        picked = jnp.where(group_id == cluster, total, 0.0).astype(jnp.bfloat16)
        result = jnp.dot(picked, flat_basis, preferred_element_type=jnp.float32)
        u = cluster % NEARC
        for turn in range(2 * NEARC + 1):
            reach = turn - NEARC
            lower = cluster + min(reach, 0)
            source = 0 if lower >= 0 else 1
            kind = (lower if lower >= 0 else lower + clusters) * (NEARC + 1) + abs(reach)
            count = counts[source][kind : kind + 1, LANES - 1 : LANES]
            mine, theirs = own_ref[u + turn, u], other_ref[u + turn, u]
            here = even if cluster < NEARC else jnp.logical_not(even)
            result = result + count * jnp.where(here, mine, theirs).astype(jnp.float32)
        out_ref[cluster] = result


def shards(slip, vertices, triangles, elem_map, near_pairs, near_count, far_pairs, far_coef, basis):
    clusters, rhs_count, unknowns = slip.shape
    rank_size = basis.shape[1]
    size = elem_map.shape[1]
    row_count = lax.axis_size("row")
    long_count = lax.axis_size("long")
    devices = row_count * long_count
    coupling = far_coef.reshape(-1, rank_size, rank_size)
    slots = clusters + NEARC

    pay = pl.pallas_call(
        coeffs_kernel,
        out_shape=jax.ShapeDtypeStruct((devices, rhs_count, LANES), jnp.bfloat16),
        in_specs=[HBM] * 3 + [SMEM],
        out_specs=VMEM,
        scratch_shapes=[
            pltpu.VMEM(slip.shape[1:], slip.dtype),
            pltpu.VMEM(basis.shape[1:], basis.dtype),
            pltpu.VMEM(near_pairs.shape, near_pairs.dtype),
            pltpu.SemaphoreType.DMA((3,)),
        ],
        compiler_params=pltpu.CompilerParams(vmem_limit_bytes=16 << 20),
        name="coeffs",
    )(
        *[
            pltpu.with_memory_space_constraint(array, pltpu.HBM)
            for array in (slip, basis, near_pairs)
        ],
        near_count,
    )
    everyone = lax.all_to_all(pay, ("row", "long"), 0, 0, tiled=True)

    xs, to_neighbour, geometry = pl.pallas_call(
        geometry_kernel,
        out_shape=[
            jax.ShapeDtypeStruct(slip.shape, jnp.bfloat16),
            jax.ShapeDtypeStruct((NEARC, rhs_count, unknowns + size), jnp.bfloat16),
            jax.ShapeDtypeStruct((clusters, 4, size), jnp.float32),
        ],
        in_specs=[VMEM] * 4 + [ANY],
        out_specs=[VMEM] * 3,
        compiler_params=pltpu.CompilerParams(vmem_limit_bytes=16 << 20),
        cost_estimate=pl.CostEstimate(
            flops=2_000_000, bytes_accessed=1_000_000, transcendentals=1_000
        ),
        name="geometry",
    )(slip, vertices, triangles, elem_map, pay)
    route = []
    for row in range(row_count):
        step = 1 if row % 2 == 0 else -1
        for owner in range(long_count):
            if 0 <= owner - step < long_count:
                route.append((row * long_count + owner - step, row * long_count + owner))
    halo = lax.ppermute(to_neighbour, ("row", "long"), route)

    window, places = pl.pallas_call(
        window_kernel,
        out_shape=[
            jax.ShapeDtypeStruct((slots, rhs_count, unknowns), jnp.bfloat16),
            jax.ShapeDtypeStruct((slots, 4, size), jnp.float32),
        ],
        in_specs=[VMEM] * 3,
        out_specs=[VMEM] * 2,
        compiler_params=pltpu.CompilerParams(vmem_limit_bytes=16 << 20),
        cost_estimate=pl.CostEstimate(flops=1000, bytes_accessed=1000, transcendentals=0),
        name="window",
    )(xs, geometry, halo)

    far = pl.pallas_call(
        functools.partial(far_kernel, clusters=clusters),
        out_shape=jax.ShapeDtypeStruct((devices, rhs_count, clusters * rank_size), jnp.bfloat16),
        in_specs=[SMEM, VMEM, VMEM, ANY],
        out_specs=VMEM,
        scratch_shapes=[pltpu.VMEM((long_count, rhs_count, clusters * rank_size), jnp.float32)],
        compiler_params=pltpu.CompilerParams(vmem_limit_bytes=16 << 20),
        name="far",
    )(far_pairs, everyone, coupling, places)
    far_terms = lax.all_to_all(far, ("row", "long"), 0, 0, tiled=True)

    near = pl.pallas_call(
        near_kernel,
        out_shape=jax.ShapeDtypeStruct((slots, NEARC, rhs_count, unknowns), jnp.bfloat16),
        in_specs=[VMEM] * 2,
        out_specs=VMEM,
        scratch_shapes=[
            pltpu.VMEM((slots, size, 8), jnp.float32),
            pltpu.VMEM((NEARC, 6, size, size), jnp.bfloat16),
            pltpu.VMEM((NEARC, 6, size, size), jnp.bfloat16),
        ],
        compiler_params=pltpu.CompilerParams(vmem_limit_bytes=24 << 20),
        cost_estimate=pl.CostEstimate(
            flops=1_000_000_000, bytes_accessed=1_000_000, transcendentals=660_000
        ),
        name="near",
    )(window, places)
    partner = [(row, row ^ 1) for row in range(row_count)]
    other = lax.ppermute(near, "row", partner)

    return pl.pallas_call(
        functools.partial(finish_kernel, long_count=long_count),
        out_shape=jax.ShapeDtypeStruct(slip.shape, jnp.float32),
        in_specs=[VMEM] * 5,
        out_specs=VMEM,
        compiler_params=pltpu.CompilerParams(vmem_limit_bytes=16 << 20),
        name="finish",
    )(near, other, everyone, far_terms, basis)


def solution(mesh):
    placed = (
        P("long", None, None),
        P(None, "long"),
        P(None, "long"),
        P("long", None),
        P(None, ("row", "long")),
        P(("row", "long")),
        P(None, ("row", "long")),
        P(("row", "long"), None),
        P("long", None, None),
    )
    return jax.shard_map(
        shards, mesh=mesh, in_specs=placed, out_specs=P("long", None, None), check_vma=False
    )
```

```python
import functools

import jax
import jax.numpy as jnp
from jax import lax
from jax.experimental import pallas as pl
from jax.experimental.pallas import tpu as pltpu
from jax.sharding import PartitionSpec as P

NEARC = 2
LANES = 128
ROWS = 16

soften = 0.25

VMEM = pl.BlockSpec(memory_space=pltpu.VMEM)
SMEM = pl.BlockSpec(memory_space=pltpu.SMEM)
HBM = pl.BlockSpec(memory_space=pltpu.HBM)
ANY = pl.BlockSpec(memory_space=pl.ANY)


def lane_gather(table, index):
    length = table.shape[1]
    lane = index & (LANES - 1)
    chunk = index // LANES
    found = jnp.zeros(index.shape, table.dtype)
    for piece_id in range(-(-length // LANES)):
        piece = table[:, piece_id * LANES : min(length, (piece_id + 1) * LANES)]
        missing = LANES - piece.shape[1]
        if missing:
            piece = jnp.concatenate([piece, jnp.zeros((1, missing), table.dtype)], axis=1)
        picked = jnp.take_along_axis(jnp.broadcast_to(piece, index.shape), lane, axis=1)
        found = jnp.where(chunk == piece_id, picked, found)
    return found


def split_three(value):
    high = value.astype(jnp.bfloat16).astype(jnp.float32)
    rest = value - high
    middle = rest.astype(jnp.bfloat16).astype(jnp.float32)
    return [high, middle, rest - middle]


def coeffs_kernel(
    slip_hbm, basis_hbm, pairs_hbm, count_ref, pay_ref, slip_ref, basis_ref, pairs_ref, sems
):
    clusters = slip_hbm.shape[0]
    rhs_count = slip_ref.shape[0]
    rank_size = basis_ref.shape[0]
    mine = lax.axis_index("row") % clusters
    copies = [
        pltpu.make_async_copy(slip_hbm.at[mine], slip_ref, sems.at[0]),
        pltpu.make_async_copy(basis_hbm.at[mine], basis_ref, sems.at[1]),
        pltpu.make_async_copy(pairs_hbm, pairs_ref, sems.at[2]),
    ]
    for copy in copies:
        copy.start()
    for copy in copies:
        copy.wait()
    wide = jnp.concatenate([basis_ref[...]] * (LANES // rank_size), axis=0)
    coeffs = lax.dot_general(
        slip_ref[...].astype(jnp.bfloat16),
        wide,
        (((1,), (1,)), ((), ())),
        preferred_element_type=jnp.float32,
    )
    first = pairs_ref[0:1, :]
    kind = (first - lax.axis_index("long") * clusters) * (NEARC + 1) + pairs_ref[1:2, :] - first
    kinds = lax.broadcasted_iota(jnp.int32, (rhs_count, kind.shape[1]), 0)
    live = lax.broadcasted_iota(jnp.int32, kinds.shape, 1) < count_ref[0]
    counts = jnp.sum(jnp.where(live & (kinds == kind), 1.0, 0.0), axis=1, keepdims=True)
    lane_id = lax.broadcasted_iota(jnp.int32, coeffs.shape, 1)
    pay = jnp.where(lane_id < rank_size, coeffs, counts).astype(jnp.bfloat16)
    for target in range(pay_ref.shape[0]):
        pay_ref[target] = pay


def geometry_kernel(
    slip_ref, vertices_ref, triangles_ref, map_ref, after_ref, xs_ref, halo_ref, geom_ref
):
    clusters, rhs_count, unknowns = slip_ref.shape
    xs_ref[...] = slip_ref[...].astype(jnp.bfloat16)
    long_index = lax.axis_index("long")

    size = map_ref.shape[1]
    half = size // LANES
    slot_map = map_ref[...]
    index = jnp.concatenate(
        [slot_map[:, part * LANES : (part + 1) * LANES] for part in range(half)], axis=0
    )
    vertex_base = long_index * vertices_ref.shape[1]
    corners = []
    for corner_id in range(3):
        vertex = lane_gather(triangles_ref[corner_id : corner_id + 1, :], index) - vertex_base
        corners.append(
            [lane_gather(vertices_ref[axis_id : axis_id + 1, :], vertex) for axis_id in range(3)]
        )
    one, two, three = corners
    centre = [(one[a] + two[a] + three[a]) / 3.0 for a in range(3)]
    edge_one = [two[a] - one[a] for a in range(3)]
    edge_two = [three[a] - one[a] for a in range(3)]
    normal = [
        edge_one[1] * edge_two[2] - edge_one[2] * edge_two[1],
        edge_one[2] * edge_two[0] - edge_one[0] * edge_two[2],
        edge_one[0] * edge_two[1] - edge_one[1] * edge_two[0],
    ]
    area = 0.5 * jnp.sqrt(normal[0] * normal[0] + normal[1] * normal[1] + normal[2] * normal[2])
    geometry = []
    for value in centre + [area]:
        geometry.append(
            jnp.concatenate(
                [value[part * clusters : (part + 1) * clusters] for part in range(half)], axis=1
            )
        )
    for cluster in range(clusters):
        geom_ref[cluster] = jnp.concatenate(
            [whole[cluster : cluster + 1, :] for whole in geometry], axis=0
        )

    upward = lax.axis_index("row") % 2 == 0
    start = jnp.where(upward, clusters - NEARC, 0)
    pieces = [piece for whole in geometry for piece in split_three(whole)]
    for turn in range(NEARC):
        last = clusters - NEARC + turn
        rows = [
            jnp.where(upward, piece[last : last + 1, :], piece[turn : turn + 1, :])
            for piece in pieces
        ]
        rows.append(jnp.zeros((rhs_count - len(rows), size), jnp.float32))
        halo_ref[turn, :, 0:unknowns] = xs_ref[start + turn]
        halo_ref[turn, :, unknowns : unknowns + size] = jnp.concatenate(rows, axis=0).astype(
            jnp.bfloat16
        )


def window_kernel(xs_ref, geom_ref, halo_ref, slip_ref, place_ref):
    clusters, rhs_count, unknowns = xs_ref.shape
    size = geom_ref.shape[2]
    slots = clusters + NEARC
    odd = lax.axis_index("row") % 2

    def place_of(cluster):
        return (cluster + NEARC * (1 - odd) + slots) % slots

    for cluster in range(clusters):
        slip_ref[place_of(cluster)] = xs_ref[cluster]
        place_ref[place_of(cluster)] = geom_ref[cluster]
    for turn in range(NEARC):
        at = place_of(clusters + turn)
        slip_ref[at] = halo_ref[turn, :, 0:unknowns]
        pieces = halo_ref[turn, :, unknowns : unknowns + size].astype(jnp.float32)
        place_ref[at] = jnp.concatenate(
            [
                (pieces[3 * p + 2 : 3 * p + 3] + pieces[3 * p + 1 : 3 * p + 2])
                + pieces[3 * p : 3 * p + 1]
                for p in range(4)
            ],
            axis=0,
        )


def near_kernel(slip_ref, place_ref, after_ref, out_ref, cols_ref, even_ref, odd_ref):
    slots, rhs_count, unknowns = slip_ref.shape
    size = place_ref.shape[2]
    for place in range(slots):
        rows = jnp.concatenate([place_ref[place], jnp.zeros((4, size), jnp.float32)], axis=0)
        cols_ref[place] = rows.T
    right = [[place_ref[NEARC + u, p : p + 1, :] for p in range(4)] for u in range(NEARC)]
    parts = [(0, 0), (1, 1), (2, 2), (0, 1), (0, 2), (1, 2)]

    def fill(place, targets, block_ref):
        for step in range(size // ROWS):
            here = pl.ds(step * ROWS, ROWS)
            column = cols_ref[place, here, :]
            left = [jnp.broadcast_to(column[:, p : p + 1], (ROWS, size)) for p in range(4)]
            for u in targets:
                offset = [left[p] - right[u][p] for p in range(3)]
                radius_sq = offset[0] * offset[0] + offset[1] * offset[1] + offset[2] * offset[2]
                inverse = lax.rsqrt(radius_sq + soften)
                flat = (left[3] * right[u][3]) * inverse
                cubed = flat * (inverse * inverse)
                scaled = [offset[p] * cubed for p in range(3)]
                for part_id, (i, j) in enumerate(parts):
                    term = offset[i] * scaled[j]
                    if i == j:
                        term = term + flat
                    block_ref[u, part_id, here, :] = term.astype(jnp.bfloat16)

    def apply(place, targets, block_ref):
        slip = slip_ref[place]
        pieces = [slip[:, p * size : (p + 1) * size] for p in range(3)]
        for u in targets:
            sums = [
                jnp.dot(pieces[p], block_ref[u, p], preferred_element_type=jnp.float32)
                for p in range(3)
            ]
            for part_id in range(3, 6):
                i, j = parts[part_id]
                both = jnp.dot(
                    jnp.concatenate([pieces[j], pieces[i]], axis=0),
                    block_ref[u, part_id],
                    preferred_element_type=jnp.float32,
                )
                sums[i] = sums[i] + both[0:rhs_count]
                sums[j] = sums[j] + both[rhs_count : 2 * rhs_count]
            for p in range(3):
                out_ref[place, u, :, p * size : (p + 1) * size] = sums[p].astype(jnp.bfloat16)

    every = list(range(NEARC))
    fill(0, [0], even_ref)
    even_ref[1] = jnp.zeros(even_ref.shape[1:], jnp.bfloat16)

    def two_places(turn, carry):
        place = 2 * turn
        fill(place + 1, every, odd_ref)
        apply(place, every, even_ref)
        fill(place + 2, every, even_ref)
        apply(place + 1, every, odd_ref)
        return carry

    lax.fori_loop(0, (slots - 2) // 2, two_places, 0)
    fill(slots - 1, [NEARC - 1], odd_ref)
    apply(slots - 2, every, even_ref)
    apply(slots - 1, [NEARC - 1], odd_ref)
    out_ref[slots - 1, 0] = jnp.zeros(out_ref.shape[2:], jnp.bfloat16)


def far_kernel(
    pairs_ref, coeff_ref, coupling_ref, after_ref, out_ref, done_ref, total_ref, *, clusters
):
    done_ref[...] = jnp.zeros(done_ref.shape, jnp.float32)
    long_count, rhs_count, _ = total_ref.shape
    rank_size = coupling_ref.shape[1]
    groups = LANES // rank_size
    group_id = lax.broadcasted_iota(jnp.int32, (rhs_count, LANES), 1) // rank_size
    total_ref[...] = jnp.zeros(total_ref.shape, jnp.float32)

    def coeff_of(cluster):
        at = (cluster % clusters) * long_count + cluster // clusters
        return coeff_ref[at][:, 0:rank_size]

    results = []
    for pair_id in range(pairs_ref.shape[1]):
        first = pairs_ref[0, pair_id]
        second = pairs_ref[1, pair_id]
        coupling = coupling_ref[pair_id]
        to_first = lax.dot_general(
            coeff_of(second),
            jnp.concatenate([coupling] * groups, axis=0),
            (((1,), (1,)), ((), ())),
            preferred_element_type=jnp.float32,
        )
        to_second = jnp.dot(
            coeff_of(first),
            jnp.concatenate([coupling] * groups, axis=1),
            preferred_element_type=jnp.float32,
        )
        results.append((first, to_first))
        results.append((second, to_second))
    for cluster, value in results:
        owner = cluster // clusters
        total_ref[owner] += jnp.where(group_id == cluster % clusters, value, 0.0)

    sent = total_ref[...].astype(jnp.bfloat16)
    for copy_id in range(out_ref.shape[0] // long_count):
        out_ref[copy_id * long_count : (copy_id + 1) * long_count] = sent


def weigh_kernel(own_ref, other_ref, pay_ref, out_ref, *, long_count):
    clusters = out_ref.shape[0]
    long_index = lax.axis_index("long")
    before = jnp.maximum(long_index - 1, 0)
    counts = [jnp.zeros(pay_ref.shape[1:], jnp.float32) for _ in range(2)]
    for row in range(pay_ref.shape[0] // long_count):
        for source, owner in enumerate((long_index, before)):
            counts[source] += pay_ref[row * long_count + owner].astype(jnp.float32)
    even = lax.axis_index("row") % 2 == 0
    for cluster in range(clusters):
        result = jnp.zeros(out_ref.shape[1:], jnp.float32)
        u = cluster % NEARC
        for turn in range(2 * NEARC + 1):
            reach = turn - NEARC
            lower = cluster + min(reach, 0)
            source = 0 if lower >= 0 else 1
            kind = (lower if lower >= 0 else lower + clusters) * (NEARC + 1) + abs(reach)
            count = counts[source][kind : kind + 1, LANES - 1 : LANES]
            mine, theirs = own_ref[u + turn, u], other_ref[u + turn, u]
            here = even if cluster < NEARC else jnp.logical_not(even)
            result = result + count * jnp.where(here, mine, theirs).astype(jnp.float32)
        out_ref[cluster] = result


def finish_kernel(near_ref, far_ref, basis_ref, out_ref):
    clusters, rank_size, unknowns = basis_ref.shape
    total = jnp.sum(far_ref[...].astype(jnp.float32), axis=0)
    group_id = lax.broadcasted_iota(jnp.int32, total.shape, 1) // rank_size
    flat_basis = basis_ref[...].reshape(clusters * rank_size, unknowns)
    for cluster in range(clusters):
        picked = jnp.where(group_id == cluster, total, 0.0).astype(jnp.bfloat16)
        result = jnp.dot(picked, flat_basis, preferred_element_type=jnp.float32)
        out_ref[cluster] = result + near_ref[cluster]


def shards(slip, vertices, triangles, elem_map, near_pairs, near_count, far_pairs, far_coef, basis):
    clusters, rhs_count, unknowns = slip.shape
    rank_size = basis.shape[1]
    size = elem_map.shape[1]
    row_count = lax.axis_size("row")
    long_count = lax.axis_size("long")
    devices = row_count * long_count
    coupling = far_coef.reshape(-1, rank_size, rank_size)
    slots = clusters + NEARC

    pay = pl.pallas_call(
        coeffs_kernel,
        out_shape=jax.ShapeDtypeStruct((devices, rhs_count, LANES), jnp.bfloat16),
        in_specs=[HBM] * 3 + [SMEM],
        out_specs=VMEM,
        scratch_shapes=[
            pltpu.VMEM(slip.shape[1:], slip.dtype),
            pltpu.VMEM(basis.shape[1:], basis.dtype),
            pltpu.VMEM(near_pairs.shape, near_pairs.dtype),
            pltpu.SemaphoreType.DMA((3,)),
        ],
        compiler_params=pltpu.CompilerParams(vmem_limit_bytes=16 << 20),
        name="coeffs",
    )(
        *[
            pltpu.with_memory_space_constraint(array, pltpu.HBM)
            for array in (slip, basis, near_pairs)
        ],
        near_count,
    )
    everyone = lax.all_to_all(pay, ("row", "long"), 0, 0, tiled=True)

    xs, to_neighbour, geometry = pl.pallas_call(
        geometry_kernel,
        out_shape=[
            jax.ShapeDtypeStruct(slip.shape, jnp.bfloat16),
            jax.ShapeDtypeStruct((NEARC, rhs_count, unknowns + size), jnp.bfloat16),
            jax.ShapeDtypeStruct((clusters, 4, size), jnp.float32),
        ],
        in_specs=[VMEM] * 4 + [ANY],
        out_specs=[VMEM] * 3,
        compiler_params=pltpu.CompilerParams(vmem_limit_bytes=16 << 20),
        cost_estimate=pl.CostEstimate(
            flops=2_000_000, bytes_accessed=1_000_000, transcendentals=1_000
        ),
        name="geometry",
    )(slip, vertices, triangles, elem_map, pay)
    route = []
    for row in range(row_count):
        step = 1 if row % 2 == 0 else -1
        for owner in range(long_count):
            if 0 <= owner - step < long_count:
                route.append((row * long_count + owner - step, row * long_count + owner))
    halo = lax.ppermute(to_neighbour, ("row", "long"), route)

    window, places = pl.pallas_call(
        window_kernel,
        out_shape=[
            jax.ShapeDtypeStruct((slots, rhs_count, unknowns), jnp.bfloat16),
            jax.ShapeDtypeStruct((slots, 4, size), jnp.float32),
        ],
        in_specs=[VMEM] * 3,
        out_specs=[VMEM] * 2,
        compiler_params=pltpu.CompilerParams(vmem_limit_bytes=16 << 20),
        cost_estimate=pl.CostEstimate(flops=1000, bytes_accessed=1000, transcendentals=0),
        name="window",
    )(xs, geometry, halo)

    far, far_done = pl.pallas_call(
        functools.partial(far_kernel, clusters=clusters),
        out_shape=[
            jax.ShapeDtypeStruct((devices, rhs_count, clusters * rank_size), jnp.bfloat16),
            jax.ShapeDtypeStruct((8, LANES), jnp.float32),
        ],
        in_specs=[SMEM, VMEM, VMEM, ANY],
        out_specs=[VMEM] * 2,
        scratch_shapes=[pltpu.VMEM((long_count, rhs_count, clusters * rank_size), jnp.float32)],
        compiler_params=pltpu.CompilerParams(vmem_limit_bytes=16 << 20),
        name="far",
    )(far_pairs, everyone, coupling, places)
    far_terms = lax.all_to_all(far, ("row", "long"), 0, 0, tiled=True)

    near = pl.pallas_call(
        near_kernel,
        out_shape=jax.ShapeDtypeStruct((slots, NEARC, rhs_count, unknowns), jnp.bfloat16),
        in_specs=[VMEM] * 2 + [ANY],
        out_specs=VMEM,
        scratch_shapes=[
            pltpu.VMEM((slots, size, 8), jnp.float32),
            pltpu.VMEM((NEARC, 6, size, size), jnp.bfloat16),
            pltpu.VMEM((NEARC, 6, size, size), jnp.bfloat16),
        ],
        compiler_params=pltpu.CompilerParams(vmem_limit_bytes=24 << 20),
        cost_estimate=pl.CostEstimate(
            flops=1_000_000_000, bytes_accessed=1_000_000, transcendentals=660_000
        ),
        name="near",
    )(window, places, far_done)
    partner = [(row, row ^ 1) for row in range(row_count)]
    other = lax.ppermute(near, "row", partner)

    near_field = pl.pallas_call(
        functools.partial(weigh_kernel, long_count=long_count),
        out_shape=jax.ShapeDtypeStruct(slip.shape, jnp.float32),
        in_specs=[VMEM] * 3,
        out_specs=VMEM,
        compiler_params=pltpu.CompilerParams(vmem_limit_bytes=16 << 20),
        cost_estimate=pl.CostEstimate(
            flops=500_000_000, bytes_accessed=1_000_000, transcendentals=0
        ),
        name="weigh",
    )(near, other, everyone)

    return pl.pallas_call(
        finish_kernel,
        out_shape=jax.ShapeDtypeStruct(slip.shape, jnp.float32),
        in_specs=[VMEM] * 3,
        out_specs=VMEM,
        compiler_params=pltpu.CompilerParams(vmem_limit_bytes=16 << 20),
        name="finish",
    )(near_field, far_terms, basis)


def solution(mesh):
    placed = (
        P("long", None, None),
        P(None, "long"),
        P(None, "long"),
        P("long", None),
        P(None, ("row", "long")),
        P(("row", "long")),
        P(None, ("row", "long")),
        P(("row", "long"), None),
        P("long", None, None),
    )
    return jax.shard_map(
        shards, mesh=mesh, in_specs=placed, out_specs=P("long", None, None), check_vma=False
    )
```

```python
import functools

import jax
import jax.numpy as jnp
from jax import lax
from jax.experimental import pallas as pl
from jax.experimental.pallas import tpu as pltpu
from jax.sharding import PartitionSpec as P

NEARC = 2
LANES = 128
ROWS = 16

soften = 0.25

VMEM = pl.BlockSpec(memory_space=pltpu.VMEM)
SMEM = pl.BlockSpec(memory_space=pltpu.SMEM)
HBM = pl.BlockSpec(memory_space=pltpu.HBM)
ANY = pl.BlockSpec(memory_space=pl.ANY)


def lane_gather(table, index):
    length = table.shape[1]
    lane = index & (LANES - 1)
    chunk = index // LANES
    found = jnp.zeros(index.shape, table.dtype)
    for piece_id in range(-(-length // LANES)):
        piece = table[:, piece_id * LANES : min(length, (piece_id + 1) * LANES)]
        missing = LANES - piece.shape[1]
        if missing:
            piece = jnp.concatenate([piece, jnp.zeros((1, missing), table.dtype)], axis=1)
        picked = jnp.take_along_axis(jnp.broadcast_to(piece, index.shape), lane, axis=1)
        found = jnp.where(chunk == piece_id, picked, found)
    return found


def split_three(value):
    high = value.astype(jnp.bfloat16).astype(jnp.float32)
    rest = value - high
    middle = rest.astype(jnp.bfloat16).astype(jnp.float32)
    return [high, middle, rest - middle]


def coeffs_kernel(
    slip_hbm, basis_hbm, pairs_hbm, count_ref, pay_ref, slip_ref, basis_ref, pairs_ref, sems
):
    clusters = slip_hbm.shape[0]
    rhs_count = slip_ref.shape[0]
    rank_size = basis_ref.shape[0]
    mine = lax.axis_index("row") % clusters
    copies = [
        pltpu.make_async_copy(slip_hbm.at[mine], slip_ref, sems.at[0]),
        pltpu.make_async_copy(basis_hbm.at[mine], basis_ref, sems.at[1]),
        pltpu.make_async_copy(pairs_hbm, pairs_ref, sems.at[2]),
    ]
    for copy in copies:
        copy.start()
    for copy in copies:
        copy.wait()
    wide = jnp.concatenate([basis_ref[...]] * (LANES // rank_size), axis=0)
    coeffs = lax.dot_general(
        slip_ref[...].astype(jnp.bfloat16),
        wide,
        (((1,), (1,)), ((), ())),
        preferred_element_type=jnp.float32,
    )
    first = pairs_ref[0:1, :]
    kind = (first - lax.axis_index("long") * clusters) * (NEARC + 1) + pairs_ref[1:2, :] - first
    kinds = lax.broadcasted_iota(jnp.int32, (rhs_count, kind.shape[1]), 0)
    live = lax.broadcasted_iota(jnp.int32, kinds.shape, 1) < count_ref[0]
    counts = jnp.sum(jnp.where(live & (kinds == kind), 1.0, 0.0), axis=1, keepdims=True)
    lane_id = lax.broadcasted_iota(jnp.int32, coeffs.shape, 1)
    pay = jnp.where(lane_id < rank_size, coeffs, counts).astype(jnp.bfloat16)
    for target in range(pay_ref.shape[0]):
        pay_ref[target] = pay


def geometry_kernel(
    slip_ref, vertices_ref, triangles_ref, map_ref, after_ref, xs_ref, halo_ref, geom_ref
):
    clusters, rhs_count, unknowns = slip_ref.shape
    xs_ref[...] = slip_ref[...].astype(jnp.bfloat16)
    long_index = lax.axis_index("long")

    size = map_ref.shape[1]
    half = size // LANES
    slot_map = map_ref[...]
    index = jnp.concatenate(
        [slot_map[:, part * LANES : (part + 1) * LANES] for part in range(half)], axis=0
    )
    vertex_base = long_index * vertices_ref.shape[1]
    corners = []
    for corner_id in range(3):
        vertex = lane_gather(triangles_ref[corner_id : corner_id + 1, :], index) - vertex_base
        corners.append(
            [lane_gather(vertices_ref[axis_id : axis_id + 1, :], vertex) for axis_id in range(3)]
        )
    one, two, three = corners
    centre = [(one[a] + two[a] + three[a]) / 3.0 for a in range(3)]
    edge_one = [two[a] - one[a] for a in range(3)]
    edge_two = [three[a] - one[a] for a in range(3)]
    normal = [
        edge_one[1] * edge_two[2] - edge_one[2] * edge_two[1],
        edge_one[2] * edge_two[0] - edge_one[0] * edge_two[2],
        edge_one[0] * edge_two[1] - edge_one[1] * edge_two[0],
    ]
    area = 0.5 * jnp.sqrt(normal[0] * normal[0] + normal[1] * normal[1] + normal[2] * normal[2])
    geometry = []
    for value in centre + [area]:
        geometry.append(
            jnp.concatenate(
                [value[part * clusters : (part + 1) * clusters] for part in range(half)], axis=1
            )
        )
    for cluster in range(clusters):
        geom_ref[cluster] = jnp.concatenate(
            [whole[cluster : cluster + 1, :] for whole in geometry], axis=0
        )

    upward = lax.axis_index("row") % 2 == 0
    start = jnp.where(upward, clusters - NEARC, 0)
    pieces = [piece for whole in geometry for piece in split_three(whole)]
    for turn in range(NEARC):
        last = clusters - NEARC + turn
        rows = [
            jnp.where(upward, piece[last : last + 1, :], piece[turn : turn + 1, :])
            for piece in pieces
        ]
        rows.append(jnp.zeros((rhs_count - len(rows), size), jnp.float32))
        halo_ref[turn, :, 0:unknowns] = xs_ref[start + turn]
        halo_ref[turn, :, unknowns : unknowns + size] = jnp.concatenate(rows, axis=0).astype(
            jnp.bfloat16
        )


def window_kernel(xs_ref, geom_ref, halo_ref, slip_ref, place_ref):
    clusters, rhs_count, unknowns = xs_ref.shape
    size = geom_ref.shape[2]
    slots = clusters + NEARC
    odd = lax.axis_index("row") % 2

    def place_of(cluster):
        return (cluster + NEARC * (1 - odd) + slots) % slots

    for cluster in range(clusters):
        slip_ref[place_of(cluster)] = xs_ref[cluster]
        place_ref[place_of(cluster)] = geom_ref[cluster]
    for turn in range(NEARC):
        at = place_of(clusters + turn)
        slip_ref[at] = halo_ref[turn, :, 0:unknowns]
        pieces = halo_ref[turn, :, unknowns : unknowns + size].astype(jnp.float32)
        place_ref[at] = jnp.concatenate(
            [
                (pieces[3 * p + 2 : 3 * p + 3] + pieces[3 * p + 1 : 3 * p + 2])
                + pieces[3 * p : 3 * p + 1]
                for p in range(4)
            ],
            axis=0,
        )


def near_kernel(
    slip_ref, place_ref, pay_ref, after_ref, out_ref, cols_ref, even_ref, odd_ref, *, long_count, clusters
):
    slots, rhs_count, unknowns = slip_ref.shape
    size = place_ref.shape[2]
    long_index = lax.axis_index("long")
    before = jnp.maximum(long_index - 1, 0)
    totals = [jnp.zeros(pay_ref.shape[1:], jnp.float32) for _ in range(2)]
    for row in range(pay_ref.shape[0] // long_count):
        for source, owner in enumerate((long_index, before)):
            totals[source] += pay_ref[row * long_count + owner].astype(jnp.float32)
    even = lax.axis_index("row") % 2 == 0
    kinds = lax.broadcasted_iota(jnp.int32, (rhs_count, LANES), 0)

    def count_of(place, u):
        both = []
        for cluster in (u, clusters - NEARC + u):
            reach = place - u - NEARC
            lower = cluster + jnp.minimum(reach, 0)
            inside = lower >= 0
            kind = jnp.where(inside, lower, lower + clusters) * (NEARC + 1) + jnp.abs(reach)
            source = jnp.where(inside, totals[0], totals[1])
            both.append(jnp.sum(jnp.where(kinds == kind, source, 0.0), axis=0, keepdims=True))
        return jnp.where(even, both[0], both[1])[:, LANES - 1 : LANES]

    out_ref[...] = jnp.zeros(out_ref.shape, jnp.float32)
    for place in range(slots):
        rows = jnp.concatenate([place_ref[place], jnp.zeros((4, size), jnp.float32)], axis=0)
        cols_ref[place] = rows.T
    right = [[place_ref[NEARC + u, p : p + 1, :] for p in range(4)] for u in range(NEARC)]
    parts = [(0, 0), (1, 1), (2, 2), (0, 1), (0, 2), (1, 2)]

    def fill(place, targets, block_ref):
        for step in range(size // ROWS):
            here = pl.ds(step * ROWS, ROWS)
            column = cols_ref[place, here, :]
            left = [jnp.broadcast_to(column[:, p : p + 1], (ROWS, size)) for p in range(4)]
            for u in targets:
                offset = [left[p] - right[u][p] for p in range(3)]
                radius_sq = offset[0] * offset[0] + offset[1] * offset[1] + offset[2] * offset[2]
                inverse = lax.rsqrt(radius_sq + soften)
                flat = (left[3] * right[u][3]) * inverse
                cubed = flat * (inverse * inverse)
                scaled = [offset[p] * cubed for p in range(3)]
                for part_id, (i, j) in enumerate(parts):
                    term = offset[i] * scaled[j]
                    if i == j:
                        term = term + flat
                    block_ref[u, part_id, here, :] = term.astype(jnp.bfloat16)

    def apply(place, targets, block_ref):
        slip = slip_ref[place]
        pieces = [slip[:, p * size : (p + 1) * size] for p in range(3)]
        for u in targets:
            count = count_of(place, u)
            sums = [
                jnp.dot(pieces[p], block_ref[u, p], preferred_element_type=jnp.float32)
                for p in range(3)
            ]
            for part_id in range(3, 6):
                i, j = parts[part_id]
                both = jnp.dot(
                    jnp.concatenate([pieces[j], pieces[i]], axis=0),
                    block_ref[u, part_id],
                    preferred_element_type=jnp.float32,
                )
                sums[i] = sums[i] + both[0:rhs_count]
                sums[j] = sums[j] + both[rhs_count : 2 * rhs_count]
            for p in range(3):
                out_ref[u, :, p * size : (p + 1) * size] += count * sums[p]

    every = list(range(NEARC))
    fill(0, [0], even_ref)
    for u in range(1, NEARC):
        even_ref[u] = jnp.zeros(even_ref.shape[1:], jnp.bfloat16)

    def two_places(turn, carry):
        place = 2 * turn
        fill(place + 1, every, odd_ref)
        apply(place, every, even_ref)
        fill(place + 2, every, even_ref)
        apply(place + 1, every, odd_ref)
        return carry

    lax.fori_loop(0, (slots - 2) // 2, two_places, 0)
    fill(slots - 1, [NEARC - 1], odd_ref)
    apply(slots - 2, every, even_ref)
    apply(slots - 1, [NEARC - 1], odd_ref)


def far_kernel(
    pairs_ref, coeff_ref, coupling_ref, out_ref, done_ref, total_ref, *, clusters
):
    done_ref[...] = jnp.zeros(done_ref.shape, jnp.float32)
    long_count, rhs_count, _ = total_ref.shape
    rank_size = coupling_ref.shape[1]
    groups = LANES // rank_size
    group_id = lax.broadcasted_iota(jnp.int32, (rhs_count, LANES), 1) // rank_size
    total_ref[...] = jnp.zeros(total_ref.shape, jnp.float32)

    def coeff_of(cluster):
        at = (cluster % clusters) * long_count + cluster // clusters
        return coeff_ref[at][:, 0:rank_size]

    results = []
    for pair_id in range(pairs_ref.shape[1]):
        first = pairs_ref[0, pair_id]
        second = pairs_ref[1, pair_id]
        coupling = coupling_ref[pair_id]
        to_first = lax.dot_general(
            coeff_of(second),
            jnp.concatenate([coupling] * groups, axis=0),
            (((1,), (1,)), ((), ())),
            preferred_element_type=jnp.float32,
        )
        to_second = jnp.dot(
            coeff_of(first),
            jnp.concatenate([coupling] * groups, axis=1),
            preferred_element_type=jnp.float32,
        )
        results.append((first, to_first))
        results.append((second, to_second))
    for cluster, value in results:
        owner = cluster // clusters
        total_ref[owner] += jnp.where(group_id == cluster % clusters, value, 0.0)

    sent = total_ref[...].astype(jnp.bfloat16)
    for copy_id in range(out_ref.shape[0] // long_count):
        out_ref[copy_id * long_count : (copy_id + 1) * long_count] = sent


def finish_kernel(own_ref, other_ref, far_ref, basis_ref, out_ref):
    clusters, rank_size, unknowns = basis_ref.shape
    total = jnp.sum(far_ref[...].astype(jnp.float32), axis=0)
    group_id = lax.broadcasted_iota(jnp.int32, total.shape, 1) // rank_size
    flat_basis = basis_ref[...].reshape(clusters * rank_size, unknowns)
    even = lax.axis_index("row") % 2 == 0
    for cluster in range(clusters):
        u = cluster % NEARC
        here = even if cluster < NEARC else jnp.logical_not(even)
        near = jnp.where(here, own_ref[u], other_ref[u])
        picked = jnp.where(group_id == cluster, total, 0.0).astype(jnp.bfloat16)
        result = jnp.dot(picked, flat_basis, preferred_element_type=jnp.float32)
        out_ref[cluster] = result + near


def shards(slip, vertices, triangles, elem_map, near_pairs, near_count, far_pairs, far_coef, basis):
    clusters, rhs_count, unknowns = slip.shape
    rank_size = basis.shape[1]
    size = elem_map.shape[1]
    row_count = lax.axis_size("row")
    long_count = lax.axis_size("long")
    devices = row_count * long_count
    coupling = far_coef.reshape(-1, rank_size, rank_size)
    slots = clusters + NEARC

    pay = pl.pallas_call(
        coeffs_kernel,
        out_shape=jax.ShapeDtypeStruct((devices, rhs_count, LANES), jnp.bfloat16),
        in_specs=[HBM] * 3 + [SMEM],
        out_specs=VMEM,
        scratch_shapes=[
            pltpu.VMEM(slip.shape[1:], slip.dtype),
            pltpu.VMEM(basis.shape[1:], basis.dtype),
            pltpu.VMEM(near_pairs.shape, near_pairs.dtype),
            pltpu.SemaphoreType.DMA((3,)),
        ],
        compiler_params=pltpu.CompilerParams(vmem_limit_bytes=16 << 20),
        name="coeffs",
    )(
        *[
            pltpu.with_memory_space_constraint(array, pltpu.HBM)
            for array in (slip, basis, near_pairs)
        ],
        near_count,
    )
    everyone = lax.all_to_all(pay, ("row", "long"), 0, 0, tiled=True)

    xs, to_neighbour, geometry = pl.pallas_call(
        geometry_kernel,
        out_shape=[
            jax.ShapeDtypeStruct(slip.shape, jnp.bfloat16),
            jax.ShapeDtypeStruct((NEARC, rhs_count, unknowns + size), jnp.bfloat16),
            jax.ShapeDtypeStruct((clusters, 4, size), jnp.float32),
        ],
        in_specs=[VMEM] * 4 + [ANY],
        out_specs=[VMEM] * 3,
        compiler_params=pltpu.CompilerParams(vmem_limit_bytes=16 << 20),
        cost_estimate=pl.CostEstimate(
            flops=2_000_000, bytes_accessed=1_000_000, transcendentals=1_000
        ),
        name="geometry",
    )(slip, vertices, triangles, elem_map, pay)
    route = []
    for row in range(row_count):
        step = 1 if row % 2 == 0 else -1
        for owner in range(long_count):
            if 0 <= owner - step < long_count:
                route.append((row * long_count + owner - step, row * long_count + owner))
    halo = lax.ppermute(to_neighbour, ("row", "long"), route)

    window, places = pl.pallas_call(
        window_kernel,
        out_shape=[
            jax.ShapeDtypeStruct((slots, rhs_count, unknowns), jnp.bfloat16),
            jax.ShapeDtypeStruct((slots, 4, size), jnp.float32),
        ],
        in_specs=[VMEM] * 3,
        out_specs=[VMEM] * 2,
        compiler_params=pltpu.CompilerParams(vmem_limit_bytes=16 << 20),
        cost_estimate=pl.CostEstimate(flops=1000, bytes_accessed=1000, transcendentals=0),
        name="window",
    )(xs, geometry, halo)

    far, far_done = pl.pallas_call(
        functools.partial(far_kernel, clusters=clusters),
        out_shape=[
            jax.ShapeDtypeStruct((devices, rhs_count, clusters * rank_size), jnp.bfloat16),
            jax.ShapeDtypeStruct((8, LANES), jnp.float32),
        ],
        in_specs=[SMEM, VMEM, VMEM],
        out_specs=[VMEM] * 2,
        scratch_shapes=[pltpu.VMEM((long_count, rhs_count, clusters * rank_size), jnp.float32)],
        compiler_params=pltpu.CompilerParams(vmem_limit_bytes=16 << 20),
        name="far",
    )(far_pairs, everyone, coupling)
    far_terms = lax.all_to_all(far, ("row", "long"), 0, 0, tiled=True)

    near = pl.pallas_call(
        functools.partial(near_kernel, long_count=long_count, clusters=clusters),
        out_shape=jax.ShapeDtypeStruct((NEARC, rhs_count, unknowns), jnp.float32),
        in_specs=[VMEM] * 3 + [ANY],
        out_specs=VMEM,
        scratch_shapes=[
            pltpu.VMEM((slots, size, 8), jnp.float32),
            pltpu.VMEM((NEARC, 6, size, size), jnp.bfloat16),
            pltpu.VMEM((NEARC, 6, size, size), jnp.bfloat16),
        ],
        compiler_params=pltpu.CompilerParams(vmem_limit_bytes=24 << 20),
        cost_estimate=pl.CostEstimate(
            flops=1_000_000_000, bytes_accessed=1_000_000, transcendentals=660_000
        ),
        name="near",
    )(window, places, everyone, far_done)
    partner = [(row, row ^ 1) for row in range(row_count)]
    other = lax.ppermute(near, "row", partner)

    return pl.pallas_call(
        finish_kernel,
        out_shape=jax.ShapeDtypeStruct(slip.shape, jnp.float32),
        in_specs=[VMEM] * 4,
        out_specs=VMEM,
        compiler_params=pltpu.CompilerParams(vmem_limit_bytes=16 << 20),
        name="finish",
    )(near, other, far_terms, basis)


def solution(mesh):
    placed = (
        P("long", None, None),
        P(None, "long"),
        P(None, "long"),
        P("long", None),
        P(None, ("row", "long")),
        P(("row", "long")),
        P(None, ("row", "long")),
        P(("row", "long"), None),
        P("long", None, None),
    )
    return jax.shard_map(
        shards, mesh=mesh, in_specs=placed, out_specs=P("long", None, None), check_vma=False
    )
```

```python
import functools

import jax
import jax.numpy as jnp
from jax import lax
from jax.experimental import pallas as pl
from jax.experimental.pallas import tpu as pltpu
from jax.sharding import PartitionSpec as P

NEARC = 2
LANES = 128
ROWS = 16

soften = 0.25

VMEM = pl.BlockSpec(memory_space=pltpu.VMEM)
SMEM = pl.BlockSpec(memory_space=pltpu.SMEM)
HBM = pl.BlockSpec(memory_space=pltpu.HBM)
ANY = pl.BlockSpec(memory_space=pl.ANY)


def lane_gather(table, index):
    length = table.shape[1]
    lane = index & (LANES - 1)
    chunk = index // LANES
    found = jnp.zeros(index.shape, table.dtype)
    for piece_id in range(-(-length // LANES)):
        piece = table[:, piece_id * LANES : min(length, (piece_id + 1) * LANES)]
        missing = LANES - piece.shape[1]
        if missing:
            piece = jnp.concatenate([piece, jnp.zeros((1, missing), table.dtype)], axis=1)
        picked = jnp.take_along_axis(jnp.broadcast_to(piece, index.shape), lane, axis=1)
        found = jnp.where(chunk == piece_id, picked, found)
    return found


def split_three(value):
    high = value.astype(jnp.bfloat16).astype(jnp.float32)
    rest = value - high
    middle = rest.astype(jnp.bfloat16).astype(jnp.float32)
    return [high, middle, rest - middle]


def coeffs_kernel(
    slip_hbm, basis_hbm, pairs_hbm, count_ref, pay_ref, slip_ref, basis_ref, pairs_ref, sems
):
    clusters = slip_hbm.shape[0]
    rhs_count = slip_ref.shape[0]
    rank_size = basis_ref.shape[0]
    mine = lax.axis_index("row") % clusters
    copies = [
        pltpu.make_async_copy(slip_hbm.at[mine], slip_ref, sems.at[0]),
        pltpu.make_async_copy(basis_hbm.at[mine], basis_ref, sems.at[1]),
        pltpu.make_async_copy(pairs_hbm, pairs_ref, sems.at[2]),
    ]
    for copy in copies:
        copy.start()
    for copy in copies:
        copy.wait()
    half = rhs_count // 2
    wide = jnp.concatenate([basis_ref[...]] * (LANES // rank_size), axis=0)
    coeffs = lax.dot_general(
        slip_ref[...].astype(jnp.bfloat16),
        wide,
        (((1,), (1,)), ((), ())),
        preferred_element_type=jnp.float32,
    )
    first = pairs_ref[0:1, :]
    kind = (first - lax.axis_index("long") * clusters) * (NEARC + 1) + pairs_ref[1:2, :] - first
    kinds = lax.broadcasted_iota(jnp.int32, (half, kind.shape[1]), 0)
    live = lax.broadcasted_iota(jnp.int32, kinds.shape, 1) < count_ref[0]
    low = jnp.sum(jnp.where(live & (kinds == kind), 1.0, 0.0), axis=1, keepdims=True)
    high = jnp.sum(jnp.where(live & (kinds + half == kind), 1.0, 0.0), axis=1, keepdims=True)
    group = lax.broadcasted_iota(jnp.int32, (half, LANES), 1) // rank_size
    pay = jnp.where(
        group == 0, coeffs[0:half], jnp.where(group == 1, coeffs[half:], jnp.where(group == 2, low, high))
    ).astype(jnp.bfloat16)
    for target in range(pay_ref.shape[0]):
        pay_ref[target] = pay


def geometry_kernel(
    slip_ref, vertices_ref, triangles_ref, map_ref, after_ref, xs_ref, halo_ref, geom_ref
):
    clusters, rhs_count, unknowns = slip_ref.shape
    xs_ref[...] = slip_ref[...].astype(jnp.bfloat16)
    long_index = lax.axis_index("long")

    size = map_ref.shape[1]
    half = size // LANES
    slot_map = map_ref[...]
    index = jnp.concatenate(
        [slot_map[:, part * LANES : (part + 1) * LANES] for part in range(half)], axis=0
    )
    vertex_base = long_index * vertices_ref.shape[1]
    corners = []
    for corner_id in range(3):
        vertex = lane_gather(triangles_ref[corner_id : corner_id + 1, :], index) - vertex_base
        corners.append(
            [lane_gather(vertices_ref[axis_id : axis_id + 1, :], vertex) for axis_id in range(3)]
        )
    one, two, three = corners
    centre = [(one[a] + two[a] + three[a]) / 3.0 for a in range(3)]
    edge_one = [two[a] - one[a] for a in range(3)]
    edge_two = [three[a] - one[a] for a in range(3)]
    normal = [
        edge_one[1] * edge_two[2] - edge_one[2] * edge_two[1],
        edge_one[2] * edge_two[0] - edge_one[0] * edge_two[2],
        edge_one[0] * edge_two[1] - edge_one[1] * edge_two[0],
    ]
    area = 0.5 * jnp.sqrt(normal[0] * normal[0] + normal[1] * normal[1] + normal[2] * normal[2])
    geometry = []
    for value in centre + [area]:
        geometry.append(
            jnp.concatenate(
                [value[part * clusters : (part + 1) * clusters] for part in range(half)], axis=1
            )
        )
    for cluster in range(clusters):
        geom_ref[cluster] = jnp.concatenate(
            [whole[cluster : cluster + 1, :] for whole in geometry], axis=0
        )

    upward = lax.axis_index("row") % 2 == 0
    start = jnp.where(upward, clusters - NEARC, 0)
    pieces = [piece for whole in geometry for piece in split_three(whole)]
    for turn in range(NEARC):
        last = clusters - NEARC + turn
        rows = [
            jnp.where(upward, piece[last : last + 1, :], piece[turn : turn + 1, :])
            for piece in pieces
        ]
        rows.append(jnp.zeros((rhs_count - len(rows), size), jnp.float32))
        halo_ref[turn, :, 0:unknowns] = xs_ref[start + turn]
        halo_ref[turn, :, unknowns : unknowns + size] = jnp.concatenate(rows, axis=0).astype(
            jnp.bfloat16
        )


def window_kernel(xs_ref, geom_ref, halo_ref, slip_ref, place_ref):
    clusters, rhs_count, unknowns = xs_ref.shape
    size = geom_ref.shape[2]
    slots = clusters + NEARC
    odd = lax.axis_index("row") % 2

    def place_of(cluster):
        return (cluster + NEARC * (1 - odd) + slots) % slots

    for cluster in range(clusters):
        slip_ref[place_of(cluster)] = xs_ref[cluster]
        place_ref[place_of(cluster)] = geom_ref[cluster]
    for turn in range(NEARC):
        at = place_of(clusters + turn)
        slip_ref[at] = halo_ref[turn, :, 0:unknowns]
        pieces = halo_ref[turn, :, unknowns : unknowns + size].astype(jnp.float32)
        place_ref[at] = jnp.concatenate(
            [
                (pieces[3 * p + 2 : 3 * p + 3] + pieces[3 * p + 1 : 3 * p + 2])
                + pieces[3 * p : 3 * p + 1]
                for p in range(4)
            ],
            axis=0,
        )


def near_kernel(
    slip_ref, place_ref, pay_ref, after_ref, out_ref, cols_ref, even_ref, odd_ref, *, long_count, clusters
):
    slots, rhs_count, unknowns = slip_ref.shape
    size = place_ref.shape[2]
    long_index = lax.axis_index("long")
    before = jnp.maximum(long_index - 1, 0)
    totals = [jnp.zeros(pay_ref.shape[1:], jnp.float32) for _ in range(2)]
    for row in range(pay_ref.shape[0] // long_count):
        for source, owner in enumerate((long_index, before)):
            totals[source] += pay_ref[row * long_count + owner].astype(jnp.float32)
    even = lax.axis_index("row") % 2 == 0
    half = pay_ref.shape[1]
    rank_size = pay_ref.shape[2] // 4
    group = lax.broadcasted_iota(jnp.int32, (half, LANES), 1) // rank_size
    kinds = lax.broadcasted_iota(jnp.int32, (half, LANES), 0) + jnp.where(group == 3, half, 0)
    kinds = jnp.where(group < 2, -1, kinds)
    lane_id = lax.broadcasted_iota(jnp.int32, (half, LANES), 1)
    kinds = jnp.where(lane_id % rank_size == 0, kinds, -1)

    def count_of(place, u):
        both = []
        for cluster in (u, clusters - NEARC + u):
            reach = place - u - NEARC
            lower = cluster + jnp.minimum(reach, 0)
            inside = lower >= 0
            kind = jnp.where(inside, lower, lower + clusters) * (NEARC + 1) + jnp.abs(reach)
            source = jnp.where(inside, totals[0], totals[1])
            both.append(jnp.where(kinds == kind, source, 0.0))
        picked = jnp.sum(jnp.where(even, both[0], both[1]), axis=0, keepdims=True)
        return jnp.sum(picked, axis=1, keepdims=True)

    out_ref[...] = jnp.zeros(out_ref.shape, jnp.float32)
    for place in range(slots):
        rows = jnp.concatenate([place_ref[place], jnp.zeros((4, size), jnp.float32)], axis=0)
        cols_ref[place] = rows.T
    right = [[place_ref[NEARC + u, p : p + 1, :] for p in range(4)] for u in range(NEARC)]
    parts = [(0, 0), (1, 1), (2, 2), (0, 1), (0, 2), (1, 2)]

    def fill(place, targets, block_ref):
        for step in range(size // ROWS):
            here = pl.ds(step * ROWS, ROWS)
            column = cols_ref[place, here, :]
            left = [jnp.broadcast_to(column[:, p : p + 1], (ROWS, size)) for p in range(4)]
            for u in targets:
                offset = [left[p] - right[u][p] for p in range(3)]
                radius_sq = offset[0] * offset[0] + offset[1] * offset[1] + offset[2] * offset[2]
                inverse = lax.rsqrt(radius_sq + soften)
                flat = (left[3] * right[u][3]) * inverse
                cubed = flat * (inverse * inverse)
                scaled = [offset[p] * cubed for p in range(3)]
                for part_id, (i, j) in enumerate(parts):
                    term = offset[i] * scaled[j]
                    if i == j:
                        term = term + flat
                    block_ref[u, part_id, here, :] = term.astype(jnp.bfloat16)

    def apply(place, targets, block_ref):
        slip = slip_ref[place]
        pieces = [slip[:, p * size : (p + 1) * size] for p in range(3)]
        for u in targets:
            count = count_of(place, u)
            sums = [
                jnp.dot(pieces[p], block_ref[u, p], preferred_element_type=jnp.float32)
                for p in range(3)
            ]
            for part_id in range(3, 6):
                i, j = parts[part_id]
                both = jnp.dot(
                    jnp.concatenate([pieces[j], pieces[i]], axis=0),
                    block_ref[u, part_id],
                    preferred_element_type=jnp.float32,
                )
                sums[i] = sums[i] + both[0:rhs_count]
                sums[j] = sums[j] + both[rhs_count : 2 * rhs_count]
            for p in range(3):
                out_ref[u, :, p * size : (p + 1) * size] += count * sums[p]

    every = list(range(NEARC))
    fill(0, [0], even_ref)
    for u in range(1, NEARC):
        even_ref[u] = jnp.zeros(even_ref.shape[1:], jnp.bfloat16)

    def two_places(turn, carry):
        place = 2 * turn
        fill(place + 1, every, odd_ref)
        apply(place, every, even_ref)
        fill(place + 2, every, even_ref)
        apply(place + 1, every, odd_ref)
        return carry

    lax.fori_loop(0, (slots - 2) // 2, two_places, 0)
    fill(slots - 1, [NEARC - 1], odd_ref)
    apply(slots - 2, every, even_ref)
    apply(slots - 1, [NEARC - 1], odd_ref)


def far_kernel(
    pairs_ref, coeff_ref, coupling_ref, out_ref, done_ref, total_ref, *, clusters
):
    done_ref[...] = jnp.zeros(done_ref.shape, jnp.float32)
    long_count, rhs_count, _ = total_ref.shape
    rank_size = coupling_ref.shape[1]
    groups = LANES // rank_size
    group_id = lax.broadcasted_iota(jnp.int32, (rhs_count, LANES), 1) // rank_size
    total_ref[...] = jnp.zeros(total_ref.shape, jnp.float32)

    def coeff_of(cluster):
        whole = coeff_ref[(cluster % clusters) * long_count + cluster // clusters]
        whole = whole.astype(jnp.float32)
        return jnp.concatenate(
            [whole[:, 0:rank_size], whole[:, rank_size : 2 * rank_size]], axis=0
        ).astype(jnp.bfloat16)

    results = []
    for pair_id in range(pairs_ref.shape[1]):
        first = pairs_ref[0, pair_id]
        second = pairs_ref[1, pair_id]
        coupling = coupling_ref[pair_id]
        to_first = lax.dot_general(
            coeff_of(second),
            jnp.concatenate([coupling] * groups, axis=0),
            (((1,), (1,)), ((), ())),
            preferred_element_type=jnp.float32,
        )
        to_second = jnp.dot(
            coeff_of(first),
            jnp.concatenate([coupling] * groups, axis=1),
            preferred_element_type=jnp.float32,
        )
        results.append((first, to_first))
        results.append((second, to_second))
    for cluster, value in results:
        owner = cluster // clusters
        total_ref[owner] += jnp.where(group_id == cluster % clusters, value, 0.0)

    sent = total_ref[...].astype(jnp.bfloat16)
    for copy_id in range(out_ref.shape[0] // long_count):
        out_ref[copy_id * long_count : (copy_id + 1) * long_count] = sent


def finish_kernel(own_ref, other_ref, far_ref, basis_ref, out_ref):
    clusters, rank_size, unknowns = basis_ref.shape
    total = jnp.sum(far_ref[...].astype(jnp.float32), axis=0)
    group_id = lax.broadcasted_iota(jnp.int32, total.shape, 1) // rank_size
    flat_basis = basis_ref[...].reshape(clusters * rank_size, unknowns)
    even = lax.axis_index("row") % 2 == 0
    for cluster in range(clusters):
        u = cluster % NEARC
        here = even if cluster < NEARC else jnp.logical_not(even)
        near = jnp.where(here, own_ref[u], other_ref[u])
        picked = jnp.where(group_id == cluster, total, 0.0).astype(jnp.bfloat16)
        result = jnp.dot(picked, flat_basis, preferred_element_type=jnp.float32)
        out_ref[cluster] = result + near


def shards(slip, vertices, triangles, elem_map, near_pairs, near_count, far_pairs, far_coef, basis):
    clusters, rhs_count, unknowns = slip.shape
    rank_size = basis.shape[1]
    size = elem_map.shape[1]
    row_count = lax.axis_size("row")
    long_count = lax.axis_size("long")
    devices = row_count * long_count
    coupling = far_coef.reshape(-1, rank_size, rank_size)
    slots = clusters + NEARC

    pay = pl.pallas_call(
        coeffs_kernel,
        out_shape=pltpu.VMEM((devices, rhs_count // 2, LANES), jnp.bfloat16),
        in_specs=[HBM] * 3 + [SMEM],
        out_specs=VMEM,
        scratch_shapes=[
            pltpu.VMEM(slip.shape[1:], slip.dtype),
            pltpu.VMEM(basis.shape[1:], basis.dtype),
            pltpu.VMEM(near_pairs.shape, near_pairs.dtype),
            pltpu.SemaphoreType.DMA((3,)),
        ],
        compiler_params=pltpu.CompilerParams(vmem_limit_bytes=16 << 20),
        name="coeffs",
    )(
        *[
            pltpu.with_memory_space_constraint(array, pltpu.HBM)
            for array in (slip, basis, near_pairs)
        ],
        near_count,
    )
    everyone = lax.all_to_all(pay, ("row", "long"), 0, 0, tiled=True)

    xs, to_neighbour, geometry = pl.pallas_call(
        geometry_kernel,
        out_shape=[
            jax.ShapeDtypeStruct(slip.shape, jnp.bfloat16),
            jax.ShapeDtypeStruct((NEARC, rhs_count, unknowns + size), jnp.bfloat16),
            jax.ShapeDtypeStruct((clusters, 4, size), jnp.float32),
        ],
        in_specs=[VMEM] * 4 + [ANY],
        out_specs=[VMEM] * 3,
        compiler_params=pltpu.CompilerParams(vmem_limit_bytes=16 << 20),
        cost_estimate=pl.CostEstimate(
            flops=2_000_000, bytes_accessed=1_000_000, transcendentals=1_000
        ),
        name="geometry",
    )(slip, vertices, triangles, elem_map, pay)
    route = []
    for row in range(row_count):
        step = 1 if row % 2 == 0 else -1
        for owner in range(long_count):
            if 0 <= owner - step < long_count:
                route.append((row * long_count + owner - step, row * long_count + owner))
    halo = lax.ppermute(to_neighbour, ("row", "long"), route)

    window, places = pl.pallas_call(
        window_kernel,
        out_shape=[
            jax.ShapeDtypeStruct((slots, rhs_count, unknowns), jnp.bfloat16),
            jax.ShapeDtypeStruct((slots, 4, size), jnp.float32),
        ],
        in_specs=[VMEM] * 3,
        out_specs=[VMEM] * 2,
        compiler_params=pltpu.CompilerParams(vmem_limit_bytes=16 << 20),
        cost_estimate=pl.CostEstimate(flops=1000, bytes_accessed=1000, transcendentals=0),
        name="window",
    )(xs, geometry, halo)

    far, far_done = pl.pallas_call(
        functools.partial(far_kernel, clusters=clusters),
        out_shape=[
            pltpu.VMEM((devices, rhs_count, clusters * rank_size), jnp.bfloat16),
            jax.ShapeDtypeStruct((8, LANES), jnp.float32),
        ],
        in_specs=[SMEM, VMEM, VMEM],
        out_specs=[VMEM] * 2,
        scratch_shapes=[pltpu.VMEM((long_count, rhs_count, clusters * rank_size), jnp.float32)],
        compiler_params=pltpu.CompilerParams(vmem_limit_bytes=16 << 20),
        name="far",
    )(far_pairs, everyone, coupling)
    far_terms = lax.all_to_all(far, ("row", "long"), 0, 0, tiled=True)

    near = pl.pallas_call(
        functools.partial(near_kernel, long_count=long_count, clusters=clusters),
        out_shape=jax.ShapeDtypeStruct((NEARC, rhs_count, unknowns), jnp.float32),
        in_specs=[VMEM] * 3 + [ANY],
        out_specs=VMEM,
        scratch_shapes=[
            pltpu.VMEM((slots, size, 8), jnp.float32),
            pltpu.VMEM((NEARC, 6, size, size), jnp.bfloat16),
            pltpu.VMEM((NEARC, 6, size, size), jnp.bfloat16),
        ],
        compiler_params=pltpu.CompilerParams(vmem_limit_bytes=24 << 20),
        cost_estimate=pl.CostEstimate(
            flops=1_000_000_000, bytes_accessed=1_000_000, transcendentals=660_000
        ),
        name="near",
    )(window, places, everyone, far_done)
    partner = [(row, row ^ 1) for row in range(row_count)]
    other = lax.ppermute(near, "row", partner)

    return pl.pallas_call(
        finish_kernel,
        out_shape=jax.ShapeDtypeStruct(slip.shape, jnp.float32),
        in_specs=[VMEM] * 4,
        out_specs=VMEM,
        compiler_params=pltpu.CompilerParams(vmem_limit_bytes=16 << 20),
        name="finish",
    )(near, other, far_terms, basis)


def solution(mesh):
    placed = (
        P("long", None, None),
        P(None, "long"),
        P(None, "long"),
        P("long", None),
        P(None, ("row", "long")),
        P(("row", "long")),
        P(None, ("row", "long")),
        P(("row", "long"), None),
        P("long", None, None),
    )
    return jax.shard_map(
        shards, mesh=mesh, in_specs=placed, out_specs=P("long", None, None), check_vma=False
    )
```

```python
import functools

import jax
import jax.numpy as jnp
from jax import lax
from jax.experimental import pallas as pl
from jax.experimental.pallas import tpu as pltpu
from jax.sharding import PartitionSpec as P

NEARC = 2
LANES = 128
ROWS = 16

soften = 0.25

VMEM = pl.BlockSpec(memory_space=pltpu.VMEM)
SMEM = pl.BlockSpec(memory_space=pltpu.SMEM)
HBM = pl.BlockSpec(memory_space=pltpu.HBM)
ANY = pl.BlockSpec(memory_space=pl.ANY)


def lane_gather(table, index):
    length = table.shape[1]
    lane = index & (LANES - 1)
    chunk = index // LANES
    found = jnp.zeros(index.shape, table.dtype)
    for piece_id in range(-(-length // LANES)):
        piece = table[:, piece_id * LANES : min(length, (piece_id + 1) * LANES)]
        missing = LANES - piece.shape[1]
        if missing:
            piece = jnp.concatenate([piece, jnp.zeros((1, missing), table.dtype)], axis=1)
        picked = jnp.take_along_axis(jnp.broadcast_to(piece, index.shape), lane, axis=1)
        found = jnp.where(chunk == piece_id, picked, found)
    return found


def split_three(value):
    high = value.astype(jnp.bfloat16).astype(jnp.float32)
    rest = value - high
    middle = rest.astype(jnp.bfloat16).astype(jnp.float32)
    return [high, middle, rest - middle]


def coeffs_kernel(
    slip_hbm, basis_hbm, pairs_hbm, count_ref, pay_ref, slip_ref, basis_ref, pairs_ref, sems
):
    clusters = slip_hbm.shape[0]
    rhs_count = slip_ref.shape[0]
    rank_size = basis_ref.shape[0]
    mine = lax.axis_index("row") % clusters
    copies = [
        pltpu.make_async_copy(slip_hbm.at[mine], slip_ref, sems.at[0]),
        pltpu.make_async_copy(basis_hbm.at[mine], basis_ref, sems.at[1]),
        pltpu.make_async_copy(pairs_hbm, pairs_ref, sems.at[2]),
    ]
    for copy in copies:
        copy.start()
    for copy in copies:
        copy.wait()
    half = rhs_count // 2
    wide = jnp.concatenate([basis_ref[...]] * (LANES // rank_size), axis=0)
    coeffs = lax.dot_general(
        slip_ref[...].astype(jnp.bfloat16),
        wide,
        (((1,), (1,)), ((), ())),
        preferred_element_type=jnp.float32,
    )
    first = pairs_ref[0:1, :]
    kind = (first - lax.axis_index("long") * clusters) * (NEARC + 1) + pairs_ref[1:2, :] - first
    kinds = lax.broadcasted_iota(jnp.int32, (half, kind.shape[1]), 0)
    live = lax.broadcasted_iota(jnp.int32, kinds.shape, 1) < count_ref[0]
    low = jnp.sum(jnp.where(live & (kinds == kind), 1.0, 0.0), axis=1, keepdims=True)
    high = jnp.sum(jnp.where(live & (kinds + half == kind), 1.0, 0.0), axis=1, keepdims=True)
    group = lax.broadcasted_iota(jnp.int32, (half, LANES), 1) // rank_size
    pay = jnp.where(
        group == 0, coeffs[0:half], jnp.where(group == 1, coeffs[half:], jnp.where(group == 2, low, high))
    ).astype(jnp.bfloat16)
    for target in range(pay_ref.shape[0]):
        pay_ref[target] = pay


def geometry_kernel(
    slip_ref, vertices_ref, triangles_ref, map_ref, after_ref, xs_ref, halo_ref, geom_ref
):
    clusters, rhs_count, unknowns = slip_ref.shape
    xs_ref[...] = slip_ref[...].astype(jnp.bfloat16)
    long_index = lax.axis_index("long")

    size = map_ref.shape[1]
    half = size // LANES
    slot_map = map_ref[...]
    index = jnp.concatenate(
        [slot_map[:, part * LANES : (part + 1) * LANES] for part in range(half)], axis=0
    )
    vertex_base = long_index * vertices_ref.shape[1]
    corners = []
    for corner_id in range(3):
        vertex = lane_gather(triangles_ref[corner_id : corner_id + 1, :], index) - vertex_base
        corners.append(
            [lane_gather(vertices_ref[axis_id : axis_id + 1, :], vertex) for axis_id in range(3)]
        )
    one, two, three = corners
    centre = [(one[a] + two[a] + three[a]) / 3.0 for a in range(3)]
    edge_one = [two[a] - one[a] for a in range(3)]
    edge_two = [three[a] - one[a] for a in range(3)]
    normal = [
        edge_one[1] * edge_two[2] - edge_one[2] * edge_two[1],
        edge_one[2] * edge_two[0] - edge_one[0] * edge_two[2],
        edge_one[0] * edge_two[1] - edge_one[1] * edge_two[0],
    ]
    area = 0.5 * jnp.sqrt(normal[0] * normal[0] + normal[1] * normal[1] + normal[2] * normal[2])
    geometry = []
    for value in centre + [area]:
        geometry.append(
            jnp.concatenate(
                [value[part * clusters : (part + 1) * clusters] for part in range(half)], axis=1
            )
        )
    for cluster in range(clusters):
        geom_ref[cluster] = jnp.concatenate(
            [whole[cluster : cluster + 1, :] for whole in geometry], axis=0
        )

    upward = lax.axis_index("row") % 2 == 0
    start = jnp.where(upward, clusters - NEARC, 0)
    pieces = [piece for whole in geometry for piece in split_three(whole)]
    for turn in range(NEARC):
        last = clusters - NEARC + turn
        rows = [
            jnp.where(upward, piece[last : last + 1, :], piece[turn : turn + 1, :])
            for piece in pieces
        ]
        rows.append(jnp.zeros((rhs_count - len(rows), size), jnp.float32))
        halo_ref[turn, :, 0:unknowns] = xs_ref[start + turn]
        halo_ref[turn, :, unknowns : unknowns + size] = jnp.concatenate(rows, axis=0).astype(
            jnp.bfloat16
        )


def window_kernel(xs_ref, geom_ref, halo_ref, slip_ref, place_ref):
    clusters, rhs_count, unknowns = xs_ref.shape
    size = geom_ref.shape[2]
    slots = clusters + NEARC
    odd = lax.axis_index("row") % 2

    def place_of(cluster):
        return (cluster + NEARC * (1 - odd) + slots) % slots

    for cluster in range(clusters):
        slip_ref[place_of(cluster)] = xs_ref[cluster]
        place_ref[place_of(cluster)] = geom_ref[cluster]
    for turn in range(NEARC):
        at = place_of(clusters + turn)
        slip_ref[at] = halo_ref[turn, :, 0:unknowns]
        pieces = halo_ref[turn, :, unknowns : unknowns + size].astype(jnp.float32)
        place_ref[at] = jnp.concatenate(
            [
                (pieces[3 * p + 2 : 3 * p + 3] + pieces[3 * p + 1 : 3 * p + 2])
                + pieces[3 * p : 3 * p + 1]
                for p in range(4)
            ],
            axis=0,
        )


def near_kernel(
    slip_ref, place_ref, pay_ref, after_ref, out_ref, cols_ref, even_ref, odd_ref, *, long_count, clusters
):
    slots, rhs_count, unknowns = slip_ref.shape
    size = place_ref.shape[2]
    long_index = lax.axis_index("long")
    before = jnp.maximum(long_index - 1, 0)
    totals = [jnp.zeros(pay_ref.shape[1:], jnp.float32) for _ in range(2)]
    row_count = pay_ref.shape[0] // long_count
    for row in range(row_count):
        for source, owner in enumerate((long_index, before)):
            totals[source] += pay_ref[owner * row_count + row].astype(jnp.float32)
    even = lax.axis_index("row") % 2 == 0
    half = pay_ref.shape[1]
    rank_size = pay_ref.shape[2] // 4
    group = lax.broadcasted_iota(jnp.int32, (half, LANES), 1) // rank_size
    kinds = lax.broadcasted_iota(jnp.int32, (half, LANES), 0) + jnp.where(group == 3, half, 0)
    kinds = jnp.where(group < 2, -1, kinds)
    lane_id = lax.broadcasted_iota(jnp.int32, (half, LANES), 1)
    kinds = jnp.where(lane_id % rank_size == 0, kinds, -1)

    def count_of(place, u):
        both = []
        for cluster in (u, clusters - NEARC + u):
            reach = place - u - NEARC
            lower = cluster + jnp.minimum(reach, 0)
            inside = lower >= 0
            kind = jnp.where(inside, lower, lower + clusters) * (NEARC + 1) + jnp.abs(reach)
            source = jnp.where(inside, totals[0], totals[1])
            both.append(jnp.where(kinds == kind, source, 0.0))
        picked = jnp.sum(jnp.where(even, both[0], both[1]), axis=0, keepdims=True)
        return jnp.sum(picked, axis=1, keepdims=True)

    out_ref[...] = jnp.zeros(out_ref.shape, jnp.float32)
    for place in range(slots):
        rows = jnp.concatenate([place_ref[place], jnp.zeros((4, size), jnp.float32)], axis=0)
        cols_ref[place] = rows.T
    right = [[place_ref[NEARC + u, p : p + 1, :] for p in range(4)] for u in range(NEARC)]
    parts = [(0, 0), (1, 1), (2, 2), (0, 1), (0, 2), (1, 2)]

    def fill(place, targets, block_ref):
        for step in range(size // ROWS):
            here = pl.ds(step * ROWS, ROWS)
            column = cols_ref[place, here, :]
            left = [jnp.broadcast_to(column[:, p : p + 1], (ROWS, size)) for p in range(4)]
            for u in targets:
                offset = [left[p] - right[u][p] for p in range(3)]
                radius_sq = offset[0] * offset[0] + offset[1] * offset[1] + offset[2] * offset[2]
                inverse = lax.rsqrt(radius_sq + soften)
                flat = (left[3] * right[u][3]) * inverse
                cubed = flat * (inverse * inverse)
                scaled = [offset[p] * cubed for p in range(3)]
                for part_id, (i, j) in enumerate(parts):
                    term = offset[i] * scaled[j]
                    if i == j:
                        term = term + flat
                    block_ref[u, part_id, here, :] = term.astype(jnp.bfloat16)

    def apply(place, targets, block_ref):
        slip = slip_ref[place]
        pieces = [slip[:, p * size : (p + 1) * size] for p in range(3)]
        for u in targets:
            count = count_of(place, u)
            sums = [
                jnp.dot(pieces[p], block_ref[u, p], preferred_element_type=jnp.float32)
                for p in range(3)
            ]
            for part_id in range(3, 6):
                i, j = parts[part_id]
                both = jnp.dot(
                    jnp.concatenate([pieces[j], pieces[i]], axis=0),
                    block_ref[u, part_id],
                    preferred_element_type=jnp.float32,
                )
                sums[i] = sums[i] + both[0:rhs_count]
                sums[j] = sums[j] + both[rhs_count : 2 * rhs_count]
            for p in range(3):
                out_ref[u, :, p * size : (p + 1) * size] += count * sums[p]

    every = list(range(NEARC))
    fill(0, [0], even_ref)
    for u in range(1, NEARC):
        even_ref[u] = jnp.zeros(even_ref.shape[1:], jnp.bfloat16)

    def two_places(turn, carry):
        place = 2 * turn
        fill(place + 1, every, odd_ref)
        apply(place, every, even_ref)
        fill(place + 2, every, even_ref)
        apply(place + 1, every, odd_ref)
        return carry

    lax.fori_loop(0, (slots - 2) // 2, two_places, 0)
    fill(slots - 1, [NEARC - 1], odd_ref)
    apply(slots - 2, every, even_ref)
    apply(slots - 1, [NEARC - 1], odd_ref)


def far_kernel(
    pairs_ref, coeff_ref, coupling_ref, out_ref, done_ref, total_ref, *, clusters
):
    done_ref[...] = jnp.zeros(done_ref.shape, jnp.float32)
    long_count, rhs_count, _ = total_ref.shape
    rank_size = coupling_ref.shape[1]
    row_count = out_ref.shape[0] // long_count
    groups = LANES // rank_size
    group_id = lax.broadcasted_iota(jnp.int32, (rhs_count, LANES), 1) // rank_size
    total_ref[...] = jnp.zeros(total_ref.shape, jnp.float32)

    def coeff_of(cluster):
        whole = coeff_ref[(cluster // clusters) * row_count + cluster % clusters]
        whole = whole.astype(jnp.float32)
        return jnp.concatenate(
            [whole[:, 0:rank_size], whole[:, rank_size : 2 * rank_size]], axis=0
        ).astype(jnp.bfloat16)

    results = []
    for pair_id in range(pairs_ref.shape[1]):
        first = pairs_ref[0, pair_id]
        second = pairs_ref[1, pair_id]
        coupling = coupling_ref[pair_id]
        to_first = lax.dot_general(
            coeff_of(second),
            jnp.concatenate([coupling] * groups, axis=0),
            (((1,), (1,)), ((), ())),
            preferred_element_type=jnp.float32,
        )
        to_second = jnp.dot(
            coeff_of(first),
            jnp.concatenate([coupling] * groups, axis=1),
            preferred_element_type=jnp.float32,
        )
        results.append((first, to_first))
        results.append((second, to_second))
    for cluster, value in results:
        owner = cluster // clusters
        total_ref[owner] += jnp.where(group_id == cluster % clusters, value, 0.0)

    for owner in range(long_count):
        sent = total_ref[owner].astype(jnp.bfloat16)
        for row in range(row_count):
            out_ref[owner * row_count + row] = sent


def finish_kernel(own_ref, other_ref, far_ref, basis_ref, out_ref):
    clusters, rank_size, unknowns = basis_ref.shape
    total = jnp.sum(far_ref[...].astype(jnp.float32), axis=0)
    group_id = lax.broadcasted_iota(jnp.int32, total.shape, 1) // rank_size
    flat_basis = basis_ref[...].reshape(clusters * rank_size, unknowns)
    even = lax.axis_index("row") % 2 == 0
    for cluster in range(clusters):
        u = cluster % NEARC
        here = even if cluster < NEARC else jnp.logical_not(even)
        near = jnp.where(here, own_ref[u], other_ref[u])
        picked = jnp.where(group_id == cluster, total, 0.0).astype(jnp.bfloat16)
        result = jnp.dot(picked, flat_basis, preferred_element_type=jnp.float32)
        out_ref[cluster] = result + near


def shards(slip, vertices, triangles, elem_map, near_pairs, near_count, far_pairs, far_coef, basis):
    clusters, rhs_count, unknowns = slip.shape
    rank_size = basis.shape[1]
    size = elem_map.shape[1]
    row_count = lax.axis_size("row")
    long_count = lax.axis_size("long")
    devices = row_count * long_count
    coupling = far_coef.reshape(-1, rank_size, rank_size)
    slots = clusters + NEARC

    pay = pl.pallas_call(
        coeffs_kernel,
        out_shape=jax.ShapeDtypeStruct((devices, rhs_count // 2, LANES), jnp.bfloat16),
        in_specs=[HBM] * 3 + [SMEM],
        out_specs=VMEM,
        scratch_shapes=[
            pltpu.VMEM(slip.shape[1:], slip.dtype),
            pltpu.VMEM(basis.shape[1:], basis.dtype),
            pltpu.VMEM(near_pairs.shape, near_pairs.dtype),
            pltpu.SemaphoreType.DMA((3,)),
        ],
        compiler_params=pltpu.CompilerParams(vmem_limit_bytes=16 << 20),
        name="coeffs",
    )(
        *[
            pltpu.with_memory_space_constraint(array, pltpu.HBM)
            for array in (slip, basis, near_pairs)
        ],
        near_count,
    )
    everyone = lax.all_to_all(pay, ("long", "row"), 0, 0, tiled=True)

    xs, to_neighbour, geometry = pl.pallas_call(
        geometry_kernel,
        out_shape=[
            jax.ShapeDtypeStruct(slip.shape, jnp.bfloat16),
            jax.ShapeDtypeStruct((NEARC, rhs_count, unknowns + size), jnp.bfloat16),
            jax.ShapeDtypeStruct((clusters, 4, size), jnp.float32),
        ],
        in_specs=[VMEM] * 4 + [ANY],
        out_specs=[VMEM] * 3,
        compiler_params=pltpu.CompilerParams(vmem_limit_bytes=16 << 20),
        cost_estimate=pl.CostEstimate(
            flops=2_000_000, bytes_accessed=1_000_000, transcendentals=1_000
        ),
        name="geometry",
    )(slip, vertices, triangles, elem_map, pay)
    route = []
    for row in range(row_count):
        step = 1 if row % 2 == 0 else -1
        for owner in range(long_count):
            if 0 <= owner - step < long_count:
                route.append((row * long_count + owner - step, row * long_count + owner))
    halo = lax.ppermute(to_neighbour, ("row", "long"), route)

    window, places = pl.pallas_call(
        window_kernel,
        out_shape=[
            jax.ShapeDtypeStruct((slots, rhs_count, unknowns), jnp.bfloat16),
            jax.ShapeDtypeStruct((slots, 4, size), jnp.float32),
        ],
        in_specs=[VMEM] * 3,
        out_specs=[VMEM] * 2,
        compiler_params=pltpu.CompilerParams(vmem_limit_bytes=16 << 20),
        cost_estimate=pl.CostEstimate(flops=1000, bytes_accessed=1000, transcendentals=0),
        name="window",
    )(xs, geometry, halo)

    far, far_done = pl.pallas_call(
        functools.partial(far_kernel, clusters=clusters),
        out_shape=[
            jax.ShapeDtypeStruct((devices, rhs_count, clusters * rank_size), jnp.bfloat16),
            jax.ShapeDtypeStruct((8, LANES), jnp.float32),
        ],
        in_specs=[SMEM, VMEM, VMEM],
        out_specs=[VMEM] * 2,
        scratch_shapes=[pltpu.VMEM((long_count, rhs_count, clusters * rank_size), jnp.float32)],
        compiler_params=pltpu.CompilerParams(vmem_limit_bytes=16 << 20),
        name="far",
    )(far_pairs, everyone, coupling)
    far_terms = lax.all_to_all(far, ("long", "row"), 0, 0, tiled=True)

    near = pl.pallas_call(
        functools.partial(near_kernel, long_count=long_count, clusters=clusters),
        out_shape=jax.ShapeDtypeStruct((NEARC, rhs_count, unknowns), jnp.float32),
        in_specs=[VMEM] * 3 + [ANY],
        out_specs=VMEM,
        scratch_shapes=[
            pltpu.VMEM((slots, size, 8), jnp.float32),
            pltpu.VMEM((NEARC, 6, size, size), jnp.bfloat16),
            pltpu.VMEM((NEARC, 6, size, size), jnp.bfloat16),
        ],
        compiler_params=pltpu.CompilerParams(vmem_limit_bytes=24 << 20),
        cost_estimate=pl.CostEstimate(
            flops=1_000_000_000, bytes_accessed=1_000_000, transcendentals=660_000
        ),
        name="near",
    )(window, places, everyone, far_done)
    partner = [(row, row ^ 1) for row in range(row_count)]
    other = lax.ppermute(near, "row", partner)

    return pl.pallas_call(
        finish_kernel,
        out_shape=jax.ShapeDtypeStruct(slip.shape, jnp.float32),
        in_specs=[VMEM] * 4,
        out_specs=VMEM,
        compiler_params=pltpu.CompilerParams(vmem_limit_bytes=16 << 20),
        name="finish",
    )(near, other, far_terms, basis)


def solution(mesh):
    placed = (
        P("long", None, None),
        P(None, "long"),
        P(None, "long"),
        P("long", None),
        P(None, ("row", "long")),
        P(("row", "long")),
        P(None, ("row", "long")),
        P(("row", "long"), None),
        P("long", None, None),
    )
    return jax.shard_map(
        shards, mesh=mesh, in_specs=placed, out_specs=P("long", None, None), check_vma=False
    )
```

```python
import functools

import jax
import jax.numpy as jnp
from jax import lax
from jax.experimental import pallas as pl
from jax.experimental.pallas import tpu as pltpu
from jax.sharding import PartitionSpec as P

NEARC = 2
LANES = 128
ROWS = 16

soften = 0.25

VMEM = pl.BlockSpec(memory_space=pltpu.VMEM)
SMEM = pl.BlockSpec(memory_space=pltpu.SMEM)
HBM = pl.BlockSpec(memory_space=pltpu.HBM)
ANY = pl.BlockSpec(memory_space=pl.ANY)
SMALL = pl.CostEstimate(flops=1000, bytes_accessed=1000, transcendentals=0)


def lane_gather(table, index):
    length = table.shape[1]
    lane = index & (LANES - 1)
    chunk = index // LANES
    found = jnp.zeros(index.shape, table.dtype)
    for piece_id in range(-(-length // LANES)):
        piece = table[:, piece_id * LANES : min(length, (piece_id + 1) * LANES)]
        missing = LANES - piece.shape[1]
        if missing:
            piece = jnp.concatenate([piece, jnp.zeros((1, missing), table.dtype)], axis=1)
        picked = jnp.take_along_axis(jnp.broadcast_to(piece, index.shape), lane, axis=1)
        found = jnp.where(chunk == piece_id, picked, found)
    return found


def split_three(value):
    high = value.astype(jnp.bfloat16).astype(jnp.float32)
    rest = value - high
    middle = rest.astype(jnp.bfloat16).astype(jnp.float32)
    return [high, middle, rest - middle]


def coeffs_kernel(
    slip_hbm, basis_hbm, pairs_hbm, count_ref, pay_ref, slip_ref, basis_ref, pairs_ref, sems
):
    clusters = slip_hbm.shape[0]
    rhs_count = slip_ref.shape[0]
    rank_size = basis_ref.shape[0]
    mine = lax.axis_index("row") % clusters
    copies = [
        pltpu.make_async_copy(slip_hbm.at[mine], slip_ref, sems.at[0]),
        pltpu.make_async_copy(basis_hbm.at[mine], basis_ref, sems.at[1]),
        pltpu.make_async_copy(pairs_hbm, pairs_ref, sems.at[2]),
    ]
    for copy in copies:
        copy.start()
    half = rhs_count // 2
    copies[2].wait()
    first = pairs_ref[0:1, :]
    kind = (first - lax.axis_index("long") * clusters) * (NEARC + 1) + pairs_ref[1:2, :] - first
    kinds = lax.broadcasted_iota(jnp.int32, (half, kind.shape[1]), 0)
    live = lax.broadcasted_iota(jnp.int32, kinds.shape, 1) < count_ref[0]
    low = jnp.sum(jnp.where(live & (kinds == kind), 1.0, 0.0), axis=1, keepdims=True)
    high = jnp.sum(jnp.where(live & (kinds + half == kind), 1.0, 0.0), axis=1, keepdims=True)
    copies[0].wait()
    copies[1].wait()
    coeffs = lax.dot_general(
        slip_ref[...].astype(jnp.bfloat16),
        basis_ref[...],
        (((1,), (1,)), ((), ())),
        preferred_element_type=jnp.float32,
    )
    counts = [jnp.broadcast_to(value, (half, rank_size)) for value in (low, high)]
    pay = jnp.concatenate([coeffs[0:half], coeffs[half:]] + counts, axis=1).astype(jnp.bfloat16)
    for target in range(pay_ref.shape[0]):
        pay_ref[target] = pay


def geometry_kernel(
    slip_ref, vertices_ref, triangles_ref, map_ref, after_ref, xs_ref, halo_ref, geom_ref
):
    clusters, rhs_count, unknowns = slip_ref.shape
    xs_ref[...] = slip_ref[...].astype(jnp.bfloat16)
    long_index = lax.axis_index("long")

    size = map_ref.shape[1]
    half = size // LANES
    slot_map = map_ref[...]
    index = jnp.concatenate(
        [slot_map[:, part * LANES : (part + 1) * LANES] for part in range(half)], axis=0
    )
    vertex_base = long_index * vertices_ref.shape[1]
    corners = []
    for corner_id in range(3):
        vertex = lane_gather(triangles_ref[corner_id : corner_id + 1, :], index) - vertex_base
        corners.append(
            [lane_gather(vertices_ref[axis_id : axis_id + 1, :], vertex) for axis_id in range(3)]
        )
    one, two, three = corners
    centre = [(one[a] + two[a] + three[a]) / 3.0 for a in range(3)]
    edge_one = [two[a] - one[a] for a in range(3)]
    edge_two = [three[a] - one[a] for a in range(3)]
    normal = [
        edge_one[1] * edge_two[2] - edge_one[2] * edge_two[1],
        edge_one[2] * edge_two[0] - edge_one[0] * edge_two[2],
        edge_one[0] * edge_two[1] - edge_one[1] * edge_two[0],
    ]
    area = 0.5 * jnp.sqrt(normal[0] * normal[0] + normal[1] * normal[1] + normal[2] * normal[2])
    geometry = []
    for value in centre + [area]:
        geometry.append(
            jnp.concatenate(
                [value[part * clusters : (part + 1) * clusters] for part in range(half)], axis=1
            )
        )
    for cluster in range(clusters):
        geom_ref[cluster] = jnp.concatenate(
            [whole[cluster : cluster + 1, :] for whole in geometry], axis=0
        )

    upward = lax.axis_index("row") % 2 == 0
    start = jnp.where(upward, clusters - NEARC, 0)
    pieces = [piece for whole in geometry for piece in split_three(whole)]
    for turn in range(NEARC):
        last = clusters - NEARC + turn
        rows = [
            jnp.where(upward, piece[last : last + 1, :], piece[turn : turn + 1, :])
            for piece in pieces
        ]
        rows.append(jnp.zeros((rhs_count - len(rows), size), jnp.float32))
        halo_ref[turn, :, 0:unknowns] = xs_ref[start + turn]
        halo_ref[turn, :, unknowns : unknowns + size] = jnp.concatenate(rows, axis=0).astype(
            jnp.bfloat16
        )


def near_blocks(steps, geometry_of, slip_of, right, add, cols_ref, block_refs):
    size = cols_ref.shape[1]
    parts = [(0, 0), (1, 1), (2, 2), (0, 1), (0, 2), (1, 2)]
    for turn, (place, _) in enumerate(steps):
        rows = jnp.concatenate([geometry_of(place), jnp.zeros((4, size), jnp.float32)], axis=0)
        cols_ref[turn] = rows.T

    def fill(turn):
        block_ref = block_refs[turn % 2]
        for step in range(size // ROWS):
            here = pl.ds(step * ROWS, ROWS)
            column = cols_ref[turn, here, :]
            left = [jnp.broadcast_to(column[:, p : p + 1], (ROWS, size)) for p in range(4)]
            for v in steps[turn][1]:
                offset = [left[p] - right[v][p] for p in range(3)]
                radius_sq = offset[0] * offset[0] + offset[1] * offset[1] + offset[2] * offset[2]
                inverse = lax.rsqrt(radius_sq + soften)
                flat = (left[3] * right[v][3]) * inverse
                cubed = flat * (inverse * inverse)
                scaled = [offset[p] * cubed for p in range(3)]
                for part_id, (i, j) in enumerate(parts):
                    term = offset[i] * scaled[j]
                    if i == j:
                        term = term + flat
                    block_ref[v, part_id, here, :] = term.astype(jnp.bfloat16)

    def apply(turn):
        block_ref = block_refs[turn % 2]
        place, targets = steps[turn]
        slip = slip_of(place)
        pieces = [slip[:, p * size : (p + 1) * size] for p in range(3)]
        for v in targets:
            sums = [
                jnp.dot(pieces[p], block_ref[v, p], preferred_element_type=jnp.float32)
                for p in range(3)
            ]
            for part_id in range(3, 6):
                i, j = parts[part_id]
                both = jnp.dot(
                    jnp.concatenate([pieces[j], pieces[i]], axis=0),
                    block_ref[v, part_id],
                    preferred_element_type=jnp.float32,
                )
                rhs_count = slip.shape[0]
                sums[i] = sums[i] + both[0:rhs_count]
                sums[j] = sums[j] + both[rhs_count : 2 * rhs_count]
            add(place, v, jnp.concatenate(sums, axis=1))

    for turn in range(len(steps)):
        fill(turn)
        if turn:
            apply(turn - 1)
    apply(len(steps) - 1)


def near_counts(pay_ref, long_count):
    clusters = 2 * NEARC
    odd = lax.axis_index("row") % 2
    long_index = lax.axis_index("long")
    before = jnp.maximum(long_index - 1, 0)
    totals = [jnp.zeros(pay_ref.shape[1:], jnp.float32) for _ in range(2)]
    for row in range(pay_ref.shape[0] // long_count):
        for source, owner in enumerate((long_index, before)):
            totals[source] += pay_ref[row * long_count + owner].astype(jnp.float32)
    half, lanes = pay_ref.shape[1:]
    lane_id = lax.broadcasted_iota(jnp.int32, (half, lanes), 1)
    kinds = lax.broadcasted_iota(jnp.int32, (half, lanes), 0)
    kinds = jnp.where(lane_id == 3 * lanes // 4, kinds + half, kinds)
    kinds = jnp.where((lane_id == lanes // 2) | (lane_id == 3 * lanes // 4), kinds, -1)

    def count(place, v):
        picked = []
        for side in range(2):
            cluster = NEARC + v if side else NEARC - 1 - v
            reach = place - NEARC - v if side else NEARC + v - place
            lower = cluster + min(reach, 0)
            source = totals[0] if lower >= 0 else totals[1]
            kind = (lower if lower >= 0 else lower + clusters) * (NEARC + 1) + abs(reach)
            picked.append(jnp.where(kinds == kind, source, 0.0))
        chosen = jnp.sum(jnp.where(odd == 1, picked[1], picked[0]), axis=0, keepdims=True)
        return jnp.sum(chosen, axis=1, keepdims=True)

    return count


def own_near_kernel(xs_ref, geom_ref, pay_ref, out_ref, cols_ref, even_ref, odd_ref, *, long_count):
    clusters = xs_ref.shape[0]
    odd = lax.axis_index("row") % 2
    count = near_counts(pay_ref, long_count)

    def cluster_at(place):
        return jnp.where(odd == 1, place, clusters - 1 - place)

    right = [[geom_ref[cluster_at(NEARC + v), p : p + 1, :] for p in range(4)] for v in range(NEARC)]
    out_ref[...] = jnp.zeros(out_ref.shape, jnp.float32)

    def add(place, v, value):
        out_ref[jnp.where(odd == 1, v, NEARC - 1 - v)] += count(place, v) * value

    steps = [
        (place, [v for v in range(NEARC) if 0 <= place - v <= 2 * NEARC]) for place in range(clusters)
    ]
    near_blocks(
        steps,
        lambda place: geom_ref[cluster_at(place)],
        lambda place: xs_ref[cluster_at(place)],
        right,
        add,
        cols_ref,
        (even_ref, odd_ref),
    )


def halo_near_kernel(
    begun_ref, halo_ref, geom_ref, pay_ref, out_ref, cols_ref, even_ref, odd_ref, *, long_count, clusters
):
    unknowns = out_ref.shape[2]
    size = unknowns // 3
    odd = lax.axis_index("row") % 2
    count = near_counts(pay_ref, long_count)

    def halo_at(place):
        return jnp.where(odd == 1, place - clusters, clusters + NEARC - 1 - place)

    def geometry_of(place):
        pieces = halo_ref[halo_at(place), :, unknowns : unknowns + size].astype(jnp.float32)
        return jnp.concatenate(
            [
                (pieces[3 * p + 2 : 3 * p + 3] + pieces[3 * p + 1 : 3 * p + 2])
                + pieces[3 * p : 3 * p + 1]
                for p in range(4)
            ],
            axis=0,
        )

    right = []
    for v in range(NEARC):
        mine = jnp.where(odd == 1, NEARC + v, NEARC - 1 - v)
        right.append([geom_ref[mine, p : p + 1, :] for p in range(4)])
    out_ref[...] = begun_ref[...]

    def add(place, v, value):
        out_ref[jnp.where(odd == 1, v, NEARC - 1 - v)] += count(place, v) * value

    steps = [
        (place, [v for v in range(NEARC) if 0 <= place - v <= 2 * NEARC])
        for place in range(clusters, clusters + NEARC)
    ]
    near_blocks(
        steps,
        geometry_of,
        lambda place: halo_ref[halo_at(place), :, 0:unknowns],
        right,
        add,
        cols_ref,
        (even_ref, odd_ref),
    )


def far_kernel(
    pairs_ref, coeff_ref, coupling_ref, out_ref, done_ref, total_ref, *, clusters
):
    done_ref[...] = jnp.zeros(done_ref.shape, jnp.float32)
    long_count, rhs_count, _ = total_ref.shape
    rank_size = coupling_ref.shape[1]
    groups = LANES // rank_size
    group_id = lax.broadcasted_iota(jnp.int32, (rhs_count, LANES), 1) // rank_size
    total_ref[...] = jnp.zeros(total_ref.shape, jnp.float32)

    def coeff_of(cluster):
        whole = coeff_ref[(cluster % clusters) * long_count + cluster // clusters]
        whole = whole.astype(jnp.float32)
        return jnp.concatenate(
            [whole[:, 0:rank_size], whole[:, rank_size : 2 * rank_size]], axis=0
        ).astype(jnp.bfloat16)

    results = []
    for pair_id in range(pairs_ref.shape[1]):
        first = pairs_ref[0, pair_id]
        second = pairs_ref[1, pair_id]
        coupling = coupling_ref[pair_id]
        to_first = lax.dot_general(
            coeff_of(second),
            jnp.concatenate([coupling] * groups, axis=0),
            (((1,), (1,)), ((), ())),
            preferred_element_type=jnp.float32,
        )
        to_second = jnp.dot(
            coeff_of(first),
            jnp.concatenate([coupling] * groups, axis=1),
            preferred_element_type=jnp.float32,
        )
        results.append((first, to_first))
        results.append((second, to_second))
    for cluster, value in results:
        owner = cluster // clusters
        total_ref[owner] += jnp.where(group_id == cluster % clusters, value, 0.0)

    sent = total_ref[...].astype(jnp.bfloat16)
    for copy_id in range(out_ref.shape[0] // long_count):
        out_ref[copy_id * long_count : (copy_id + 1) * long_count] = sent


def finish_kernel(own_ref, other_ref, far_ref, basis_ref, out_ref):
    clusters, rank_size, unknowns = basis_ref.shape
    total = jnp.sum(far_ref[...].astype(jnp.float32), axis=0)
    group_id = lax.broadcasted_iota(jnp.int32, total.shape, 1) // rank_size
    flat_basis = basis_ref[...].reshape(clusters * rank_size, unknowns)
    even = lax.axis_index("row") % 2 == 0
    for cluster in range(clusters):
        u = cluster % NEARC
        here = even if cluster < NEARC else jnp.logical_not(even)
        near = jnp.where(here, own_ref[u], other_ref[u])
        picked = jnp.where(group_id == cluster, total, 0.0).astype(jnp.bfloat16)
        result = jnp.dot(picked, flat_basis, preferred_element_type=jnp.float32)
        out_ref[cluster] = result + near


def shards(slip, vertices, triangles, elem_map, near_pairs, near_count, far_pairs, far_coef, basis):
    clusters, rhs_count, unknowns = slip.shape
    rank_size = basis.shape[1]
    size = elem_map.shape[1]
    row_count = lax.axis_size("row")
    long_count = lax.axis_size("long")
    devices = row_count * long_count
    blocks = [pltpu.VMEM((NEARC, 6, size, size), jnp.bfloat16)] * 2

    pay = pl.pallas_call(
        coeffs_kernel,
        out_shape=jax.ShapeDtypeStruct((devices, rhs_count // 2, LANES), jnp.bfloat16),
        in_specs=[HBM] * 3 + [SMEM],
        out_specs=VMEM,
        scratch_shapes=[
            pltpu.VMEM(slip.shape[1:], slip.dtype),
            pltpu.VMEM(basis.shape[1:], basis.dtype),
            pltpu.VMEM(near_pairs.shape, near_pairs.dtype),
            pltpu.SemaphoreType.DMA((3,)),
        ],
        compiler_params=pltpu.CompilerParams(vmem_limit_bytes=16 << 20),
        name="coeffs",
    )(
        *[
            pltpu.with_memory_space_constraint(array, pltpu.HBM)
            for array in (slip, basis, near_pairs)
        ],
        near_count,
    )
    everyone = lax.all_to_all(pay, ("row", "long"), 0, 0, tiled=True)

    held, everyone = lax.optimization_barrier((far_coef, everyone))
    coupling = held.reshape(-1, rank_size, rank_size)

    far, far_done = pl.pallas_call(
        functools.partial(far_kernel, clusters=clusters),
        out_shape=[
            jax.ShapeDtypeStruct((devices, rhs_count, clusters * rank_size), jnp.bfloat16),
            jax.ShapeDtypeStruct((8, LANES), jnp.float32),
        ],
        in_specs=[SMEM, VMEM, VMEM],
        out_specs=[VMEM] * 2,
        scratch_shapes=[pltpu.VMEM((long_count, rhs_count, clusters * rank_size), jnp.float32)],
        compiler_params=pltpu.CompilerParams(vmem_limit_bytes=16 << 20),
        name="far",
    )(far_pairs, everyone, coupling)
    far_terms = lax.all_to_all(far, ("row", "long"), 0, 0, tiled=True)

    xs, to_neighbour, geometry = pl.pallas_call(
        geometry_kernel,
        out_shape=[
            jax.ShapeDtypeStruct(slip.shape, jnp.bfloat16),
            jax.ShapeDtypeStruct((NEARC, rhs_count, unknowns + size), jnp.bfloat16),
            jax.ShapeDtypeStruct((clusters, 4, size), jnp.float32),
        ],
        in_specs=[VMEM] * 4 + [ANY],
        out_specs=[VMEM] * 3,
        compiler_params=pltpu.CompilerParams(vmem_limit_bytes=16 << 20),
        cost_estimate=SMALL,
        name="geometry",
    )(slip, vertices, triangles, elem_map, far_done)
    route = []
    for row in range(row_count):
        step = 1 if row % 2 == 0 else -1
        for owner in range(long_count):
            if 0 <= owner - step < long_count:
                route.append((row * long_count + owner - step, row * long_count + owner))
    halo = lax.ppermute(to_neighbour, ("row", "long"), route)

    own_near = pl.pallas_call(
        functools.partial(own_near_kernel, long_count=long_count),
        out_shape=jax.ShapeDtypeStruct((NEARC, rhs_count, unknowns), jnp.float32),
        in_specs=[VMEM] * 3,
        out_specs=VMEM,
        scratch_shapes=[pltpu.VMEM((clusters, size, 8), jnp.float32)] + blocks,
        compiler_params=pltpu.CompilerParams(vmem_limit_bytes=24 << 20),
        cost_estimate=SMALL,
        name="own_near",
    )(xs, geometry, everyone)

    near = pl.pallas_call(
        functools.partial(halo_near_kernel, long_count=long_count, clusters=clusters),
        out_shape=jax.ShapeDtypeStruct((NEARC, rhs_count, unknowns), jnp.float32),
        in_specs=[VMEM] * 4,
        out_specs=VMEM,
        scratch_shapes=[pltpu.VMEM((NEARC, size, 8), jnp.float32)] + blocks,
        compiler_params=pltpu.CompilerParams(vmem_limit_bytes=24 << 20),
        cost_estimate=SMALL,
        name="halo_near",
    )(own_near, halo, geometry, everyone)
    partner = [(row, row ^ 1) for row in range(row_count)]
    other = lax.ppermute(near, "row", partner)

    return pl.pallas_call(
        finish_kernel,
        out_shape=jax.ShapeDtypeStruct(slip.shape, jnp.float32),
        in_specs=[VMEM] * 4,
        out_specs=VMEM,
        compiler_params=pltpu.CompilerParams(vmem_limit_bytes=16 << 20),
        name="finish",
    )(near, other, far_terms, basis)


def solution(mesh):
    placed = (
        P("long", None, None),
        P(None, "long"),
        P(None, "long"),
        P("long", None),
        P(None, ("row", "long")),
        P(("row", "long")),
        P(None, ("row", "long")),
        P(("row", "long"), None),
        P("long", None, None),
    )
    return jax.shard_map(
        shards, mesh=mesh, in_specs=placed, out_specs=P("long", None, None), check_vma=False
    )
```

```python
import functools

import jax
import jax.numpy as jnp
from jax import lax
from jax.experimental import pallas as pl
from jax.experimental.pallas import tpu as pltpu
from jax.sharding import PartitionSpec as P

NEARC = 2
LANES = 128
ROWS = 16

soften = 0.25

VMEM = pl.BlockSpec(memory_space=pltpu.VMEM)
SMEM = pl.BlockSpec(memory_space=pltpu.SMEM)
HBM = pl.BlockSpec(memory_space=pltpu.HBM)
ANY = pl.BlockSpec(memory_space=pl.ANY)


def lane_gather(table, index):
    length = table.shape[1]
    lane = index & (LANES - 1)
    chunk = index // LANES
    found = jnp.zeros(index.shape, table.dtype)
    for piece_id in range(-(-length // LANES)):
        piece = table[:, piece_id * LANES : min(length, (piece_id + 1) * LANES)]
        missing = LANES - piece.shape[1]
        if missing:
            piece = jnp.concatenate([piece, jnp.zeros((1, missing), table.dtype)], axis=1)
        picked = jnp.take_along_axis(jnp.broadcast_to(piece, index.shape), lane, axis=1)
        found = jnp.where(chunk == piece_id, picked, found)
    return found


def split_three(value):
    high = value.astype(jnp.bfloat16).astype(jnp.float32)
    rest = value - high
    middle = rest.astype(jnp.bfloat16).astype(jnp.float32)
    return [high, middle, rest - middle]


def coeffs_kernel(
    slip_hbm, basis_hbm, pairs_hbm, count_ref, pay_ref, slip_ref, basis_ref, pairs_ref, sems
):
    clusters = slip_hbm.shape[0]
    rhs_count = slip_ref.shape[0]
    rank_size = basis_ref.shape[0]
    mine = lax.axis_index("row") % clusters
    copies = [
        pltpu.make_async_copy(slip_hbm.at[mine], slip_ref, sems.at[0]),
        pltpu.make_async_copy(basis_hbm.at[mine], basis_ref, sems.at[1]),
        pltpu.make_async_copy(pairs_hbm, pairs_ref, sems.at[2]),
    ]
    for copy in copies:
        copy.start()
    half = rhs_count // 2
    copies[2].wait()
    first = pairs_ref[0:1, :]
    kind = (first - lax.axis_index("long") * clusters) * (NEARC + 1) + pairs_ref[1:2, :] - first
    kinds = lax.broadcasted_iota(jnp.int32, (half, kind.shape[1]), 0)
    live = lax.broadcasted_iota(jnp.int32, kinds.shape, 1) < count_ref[0]
    low = jnp.sum(jnp.where(live & (kinds == kind), 1.0, 0.0), axis=1, keepdims=True)
    high = jnp.sum(jnp.where(live & (kinds + half == kind), 1.0, 0.0), axis=1, keepdims=True)
    copies[0].wait()
    copies[1].wait()
    coeffs = lax.dot_general(
        slip_ref[...].astype(jnp.bfloat16),
        basis_ref[...],
        (((1,), (1,)), ((), ())),
        preferred_element_type=jnp.float32,
    )
    counts = [jnp.broadcast_to(value, (half, rank_size)) for value in (low, high)]
    pay = jnp.concatenate([coeffs[0:half], coeffs[half:]] + counts, axis=1).astype(jnp.bfloat16)
    for target in range(pay_ref.shape[0]):
        pay_ref[target] = pay


def geometry_kernel(
    slip_ref, vertices_ref, triangles_ref, map_ref, after_ref, xs_ref, halo_ref, geom_ref
):
    clusters, rhs_count, unknowns = slip_ref.shape
    xs_ref[...] = slip_ref[...].astype(jnp.bfloat16)
    long_index = lax.axis_index("long")

    size = map_ref.shape[1]
    half = size // LANES
    slot_map = map_ref[...]
    index = jnp.concatenate(
        [slot_map[:, part * LANES : (part + 1) * LANES] for part in range(half)], axis=0
    )
    vertex_base = long_index * vertices_ref.shape[1]
    corners = []
    for corner_id in range(3):
        vertex = lane_gather(triangles_ref[corner_id : corner_id + 1, :], index) - vertex_base
        corners.append(
            [lane_gather(vertices_ref[axis_id : axis_id + 1, :], vertex) for axis_id in range(3)]
        )
    one, two, three = corners
    centre = [(one[a] + two[a] + three[a]) / 3.0 for a in range(3)]
    edge_one = [two[a] - one[a] for a in range(3)]
    edge_two = [three[a] - one[a] for a in range(3)]
    normal = [
        edge_one[1] * edge_two[2] - edge_one[2] * edge_two[1],
        edge_one[2] * edge_two[0] - edge_one[0] * edge_two[2],
        edge_one[0] * edge_two[1] - edge_one[1] * edge_two[0],
    ]
    area = 0.5 * jnp.sqrt(normal[0] * normal[0] + normal[1] * normal[1] + normal[2] * normal[2])
    geometry = []
    for value in centre + [area]:
        geometry.append(
            jnp.concatenate(
                [value[part * clusters : (part + 1) * clusters] for part in range(half)], axis=1
            )
        )
    for cluster in range(clusters):
        geom_ref[cluster] = jnp.concatenate(
            [whole[cluster : cluster + 1, :] for whole in geometry], axis=0
        )

    upward = lax.axis_index("row") % 2 == 0
    start = jnp.where(upward, clusters - NEARC, 0)
    pieces = [piece for whole in geometry for piece in split_three(whole)]
    for turn in range(NEARC):
        last = clusters - NEARC + turn
        rows = [
            jnp.where(upward, piece[last : last + 1, :], piece[turn : turn + 1, :])
            for piece in pieces
        ]
        rows.append(jnp.zeros((rhs_count - len(rows), size), jnp.float32))
        halo_ref[turn, :, 0:unknowns] = xs_ref[start + turn]
        halo_ref[turn, :, unknowns : unknowns + size] = jnp.concatenate(rows, axis=0).astype(
            jnp.bfloat16
        )


def window_kernel(xs_ref, geom_ref, halo_ref, slip_ref, place_ref):
    clusters, rhs_count, unknowns = xs_ref.shape
    size = geom_ref.shape[2]
    slots = clusters + NEARC
    odd = lax.axis_index("row") % 2

    def place_of(cluster):
        return (cluster + NEARC * (1 - odd) + slots) % slots

    for cluster in range(clusters):
        slip_ref[place_of(cluster)] = xs_ref[cluster]
        place_ref[place_of(cluster)] = geom_ref[cluster]
    for turn in range(NEARC):
        at = place_of(clusters + turn)
        slip_ref[at] = halo_ref[turn, :, 0:unknowns]
        pieces = halo_ref[turn, :, unknowns : unknowns + size].astype(jnp.float32)
        place_ref[at] = jnp.concatenate(
            [
                (pieces[3 * p + 2 : 3 * p + 3] + pieces[3 * p + 1 : 3 * p + 2])
                + pieces[3 * p : 3 * p + 1]
                for p in range(4)
            ],
            axis=0,
        )


def near_kernel(
    slip_ref, place_ref, pay_ref, after_ref, out_ref, cols_ref, even_ref, odd_ref, *, long_count, clusters
):
    slots, rhs_count, unknowns = slip_ref.shape
    size = place_ref.shape[2]
    long_index = lax.axis_index("long")
    before = jnp.maximum(long_index - 1, 0)
    totals = [jnp.zeros(pay_ref.shape[1:], jnp.float32) for _ in range(2)]
    for row in range(pay_ref.shape[0] // long_count):
        for source, owner in enumerate((long_index, before)):
            totals[source] += pay_ref[row * long_count + owner].astype(jnp.float32)
    even = lax.axis_index("row") % 2 == 0
    half = pay_ref.shape[1]
    rank_size = pay_ref.shape[2] // 4
    group = lax.broadcasted_iota(jnp.int32, (half, LANES), 1) // rank_size
    kinds = lax.broadcasted_iota(jnp.int32, (half, LANES), 0) + jnp.where(group == 3, half, 0)
    kinds = jnp.where(group < 2, -1, kinds)
    lane_id = lax.broadcasted_iota(jnp.int32, (half, LANES), 1)
    kinds = jnp.where(lane_id % rank_size == 0, kinds, -1)

    def count_of(place, u):
        both = []
        for cluster in (u, clusters - NEARC + u):
            reach = place - u - NEARC
            lower = cluster + jnp.minimum(reach, 0)
            inside = lower >= 0
            kind = jnp.where(inside, lower, lower + clusters) * (NEARC + 1) + jnp.abs(reach)
            source = jnp.where(inside, totals[0], totals[1])
            both.append(jnp.where(kinds == kind, source, 0.0))
        picked = jnp.sum(jnp.where(even, both[0], both[1]), axis=0, keepdims=True)
        return jnp.sum(picked, axis=1, keepdims=True)

    out_ref[...] = jnp.zeros(out_ref.shape, jnp.float32)
    for place in range(slots):
        rows = jnp.concatenate([place_ref[place], jnp.zeros((4, size), jnp.float32)], axis=0)
        cols_ref[place] = rows.T
    right = [[place_ref[NEARC + u, p : p + 1, :] for p in range(4)] for u in range(NEARC)]
    parts = [(0, 0), (1, 1), (2, 2), (0, 1), (0, 2), (1, 2)]

    def fill(place, targets, block_ref):
        for step in range(size // ROWS):
            here = pl.ds(step * ROWS, ROWS)
            column = cols_ref[place, here, :]
            left = [jnp.broadcast_to(column[:, p : p + 1], (ROWS, size)) for p in range(4)]
            for u in targets:
                offset = [left[p] - right[u][p] for p in range(3)]
                radius_sq = offset[0] * offset[0] + offset[1] * offset[1] + offset[2] * offset[2]
                inverse = lax.rsqrt(radius_sq + soften)
                flat = (left[3] * right[u][3]) * inverse
                cubed = flat * (inverse * inverse)
                scaled = [offset[p] * cubed for p in range(3)]
                for part_id, (i, j) in enumerate(parts):
                    term = offset[i] * scaled[j]
                    if i == j:
                        term = term + flat
                    block_ref[u, part_id, here, :] = term.astype(jnp.bfloat16)

    def apply(place, targets, block_ref):
        slip = slip_ref[place]
        pieces = [slip[:, p * size : (p + 1) * size] for p in range(3)]
        for u in targets:
            count = count_of(place, u)
            sums = [
                jnp.dot(pieces[p], block_ref[u, p], preferred_element_type=jnp.float32)
                for p in range(3)
            ]
            for part_id in range(3, 6):
                i, j = parts[part_id]
                both = jnp.dot(
                    jnp.concatenate([pieces[j], pieces[i]], axis=0),
                    block_ref[u, part_id],
                    preferred_element_type=jnp.float32,
                )
                sums[i] = sums[i] + both[0:rhs_count]
                sums[j] = sums[j] + both[rhs_count : 2 * rhs_count]
            for p in range(3):
                out_ref[u, :, p * size : (p + 1) * size] += count * sums[p]

    every = list(range(NEARC))
    fill(0, [0], even_ref)
    for u in range(1, NEARC):
        even_ref[u] = jnp.zeros(even_ref.shape[1:], jnp.bfloat16)

    def two_places(turn, carry):
        place = 2 * turn
        fill(place + 1, every, odd_ref)
        apply(place, every, even_ref)
        fill(place + 2, every, even_ref)
        apply(place + 1, every, odd_ref)
        return carry

    lax.fori_loop(0, (slots - 2) // 2, two_places, 0)
    fill(slots - 1, [NEARC - 1], odd_ref)
    apply(slots - 2, every, even_ref)
    apply(slots - 1, [NEARC - 1], odd_ref)


def coupling_kernel(coupling_ref, after_ref, to_second_ref, to_first_ref):
    pair_count, rank_size, _ = coupling_ref.shape
    groups = LANES // rank_size
    for pair_id in range(pair_count):
        here = pl.ds(pair_id * rank_size, rank_size)
        coupling = coupling_ref[pair_id].astype(jnp.float32)
        for out_ref, value in ((to_second_ref, coupling), (to_first_ref, coupling.T)):
            out_ref[here, :] = jnp.concatenate([value] * groups, axis=1).astype(jnp.bfloat16)


def far_kernel(
    pairs_ref, coeff_ref, to_second_ref, to_first_ref, out_ref, done_ref, *total_refs, clusters
):
    done_ref[...] = jnp.zeros(done_ref.shape, jnp.float32)
    long_count, rhs_count, _ = total_refs[0].shape
    pair_count = pairs_ref.shape[1]
    rank_size = LANES // clusters
    group_id = lax.broadcasted_iota(jnp.int32, (rhs_count, LANES), 1) // rank_size
    for total_ref in total_refs:
        total_ref[...] = jnp.zeros(total_ref.shape, jnp.float32)

    def coeff_of(cluster, group):
        whole = coeff_ref[(cluster % clusters) * long_count + cluster // clusters]
        whole = whole.astype(jnp.float32)
        low = pltpu.roll(whole, rank_size * group, 1) if group else whole
        high = pltpu.roll(whole, (rank_size * (group - 1)) % LANES, 1) if group != 1 else whole
        both = jnp.concatenate([low, high], axis=0)
        return jnp.where(group_id == group, both, 0.0)

    results = []
    for begin in range(0, pair_count, clusters):
        pair_ids = range(begin, min(begin + clusters, pair_count))
        depth = len(pair_ids) * rank_size
        here = pl.ds(begin * rank_size, depth)
        for source, target, matrix_ref in ((0, 1, to_second_ref), (1, 0, to_first_ref)):
            coeffs = jnp.concatenate(
                [coeff_of(pairs_ref[source, f], f - begin) for f in pair_ids], axis=0
            ).astype(jnp.bfloat16)
            value = jnp.dot(
                coeffs[:, 0:depth], matrix_ref[here, :], preferred_element_type=jnp.float32
            )
            for turn, f in enumerate(pair_ids):
                results.append(
                    (pairs_ref[target, f], value[turn * rhs_count : (turn + 1) * rhs_count])
                )
    for turn, (cluster, value) in enumerate(results):
        total_ref = total_refs[turn % len(total_refs)]
        total_ref[cluster // clusters] += jnp.where(group_id == cluster % clusters, value, 0.0)
    total = total_refs[0][...]
    for total_ref in total_refs[1:]:
        total = total + total_ref[...]
    sent = total.astype(jnp.bfloat16)
    for copy_id in range(out_ref.shape[0] // long_count):
        out_ref[copy_id * long_count : (copy_id + 1) * long_count] = sent


def finish_kernel(own_ref, other_ref, far_ref, basis_ref, out_ref):
    clusters, rank_size, unknowns = basis_ref.shape
    total = jnp.sum(far_ref[...].astype(jnp.float32), axis=0)
    group_id = lax.broadcasted_iota(jnp.int32, total.shape, 1) // rank_size
    flat_basis = basis_ref[...].reshape(clusters * rank_size, unknowns)
    even = lax.axis_index("row") % 2 == 0
    for cluster in range(clusters):
        u = cluster % NEARC
        here = even if cluster < NEARC else jnp.logical_not(even)
        near = jnp.where(here, own_ref[u], other_ref[u])
        picked = jnp.where(group_id == cluster, total, 0.0).astype(jnp.bfloat16)
        result = jnp.dot(picked, flat_basis, preferred_element_type=jnp.float32)
        out_ref[cluster] = result + near


def shards(slip, vertices, triangles, elem_map, near_pairs, near_count, far_pairs, far_coef, basis):
    clusters, rhs_count, unknowns = slip.shape
    rank_size = basis.shape[1]
    size = elem_map.shape[1]
    row_count = lax.axis_size("row")
    long_count = lax.axis_size("long")
    devices = row_count * long_count
    coupling = far_coef.reshape(-1, rank_size, rank_size)
    slots = clusters + NEARC

    pay = pl.pallas_call(
        coeffs_kernel,
        out_shape=jax.ShapeDtypeStruct((devices, rhs_count // 2, LANES), jnp.bfloat16),
        in_specs=[HBM] * 3 + [SMEM],
        out_specs=VMEM,
        scratch_shapes=[
            pltpu.VMEM(slip.shape[1:], slip.dtype),
            pltpu.VMEM(basis.shape[1:], basis.dtype),
            pltpu.VMEM(near_pairs.shape, near_pairs.dtype),
            pltpu.SemaphoreType.DMA((3,)),
        ],
        compiler_params=pltpu.CompilerParams(vmem_limit_bytes=16 << 20),
        name="coeffs",
    )(
        *[
            pltpu.with_memory_space_constraint(array, pltpu.HBM)
            for array in (slip, basis, near_pairs)
        ],
        near_count,
    )
    everyone = lax.all_to_all(pay, ("row", "long"), 0, 0, tiled=True)

    xs, to_neighbour, geometry = pl.pallas_call(
        geometry_kernel,
        out_shape=[
            jax.ShapeDtypeStruct(slip.shape, jnp.bfloat16),
            jax.ShapeDtypeStruct((NEARC, rhs_count, unknowns + size), jnp.bfloat16),
            jax.ShapeDtypeStruct((clusters, 4, size), jnp.float32),
        ],
        in_specs=[VMEM] * 4 + [ANY],
        out_specs=[VMEM] * 3,
        compiler_params=pltpu.CompilerParams(vmem_limit_bytes=16 << 20),
        cost_estimate=pl.CostEstimate(
            flops=2_000_000, bytes_accessed=1_000_000, transcendentals=1_000
        ),
        name="geometry",
    )(slip, vertices, triangles, elem_map, pay)
    route = []
    for row in range(row_count):
        step = 1 if row % 2 == 0 else -1
        for owner in range(long_count):
            if 0 <= owner - step < long_count:
                route.append((row * long_count + owner - step, row * long_count + owner))
    halo = lax.ppermute(to_neighbour, ("row", "long"), route)

    window, places = pl.pallas_call(
        window_kernel,
        out_shape=[
            jax.ShapeDtypeStruct((slots, rhs_count, unknowns), jnp.bfloat16),
            jax.ShapeDtypeStruct((slots, 4, size), jnp.float32),
        ],
        in_specs=[VMEM] * 3,
        out_specs=[VMEM] * 2,
        compiler_params=pltpu.CompilerParams(vmem_limit_bytes=16 << 20),
        cost_estimate=pl.CostEstimate(flops=1000, bytes_accessed=1000, transcendentals=0),
        name="window",
    )(xs, geometry, halo)

    couplings = pl.pallas_call(
        coupling_kernel,
        out_shape=[jax.ShapeDtypeStruct((coupling.shape[0] * rank_size, LANES), jnp.bfloat16)] * 2,
        in_specs=[VMEM, ANY],
        out_specs=[VMEM] * 2,
        compiler_params=pltpu.CompilerParams(vmem_limit_bytes=16 << 20),
        cost_estimate=pl.CostEstimate(flops=1000, bytes_accessed=1000, transcendentals=0),
        name="coupling",
    )(coupling, pay)
    far, far_done = pl.pallas_call(
        functools.partial(far_kernel, clusters=clusters),
        out_shape=[
            jax.ShapeDtypeStruct((devices, rhs_count, clusters * rank_size), jnp.bfloat16),
            jax.ShapeDtypeStruct((8, LANES), jnp.float32),
        ],
        in_specs=[SMEM, VMEM, VMEM, VMEM],
        out_specs=[VMEM] * 2,
        scratch_shapes=[pltpu.VMEM((long_count, rhs_count, clusters * rank_size), jnp.float32)] * 4,
        compiler_params=pltpu.CompilerParams(vmem_limit_bytes=16 << 20),
        name="far",
    )(far_pairs, everyone, *couplings)
    far_terms = lax.all_to_all(far, ("row", "long"), 0, 0, tiled=True)

    near = pl.pallas_call(
        functools.partial(near_kernel, long_count=long_count, clusters=clusters),
        out_shape=jax.ShapeDtypeStruct((NEARC, rhs_count, unknowns), jnp.float32),
        in_specs=[VMEM] * 3 + [ANY],
        out_specs=VMEM,
        scratch_shapes=[
            pltpu.VMEM((slots, size, 8), jnp.float32),
            pltpu.VMEM((NEARC, 6, size, size), jnp.bfloat16),
            pltpu.VMEM((NEARC, 6, size, size), jnp.bfloat16),
        ],
        compiler_params=pltpu.CompilerParams(vmem_limit_bytes=24 << 20),
        cost_estimate=pl.CostEstimate(
            flops=1_000_000_000, bytes_accessed=1_000_000, transcendentals=660_000
        ),
        name="near",
    )(window, places, everyone, far_done)
    partner = [(row, row ^ 1) for row in range(row_count)]
    other = lax.ppermute(near, "row", partner)

    return pl.pallas_call(
        finish_kernel,
        out_shape=jax.ShapeDtypeStruct(slip.shape, jnp.float32),
        in_specs=[VMEM] * 4,
        out_specs=VMEM,
        compiler_params=pltpu.CompilerParams(vmem_limit_bytes=16 << 20),
        name="finish",
    )(near, other, far_terms, basis)


def solution(mesh):
    placed = (
        P("long", None, None),
        P(None, "long"),
        P(None, "long"),
        P("long", None),
        P(None, ("row", "long")),
        P(("row", "long")),
        P(None, ("row", "long")),
        P(("row", "long"), None),
        P("long", None, None),
    )
    return jax.shard_map(
        shards, mesh=mesh, in_specs=placed, out_specs=P("long", None, None), check_vma=False
    )
```

```python
import functools

import jax
import jax.numpy as jnp
from jax import lax
from jax.experimental import pallas as pl
from jax.experimental.pallas import tpu as pltpu
from jax.sharding import PartitionSpec as P

NEARC = 2
LANES = 128
ROWS = 16

soften = 0.25

VMEM = pl.BlockSpec(memory_space=pltpu.VMEM)
SMEM = pl.BlockSpec(memory_space=pltpu.SMEM)
HBM = pl.BlockSpec(memory_space=pltpu.HBM)
ANY = pl.BlockSpec(memory_space=pl.ANY)


def lane_gather(table, index):
    length = table.shape[1]
    lane = index & (LANES - 1)
    chunk = index // LANES
    found = jnp.zeros(index.shape, table.dtype)
    for piece_id in range(-(-length // LANES)):
        piece = table[:, piece_id * LANES : min(length, (piece_id + 1) * LANES)]
        missing = LANES - piece.shape[1]
        if missing:
            piece = jnp.concatenate([piece, jnp.zeros((1, missing), table.dtype)], axis=1)
        picked = jnp.take_along_axis(jnp.broadcast_to(piece, index.shape), lane, axis=1)
        found = jnp.where(chunk == piece_id, picked, found)
    return found


def split_three(value):
    high = value.astype(jnp.bfloat16).astype(jnp.float32)
    rest = value - high
    middle = rest.astype(jnp.bfloat16).astype(jnp.float32)
    return [high, middle, rest - middle]


def coeffs_kernel(
    slip_hbm, basis_hbm, pairs_hbm, count_ref, pay_hbm, slip_ref, basis_ref, pairs_ref, sent_ref, sems, out_sems
):
    clusters = slip_hbm.shape[0]
    rhs_count = slip_ref.shape[0]
    rank_size = basis_ref.shape[0]
    mine = lax.axis_index("row") % clusters
    copies = [
        pltpu.make_async_copy(slip_hbm.at[mine], slip_ref, sems.at[0]),
        pltpu.make_async_copy(basis_hbm.at[mine], basis_ref, sems.at[1]),
        pltpu.make_async_copy(pairs_hbm, pairs_ref, sems.at[2]),
    ]
    for copy in copies:
        copy.start()
    half = rhs_count // 2
    copies[2].wait()
    first = pairs_ref[0:1, :]
    kind = (first - lax.axis_index("long") * clusters) * (NEARC + 1) + pairs_ref[1:2, :] - first
    kinds = lax.broadcasted_iota(jnp.int32, (half, kind.shape[1]), 0)
    live = lax.broadcasted_iota(jnp.int32, kinds.shape, 1) < count_ref[0]
    low = jnp.sum(jnp.where(live & (kinds == kind), 1.0, 0.0), axis=1, keepdims=True)
    high = jnp.sum(jnp.where(live & (kinds + half == kind), 1.0, 0.0), axis=1, keepdims=True)
    copies[0].wait()
    copies[1].wait()
    coeffs = lax.dot_general(
        slip_ref[...].astype(jnp.bfloat16),
        basis_ref[...],
        (((1,), (1,)), ((), ())),
        preferred_element_type=jnp.float32,
    )
    counts = [jnp.broadcast_to(value, (half, rank_size)) for value in (low, high)]
    pay = jnp.concatenate([coeffs[0:half], coeffs[half:]] + counts, axis=1).astype(jnp.bfloat16)
    for target in range(sent_ref.shape[0]):
        sent_ref[target] = pay
    parts = pay_hbm.shape[0] // sent_ref.shape[0]
    sends = [
        pltpu.make_async_copy(
            sent_ref, pay_hbm.at[pl.ds(part * sent_ref.shape[0], sent_ref.shape[0])], out_sems.at[part]
        )
        for part in range(parts)
    ]
    for send in sends:
        send.start()
    for send in sends:
        send.wait()


def geometry_kernel(
    slip_ref, vertices_ref, triangles_ref, map_ref, after_ref, xs_ref, halo_ref, geom_ref
):
    clusters, rhs_count, unknowns = slip_ref.shape
    xs_ref[...] = slip_ref[...].astype(jnp.bfloat16)
    long_index = lax.axis_index("long")

    size = map_ref.shape[1]
    half = size // LANES
    slot_map = map_ref[...]
    index = jnp.concatenate(
        [slot_map[:, part * LANES : (part + 1) * LANES] for part in range(half)], axis=0
    )
    vertex_base = long_index * vertices_ref.shape[1]
    corners = []
    for corner_id in range(3):
        vertex = lane_gather(triangles_ref[corner_id : corner_id + 1, :], index) - vertex_base
        corners.append(
            [lane_gather(vertices_ref[axis_id : axis_id + 1, :], vertex) for axis_id in range(3)]
        )
    one, two, three = corners
    centre = [(one[a] + two[a] + three[a]) / 3.0 for a in range(3)]
    edge_one = [two[a] - one[a] for a in range(3)]
    edge_two = [three[a] - one[a] for a in range(3)]
    normal = [
        edge_one[1] * edge_two[2] - edge_one[2] * edge_two[1],
        edge_one[2] * edge_two[0] - edge_one[0] * edge_two[2],
        edge_one[0] * edge_two[1] - edge_one[1] * edge_two[0],
    ]
    area = 0.5 * jnp.sqrt(normal[0] * normal[0] + normal[1] * normal[1] + normal[2] * normal[2])
    geometry = []
    for value in centre + [area]:
        geometry.append(
            jnp.concatenate(
                [value[part * clusters : (part + 1) * clusters] for part in range(half)], axis=1
            )
        )
    for cluster in range(clusters):
        geom_ref[cluster] = jnp.concatenate(
            [whole[cluster : cluster + 1, :] for whole in geometry], axis=0
        )

    upward = lax.axis_index("row") % 2 == 0
    start = jnp.where(upward, clusters - NEARC, 0)
    pieces = [piece for whole in geometry for piece in split_three(whole)]
    for turn in range(NEARC):
        last = clusters - NEARC + turn
        rows = [
            jnp.where(upward, piece[last : last + 1, :], piece[turn : turn + 1, :])
            for piece in pieces
        ]
        rows.append(jnp.zeros((rhs_count - len(rows), size), jnp.float32))
        halo_ref[turn, :, 0:unknowns] = xs_ref[start + turn]
        halo_ref[turn, :, unknowns : unknowns + size] = jnp.concatenate(rows, axis=0).astype(
            jnp.bfloat16
        )


def window_kernel(xs_ref, geom_ref, halo_ref, slip_ref, place_ref):
    clusters, rhs_count, unknowns = xs_ref.shape
    size = geom_ref.shape[2]
    slots = clusters + NEARC
    odd = lax.axis_index("row") % 2

    def place_of(cluster):
        return (cluster + NEARC * (1 - odd) + slots) % slots

    for cluster in range(clusters):
        slip_ref[place_of(cluster)] = xs_ref[cluster]
        place_ref[place_of(cluster)] = geom_ref[cluster]
    for turn in range(NEARC):
        at = place_of(clusters + turn)
        slip_ref[at] = halo_ref[turn, :, 0:unknowns]
        pieces = halo_ref[turn, :, unknowns : unknowns + size].astype(jnp.float32)
        place_ref[at] = jnp.concatenate(
            [
                (pieces[3 * p + 2 : 3 * p + 3] + pieces[3 * p + 1 : 3 * p + 2])
                + pieces[3 * p : 3 * p + 1]
                for p in range(4)
            ],
            axis=0,
        )


def near_kernel(
    slip_ref, place_ref, pay_ref, after_ref, out_ref, cols_ref, even_ref, odd_ref, *, long_count, clusters
):
    slots, rhs_count, unknowns = slip_ref.shape
    size = place_ref.shape[2]
    long_index = lax.axis_index("long")
    before = jnp.maximum(long_index - 1, 0)
    totals = [jnp.zeros(pay_ref.shape[1:], jnp.float32) for _ in range(2)]
    for row in range(pay_ref.shape[0] // long_count):
        for source, owner in enumerate((long_index, before)):
            totals[source] += pay_ref[row * long_count + owner].astype(jnp.float32)
    even = lax.axis_index("row") % 2 == 0
    half = pay_ref.shape[1]
    rank_size = pay_ref.shape[2] // 4
    group = lax.broadcasted_iota(jnp.int32, (half, LANES), 1) // rank_size
    kinds = lax.broadcasted_iota(jnp.int32, (half, LANES), 0) + jnp.where(group == 3, half, 0)
    kinds = jnp.where(group < 2, -1, kinds)
    lane_id = lax.broadcasted_iota(jnp.int32, (half, LANES), 1)
    kinds = jnp.where(lane_id % rank_size == 0, kinds, -1)

    def count_of(place, u):
        both = []
        for cluster in (u, clusters - NEARC + u):
            reach = place - u - NEARC
            lower = cluster + jnp.minimum(reach, 0)
            inside = lower >= 0
            kind = jnp.where(inside, lower, lower + clusters) * (NEARC + 1) + jnp.abs(reach)
            source = jnp.where(inside, totals[0], totals[1])
            both.append(jnp.where(kinds == kind, source, 0.0))
        picked = jnp.sum(jnp.where(even, both[0], both[1]), axis=0, keepdims=True)
        return jnp.sum(picked, axis=1, keepdims=True)

    out_ref[...] = jnp.zeros(out_ref.shape, jnp.float32)
    for place in range(slots):
        rows = jnp.concatenate([place_ref[place], jnp.zeros((4, size), jnp.float32)], axis=0)
        cols_ref[place] = rows.T
    right = [[place_ref[NEARC + u, p : p + 1, :] for p in range(4)] for u in range(NEARC)]
    parts = [(0, 0), (1, 1), (2, 2), (0, 1), (0, 2), (1, 2)]

    def fill(place, targets, block_ref):
        for step in range(size // ROWS):
            here = pl.ds(step * ROWS, ROWS)
            column = cols_ref[place, here, :]
            left = [jnp.broadcast_to(column[:, p : p + 1], (ROWS, size)) for p in range(4)]
            for u in targets:
                offset = [left[p] - right[u][p] for p in range(3)]
                radius_sq = offset[0] * offset[0] + offset[1] * offset[1] + offset[2] * offset[2]
                inverse = lax.rsqrt(radius_sq + soften)
                flat = (left[3] * right[u][3]) * inverse
                cubed = flat * (inverse * inverse)
                scaled = [offset[p] * cubed for p in range(3)]
                for part_id, (i, j) in enumerate(parts):
                    term = offset[i] * scaled[j]
                    if i == j:
                        term = term + flat
                    block_ref[u, part_id, here, :] = term.astype(jnp.bfloat16)

    def apply(place, targets, block_ref):
        slip = slip_ref[place]
        pieces = [slip[:, p * size : (p + 1) * size] for p in range(3)]
        for u in targets:
            count = count_of(place, u)
            sums = [
                jnp.dot(pieces[p], block_ref[u, p], preferred_element_type=jnp.float32)
                for p in range(3)
            ]
            for part_id in range(3, 6):
                i, j = parts[part_id]
                both = jnp.dot(
                    jnp.concatenate([pieces[j], pieces[i]], axis=0),
                    block_ref[u, part_id],
                    preferred_element_type=jnp.float32,
                )
                sums[i] = sums[i] + both[0:rhs_count]
                sums[j] = sums[j] + both[rhs_count : 2 * rhs_count]
            for p in range(3):
                out_ref[u, :, p * size : (p + 1) * size] += count * sums[p]

    every = list(range(NEARC))
    fill(0, [0], even_ref)
    for u in range(1, NEARC):
        even_ref[u] = jnp.zeros(even_ref.shape[1:], jnp.bfloat16)

    def two_places(turn, carry):
        place = 2 * turn
        fill(place + 1, every, odd_ref)
        apply(place, every, even_ref)
        fill(place + 2, every, even_ref)
        apply(place + 1, every, odd_ref)
        return carry

    lax.fori_loop(0, (slots - 2) // 2, two_places, 0)
    fill(slots - 1, [NEARC - 1], odd_ref)
    apply(slots - 2, every, even_ref)
    apply(slots - 1, [NEARC - 1], odd_ref)


def coupling_kernel(coupling_ref, pairs_ref, after_ref, to_second_ref, to_first_ref, list_ref):
    list_ref[...] = pairs_ref[...]
    pair_count, rank_size, _ = coupling_ref.shape
    groups = LANES // rank_size
    for pair_id in range(pair_count):
        here = pl.ds(pair_id * rank_size, rank_size)
        coupling = coupling_ref[pair_id].astype(jnp.float32)
        for out_ref, value in ((to_second_ref, coupling), (to_first_ref, coupling.T)):
            out_ref[here, :] = jnp.concatenate([value] * groups, axis=1).astype(jnp.bfloat16)


def far_kernel(
    pairs_ref, coeff_ref, to_second_ref, to_first_ref, out_hbm, done_ref, sent_ref, sems, *total_refs, clusters
):
    done_ref[...] = jnp.zeros(done_ref.shape, jnp.float32)
    long_count, rhs_count, _ = total_refs[0].shape
    pair_count = pairs_ref.shape[1]
    rank_size = LANES // clusters
    group_id = lax.broadcasted_iota(jnp.int32, (rhs_count, LANES), 1) // rank_size
    for total_ref in total_refs:
        total_ref[...] = jnp.zeros(total_ref.shape, jnp.float32)

    def coeff_of(cluster, group):
        whole = coeff_ref[(cluster % clusters) * long_count + cluster // clusters]
        whole = whole.astype(jnp.float32)
        low = pltpu.roll(whole, rank_size * group, 1) if group else whole
        high = pltpu.roll(whole, (rank_size * (group - 1)) % LANES, 1) if group != 1 else whole
        both = jnp.concatenate([low, high], axis=0)
        return jnp.where(group_id == group, both, 0.0)

    results = []
    for begin in range(0, pair_count, clusters):
        pair_ids = range(begin, min(begin + clusters, pair_count))
        depth = len(pair_ids) * rank_size
        here = pl.ds(begin * rank_size, depth)
        for source, target, matrix_ref in ((0, 1, to_second_ref), (1, 0, to_first_ref)):
            coeffs = jnp.concatenate(
                [coeff_of(pairs_ref[source, f], f - begin) for f in pair_ids], axis=0
            ).astype(jnp.bfloat16)
            value = jnp.dot(
                coeffs[:, 0:depth], matrix_ref[here, :], preferred_element_type=jnp.float32
            )
            for turn, f in enumerate(pair_ids):
                results.append(
                    (pairs_ref[target, f], value[turn * rhs_count : (turn + 1) * rhs_count])
                )
    for turn, (cluster, value) in enumerate(results):
        total_ref = total_refs[turn % len(total_refs)]
        total_ref[cluster // clusters] += jnp.where(group_id == cluster % clusters, value, 0.0)
    total = total_refs[0][...]
    for total_ref in total_refs[1:]:
        total = total + total_ref[...]
    sent_ref[...] = total.astype(jnp.bfloat16)
    copies = [
        pltpu.make_async_copy(
            sent_ref, out_hbm.at[pl.ds(copy_id * long_count, long_count)], sems.at[copy_id]
        )
        for copy_id in range(out_hbm.shape[0] // long_count)
    ]
    for copy in copies:
        copy.start()
    for copy in copies:
        copy.wait()


def finish_kernel(own_ref, other_ref, far_ref, basis_ref, out_hbm, sent_ref, sems):
    clusters, rank_size, unknowns = basis_ref.shape
    total = jnp.sum(far_ref[...].astype(jnp.float32), axis=0)
    group_id = lax.broadcasted_iota(jnp.int32, total.shape, 1) // rank_size
    flat_basis = basis_ref[...].reshape(clusters * rank_size, unknowns)
    even = lax.axis_index("row") % 2 == 0
    copies = []
    for cluster in range(clusters):
        u = cluster % NEARC
        here = even if cluster < NEARC else jnp.logical_not(even)
        near = jnp.where(here, own_ref[u], other_ref[u])
        picked = jnp.where(group_id == cluster, total, 0.0).astype(jnp.bfloat16)
        result = jnp.dot(picked, flat_basis, preferred_element_type=jnp.float32)
        sent_ref[cluster] = result + near
        copies.append(
            pltpu.make_async_copy(sent_ref.at[cluster], out_hbm.at[cluster], sems.at[cluster])
        )
        copies[-1].start()
    for copy in copies:
        copy.wait()


def shards(slip, vertices, triangles, elem_map, near_pairs, near_count, far_pairs, far_coef, basis):
    clusters, rhs_count, unknowns = slip.shape
    rank_size = basis.shape[1]
    size = elem_map.shape[1]
    row_count = lax.axis_size("row")
    long_count = lax.axis_size("long")
    devices = row_count * long_count
    coupling = far_coef.reshape(-1, rank_size, rank_size)
    slots = clusters + NEARC

    pay = pl.pallas_call(
        coeffs_kernel,
        out_shape=jax.ShapeDtypeStruct((devices, rhs_count // 2, LANES), jnp.bfloat16),
        in_specs=[HBM] * 3 + [SMEM],
        out_specs=HBM,
        scratch_shapes=[
            pltpu.VMEM(slip.shape[1:], slip.dtype),
            pltpu.VMEM(basis.shape[1:], basis.dtype),
            pltpu.VMEM(near_pairs.shape, near_pairs.dtype),
            pltpu.VMEM((long_count, rhs_count // 2, LANES), jnp.bfloat16),
            pltpu.SemaphoreType.DMA((3,)),
            pltpu.SemaphoreType.DMA((row_count,)),
        ],
        compiler_params=pltpu.CompilerParams(vmem_limit_bytes=16 << 20),
        name="coeffs",
    )(
        *[
            pltpu.with_memory_space_constraint(array, pltpu.HBM)
            for array in (slip, basis, near_pairs)
        ],
        near_count,
    )
    everyone = lax.all_to_all(pay, ("row", "long"), 0, 0, tiled=True)

    xs, to_neighbour, geometry = pl.pallas_call(
        geometry_kernel,
        out_shape=[
            jax.ShapeDtypeStruct(slip.shape, jnp.bfloat16),
            jax.ShapeDtypeStruct((NEARC, rhs_count, unknowns + size), jnp.bfloat16),
            jax.ShapeDtypeStruct((clusters, 4, size), jnp.float32),
        ],
        in_specs=[VMEM] * 4 + [ANY],
        out_specs=[VMEM] * 3,
        compiler_params=pltpu.CompilerParams(vmem_limit_bytes=16 << 20),
        cost_estimate=pl.CostEstimate(
            flops=2_000_000, bytes_accessed=1_000_000, transcendentals=1_000
        ),
        name="geometry",
    )(slip, vertices, triangles, elem_map, pay)
    route = []
    for row in range(row_count):
        step = 1 if row % 2 == 0 else -1
        for owner in range(long_count):
            if 0 <= owner - step < long_count:
                route.append((row * long_count + owner - step, row * long_count + owner))
    halo = lax.ppermute(to_neighbour, ("row", "long"), route)

    window, places = pl.pallas_call(
        window_kernel,
        out_shape=[
            jax.ShapeDtypeStruct((slots, rhs_count, unknowns), jnp.bfloat16),
            jax.ShapeDtypeStruct((slots, 4, size), jnp.float32),
        ],
        in_specs=[VMEM] * 3,
        out_specs=[VMEM] * 2,
        compiler_params=pltpu.CompilerParams(vmem_limit_bytes=16 << 20),
        cost_estimate=pl.CostEstimate(flops=1000, bytes_accessed=1000, transcendentals=0),
        name="window",
    )(xs, geometry, halo)

    to_second, to_first, pair_list = pl.pallas_call(
        coupling_kernel,
        out_shape=[jax.ShapeDtypeStruct((coupling.shape[0] * rank_size, LANES), jnp.bfloat16)] * 2
        + [jax.ShapeDtypeStruct(far_pairs.shape, far_pairs.dtype)],
        in_specs=[VMEM, VMEM, ANY],
        out_specs=[VMEM] * 3,
        compiler_params=pltpu.CompilerParams(vmem_limit_bytes=16 << 20),
        cost_estimate=pl.CostEstimate(flops=1000, bytes_accessed=1000, transcendentals=0),
        name="coupling",
    )(coupling, far_pairs, pay)
    far, far_done = pl.pallas_call(
        functools.partial(far_kernel, clusters=clusters),
        out_shape=[
            jax.ShapeDtypeStruct((devices, rhs_count, clusters * rank_size), jnp.bfloat16),
            jax.ShapeDtypeStruct((8, LANES), jnp.float32),
        ],
        in_specs=[SMEM, VMEM, VMEM, VMEM],
        out_specs=[HBM, VMEM],
        scratch_shapes=[
            pltpu.VMEM((long_count, rhs_count, clusters * rank_size), jnp.bfloat16),
            pltpu.SemaphoreType.DMA((row_count,)),
        ]
        + [pltpu.VMEM((long_count, rhs_count, clusters * rank_size), jnp.float32)] * 4,
        compiler_params=pltpu.CompilerParams(vmem_limit_bytes=16 << 20),
        name="far",
    )(pair_list, everyone, to_second, to_first)
    far_terms = lax.all_to_all(far, ("row", "long"), 0, 0, tiled=True)

    near = pl.pallas_call(
        functools.partial(near_kernel, long_count=long_count, clusters=clusters),
        out_shape=jax.ShapeDtypeStruct((NEARC, rhs_count, unknowns), jnp.float32),
        in_specs=[VMEM] * 3 + [ANY],
        out_specs=VMEM,
        scratch_shapes=[
            pltpu.VMEM((slots, size, 8), jnp.float32),
            pltpu.VMEM((NEARC, 6, size, size), jnp.bfloat16),
            pltpu.VMEM((NEARC, 6, size, size), jnp.bfloat16),
        ],
        compiler_params=pltpu.CompilerParams(vmem_limit_bytes=24 << 20),
        cost_estimate=pl.CostEstimate(
            flops=1_000_000_000, bytes_accessed=1_000_000, transcendentals=660_000
        ),
        name="near",
    )(window, places, everyone, far_done)
    partner = [(row, row ^ 1) for row in range(row_count)]
    other = lax.ppermute(near, "row", partner)

    return pl.pallas_call(
        finish_kernel,
        out_shape=jax.ShapeDtypeStruct(slip.shape, jnp.float32),
        in_specs=[VMEM] * 4,
        out_specs=HBM,
        scratch_shapes=[
            pltpu.VMEM(slip.shape, jnp.float32),
            pltpu.SemaphoreType.DMA((clusters,)),
        ],
        compiler_params=pltpu.CompilerParams(vmem_limit_bytes=16 << 20),
        name="finish",
    )(near, other, far_terms, basis)


def solution(mesh):
    placed = (
        P("long", None, None),
        P(None, "long"),
        P(None, "long"),
        P("long", None),
        P(None, ("row", "long")),
        P(("row", "long")),
        P(None, ("row", "long")),
        P(("row", "long"), None),
        P("long", None, None),
    )
    return jax.shard_map(
        shards, mesh=mesh, in_specs=placed, out_specs=P("long", None, None), check_vma=False
    )
```

```python
import functools

import jax
import jax.numpy as jnp
from jax import lax
from jax.experimental import pallas as pl
from jax.experimental.pallas import tpu as pltpu
from jax.sharding import PartitionSpec as P

NEARC = 2
LANES = 128
ROWS = 16

soften = 0.25

VMEM = pl.BlockSpec(memory_space=pltpu.VMEM)
SMEM = pl.BlockSpec(memory_space=pltpu.SMEM)
HBM = pl.BlockSpec(memory_space=pltpu.HBM)
ANY = pl.BlockSpec(memory_space=pl.ANY)
SMALL = pl.CostEstimate(flops=1000, bytes_accessed=1000, transcendentals=0)


def first_place(row_count, long_count):
    return row_count // 2 * long_count // 2 + long_count // 2 - 1


def same_core(row_count, long_count):
    total = row_count // 2 * long_count
    order = [(place + first_place(row_count, long_count)) % total for place in range(total)]
    return [
        [(2 * (at // long_count) + core) * long_count + at % long_count for at in order]
        for core in range(2)
    ]


def place_in_core(row, owner, row_count, long_count):
    total = row_count // 2 * long_count
    return (row * long_count + owner + total - first_place(row_count, long_count)) % total


def lane_gather(table, index):
    length = table.shape[1]
    lane = index & (LANES - 1)
    chunk = index // LANES
    found = jnp.zeros(index.shape, table.dtype)
    for piece_id in range(-(-length // LANES)):
        piece = table[:, piece_id * LANES : min(length, (piece_id + 1) * LANES)]
        missing = LANES - piece.shape[1]
        if missing:
            piece = jnp.concatenate([piece, jnp.zeros((1, missing), table.dtype)], axis=1)
        picked = jnp.take_along_axis(jnp.broadcast_to(piece, index.shape), lane, axis=1)
        found = jnp.where(chunk == piece_id, picked, found)
    return found


def split_three(value):
    high = value.astype(jnp.bfloat16).astype(jnp.float32)
    rest = value - high
    middle = rest.astype(jnp.bfloat16).astype(jnp.float32)
    return [high, middle, rest - middle]


def coeffs_kernel(
    slip_hbm, basis_hbm, pairs_hbm, count_ref, pay_hbm, slip_ref, basis_ref, pairs_ref, sent_ref, sems, out_sems
):
    clusters = slip_hbm.shape[0]
    share, rhs_count, _ = slip_ref.shape
    rank_size = basis_ref.shape[1]
    begin = (lax.axis_index("row") // 2) % (clusters // share) * share
    copies = [
        pltpu.make_async_copy(slip_hbm.at[pl.ds(begin, share)], slip_ref, sems.at[0]),
        pltpu.make_async_copy(basis_hbm.at[pl.ds(begin, share)], basis_ref, sems.at[1]),
        pltpu.make_async_copy(pairs_hbm, pairs_ref, sems.at[2]),
    ]
    for copy in copies:
        copy.start()
    copies[2].wait()
    first = pairs_ref[0:1, :]
    kind = (first - lax.axis_index("long") * clusters) * (NEARC + 1) + pairs_ref[1:2, :] - first
    kinds = lax.broadcasted_iota(jnp.int32, (rhs_count, kind.shape[1]), 0)
    live = lax.broadcasted_iota(jnp.int32, kinds.shape, 1) < count_ref[0]
    counts = jnp.sum(jnp.where(live & (kinds == kind), 1.0, 0.0), axis=1, keepdims=True)
    copies[0].wait()
    copies[1].wait()
    coeffs = [
        lax.dot_general(
            slip_ref[turn].astype(jnp.bfloat16),
            basis_ref[turn],
            (((1,), (1,)), ((), ())),
            preferred_element_type=jnp.float32,
        )
        for turn in range(share)
    ]
    counts = jnp.broadcast_to(counts, (rhs_count, LANES - share * rank_size))
    pay = jnp.concatenate(coeffs + [counts], axis=1).astype(jnp.bfloat16)
    for target in range(sent_ref.shape[0]):
        sent_ref[target] = pay
    parts = pay_hbm.shape[0] // sent_ref.shape[0]
    sends = [
        pltpu.make_async_copy(
            sent_ref, pay_hbm.at[pl.ds(part * sent_ref.shape[0], sent_ref.shape[0])], out_sems.at[part]
        )
        for part in range(parts)
    ]
    for send in sends:
        send.start()
    for send in sends:
        send.wait()


def geometry_kernel(
    slip_ref, vertices_ref, triangles_ref, map_ref, after_ref, xs_ref, halo_ref, geom_ref
):
    clusters, rhs_count, unknowns = slip_ref.shape
    xs_ref[...] = slip_ref[...].astype(jnp.bfloat16)
    long_index = lax.axis_index("long")

    size = map_ref.shape[1]
    half = size // LANES
    slot_map = map_ref[...]
    index = jnp.concatenate(
        [slot_map[:, part * LANES : (part + 1) * LANES] for part in range(half)], axis=0
    )
    vertex_base = long_index * vertices_ref.shape[1]
    corners = []
    for corner_id in range(3):
        vertex = lane_gather(triangles_ref[corner_id : corner_id + 1, :], index) - vertex_base
        corners.append(
            [lane_gather(vertices_ref[axis_id : axis_id + 1, :], vertex) for axis_id in range(3)]
        )
    one, two, three = corners
    centre = [(one[a] + two[a] + three[a]) / 3.0 for a in range(3)]
    edge_one = [two[a] - one[a] for a in range(3)]
    edge_two = [three[a] - one[a] for a in range(3)]
    normal = [
        edge_one[1] * edge_two[2] - edge_one[2] * edge_two[1],
        edge_one[2] * edge_two[0] - edge_one[0] * edge_two[2],
        edge_one[0] * edge_two[1] - edge_one[1] * edge_two[0],
    ]
    area = 0.5 * jnp.sqrt(normal[0] * normal[0] + normal[1] * normal[1] + normal[2] * normal[2])
    geometry = []
    for value in centre + [area]:
        geometry.append(
            jnp.concatenate(
                [value[part * clusters : (part + 1) * clusters] for part in range(half)], axis=1
            )
        )
    for cluster in range(clusters):
        geom_ref[cluster] = jnp.concatenate(
            [whole[cluster : cluster + 1, :] for whole in geometry], axis=0
        )

    upward = lax.axis_index("row") % 2 == 0
    start = jnp.where(upward, clusters - NEARC, 0)
    pieces = [piece for whole in geometry for piece in split_three(whole)]
    for turn in range(NEARC):
        last = clusters - NEARC + turn
        rows = [
            jnp.where(upward, piece[last : last + 1, :], piece[turn : turn + 1, :])
            for piece in pieces
        ]
        rows.append(jnp.zeros((rhs_count - len(rows), size), jnp.float32))
        halo_ref[turn, :, 0:unknowns] = xs_ref[start + turn]
        halo_ref[turn, :, unknowns : unknowns + size] = jnp.concatenate(rows, axis=0).astype(
            jnp.bfloat16
        )


def window_kernel(xs_ref, geom_ref, halo_ref, slip_ref, place_ref):
    clusters, rhs_count, unknowns = xs_ref.shape
    size = geom_ref.shape[2]
    slots = clusters + NEARC
    odd = lax.axis_index("row") % 2

    def place_of(cluster):
        return (cluster + NEARC * (1 - odd) + slots) % slots

    for cluster in range(clusters):
        slip_ref[place_of(cluster)] = xs_ref[cluster]
        place_ref[place_of(cluster)] = geom_ref[cluster]
    for turn in range(NEARC):
        at = place_of(clusters + turn)
        slip_ref[at] = halo_ref[turn, :, 0:unknowns]
        pieces = halo_ref[turn, :, unknowns : unknowns + size].astype(jnp.float32)
        place_ref[at] = jnp.concatenate(
            [
                (pieces[3 * p + 2 : 3 * p + 3] + pieces[3 * p + 1 : 3 * p + 2])
                + pieces[3 * p : 3 * p + 1]
                for p in range(4)
            ],
            axis=0,
        )


def totals_kernel(pay_ref, after_ref, out_ref, *, long_count):
    row_count = 2 * pay_ref.shape[0] // long_count
    long_index = lax.axis_index("long")
    totals = [jnp.zeros(pay_ref.shape[1:], jnp.float32) for _ in range(2)]
    for row in range(row_count // 2):
        for source, owner in enumerate((long_index, jnp.maximum(long_index - 1, 0))):
            at = place_in_core(row, owner, row_count, long_count)
            totals[source] += pay_ref[at].astype(jnp.float32)
    lane_id = lax.broadcasted_iota(jnp.int32, out_ref.shape, 1)
    out_ref[...] = jnp.where(lane_id < 3 * LANES // 4, totals[0], totals[1])


def near_kernel(
    slip_ref, place_ref, mine_ref, theirs_ref, out_ref, cols_ref, even_ref, odd_ref, *, clusters
):
    slots, rhs_count, unknowns = slip_ref.shape
    size = place_ref.shape[2]
    totals = mine_ref[...] + theirs_ref[...]
    even = lax.axis_index("row") % 2 == 0
    kinds = lax.broadcasted_iota(jnp.int32, totals.shape, 0)
    lane_id = lax.broadcasted_iota(jnp.int32, totals.shape, 1)

    def count_of(place, u):
        both = []
        for cluster in (u, clusters - NEARC + u):
            reach = place - u - NEARC
            lower = cluster + jnp.minimum(reach, 0)
            inside = lower >= 0
            kind = jnp.where(inside, lower, lower + clusters) * (NEARC + 1) + jnp.abs(reach)
            lane = jnp.where(inside, LANES // 2, 3 * LANES // 4)
            both.append(jnp.where((kinds == kind) & (lane_id == lane), totals, 0.0))
        picked = jnp.sum(jnp.where(even, both[0], both[1]), axis=0, keepdims=True)
        return jnp.sum(picked, axis=1, keepdims=True)

    out_ref[...] = jnp.zeros(out_ref.shape, jnp.float32)
    for place in range(slots):
        rows = jnp.concatenate([place_ref[place], jnp.zeros((4, size), jnp.float32)], axis=0)
        cols_ref[place] = rows.T
    right = [[place_ref[NEARC + u, p : p + 1, :] for p in range(4)] for u in range(NEARC)]
    parts = [(0, 0), (1, 1), (2, 2), (0, 1), (0, 2), (1, 2)]

    def fill(place, targets, block_ref):
        for step in range(size // ROWS):
            here = pl.ds(step * ROWS, ROWS)
            column = cols_ref[place, here, :]
            left = [jnp.broadcast_to(column[:, p : p + 1], (ROWS, size)) for p in range(4)]
            for u in targets:
                offset = [left[p] - right[u][p] for p in range(3)]
                radius_sq = offset[0] * offset[0] + offset[1] * offset[1] + offset[2] * offset[2]
                inverse = lax.rsqrt(radius_sq + soften)
                flat = (left[3] * right[u][3]) * inverse
                cubed = flat * (inverse * inverse)
                scaled = [offset[p] * cubed for p in range(3)]
                for part_id, (i, j) in enumerate(parts):
                    term = offset[i] * scaled[j]
                    if i == j:
                        term = term + flat
                    block_ref[u, part_id, here, :] = term.astype(jnp.bfloat16)

    def apply(place, targets, block_ref):
        slip = slip_ref[place]
        pieces = [slip[:, p * size : (p + 1) * size] for p in range(3)]
        for u in targets:
            count = count_of(place, u)
            sums = [
                jnp.dot(pieces[p], block_ref[u, p], preferred_element_type=jnp.float32)
                for p in range(3)
            ]
            for part_id in range(3, 6):
                i, j = parts[part_id]
                both = jnp.dot(
                    jnp.concatenate([pieces[j], pieces[i]], axis=0),
                    block_ref[u, part_id],
                    preferred_element_type=jnp.float32,
                )
                sums[i] = sums[i] + both[0:rhs_count]
                sums[j] = sums[j] + both[rhs_count : 2 * rhs_count]
            for p in range(3):
                out_ref[u, :, p * size : (p + 1) * size] += count * sums[p]

    every = list(range(NEARC))
    fill(0, [0], even_ref)
    for u in range(1, NEARC):
        even_ref[u] = jnp.zeros(even_ref.shape[1:], jnp.bfloat16)

    def two_places(turn, carry):
        place = 2 * turn
        fill(place + 1, every, odd_ref)
        apply(place, every, even_ref)
        fill(place + 2, every, even_ref)
        apply(place + 1, every, odd_ref)
        return carry

    lax.fori_loop(0, (slots - 2) // 2, two_places, 0)
    fill(slots - 1, [NEARC - 1], odd_ref)
    apply(slots - 2, every, even_ref)
    apply(slots - 1, [NEARC - 1], odd_ref)


def coupling_kernel(coupling_ref, pairs_ref, after_ref, to_second_ref, to_first_ref, list_ref):
    list_ref[...] = pairs_ref[...]
    pair_count, rank_size, _ = coupling_ref.shape
    groups = LANES // rank_size
    for pair_id in range(pair_count):
        here = pl.ds(pair_id * rank_size, rank_size)
        coupling = coupling_ref[pair_id].astype(jnp.float32)
        for out_ref, value in ((to_second_ref, coupling), (to_first_ref, coupling.T)):
            out_ref[here, :] = jnp.concatenate([value] * groups, axis=1).astype(jnp.bfloat16)


def far_kernel(
    pairs_ref, coeff_ref, to_second_ref, to_first_ref, out_hbm, done_ref, sent_ref, sems, *total_refs, clusters
):
    done_ref[...] = jnp.zeros(done_ref.shape, jnp.float32)
    long_count, rhs_count, _ = total_refs[0].shape
    row_count = out_hbm.shape[0] // long_count
    pair_count = pairs_ref.shape[1]
    rank_size = LANES // clusters
    group_id = lax.broadcasted_iota(jnp.int32, (rhs_count, LANES), 1) // rank_size
    for total_ref in total_refs:
        total_ref[...] = jnp.zeros(total_ref.shape, jnp.float32)

    def coeff_of(cluster, group):
        share = clusters // 2
        at = place_in_core(cluster % clusters // share, cluster // clusters, row_count, long_count)
        whole = coeff_ref[at].astype(jnp.float32)
        both = pltpu.roll(whole, (LANES + rank_size * (group - cluster % share)) % LANES, 1)
        return jnp.where(group_id == group, both, 0.0)

    results = []
    for begin in range(0, pair_count, clusters):
        pair_ids = range(begin, min(begin + clusters, pair_count))
        depth = len(pair_ids) * rank_size
        here = pl.ds(begin * rank_size, depth)
        for source, target, matrix_ref in ((0, 1, to_second_ref), (1, 0, to_first_ref)):
            coeffs = jnp.concatenate(
                [coeff_of(pairs_ref[source, f], f - begin) for f in pair_ids], axis=0
            ).astype(jnp.bfloat16)
            value = jnp.dot(
                coeffs[:, 0:depth], matrix_ref[here, :], preferred_element_type=jnp.float32
            )
            for turn, f in enumerate(pair_ids):
                results.append(
                    (pairs_ref[target, f], value[turn * rhs_count : (turn + 1) * rhs_count])
                )
    for turn, (cluster, value) in enumerate(results):
        total_ref = total_refs[turn % len(total_refs)]
        total_ref[cluster // clusters] += jnp.where(group_id == cluster % clusters, value, 0.0)
    total = total_refs[0][...]
    for total_ref in total_refs[1:]:
        total = total + total_ref[...]
    sent_ref[...] = total.astype(jnp.bfloat16)
    copies = [
        pltpu.make_async_copy(
            sent_ref, out_hbm.at[pl.ds(copy_id * long_count, long_count)], sems.at[copy_id]
        )
        for copy_id in range(out_hbm.shape[0] // long_count)
    ]
    for copy in copies:
        copy.start()
    for copy in copies:
        copy.wait()


def finish_kernel(own_ref, other_ref, far_ref, basis_ref, out_hbm, sent_ref, sems):
    clusters, rank_size, unknowns = basis_ref.shape
    total = jnp.sum(far_ref[...].astype(jnp.float32), axis=0)
    group_id = lax.broadcasted_iota(jnp.int32, total.shape, 1) // rank_size
    flat_basis = basis_ref[...].reshape(clusters * rank_size, unknowns)
    even = lax.axis_index("row") % 2 == 0
    copies = []
    for cluster in range(clusters):
        u = cluster % NEARC
        here = even if cluster < NEARC else jnp.logical_not(even)
        near = jnp.where(here, own_ref[u], other_ref[u])
        picked = jnp.where(group_id == cluster, total, 0.0).astype(jnp.bfloat16)
        result = jnp.dot(picked, flat_basis, preferred_element_type=jnp.float32)
        sent_ref[cluster] = result + near
        copies.append(
            pltpu.make_async_copy(sent_ref.at[cluster], out_hbm.at[cluster], sems.at[cluster])
        )
        copies[-1].start()
    for copy in copies:
        copy.wait()


def shards(slip, vertices, triangles, elem_map, near_pairs, near_count, far_pairs, far_coef, basis):
    clusters, rhs_count, unknowns = slip.shape
    rank_size = basis.shape[1]
    size = elem_map.shape[1]
    row_count = lax.axis_size("row")
    long_count = lax.axis_size("long")
    devices = row_count * long_count
    share = clusters // 2
    coupling = far_coef.reshape(-1, rank_size, rank_size)
    slots = clusters + NEARC

    pay = pl.pallas_call(
        coeffs_kernel,
        out_shape=jax.ShapeDtypeStruct((devices // 2, rhs_count, LANES), jnp.bfloat16),
        in_specs=[HBM] * 3 + [SMEM],
        out_specs=HBM,
        scratch_shapes=[
            pltpu.VMEM((share,) + slip.shape[1:], slip.dtype),
            pltpu.VMEM((share,) + basis.shape[1:], basis.dtype),
            pltpu.VMEM(near_pairs.shape, near_pairs.dtype),
            pltpu.VMEM((long_count, rhs_count, LANES), jnp.bfloat16),
            pltpu.SemaphoreType.DMA((3,)),
            pltpu.SemaphoreType.DMA((row_count // 2,)),
        ],
        compiler_params=pltpu.CompilerParams(vmem_limit_bytes=16 << 20),
        name="coeffs",
    )(
        *[
            pltpu.with_memory_space_constraint(array, pltpu.HBM)
            for array in (slip, basis, near_pairs)
        ],
        near_count,
    )
    everyone = lax.all_to_all(
        pay, ("row", "long"), 0, 0, axis_index_groups=same_core(row_count, long_count), tiled=True
    )

    xs, to_neighbour, geometry = pl.pallas_call(
        geometry_kernel,
        out_shape=[
            jax.ShapeDtypeStruct(slip.shape, jnp.bfloat16),
            jax.ShapeDtypeStruct((NEARC, rhs_count, unknowns + size), jnp.bfloat16),
            jax.ShapeDtypeStruct((clusters, 4, size), jnp.float32),
        ],
        in_specs=[VMEM] * 4 + [ANY],
        out_specs=[VMEM] * 3,
        compiler_params=pltpu.CompilerParams(vmem_limit_bytes=16 << 20),
        cost_estimate=pl.CostEstimate(
            flops=2_000_000, bytes_accessed=1_000_000, transcendentals=1_000
        ),
        name="geometry",
    )(slip, vertices, triangles, elem_map, pay)
    route = []
    for row in range(row_count):
        step = 1 if row % 2 == 0 else -1
        for owner in range(long_count):
            if 0 <= owner - step < long_count:
                route.append((row * long_count + owner - step, row * long_count + owner))
    halo = lax.ppermute(to_neighbour, ("row", "long"), route)

    window, places = pl.pallas_call(
        window_kernel,
        out_shape=[
            jax.ShapeDtypeStruct((slots, rhs_count, unknowns), jnp.bfloat16),
            jax.ShapeDtypeStruct((slots, 4, size), jnp.float32),
        ],
        in_specs=[VMEM] * 3,
        out_specs=[VMEM] * 2,
        compiler_params=pltpu.CompilerParams(vmem_limit_bytes=16 << 20),
        cost_estimate=pl.CostEstimate(flops=1000, bytes_accessed=1000, transcendentals=0),
        name="window",
    )(xs, geometry, halo)

    to_second, to_first, pair_list = pl.pallas_call(
        coupling_kernel,
        out_shape=[jax.ShapeDtypeStruct((coupling.shape[0] * rank_size, LANES), jnp.bfloat16)] * 2
        + [jax.ShapeDtypeStruct(far_pairs.shape, far_pairs.dtype)],
        in_specs=[VMEM, VMEM, ANY],
        out_specs=[VMEM] * 3,
        compiler_params=pltpu.CompilerParams(vmem_limit_bytes=16 << 20),
        cost_estimate=pl.CostEstimate(flops=1000, bytes_accessed=1000, transcendentals=0),
        name="coupling",
    )(coupling, far_pairs, pay)
    far, far_done = pl.pallas_call(
        functools.partial(far_kernel, clusters=clusters),
        out_shape=[
            jax.ShapeDtypeStruct((devices, rhs_count, clusters * rank_size), jnp.bfloat16),
            jax.ShapeDtypeStruct((8, LANES), jnp.float32),
        ],
        in_specs=[SMEM, VMEM, VMEM, VMEM],
        out_specs=[HBM, VMEM],
        scratch_shapes=[
            pltpu.VMEM((long_count, rhs_count, clusters * rank_size), jnp.bfloat16),
            pltpu.SemaphoreType.DMA((row_count,)),
        ]
        + [pltpu.VMEM((long_count, rhs_count, clusters * rank_size), jnp.float32)] * 4,
        compiler_params=pltpu.CompilerParams(vmem_limit_bytes=16 << 20),
        name="far",
    )(pair_list, everyone, to_second, to_first)
    far_terms = lax.all_to_all(far, ("row", "long"), 0, 0, tiled=True)

    totals = pl.pallas_call(
        functools.partial(totals_kernel, long_count=long_count),
        out_shape=jax.ShapeDtypeStruct((rhs_count, LANES), jnp.float32),
        in_specs=[VMEM, ANY],
        out_specs=VMEM,
        compiler_params=pltpu.CompilerParams(vmem_limit_bytes=16 << 20),
        cost_estimate=SMALL,
        name="totals",
    )(everyone, far_done)
    partner = [(row, row ^ 1) for row in range(row_count)]
    totals_other = lax.ppermute(totals, "row", partner)

    near = pl.pallas_call(
        functools.partial(near_kernel, clusters=clusters),
        out_shape=jax.ShapeDtypeStruct((NEARC, rhs_count, unknowns), jnp.float32),
        in_specs=[VMEM] * 4,
        out_specs=VMEM,
        scratch_shapes=[
            pltpu.VMEM((slots, size, 8), jnp.float32),
            pltpu.VMEM((NEARC, 6, size, size), jnp.bfloat16),
            pltpu.VMEM((NEARC, 6, size, size), jnp.bfloat16),
        ],
        compiler_params=pltpu.CompilerParams(vmem_limit_bytes=24 << 20),
        cost_estimate=SMALL,
        name="near",
    )(window, places, totals, totals_other)
    other = lax.ppermute(near, "row", partner)

    return pl.pallas_call(
        finish_kernel,
        out_shape=jax.ShapeDtypeStruct(slip.shape, jnp.float32),
        in_specs=[VMEM] * 4,
        out_specs=HBM,
        scratch_shapes=[
            pltpu.VMEM(slip.shape, jnp.float32),
            pltpu.SemaphoreType.DMA((clusters,)),
        ],
        compiler_params=pltpu.CompilerParams(vmem_limit_bytes=16 << 20),
        name="finish",
    )(near, other, far_terms, basis)


def solution(mesh):
    placed = (
        P("long", None, None),
        P(None, "long"),
        P(None, "long"),
        P("long", None),
        P(None, ("row", "long")),
        P(("row", "long")),
        P(None, ("row", "long")),
        P(("row", "long"), None),
        P("long", None, None),
    )
    return jax.shard_map(
        shards, mesh=mesh, in_specs=placed, out_specs=P("long", None, None), check_vma=False
    )
```

```python
import functools

import jax
import jax.numpy as jnp
from jax import lax
from jax.experimental import pallas as pl
from jax.experimental.pallas import tpu as pltpu
from jax.sharding import PartitionSpec as P

NEARC = 2
LANES = 128
ROWS = 16

soften = 0.25

VMEM = pl.BlockSpec(memory_space=pltpu.VMEM)
SMEM = pl.BlockSpec(memory_space=pltpu.SMEM)
HBM = pl.BlockSpec(memory_space=pltpu.HBM)
ANY = pl.BlockSpec(memory_space=pl.ANY)
SMALL = pl.CostEstimate(flops=1000, bytes_accessed=1000, transcendentals=0)


def first_place(row_count, long_count):
    return row_count // 2 * long_count // 2 + long_count // 2 - 1


def same_core(row_count, long_count):
    total = row_count // 2 * long_count
    order = [(place + first_place(row_count, long_count)) % total for place in range(total)]
    return [
        [(2 * (at // long_count) + core) * long_count + at % long_count for at in order]
        for core in range(2)
    ]


def place_in_core(row, owner, row_count, long_count):
    total = row_count // 2 * long_count
    return (row * long_count + owner + total - first_place(row_count, long_count)) % total


def lane_gather(table, index):
    length = table.shape[1]
    lane = index & (LANES - 1)
    chunk = index // LANES
    found = jnp.zeros(index.shape, table.dtype)
    for piece_id in range(-(-length // LANES)):
        piece = table[:, piece_id * LANES : min(length, (piece_id + 1) * LANES)]
        missing = LANES - piece.shape[1]
        if missing:
            piece = jnp.concatenate([piece, jnp.zeros((1, missing), table.dtype)], axis=1)
        picked = jnp.take_along_axis(jnp.broadcast_to(piece, index.shape), lane, axis=1)
        found = jnp.where(chunk == piece_id, picked, found)
    return found


def split_three(value):
    high = value.astype(jnp.bfloat16).astype(jnp.float32)
    rest = value - high
    middle = rest.astype(jnp.bfloat16).astype(jnp.float32)
    return [high, middle, rest - middle]


def coeffs_kernel(
    slip_hbm, basis_hbm, pairs_hbm, count_ref, pay_hbm, slip_ref, basis_ref, pairs_ref, sent_ref, sems, out_sems
):
    clusters = slip_hbm.shape[0]
    share, rhs_count, _ = slip_ref.shape
    rank_size = basis_ref.shape[1]
    begin = (lax.axis_index("row") // 2) % (clusters // share) * share
    copies = [
        pltpu.make_async_copy(slip_hbm.at[pl.ds(begin, share)], slip_ref, sems.at[0]),
        pltpu.make_async_copy(basis_hbm.at[pl.ds(begin, share)], basis_ref, sems.at[1]),
        pltpu.make_async_copy(pairs_hbm, pairs_ref, sems.at[2]),
    ]
    for copy in copies:
        copy.start()
    copies[2].wait()
    first = pairs_ref[0:1, :]
    kind = (first - lax.axis_index("long") * clusters) * (NEARC + 1) + pairs_ref[1:2, :] - first
    kinds = lax.broadcasted_iota(jnp.int32, (rhs_count, kind.shape[1]), 0)
    live = lax.broadcasted_iota(jnp.int32, kinds.shape, 1) < count_ref[0]
    counts = jnp.sum(jnp.where(live & (kinds == kind), 1.0, 0.0), axis=1, keepdims=True)
    copies[0].wait()
    copies[1].wait()
    coeffs = [
        lax.dot_general(
            slip_ref[turn].astype(jnp.bfloat16),
            basis_ref[turn],
            (((1,), (1,)), ((), ())),
            preferred_element_type=jnp.float32,
        )
        for turn in range(share)
    ]
    counts = jnp.broadcast_to(counts, (rhs_count, LANES - share * rank_size))
    pay = jnp.concatenate(coeffs + [counts], axis=1).astype(jnp.bfloat16)
    for target in range(sent_ref.shape[0]):
        sent_ref[target] = pay
    parts = pay_hbm.shape[0] // sent_ref.shape[0]
    sends = [
        pltpu.make_async_copy(
            sent_ref, pay_hbm.at[pl.ds(part * sent_ref.shape[0], sent_ref.shape[0])], out_sems.at[part]
        )
        for part in range(parts)
    ]
    for send in sends:
        send.start()
    for send in sends:
        send.wait()


def geometry_kernel(
    slip_ref, vertices_ref, triangles_ref, map_ref, after_ref, xs_ref, halo_ref, geom_ref
):
    clusters, rhs_count, unknowns = slip_ref.shape
    xs_ref[...] = slip_ref[...].astype(jnp.bfloat16)
    long_index = lax.axis_index("long")

    size = map_ref.shape[1]
    half = size // LANES
    slot_map = map_ref[...]
    index = jnp.concatenate(
        [slot_map[:, part * LANES : (part + 1) * LANES] for part in range(half)], axis=0
    )
    vertex_base = long_index * vertices_ref.shape[1]
    corners = []
    for corner_id in range(3):
        vertex = lane_gather(triangles_ref[corner_id : corner_id + 1, :], index) - vertex_base
        corners.append(
            [lane_gather(vertices_ref[axis_id : axis_id + 1, :], vertex) for axis_id in range(3)]
        )
    one, two, three = corners
    centre = [(one[a] + two[a] + three[a]) / 3.0 for a in range(3)]
    edge_one = [two[a] - one[a] for a in range(3)]
    edge_two = [three[a] - one[a] for a in range(3)]
    normal = [
        edge_one[1] * edge_two[2] - edge_one[2] * edge_two[1],
        edge_one[2] * edge_two[0] - edge_one[0] * edge_two[2],
        edge_one[0] * edge_two[1] - edge_one[1] * edge_two[0],
    ]
    area = 0.5 * jnp.sqrt(normal[0] * normal[0] + normal[1] * normal[1] + normal[2] * normal[2])
    geometry = []
    for value in centre + [area]:
        geometry.append(
            jnp.concatenate(
                [value[part * clusters : (part + 1) * clusters] for part in range(half)], axis=1
            )
        )
    for cluster in range(clusters):
        geom_ref[cluster] = jnp.concatenate(
            [whole[cluster : cluster + 1, :] for whole in geometry], axis=0
        )

    upward = lax.axis_index("row") % 2 == 0
    start = jnp.where(upward, clusters - NEARC, 0)
    pieces = [piece for whole in geometry for piece in split_three(whole)]
    for turn in range(NEARC):
        last = clusters - NEARC + turn
        rows = [
            jnp.where(upward, piece[last : last + 1, :], piece[turn : turn + 1, :])
            for piece in pieces
        ]
        rows.append(jnp.zeros((rhs_count - len(rows), size), jnp.float32))
        halo_ref[turn, :, 0:unknowns] = xs_ref[start + turn]
        halo_ref[turn, :, unknowns : unknowns + size] = jnp.concatenate(rows, axis=0).astype(
            jnp.bfloat16
        )


def window_kernel(xs_ref, geom_ref, halo_ref, slip_ref, place_ref):
    clusters, rhs_count, unknowns = xs_ref.shape
    size = geom_ref.shape[2]
    slots = clusters + NEARC
    odd = lax.axis_index("row") % 2

    def place_of(cluster):
        return (cluster + NEARC * (1 - odd) + slots) % slots

    for cluster in range(clusters):
        slip_ref[place_of(cluster)] = xs_ref[cluster]
        place_ref[place_of(cluster)] = geom_ref[cluster]
    for turn in range(NEARC):
        at = place_of(clusters + turn)
        slip_ref[at] = halo_ref[turn, :, 0:unknowns]
        pieces = halo_ref[turn, :, unknowns : unknowns + size].astype(jnp.float32)
        place_ref[at] = jnp.concatenate(
            [
                (pieces[3 * p + 2 : 3 * p + 3] + pieces[3 * p + 1 : 3 * p + 2])
                + pieces[3 * p : 3 * p + 1]
                for p in range(4)
            ],
            axis=0,
        )


def totals_kernel(pay_ref, out_ref, *, long_count):
    row_count = 2 * pay_ref.shape[0] // long_count
    long_index = lax.axis_index("long")
    totals = [jnp.zeros(pay_ref.shape[1:], jnp.float32) for _ in range(2)]
    for row in range(row_count // 2):
        for source, owner in enumerate((long_index, jnp.maximum(long_index - 1, 0))):
            at = place_in_core(row, owner, row_count, long_count)
            totals[source] += pay_ref[at].astype(jnp.float32)
    lane_id = lax.broadcasted_iota(jnp.int32, out_ref.shape, 1)
    out_ref[...] = jnp.where(lane_id < 3 * LANES // 4, totals[0], totals[1])


def near_kernel(
    slip_ref, place_ref, mine_ref, theirs_ref, after_ref, out_ref, cols_ref, even_ref, odd_ref, *, clusters
):
    slots, rhs_count, unknowns = slip_ref.shape
    size = place_ref.shape[2]
    totals = mine_ref[...] + theirs_ref[...]
    even = lax.axis_index("row") % 2 == 0
    kinds = lax.broadcasted_iota(jnp.int32, totals.shape, 0)
    lane_id = lax.broadcasted_iota(jnp.int32, totals.shape, 1)

    def count_of(place, u):
        both = []
        for cluster in (u, clusters - NEARC + u):
            reach = place - u - NEARC
            lower = cluster + jnp.minimum(reach, 0)
            inside = lower >= 0
            kind = jnp.where(inside, lower, lower + clusters) * (NEARC + 1) + jnp.abs(reach)
            lane = jnp.where(inside, LANES // 2, 3 * LANES // 4)
            both.append(jnp.where((kinds == kind) & (lane_id == lane), totals, 0.0))
        picked = jnp.sum(jnp.where(even, both[0], both[1]), axis=0, keepdims=True)
        return jnp.sum(picked, axis=1, keepdims=True)

    out_ref[...] = jnp.zeros(out_ref.shape, jnp.float32)
    for place in range(slots):
        rows = jnp.concatenate([place_ref[place], jnp.zeros((4, size), jnp.float32)], axis=0)
        cols_ref[place] = rows.T
    right = [[place_ref[NEARC + u, p : p + 1, :] for p in range(4)] for u in range(NEARC)]
    parts = [(0, 0), (1, 1), (2, 2), (0, 1), (0, 2), (1, 2)]

    def fill(place, targets, block_ref):
        for step in range(size // ROWS):
            here = pl.ds(step * ROWS, ROWS)
            column = cols_ref[place, here, :]
            left = [jnp.broadcast_to(column[:, p : p + 1], (ROWS, size)) for p in range(4)]
            for u in targets:
                offset = [left[p] - right[u][p] for p in range(3)]
                radius_sq = offset[0] * offset[0] + offset[1] * offset[1] + offset[2] * offset[2]
                inverse = lax.rsqrt(radius_sq + soften)
                flat = (left[3] * right[u][3]) * inverse
                cubed = flat * (inverse * inverse)
                scaled = [offset[p] * cubed for p in range(3)]
                for part_id, (i, j) in enumerate(parts):
                    term = offset[i] * scaled[j]
                    if i == j:
                        term = term + flat
                    block_ref[u, part_id, here, :] = term.astype(jnp.bfloat16)

    def apply(place, targets, block_ref):
        slip = slip_ref[place]
        pieces = [slip[:, p * size : (p + 1) * size] for p in range(3)]
        for u in targets:
            count = count_of(place, u)
            sums = [
                jnp.dot(pieces[p], block_ref[u, p], preferred_element_type=jnp.float32)
                for p in range(3)
            ]
            for part_id in range(3, 6):
                i, j = parts[part_id]
                both = jnp.dot(
                    jnp.concatenate([pieces[j], pieces[i]], axis=0),
                    block_ref[u, part_id],
                    preferred_element_type=jnp.float32,
                )
                sums[i] = sums[i] + both[0:rhs_count]
                sums[j] = sums[j] + both[rhs_count : 2 * rhs_count]
            for p in range(3):
                out_ref[u, :, p * size : (p + 1) * size] += count * sums[p]

    every = list(range(NEARC))
    fill(0, [0], even_ref)
    for u in range(1, NEARC):
        even_ref[u] = jnp.zeros(even_ref.shape[1:], jnp.bfloat16)

    def two_places(turn, carry):
        place = 2 * turn
        fill(place + 1, every, odd_ref)
        apply(place, every, even_ref)
        fill(place + 2, every, even_ref)
        apply(place + 1, every, odd_ref)
        return carry

    lax.fori_loop(0, (slots - 2) // 2, two_places, 0)
    fill(slots - 1, [NEARC - 1], odd_ref)
    apply(slots - 2, every, even_ref)
    apply(slots - 1, [NEARC - 1], odd_ref)


def coupling_kernel(coupling_ref, pairs_ref, after_ref, to_second_ref, to_first_ref, list_ref):
    list_ref[...] = pairs_ref[...]
    pair_count, rank_size, _ = coupling_ref.shape
    groups = LANES // rank_size
    for pair_id in range(pair_count):
        here = pl.ds(pair_id * rank_size, rank_size)
        coupling = coupling_ref[pair_id].astype(jnp.float32)
        for out_ref, value in ((to_second_ref, coupling), (to_first_ref, coupling.T)):
            out_ref[here, :] = jnp.concatenate([value] * groups, axis=1).astype(jnp.bfloat16)


def far_kernel(
    pairs_ref, coeff_ref, to_second_ref, to_first_ref, out_hbm, done_ref, sent_ref, sems, moved_ref, *total_refs, clusters, row_count
):
    done_ref[...] = jnp.zeros(done_ref.shape, jnp.float32)
    long_count, rhs_count, _ = total_refs[0].shape
    pair_count = pairs_ref.shape[1]
    rank_size = LANES // clusters
    group_id = lax.broadcasted_iota(jnp.int32, (rhs_count, LANES), 1) // rank_size
    for total_ref in total_refs:
        total_ref[...] = jnp.zeros(total_ref.shape, jnp.float32)

    share = clusters // 2
    for at in range(coeff_ref.shape[0]):
        whole = coeff_ref[at].astype(jnp.float32)
        for turn in range(share):
            moved_ref[at * share + turn] = (
                pltpu.roll(whole, LANES - rank_size * turn, 1) if turn else whole
            )

    def coeff_of(cluster, group):
        at = place_in_core(cluster % clusters // share, cluster // clusters, row_count, long_count)
        whole = moved_ref[at * share + cluster % share]
        both = pltpu.roll(whole, rank_size * group, 1) if group else whole
        return jnp.where(group_id == group, both, 0.0)

    results = []
    for begin in range(0, pair_count, clusters):
        pair_ids = range(begin, min(begin + clusters, pair_count))
        depth = len(pair_ids) * rank_size
        here = pl.ds(begin * rank_size, depth)
        for source, target, matrix_ref in ((0, 1, to_second_ref), (1, 0, to_first_ref)):
            coeffs = jnp.concatenate(
                [coeff_of(pairs_ref[source, f], f - begin) for f in pair_ids], axis=0
            ).astype(jnp.bfloat16)
            value = jnp.dot(
                coeffs[:, 0:depth], matrix_ref[here, :], preferred_element_type=jnp.float32
            )
            for turn, f in enumerate(pair_ids):
                results.append(
                    (pairs_ref[target, f], value[turn * rhs_count : (turn + 1) * rhs_count])
                )
    for turn, (cluster, value) in enumerate(results):
        total_ref = total_refs[turn % len(total_refs)]
        total_ref[cluster // clusters] += jnp.where(group_id == cluster % clusters, value, 0.0)
    total = total_refs[0][...]
    for total_ref in total_refs[1:]:
        total = total + total_ref[...]
    sent_ref[...] = total
    copies = []
    for row in range(row_count // 2):
        first = place_in_core(row, 0, row_count, long_count)
        kept = min(long_count, out_hbm.shape[0] - first)
        pieces = [(0, first, kept)]
        if kept < long_count:
            pieces.append((kept, 0, long_count - kept))
        for source, target, length in pieces:
            copies.append(
                pltpu.make_async_copy(
                    sent_ref.at[pl.ds(source, length)],
                    out_hbm.at[pl.ds(target, length)],
                    sems.at[len(copies)],
                )
            )
    for copy in copies:
        copy.start()
    for copy in copies:
        copy.wait()


def finish_kernel(own_ref, other_ref, far_ref, far_other_ref, basis_ref, out_hbm, sent_ref, sems):
    clusters, rank_size, unknowns = basis_ref.shape
    even = lax.axis_index("row") % 2 == 0
    mine = jnp.sum(far_ref[...], axis=0)
    theirs = jnp.sum(far_other_ref[...], axis=0)
    total = jnp.where(even, mine, theirs) + jnp.where(even, theirs, mine)
    group_id = lax.broadcasted_iota(jnp.int32, total.shape, 1) // rank_size
    flat_basis = basis_ref[...].reshape(clusters * rank_size, unknowns)
    copies = []
    for cluster in range(clusters):
        u = cluster % NEARC
        here = even if cluster < NEARC else jnp.logical_not(even)
        near = jnp.where(here, own_ref[u], other_ref[u])
        picked = jnp.where(group_id == cluster, total, 0.0).astype(jnp.bfloat16)
        result = jnp.dot(picked, flat_basis, preferred_element_type=jnp.float32)
        sent_ref[cluster] = result + near
        copies.append(
            pltpu.make_async_copy(sent_ref.at[cluster], out_hbm.at[cluster], sems.at[cluster])
        )
        copies[-1].start()
    for copy in copies:
        copy.wait()


def shards(slip, vertices, triangles, elem_map, near_pairs, near_count, far_pairs, far_coef, basis):
    clusters, rhs_count, unknowns = slip.shape
    rank_size = basis.shape[1]
    size = elem_map.shape[1]
    row_count = lax.axis_size("row")
    long_count = lax.axis_size("long")
    devices = row_count * long_count
    share = clusters // 2
    coupling = far_coef.reshape(-1, rank_size, rank_size)
    slots = clusters + NEARC

    pay = pl.pallas_call(
        coeffs_kernel,
        out_shape=jax.ShapeDtypeStruct((devices // 2, rhs_count, LANES), jnp.bfloat16),
        in_specs=[HBM] * 3 + [SMEM],
        out_specs=HBM,
        scratch_shapes=[
            pltpu.VMEM((share,) + slip.shape[1:], slip.dtype),
            pltpu.VMEM((share,) + basis.shape[1:], basis.dtype),
            pltpu.VMEM(near_pairs.shape, near_pairs.dtype),
            pltpu.VMEM((long_count, rhs_count, LANES), jnp.bfloat16),
            pltpu.SemaphoreType.DMA((3,)),
            pltpu.SemaphoreType.DMA((row_count // 2,)),
        ],
        compiler_params=pltpu.CompilerParams(vmem_limit_bytes=16 << 20),
        name="coeffs",
    )(
        *[
            pltpu.with_memory_space_constraint(array, pltpu.HBM)
            for array in (slip, basis, near_pairs)
        ],
        near_count,
    )
    everyone = lax.all_to_all(
        pay, ("row", "long"), 0, 0, axis_index_groups=same_core(row_count, long_count), tiled=True
    )

    xs, to_neighbour, geometry = pl.pallas_call(
        geometry_kernel,
        out_shape=[
            jax.ShapeDtypeStruct(slip.shape, jnp.bfloat16),
            jax.ShapeDtypeStruct((NEARC, rhs_count, unknowns + size), jnp.bfloat16),
            jax.ShapeDtypeStruct((clusters, 4, size), jnp.float32),
        ],
        in_specs=[VMEM] * 4 + [ANY],
        out_specs=[VMEM] * 3,
        compiler_params=pltpu.CompilerParams(vmem_limit_bytes=16 << 20),
        cost_estimate=pl.CostEstimate(
            flops=2_000_000, bytes_accessed=1_000_000, transcendentals=1_000
        ),
        name="geometry",
    )(slip, vertices, triangles, elem_map, pay)
    route = []
    for row in range(row_count):
        step = 1 if row % 2 == 0 else -1
        for owner in range(long_count):
            if 0 <= owner - step < long_count:
                route.append((row * long_count + owner - step, row * long_count + owner))
    halo = lax.ppermute(to_neighbour, ("row", "long"), route)

    window, places = pl.pallas_call(
        window_kernel,
        out_shape=[
            jax.ShapeDtypeStruct((slots, rhs_count, unknowns), jnp.bfloat16),
            jax.ShapeDtypeStruct((slots, 4, size), jnp.float32),
        ],
        in_specs=[VMEM] * 3,
        out_specs=[VMEM] * 2,
        compiler_params=pltpu.CompilerParams(vmem_limit_bytes=16 << 20),
        cost_estimate=pl.CostEstimate(flops=1000, bytes_accessed=1000, transcendentals=0),
        name="window",
    )(xs, geometry, halo)

    to_second, to_first, pair_list = pl.pallas_call(
        coupling_kernel,
        out_shape=[jax.ShapeDtypeStruct((coupling.shape[0] * rank_size, LANES), jnp.bfloat16)] * 2
        + [jax.ShapeDtypeStruct(far_pairs.shape, far_pairs.dtype)],
        in_specs=[VMEM, VMEM, ANY],
        out_specs=[VMEM] * 3,
        compiler_params=pltpu.CompilerParams(vmem_limit_bytes=16 << 20),
        cost_estimate=pl.CostEstimate(flops=1000, bytes_accessed=1000, transcendentals=0),
        name="coupling",
    )(coupling, far_pairs, pay)
    far, far_done = pl.pallas_call(
        functools.partial(far_kernel, clusters=clusters, row_count=row_count),
        out_shape=[
            jax.ShapeDtypeStruct((devices // 2, rhs_count, clusters * rank_size), jnp.float32),
            jax.ShapeDtypeStruct((8, LANES), jnp.float32),
        ],
        in_specs=[SMEM, VMEM, VMEM, VMEM],
        out_specs=[HBM, VMEM],
        scratch_shapes=[
            pltpu.VMEM((long_count, rhs_count, clusters * rank_size), jnp.float32),
            pltpu.SemaphoreType.DMA((row_count,)),
            pltpu.VMEM((devices // 2 * share, rhs_count, LANES), jnp.float32),
        ]
        + [pltpu.VMEM((long_count, rhs_count, clusters * rank_size), jnp.float32)] * 4,
        compiler_params=pltpu.CompilerParams(vmem_limit_bytes=16 << 20),
        name="far",
    )(pair_list, everyone, to_second, to_first)
    far_terms = lax.all_to_all(
        far, ("row", "long"), 0, 0, axis_index_groups=same_core(row_count, long_count), tiled=True
    )
    partner = [(row, row ^ 1) for row in range(row_count)]
    far_other = lax.ppermute(far_terms, "row", partner)

    totals = pl.pallas_call(
        functools.partial(totals_kernel, long_count=long_count),
        out_shape=jax.ShapeDtypeStruct((rhs_count, LANES), jnp.float32),
        in_specs=[VMEM],
        out_specs=VMEM,
        compiler_params=pltpu.CompilerParams(vmem_limit_bytes=16 << 20),
        cost_estimate=SMALL,
        name="totals",
    )(everyone)
    totals_other = lax.ppermute(totals, "row", partner)

    near = pl.pallas_call(
        functools.partial(near_kernel, clusters=clusters),
        out_shape=jax.ShapeDtypeStruct((NEARC, rhs_count, unknowns), jnp.float32),
        in_specs=[VMEM] * 4 + [ANY],
        out_specs=VMEM,
        scratch_shapes=[
            pltpu.VMEM((slots, size, 8), jnp.float32),
            pltpu.VMEM((NEARC, 6, size, size), jnp.bfloat16),
            pltpu.VMEM((NEARC, 6, size, size), jnp.bfloat16),
        ],
        compiler_params=pltpu.CompilerParams(vmem_limit_bytes=24 << 20),
        cost_estimate=pl.CostEstimate(
            flops=1_000_000_000, bytes_accessed=1_000_000, transcendentals=660_000
        ),
        name="near",
    )(window, places, totals, totals_other, far_done)
    other = lax.ppermute(near, "row", partner)

    return pl.pallas_call(
        finish_kernel,
        out_shape=jax.ShapeDtypeStruct(slip.shape, jnp.float32),
        in_specs=[VMEM] * 5,
        out_specs=HBM,
        scratch_shapes=[
            pltpu.VMEM(slip.shape, jnp.float32),
            pltpu.SemaphoreType.DMA((clusters,)),
        ],
        compiler_params=pltpu.CompilerParams(vmem_limit_bytes=16 << 20),
        name="finish",
    )(near, other, far_terms, far_other, basis)


def solution(mesh):
    placed = (
        P("long", None, None),
        P(None, "long"),
        P(None, "long"),
        P("long", None),
        P(None, ("row", "long")),
        P(("row", "long")),
        P(None, ("row", "long")),
        P(("row", "long"), None),
        P("long", None, None),
    )
    return jax.shard_map(
        shards, mesh=mesh, in_specs=placed, out_specs=P("long", None, None), check_vma=False
    )
```

```python
import functools

import jax
import jax.numpy as jnp
from jax import lax
from jax.experimental import pallas as pl
from jax.experimental.pallas import tpu as pltpu
from jax.sharding import PartitionSpec as P

NEARC = 2
LANES = 128
AHEAD = 2
ROWS = 16

soften = 0.25

VMEM = pl.BlockSpec(memory_space=pltpu.VMEM)
SMEM = pl.BlockSpec(memory_space=pltpu.SMEM)
HBM = pl.BlockSpec(memory_space=pltpu.HBM)
ANY = pl.BlockSpec(memory_space=pl.ANY)


def exchange_order(row_count, long_count):
    order = list(range(0, AHEAD * long_count, long_count))
    for owner in reversed(range(long_count)):
        for row in range(row_count):
            if owner or row >= AHEAD:
                order.append(row * long_count + owner)
    return order


def place_of(row, owner, row_count, long_count):
    place = AHEAD + (long_count - 1 - owner) * row_count + row
    at_first = jnp.where(row < AHEAD, row, place - AHEAD)
    return jnp.where(owner == 0, at_first, place)


def everyone_sends(chunks, row_count, long_count):
    order = [exchange_order(row_count, long_count)]
    return lax.all_to_all(chunks, ("row", "long"), 0, 0, axis_index_groups=order, tiled=True)


def lane_gather(table, index):
    length = table.shape[1]
    lane = index & (LANES - 1)
    chunk = index // LANES
    found = jnp.zeros(index.shape, table.dtype)
    for piece_id in range(-(-length // LANES)):
        piece = table[:, piece_id * LANES : min(length, (piece_id + 1) * LANES)]
        missing = LANES - piece.shape[1]
        if missing:
            piece = jnp.concatenate([piece, jnp.zeros((1, missing), table.dtype)], axis=1)
        picked = jnp.take_along_axis(jnp.broadcast_to(piece, index.shape), lane, axis=1)
        found = jnp.where(chunk == piece_id, picked, found)
    return found


def split_three(value):
    high = value.astype(jnp.bfloat16).astype(jnp.float32)
    rest = value - high
    middle = rest.astype(jnp.bfloat16).astype(jnp.float32)
    return [high, middle, rest - middle]


def coeffs_kernel(
    slip_hbm, basis_hbm, pairs_hbm, count_ref, pay_hbm, slip_ref, basis_ref, pairs_ref, sent_ref, sems, out_sems
):
    clusters = slip_hbm.shape[0]
    rhs_count = slip_ref.shape[0]
    rank_size = basis_ref.shape[0]
    mine = lax.axis_index("row") % clusters
    copies = [
        pltpu.make_async_copy(slip_hbm.at[mine], slip_ref, sems.at[0]),
        pltpu.make_async_copy(basis_hbm.at[mine], basis_ref, sems.at[1]),
        pltpu.make_async_copy(pairs_hbm, pairs_ref, sems.at[2]),
    ]
    for copy in copies:
        copy.start()
    half = rhs_count // 2
    copies[2].wait()
    first = pairs_ref[0:1, :]
    kind = (first - lax.axis_index("long") * clusters) * (NEARC + 1) + pairs_ref[1:2, :] - first
    kinds = lax.broadcasted_iota(jnp.int32, (half, kind.shape[1]), 0)
    live = lax.broadcasted_iota(jnp.int32, kinds.shape, 1) < count_ref[0]
    low = jnp.sum(jnp.where(live & (kinds == kind), 1.0, 0.0), axis=1, keepdims=True)
    high = jnp.sum(jnp.where(live & (kinds + half == kind), 1.0, 0.0), axis=1, keepdims=True)
    copies[0].wait()
    copies[1].wait()
    coeffs = lax.dot_general(
        slip_ref[...].astype(jnp.bfloat16),
        basis_ref[...],
        (((1,), (1,)), ((), ())),
        preferred_element_type=jnp.float32,
    )
    counts = [jnp.broadcast_to(value, (half, rank_size)) for value in (low, high)]
    pay = jnp.concatenate([coeffs[0:half], coeffs[half:]] + counts, axis=1).astype(jnp.bfloat16)
    for target in range(sent_ref.shape[0]):
        sent_ref[target] = pay
    parts = pay_hbm.shape[0] // sent_ref.shape[0]
    sends = [
        pltpu.make_async_copy(
            sent_ref, pay_hbm.at[pl.ds(part * sent_ref.shape[0], sent_ref.shape[0])], out_sems.at[part]
        )
        for part in range(parts)
    ]
    for send in sends:
        send.start()
    for send in sends:
        send.wait()


def geometry_kernel(
    slip_ref, vertices_ref, triangles_ref, map_ref, after_ref, xs_ref, halo_ref, geom_ref
):
    clusters, rhs_count, unknowns = slip_ref.shape
    xs_ref[...] = slip_ref[...].astype(jnp.bfloat16)
    long_index = lax.axis_index("long")

    size = map_ref.shape[1]
    half = size // LANES
    slot_map = map_ref[...]
    index = jnp.concatenate(
        [slot_map[:, part * LANES : (part + 1) * LANES] for part in range(half)], axis=0
    )
    vertex_base = long_index * vertices_ref.shape[1]
    corners = []
    for corner_id in range(3):
        vertex = lane_gather(triangles_ref[corner_id : corner_id + 1, :], index) - vertex_base
        corners.append(
            [lane_gather(vertices_ref[axis_id : axis_id + 1, :], vertex) for axis_id in range(3)]
        )
    one, two, three = corners
    centre = [(one[a] + two[a] + three[a]) / 3.0 for a in range(3)]
    edge_one = [two[a] - one[a] for a in range(3)]
    edge_two = [three[a] - one[a] for a in range(3)]
    normal = [
        edge_one[1] * edge_two[2] - edge_one[2] * edge_two[1],
        edge_one[2] * edge_two[0] - edge_one[0] * edge_two[2],
        edge_one[0] * edge_two[1] - edge_one[1] * edge_two[0],
    ]
    area = 0.5 * jnp.sqrt(normal[0] * normal[0] + normal[1] * normal[1] + normal[2] * normal[2])
    geometry = []
    for value in centre + [area]:
        geometry.append(
            jnp.concatenate(
                [value[part * clusters : (part + 1) * clusters] for part in range(half)], axis=1
            )
        )
    for cluster in range(clusters):
        geom_ref[cluster] = jnp.concatenate(
            [whole[cluster : cluster + 1, :] for whole in geometry], axis=0
        )

    upward = lax.axis_index("row") % 2 == 0
    start = jnp.where(upward, clusters - NEARC, 0)
    pieces = [piece for whole in geometry for piece in split_three(whole)]
    for turn in range(NEARC):
        last = clusters - NEARC + turn
        rows = [
            jnp.where(upward, piece[last : last + 1, :], piece[turn : turn + 1, :])
            for piece in pieces
        ]
        rows.append(jnp.zeros((rhs_count - len(rows), size), jnp.float32))
        halo_ref[turn, :, 0:unknowns] = xs_ref[start + turn]
        halo_ref[turn, :, unknowns : unknowns + size] = jnp.concatenate(rows, axis=0).astype(
            jnp.bfloat16
        )


def window_kernel(xs_ref, geom_ref, halo_ref, slip_ref, place_ref):
    clusters, rhs_count, unknowns = xs_ref.shape
    size = geom_ref.shape[2]
    slots = clusters + NEARC
    odd = lax.axis_index("row") % 2

    def place_of(cluster):
        return (cluster + NEARC * (1 - odd) + slots) % slots

    for cluster in range(clusters):
        slip_ref[place_of(cluster)] = xs_ref[cluster]
        place_ref[place_of(cluster)] = geom_ref[cluster]
    for turn in range(NEARC):
        at = place_of(clusters + turn)
        slip_ref[at] = halo_ref[turn, :, 0:unknowns]
        pieces = halo_ref[turn, :, unknowns : unknowns + size].astype(jnp.float32)
        place_ref[at] = jnp.concatenate(
            [
                (pieces[3 * p + 2 : 3 * p + 3] + pieces[3 * p + 1 : 3 * p + 2])
                + pieces[3 * p : 3 * p + 1]
                for p in range(4)
            ],
            axis=0,
        )


def near_kernel(
    slip_ref, place_ref, pay_ref, after_ref, out_ref, cols_ref, even_ref, odd_ref, *, long_count, clusters
):
    slots, rhs_count, unknowns = slip_ref.shape
    size = place_ref.shape[2]
    long_index = lax.axis_index("long")
    before = jnp.maximum(long_index - 1, 0)
    totals = [jnp.zeros(pay_ref.shape[1:], jnp.float32) for _ in range(2)]
    row_count = pay_ref.shape[0] // long_count
    for row in range(row_count):
        for source, owner in enumerate((long_index, before)):
            at = place_of(row, owner, row_count, long_count)
            totals[source] += pay_ref[at].astype(jnp.float32)
    even = lax.axis_index("row") % 2 == 0
    half = pay_ref.shape[1]
    rank_size = pay_ref.shape[2] // 4
    group = lax.broadcasted_iota(jnp.int32, (half, LANES), 1) // rank_size
    kinds = lax.broadcasted_iota(jnp.int32, (half, LANES), 0) + jnp.where(group == 3, half, 0)
    kinds = jnp.where(group < 2, -1, kinds)
    lane_id = lax.broadcasted_iota(jnp.int32, (half, LANES), 1)
    kinds = jnp.where(lane_id % rank_size == 0, kinds, -1)

    def count_of(place, u):
        both = []
        for cluster in (u, clusters - NEARC + u):
            reach = place - u - NEARC
            lower = cluster + jnp.minimum(reach, 0)
            inside = lower >= 0
            kind = jnp.where(inside, lower, lower + clusters) * (NEARC + 1) + jnp.abs(reach)
            source = jnp.where(inside, totals[0], totals[1])
            both.append(jnp.where(kinds == kind, source, 0.0))
        picked = jnp.sum(jnp.where(even, both[0], both[1]), axis=0, keepdims=True)
        return jnp.sum(picked, axis=1, keepdims=True)

    out_ref[...] = jnp.zeros(out_ref.shape, jnp.float32)
    for place in range(slots):
        rows = jnp.concatenate([place_ref[place], jnp.zeros((4, size), jnp.float32)], axis=0)
        cols_ref[place] = rows.T
    right = [[place_ref[NEARC + u, p : p + 1, :] for p in range(4)] for u in range(NEARC)]
    parts = [(0, 0), (1, 1), (2, 2), (0, 1), (0, 2), (1, 2)]

    def fill(place, targets, block_ref):
        for step in range(size // ROWS):
            here = pl.ds(step * ROWS, ROWS)
            column = cols_ref[place, here, :]
            left = [jnp.broadcast_to(column[:, p : p + 1], (ROWS, size)) for p in range(4)]
            for u in targets:
                offset = [left[p] - right[u][p] for p in range(3)]
                radius_sq = offset[0] * offset[0] + offset[1] * offset[1] + offset[2] * offset[2]
                inverse = lax.rsqrt(radius_sq + soften)
                flat = (left[3] * right[u][3]) * inverse
                cubed = flat * (inverse * inverse)
                scaled = [offset[p] * cubed for p in range(3)]
                for part_id, (i, j) in enumerate(parts):
                    term = offset[i] * scaled[j]
                    if i == j:
                        term = term + flat
                    block_ref[u, part_id, here, :] = term.astype(jnp.bfloat16)

    def apply(place, targets, block_ref):
        slip = slip_ref[place]
        pieces = [slip[:, p * size : (p + 1) * size] for p in range(3)]
        for u in targets:
            count = count_of(place, u)
            sums = [
                jnp.dot(pieces[p], block_ref[u, p], preferred_element_type=jnp.float32)
                for p in range(3)
            ]
            for part_id in range(3, 6):
                i, j = parts[part_id]
                both = jnp.dot(
                    jnp.concatenate([pieces[j], pieces[i]], axis=0),
                    block_ref[u, part_id],
                    preferred_element_type=jnp.float32,
                )
                sums[i] = sums[i] + both[0:rhs_count]
                sums[j] = sums[j] + both[rhs_count : 2 * rhs_count]
            for p in range(3):
                out_ref[u, :, p * size : (p + 1) * size] += count * sums[p]

    every = list(range(NEARC))
    fill(0, [0], even_ref)
    for u in range(1, NEARC):
        even_ref[u] = jnp.zeros(even_ref.shape[1:], jnp.bfloat16)

    def two_places(turn, carry):
        place = 2 * turn
        fill(place + 1, every, odd_ref)
        apply(place, every, even_ref)
        fill(place + 2, every, even_ref)
        apply(place + 1, every, odd_ref)
        return carry

    lax.fori_loop(0, (slots - 2) // 2, two_places, 0)
    fill(slots - 1, [NEARC - 1], odd_ref)
    apply(slots - 2, every, even_ref)
    apply(slots - 1, [NEARC - 1], odd_ref)


def coupling_kernel(coupling_ref, pairs_ref, after_ref, to_second_ref, to_first_ref, list_ref):
    list_ref[...] = pairs_ref[...]
    pair_count, rank_size, _ = coupling_ref.shape
    groups = LANES // rank_size
    for pair_id in range(pair_count):
        here = pl.ds(pair_id * rank_size, rank_size)
        coupling = coupling_ref[pair_id].astype(jnp.float32)
        for out_ref, value in ((to_second_ref, coupling), (to_first_ref, coupling.T)):
            out_ref[here, :] = jnp.concatenate([value] * groups, axis=1).astype(jnp.bfloat16)


def far_kernel(
    pairs_ref, coeff_ref, to_second_ref, to_first_ref, out_ref, done_ref, *total_refs, clusters
):
    done_ref[...] = jnp.zeros(done_ref.shape, jnp.float32)
    long_count, rhs_count, _ = total_refs[0].shape
    row_count = out_ref.shape[0] // long_count
    pair_count = pairs_ref.shape[1]
    rank_size = LANES // clusters
    group_id = lax.broadcasted_iota(jnp.int32, (rhs_count, LANES), 1) // rank_size
    for total_ref in total_refs:
        total_ref[...] = jnp.zeros(total_ref.shape, jnp.float32)

    def coeff_of(cluster, group):
        whole = coeff_ref[place_of(cluster % clusters, cluster // clusters, row_count, long_count)]
        whole = whole.astype(jnp.float32)
        low = pltpu.roll(whole, rank_size * group, 1) if group else whole
        high = pltpu.roll(whole, (rank_size * (group - 1)) % LANES, 1) if group != 1 else whole
        both = jnp.concatenate([low, high], axis=0)
        return jnp.where(group_id == group, both, 0.0)

    results = []
    for begin in range(0, pair_count, clusters):
        pair_ids = range(begin, min(begin + clusters, pair_count))
        depth = len(pair_ids) * rank_size
        here = pl.ds(begin * rank_size, depth)
        for source, target, matrix_ref in ((0, 1, to_second_ref), (1, 0, to_first_ref)):
            coeffs = jnp.concatenate(
                [coeff_of(pairs_ref[source, f], f - begin) for f in pair_ids], axis=0
            ).astype(jnp.bfloat16)
            value = jnp.dot(
                coeffs[:, 0:depth], matrix_ref[here, :], preferred_element_type=jnp.float32
            )
            for turn, f in enumerate(pair_ids):
                results.append(
                    (pairs_ref[target, f], value[turn * rhs_count : (turn + 1) * rhs_count])
                )
    for turn, (cluster, value) in enumerate(results):
        total_ref = total_refs[turn % len(total_refs)]
        total_ref[cluster // clusters] += jnp.where(group_id == cluster % clusters, value, 0.0)
    total = total_refs[0][...]
    for total_ref in total_refs[1:]:
        total = total + total_ref[...]
    sent = total.astype(jnp.bfloat16)
    for place, at in enumerate(exchange_order(row_count, long_count)):
        out_ref[place] = sent[at % long_count]


def finish_kernel(own_ref, other_ref, far_ref, basis_ref, out_hbm, sent_ref, sems):
    clusters, rank_size, unknowns = basis_ref.shape
    total = jnp.sum(far_ref[...].astype(jnp.float32), axis=0)
    group_id = lax.broadcasted_iota(jnp.int32, total.shape, 1) // rank_size
    flat_basis = basis_ref[...].reshape(clusters * rank_size, unknowns)
    even = lax.axis_index("row") % 2 == 0
    copies = []
    for cluster in range(clusters):
        u = cluster % NEARC
        here = even if cluster < NEARC else jnp.logical_not(even)
        near = jnp.where(here, own_ref[u], other_ref[u])
        picked = jnp.where(group_id == cluster, total, 0.0).astype(jnp.bfloat16)
        result = jnp.dot(picked, flat_basis, preferred_element_type=jnp.float32)
        sent_ref[cluster] = result + near
        copies.append(
            pltpu.make_async_copy(sent_ref.at[cluster], out_hbm.at[cluster], sems.at[cluster])
        )
        copies[-1].start()
    for copy in copies:
        copy.wait()


def shards(slip, vertices, triangles, elem_map, near_pairs, near_count, far_pairs, far_coef, basis):
    clusters, rhs_count, unknowns = slip.shape
    rank_size = basis.shape[1]
    size = elem_map.shape[1]
    row_count = lax.axis_size("row")
    long_count = lax.axis_size("long")
    devices = row_count * long_count
    coupling = far_coef.reshape(-1, rank_size, rank_size)
    slots = clusters + NEARC

    pay = pl.pallas_call(
        coeffs_kernel,
        out_shape=jax.ShapeDtypeStruct((devices, rhs_count // 2, LANES), jnp.bfloat16),
        in_specs=[HBM] * 3 + [SMEM],
        out_specs=HBM,
        scratch_shapes=[
            pltpu.VMEM(slip.shape[1:], slip.dtype),
            pltpu.VMEM(basis.shape[1:], basis.dtype),
            pltpu.VMEM(near_pairs.shape, near_pairs.dtype),
            pltpu.VMEM((long_count, rhs_count // 2, LANES), jnp.bfloat16),
            pltpu.SemaphoreType.DMA((3,)),
            pltpu.SemaphoreType.DMA((row_count,)),
        ],
        compiler_params=pltpu.CompilerParams(vmem_limit_bytes=16 << 20),
        name="coeffs",
    )(
        *[
            pltpu.with_memory_space_constraint(array, pltpu.HBM)
            for array in (slip, basis, near_pairs)
        ],
        near_count,
    )
    everyone = everyone_sends(pay, row_count, long_count)

    xs, to_neighbour, geometry = pl.pallas_call(
        geometry_kernel,
        out_shape=[
            jax.ShapeDtypeStruct(slip.shape, jnp.bfloat16),
            jax.ShapeDtypeStruct((NEARC, rhs_count, unknowns + size), jnp.bfloat16),
            jax.ShapeDtypeStruct((clusters, 4, size), jnp.float32),
        ],
        in_specs=[VMEM] * 4 + [ANY],
        out_specs=[VMEM] * 3,
        compiler_params=pltpu.CompilerParams(vmem_limit_bytes=16 << 20),
        cost_estimate=pl.CostEstimate(
            flops=2_000_000, bytes_accessed=1_000_000, transcendentals=1_000
        ),
        name="geometry",
    )(slip, vertices, triangles, elem_map, pay)
    route = []
    for row in range(row_count):
        step = 1 if row % 2 == 0 else -1
        for owner in range(long_count):
            if 0 <= owner - step < long_count:
                route.append((row * long_count + owner - step, row * long_count + owner))
    halo = lax.ppermute(to_neighbour, ("row", "long"), route)

    window, places = pl.pallas_call(
        window_kernel,
        out_shape=[
            jax.ShapeDtypeStruct((slots, rhs_count, unknowns), jnp.bfloat16),
            jax.ShapeDtypeStruct((slots, 4, size), jnp.float32),
        ],
        in_specs=[VMEM] * 3,
        out_specs=[VMEM] * 2,
        compiler_params=pltpu.CompilerParams(vmem_limit_bytes=16 << 20),
        cost_estimate=pl.CostEstimate(flops=1000, bytes_accessed=1000, transcendentals=0),
        name="window",
    )(xs, geometry, halo)

    to_second, to_first, pair_list = pl.pallas_call(
        coupling_kernel,
        out_shape=[jax.ShapeDtypeStruct((coupling.shape[0] * rank_size, LANES), jnp.bfloat16)] * 2
        + [jax.ShapeDtypeStruct(far_pairs.shape, far_pairs.dtype)],
        in_specs=[VMEM, VMEM, ANY],
        out_specs=[VMEM] * 3,
        compiler_params=pltpu.CompilerParams(vmem_limit_bytes=16 << 20),
        cost_estimate=pl.CostEstimate(flops=1000, bytes_accessed=1000, transcendentals=0),
        name="coupling",
    )(coupling, far_pairs, pay)
    far, far_done = pl.pallas_call(
        functools.partial(far_kernel, clusters=clusters),
        out_shape=[
            jax.ShapeDtypeStruct((devices, rhs_count, clusters * rank_size), jnp.bfloat16),
            jax.ShapeDtypeStruct((8, LANES), jnp.float32),
        ],
        in_specs=[SMEM, VMEM, VMEM, VMEM],
        out_specs=[VMEM] * 2,
        scratch_shapes=[pltpu.VMEM((long_count, rhs_count, clusters * rank_size), jnp.float32)] * 4,
        compiler_params=pltpu.CompilerParams(vmem_limit_bytes=16 << 20),
        name="far",
    )(pair_list, everyone, to_second, to_first)
    far_terms = everyone_sends(far, row_count, long_count)

    near = pl.pallas_call(
        functools.partial(near_kernel, long_count=long_count, clusters=clusters),
        out_shape=jax.ShapeDtypeStruct((NEARC, rhs_count, unknowns), jnp.float32),
        in_specs=[VMEM] * 3 + [ANY],
        out_specs=VMEM,
        scratch_shapes=[
            pltpu.VMEM((slots, size, 8), jnp.float32),
            pltpu.VMEM((NEARC, 6, size, size), jnp.bfloat16),
            pltpu.VMEM((NEARC, 6, size, size), jnp.bfloat16),
        ],
        compiler_params=pltpu.CompilerParams(vmem_limit_bytes=24 << 20),
        cost_estimate=pl.CostEstimate(
            flops=1_000_000_000, bytes_accessed=1_000_000, transcendentals=660_000
        ),
        name="near",
    )(window, places, everyone, far_done)
    partner = [(row, row ^ 1) for row in range(row_count)]
    other = lax.ppermute(near, "row", partner)

    return pl.pallas_call(
        finish_kernel,
        out_shape=jax.ShapeDtypeStruct(slip.shape, jnp.float32),
        in_specs=[VMEM] * 4,
        out_specs=HBM,
        scratch_shapes=[
            pltpu.VMEM(slip.shape, jnp.float32),
            pltpu.SemaphoreType.DMA((clusters,)),
        ],
        compiler_params=pltpu.CompilerParams(vmem_limit_bytes=16 << 20),
        name="finish",
    )(near, other, far_terms, basis)


def solution(mesh):
    placed = (
        P("long", None, None),
        P(None, "long"),
        P(None, "long"),
        P("long", None),
        P(None, ("row", "long")),
        P(("row", "long")),
        P(None, ("row", "long")),
        P(("row", "long"), None),
        P("long", None, None),
    )
    return jax.shard_map(
        shards, mesh=mesh, in_specs=placed, out_specs=P("long", None, None), check_vma=False
    )
```

```python
import functools

import jax
import jax.numpy as jnp
from jax import lax
from jax.experimental import pallas as pl
from jax.experimental.pallas import tpu as pltpu
from jax.sharding import PartitionSpec as P

NEARC = 2
LANES = 128
ROWS = 16

soften = 0.25

VMEM = pl.BlockSpec(memory_space=pltpu.VMEM)
SMEM = pl.BlockSpec(memory_space=pltpu.SMEM)
HBM = pl.BlockSpec(memory_space=pltpu.HBM)
ANY = pl.BlockSpec(memory_space=pl.ANY)
SMALL = pl.CostEstimate(flops=1000, bytes_accessed=1000, transcendentals=0)


def first_place(row_count, long_count):
    return row_count // 2 * long_count // 2 + long_count // 2 - 1


def same_core(row_count, long_count):
    total = row_count // 2 * long_count
    order = [(place + first_place(row_count, long_count)) % total for place in range(total)]
    return [
        [(2 * (at // long_count) + core) * long_count + at % long_count for at in order]
        for core in range(2)
    ]


def place_in_core(row, owner, row_count, long_count):
    total = row_count // 2 * long_count
    return (row * long_count + owner + total - first_place(row_count, long_count)) % total


def lane_gather(table, index):
    length = table.shape[1]
    lane = index & (LANES - 1)
    chunk = index // LANES
    found = jnp.zeros(index.shape, table.dtype)
    for piece_id in range(-(-length // LANES)):
        piece = table[:, piece_id * LANES : min(length, (piece_id + 1) * LANES)]
        missing = LANES - piece.shape[1]
        if missing:
            piece = jnp.concatenate([piece, jnp.zeros((1, missing), table.dtype)], axis=1)
        picked = jnp.take_along_axis(jnp.broadcast_to(piece, index.shape), lane, axis=1)
        found = jnp.where(chunk == piece_id, picked, found)
    return found


def split_three(value):
    high = value.astype(jnp.bfloat16).astype(jnp.float32)
    rest = value - high
    middle = rest.astype(jnp.bfloat16).astype(jnp.float32)
    return [high, middle, rest - middle]


def coeffs_kernel(
    slip_hbm, basis_hbm, pairs_hbm, count_ref, pay_hbm, slip_ref, basis_ref, pairs_ref, sent_ref, sems, out_sems
):
    clusters = slip_hbm.shape[0]
    share, rhs_count, _ = slip_ref.shape
    rank_size = basis_ref.shape[1]
    begin = (lax.axis_index("row") // 2) % (clusters // share) * share
    copies = [
        pltpu.make_async_copy(slip_hbm.at[pl.ds(begin, share)], slip_ref, sems.at[0]),
        pltpu.make_async_copy(basis_hbm.at[pl.ds(begin, share)], basis_ref, sems.at[1]),
        pltpu.make_async_copy(pairs_hbm, pairs_ref, sems.at[2]),
    ]
    for copy in copies:
        copy.start()
    copies[2].wait()
    first = pairs_ref[0:1, :]
    kind = (first - lax.axis_index("long") * clusters) * (NEARC + 1) + pairs_ref[1:2, :] - first
    kinds = lax.broadcasted_iota(jnp.int32, (rhs_count, kind.shape[1]), 0)
    live = lax.broadcasted_iota(jnp.int32, kinds.shape, 1) < count_ref[0]
    counts = jnp.sum(jnp.where(live & (kinds == kind), 1.0, 0.0), axis=1, keepdims=True)
    copies[0].wait()
    copies[1].wait()
    coeffs = [
        lax.dot_general(
            slip_ref[turn].astype(jnp.bfloat16),
            basis_ref[turn],
            (((1,), (1,)), ((), ())),
            preferred_element_type=jnp.float32,
        )
        for turn in range(share)
    ]
    counts = jnp.broadcast_to(counts, (rhs_count, LANES - share * rank_size))
    pay = jnp.concatenate(coeffs + [counts], axis=1).astype(jnp.bfloat16)
    for target in range(sent_ref.shape[0]):
        sent_ref[target] = pay
    parts = pay_hbm.shape[0] // sent_ref.shape[0]
    sends = [
        pltpu.make_async_copy(
            sent_ref, pay_hbm.at[pl.ds(part * sent_ref.shape[0], sent_ref.shape[0])], out_sems.at[part]
        )
        for part in range(parts)
    ]
    for send in sends:
        send.start()
    for send in sends:
        send.wait()


def geometry_kernel(
    slip_ref, vertices_ref, triangles_ref, map_ref, after_ref, xs_ref, halo_ref, geom_ref
):
    clusters, rhs_count, unknowns = slip_ref.shape
    xs_ref[...] = slip_ref[...].astype(jnp.bfloat16)
    long_index = lax.axis_index("long")

    size = map_ref.shape[1]
    half = size // LANES
    slot_map = map_ref[...]
    index = jnp.concatenate(
        [slot_map[:, part * LANES : (part + 1) * LANES] for part in range(half)], axis=0
    )
    vertex_base = long_index * vertices_ref.shape[1]
    corners = []
    for corner_id in range(3):
        vertex = lane_gather(triangles_ref[corner_id : corner_id + 1, :], index) - vertex_base
        corners.append(
            [lane_gather(vertices_ref[axis_id : axis_id + 1, :], vertex) for axis_id in range(3)]
        )
    one, two, three = corners
    centre = [(one[a] + two[a] + three[a]) / 3.0 for a in range(3)]
    edge_one = [two[a] - one[a] for a in range(3)]
    edge_two = [three[a] - one[a] for a in range(3)]
    normal = [
        edge_one[1] * edge_two[2] - edge_one[2] * edge_two[1],
        edge_one[2] * edge_two[0] - edge_one[0] * edge_two[2],
        edge_one[0] * edge_two[1] - edge_one[1] * edge_two[0],
    ]
    area = 0.5 * jnp.sqrt(normal[0] * normal[0] + normal[1] * normal[1] + normal[2] * normal[2])
    geometry = []
    for value in centre + [area]:
        geometry.append(
            jnp.concatenate(
                [value[part * clusters : (part + 1) * clusters] for part in range(half)], axis=1
            )
        )
    for cluster in range(clusters):
        geom_ref[cluster] = jnp.concatenate(
            [whole[cluster : cluster + 1, :] for whole in geometry], axis=0
        )

    upward = lax.axis_index("row") % 2 == 0
    start = jnp.where(upward, clusters - NEARC, 0)
    pieces = [piece for whole in geometry for piece in split_three(whole)]
    for turn in range(NEARC):
        last = clusters - NEARC + turn
        rows = [
            jnp.where(upward, piece[last : last + 1, :], piece[turn : turn + 1, :])
            for piece in pieces
        ]
        rows.append(jnp.zeros((rhs_count - len(rows), size), jnp.float32))
        halo_ref[turn, :, 0:unknowns] = xs_ref[start + turn]
        halo_ref[turn, :, unknowns : unknowns + size] = jnp.concatenate(rows, axis=0).astype(
            jnp.bfloat16
        )


def window_kernel(xs_ref, geom_ref, halo_ref, slip_ref, place_ref):
    clusters, rhs_count, unknowns = xs_ref.shape
    size = geom_ref.shape[2]
    slots = clusters + NEARC
    odd = lax.axis_index("row") % 2

    def place_of(cluster):
        return (cluster + NEARC * (1 - odd) + slots) % slots

    for cluster in range(clusters):
        slip_ref[place_of(cluster)] = xs_ref[cluster]
        place_ref[place_of(cluster)] = geom_ref[cluster]
    for turn in range(NEARC):
        at = place_of(clusters + turn)
        slip_ref[at] = halo_ref[turn, :, 0:unknowns]
        pieces = halo_ref[turn, :, unknowns : unknowns + size].astype(jnp.float32)
        place_ref[at] = jnp.concatenate(
            [
                (pieces[3 * p + 2 : 3 * p + 3] + pieces[3 * p + 1 : 3 * p + 2])
                + pieces[3 * p : 3 * p + 1]
                for p in range(4)
            ],
            axis=0,
        )


def totals_kernel(pay_ref, out_ref, *, long_count):
    row_count = 2 * pay_ref.shape[0] // long_count
    long_index = lax.axis_index("long")
    totals = [jnp.zeros(pay_ref.shape[1:], jnp.float32) for _ in range(2)]
    for row in range(row_count // 2):
        for source, owner in enumerate((long_index, jnp.maximum(long_index - 1, 0))):
            at = place_in_core(row, owner, row_count, long_count)
            totals[source] += pay_ref[at].astype(jnp.float32)
    lane_id = lax.broadcasted_iota(jnp.int32, out_ref.shape, 1)
    out_ref[...] = jnp.where(lane_id < 3 * LANES // 4, totals[0], totals[1])


def near_kernel(
    slip_ref, place_ref, mine_ref, theirs_ref, after_ref, out_ref, cols_ref, even_ref, odd_ref, *, clusters
):
    slots, rhs_count, unknowns = slip_ref.shape
    size = place_ref.shape[2]
    totals = mine_ref[...] + theirs_ref[...]
    even = lax.axis_index("row") % 2 == 0
    kinds = lax.broadcasted_iota(jnp.int32, totals.shape, 0)
    lane_id = lax.broadcasted_iota(jnp.int32, totals.shape, 1)

    def count_of(place, u):
        both = []
        for cluster in (u, clusters - NEARC + u):
            reach = place - u - NEARC
            lower = cluster + jnp.minimum(reach, 0)
            inside = lower >= 0
            kind = jnp.where(inside, lower, lower + clusters) * (NEARC + 1) + jnp.abs(reach)
            lane = jnp.where(inside, LANES // 2, 3 * LANES // 4)
            both.append(jnp.where((kinds == kind) & (lane_id == lane), totals, 0.0))
        picked = jnp.sum(jnp.where(even, both[0], both[1]), axis=0, keepdims=True)
        return jnp.sum(picked, axis=1, keepdims=True)

    out_ref[...] = jnp.zeros(out_ref.shape, jnp.float32)
    for place in range(slots):
        rows = jnp.concatenate([place_ref[place], jnp.zeros((4, size), jnp.float32)], axis=0)
        cols_ref[place] = rows.T
    right = [[place_ref[NEARC + u, p : p + 1, :] for p in range(4)] for u in range(NEARC)]
    parts = [(0, 0), (1, 1), (2, 2), (0, 1), (0, 2), (1, 2)]

    def fill(place, targets, block_ref):
        for step in range(size // ROWS):
            here = pl.ds(step * ROWS, ROWS)
            column = cols_ref[place, here, :]
            left = [jnp.broadcast_to(column[:, p : p + 1], (ROWS, size)) for p in range(4)]
            for u in targets:
                offset = [left[p] - right[u][p] for p in range(3)]
                radius_sq = offset[0] * offset[0] + offset[1] * offset[1] + offset[2] * offset[2]
                inverse = lax.rsqrt(radius_sq + soften)
                flat = (left[3] * right[u][3]) * inverse
                cubed = flat * (inverse * inverse)
                scaled = [offset[p] * cubed for p in range(3)]
                for part_id, (i, j) in enumerate(parts):
                    term = offset[i] * scaled[j]
                    if i == j:
                        term = term + flat
                    block_ref[u, part_id, here, :] = term.astype(jnp.bfloat16)

    def apply(place, targets, block_ref):
        slip = slip_ref[place]
        pieces = [slip[:, p * size : (p + 1) * size] for p in range(3)]
        for u in targets:
            count = count_of(place, u)
            sums = [
                jnp.dot(pieces[p], block_ref[u, p], preferred_element_type=jnp.float32)
                for p in range(3)
            ]
            for part_id in range(3, 6):
                i, j = parts[part_id]
                both = jnp.dot(
                    jnp.concatenate([pieces[j], pieces[i]], axis=0),
                    block_ref[u, part_id],
                    preferred_element_type=jnp.float32,
                )
                sums[i] = sums[i] + both[0:rhs_count]
                sums[j] = sums[j] + both[rhs_count : 2 * rhs_count]
            for p in range(3):
                out_ref[u, :, p * size : (p + 1) * size] += count * sums[p]

    every = list(range(NEARC))
    fill(0, [0], even_ref)
    for u in range(1, NEARC):
        even_ref[u] = jnp.zeros(even_ref.shape[1:], jnp.bfloat16)

    def two_places(turn, carry):
        place = 2 * turn
        fill(place + 1, every, odd_ref)
        apply(place, every, even_ref)
        fill(place + 2, every, even_ref)
        apply(place + 1, every, odd_ref)
        return carry

    lax.fori_loop(0, (slots - 2) // 2, two_places, 0)
    fill(slots - 1, [NEARC - 1], odd_ref)
    apply(slots - 2, every, even_ref)
    apply(slots - 1, [NEARC - 1], odd_ref)


def coupling_kernel(coupling_ref, pairs_ref, after_ref, to_second_ref, to_first_ref, list_ref):
    list_ref[...] = pairs_ref[...]
    pair_count, rank_size, _ = coupling_ref.shape
    groups = LANES // rank_size
    for pair_id in range(pair_count):
        here = pl.ds(pair_id * rank_size, rank_size)
        coupling = coupling_ref[pair_id].astype(jnp.float32)
        for out_ref, value in ((to_second_ref, coupling), (to_first_ref, coupling.T)):
            out_ref[here, :] = jnp.concatenate([value] * groups, axis=1).astype(jnp.bfloat16)


def far_kernel(
    pairs_ref, coeff_ref, to_second_ref, to_first_ref, out_hbm, done_ref, sent_ref, sems, moved_ref, *total_refs, clusters
):
    done_ref[...] = jnp.zeros(done_ref.shape, jnp.float32)
    long_count, rhs_count, _ = total_refs[0].shape
    row_count = out_hbm.shape[0] // long_count
    pair_count = pairs_ref.shape[1]
    rank_size = LANES // clusters
    group_id = lax.broadcasted_iota(jnp.int32, (rhs_count, LANES), 1) // rank_size
    for total_ref in total_refs:
        total_ref[...] = jnp.zeros(total_ref.shape, jnp.float32)

    share = clusters // 2
    for at in range(coeff_ref.shape[0]):
        whole = coeff_ref[at].astype(jnp.float32)
        for turn in range(share):
            moved_ref[at * share + turn] = (
                pltpu.roll(whole, LANES - rank_size * turn, 1) if turn else whole
            )

    def coeff_of(cluster, group):
        at = place_in_core(cluster % clusters // share, cluster // clusters, row_count, long_count)
        whole = moved_ref[at * share + cluster % share]
        both = pltpu.roll(whole, rank_size * group, 1) if group else whole
        return jnp.where(group_id == group, both, 0.0)

    results = []
    for begin in range(0, pair_count, clusters):
        pair_ids = range(begin, min(begin + clusters, pair_count))
        depth = len(pair_ids) * rank_size
        here = pl.ds(begin * rank_size, depth)
        for source, target, matrix_ref in ((0, 1, to_second_ref), (1, 0, to_first_ref)):
            coeffs = jnp.concatenate(
                [coeff_of(pairs_ref[source, f], f - begin) for f in pair_ids], axis=0
            ).astype(jnp.bfloat16)
            value = jnp.dot(
                coeffs[:, 0:depth], matrix_ref[here, :], preferred_element_type=jnp.float32
            )
            for turn, f in enumerate(pair_ids):
                results.append(
                    (pairs_ref[target, f], value[turn * rhs_count : (turn + 1) * rhs_count])
                )
    for turn, (cluster, value) in enumerate(results):
        total_ref = total_refs[turn % len(total_refs)]
        total_ref[cluster // clusters] += jnp.where(group_id == cluster % clusters, value, 0.0)
    total = total_refs[0][...]
    for total_ref in total_refs[1:]:
        total = total + total_ref[...]
    sent_ref[...] = total.astype(jnp.bfloat16)
    copies = [
        pltpu.make_async_copy(
            sent_ref, out_hbm.at[pl.ds(copy_id * long_count, long_count)], sems.at[copy_id]
        )
        for copy_id in range(out_hbm.shape[0] // long_count)
    ]
    for copy in copies:
        copy.start()
    for copy in copies:
        copy.wait()


def finish_kernel(own_ref, other_ref, far_ref, basis_ref, out_hbm, sent_ref, sems):
    clusters, rank_size, unknowns = basis_ref.shape
    total = jnp.sum(far_ref[...].astype(jnp.float32), axis=0)
    group_id = lax.broadcasted_iota(jnp.int32, total.shape, 1) // rank_size
    flat_basis = basis_ref[...].reshape(clusters * rank_size, unknowns)
    even = lax.axis_index("row") % 2 == 0
    copies = []
    for cluster in range(clusters):
        u = cluster % NEARC
        here = even if cluster < NEARC else jnp.logical_not(even)
        near = jnp.where(here, own_ref[u], other_ref[u])
        picked = jnp.where(group_id == cluster, total, 0.0).astype(jnp.bfloat16)
        result = jnp.dot(picked, flat_basis, preferred_element_type=jnp.float32)
        sent_ref[cluster] = result + near
        copies.append(
            pltpu.make_async_copy(sent_ref.at[cluster], out_hbm.at[cluster], sems.at[cluster])
        )
        copies[-1].start()
    for copy in copies:
        copy.wait()


def shards(slip, vertices, triangles, elem_map, near_pairs, near_count, far_pairs, far_coef, basis):
    clusters, rhs_count, unknowns = slip.shape
    rank_size = basis.shape[1]
    size = elem_map.shape[1]
    row_count = lax.axis_size("row")
    long_count = lax.axis_size("long")
    devices = row_count * long_count
    share = clusters // 2
    coupling = far_coef.reshape(-1, rank_size, rank_size)
    slots = clusters + NEARC

    pay = pl.pallas_call(
        coeffs_kernel,
        out_shape=jax.ShapeDtypeStruct((devices // 2, rhs_count, LANES), jnp.bfloat16),
        in_specs=[HBM] * 3 + [SMEM],
        out_specs=HBM,
        scratch_shapes=[
            pltpu.VMEM((share,) + slip.shape[1:], slip.dtype),
            pltpu.VMEM((share,) + basis.shape[1:], basis.dtype),
            pltpu.VMEM(near_pairs.shape, near_pairs.dtype),
            pltpu.VMEM((long_count, rhs_count, LANES), jnp.bfloat16),
            pltpu.SemaphoreType.DMA((3,)),
            pltpu.SemaphoreType.DMA((row_count // 2,)),
        ],
        compiler_params=pltpu.CompilerParams(vmem_limit_bytes=16 << 20),
        name="coeffs",
    )(
        *[
            pltpu.with_memory_space_constraint(array, pltpu.HBM)
            for array in (slip, basis, near_pairs)
        ],
        near_count,
    )
    everyone = lax.all_to_all(
        pay, ("row", "long"), 0, 0, axis_index_groups=same_core(row_count, long_count), tiled=True
    )

    xs, to_neighbour, geometry = pl.pallas_call(
        geometry_kernel,
        out_shape=[
            jax.ShapeDtypeStruct(slip.shape, jnp.bfloat16),
            jax.ShapeDtypeStruct((NEARC, rhs_count, unknowns + size), jnp.bfloat16),
            jax.ShapeDtypeStruct((clusters, 4, size), jnp.float32),
        ],
        in_specs=[VMEM] * 4 + [ANY],
        out_specs=[VMEM] * 3,
        compiler_params=pltpu.CompilerParams(vmem_limit_bytes=16 << 20),
        cost_estimate=pl.CostEstimate(
            flops=2_000_000, bytes_accessed=1_000_000, transcendentals=1_000
        ),
        name="geometry",
    )(slip, vertices, triangles, elem_map, pay)
    route = []
    for row in range(row_count):
        step = 1 if row % 2 == 0 else -1
        for owner in range(long_count):
            if 0 <= owner - step < long_count:
                route.append((row * long_count + owner - step, row * long_count + owner))
    halo = lax.ppermute(to_neighbour, ("row", "long"), route)

    window, places = pl.pallas_call(
        window_kernel,
        out_shape=[
            jax.ShapeDtypeStruct((slots, rhs_count, unknowns), jnp.bfloat16),
            jax.ShapeDtypeStruct((slots, 4, size), jnp.float32),
        ],
        in_specs=[VMEM] * 3,
        out_specs=[VMEM] * 2,
        compiler_params=pltpu.CompilerParams(vmem_limit_bytes=16 << 20),
        cost_estimate=pl.CostEstimate(flops=1000, bytes_accessed=1000, transcendentals=0),
        name="window",
    )(xs, geometry, halo)

    to_second, to_first, pair_list = pl.pallas_call(
        coupling_kernel,
        out_shape=[jax.ShapeDtypeStruct((coupling.shape[0] * rank_size, LANES), jnp.bfloat16)] * 2
        + [jax.ShapeDtypeStruct(far_pairs.shape, far_pairs.dtype)],
        in_specs=[VMEM, VMEM, ANY],
        out_specs=[VMEM] * 3,
        compiler_params=pltpu.CompilerParams(vmem_limit_bytes=16 << 20),
        cost_estimate=pl.CostEstimate(flops=1000, bytes_accessed=1000, transcendentals=0),
        name="coupling",
    )(coupling, far_pairs, pay)
    far, far_done = pl.pallas_call(
        functools.partial(far_kernel, clusters=clusters),
        out_shape=[
            jax.ShapeDtypeStruct((devices, rhs_count, clusters * rank_size), jnp.bfloat16),
            jax.ShapeDtypeStruct((8, LANES), jnp.float32),
        ],
        in_specs=[SMEM, VMEM, VMEM, VMEM],
        out_specs=[HBM, VMEM],
        scratch_shapes=[
            pltpu.VMEM((long_count, rhs_count, clusters * rank_size), jnp.bfloat16),
            pltpu.SemaphoreType.DMA((row_count,)),
            pltpu.VMEM((devices // 2 * share, rhs_count, LANES), jnp.float32),
        ]
        + [pltpu.VMEM((long_count, rhs_count, clusters * rank_size), jnp.float32)] * 4,
        compiler_params=pltpu.CompilerParams(vmem_limit_bytes=16 << 20),
        name="far",
    )(pair_list, everyone, to_second, to_first)
    far_terms = lax.all_to_all(far, ("row", "long"), 0, 0, tiled=True)

    totals = pl.pallas_call(
        functools.partial(totals_kernel, long_count=long_count),
        out_shape=jax.ShapeDtypeStruct((rhs_count, LANES), jnp.float32),
        in_specs=[VMEM],
        out_specs=VMEM,
        compiler_params=pltpu.CompilerParams(vmem_limit_bytes=16 << 20),
        cost_estimate=SMALL,
        name="totals",
    )(everyone)
    partner = [(row, row ^ 1) for row in range(row_count)]
    totals_other = lax.ppermute(totals, "row", partner)

    near = pl.pallas_call(
        functools.partial(near_kernel, clusters=clusters),
        out_shape=jax.ShapeDtypeStruct((NEARC, rhs_count, unknowns), jnp.float32),
        in_specs=[VMEM] * 4 + [ANY],
        out_specs=VMEM,
        scratch_shapes=[
            pltpu.VMEM((slots, size, 8), jnp.float32),
            pltpu.VMEM((NEARC, 6, size, size), jnp.bfloat16),
            pltpu.VMEM((NEARC, 6, size, size), jnp.bfloat16),
        ],
        compiler_params=pltpu.CompilerParams(vmem_limit_bytes=24 << 20),
        cost_estimate=pl.CostEstimate(
            flops=1_000_000_000, bytes_accessed=1_000_000, transcendentals=660_000
        ),
        name="near",
    )(window, places, totals, totals_other, far_done)
    other = lax.ppermute(near, "row", partner)

    return pl.pallas_call(
        finish_kernel,
        out_shape=jax.ShapeDtypeStruct(slip.shape, jnp.float32),
        in_specs=[VMEM] * 4,
        out_specs=HBM,
        scratch_shapes=[
            pltpu.VMEM(slip.shape, jnp.float32),
            pltpu.SemaphoreType.DMA((clusters,)),
        ],
        compiler_params=pltpu.CompilerParams(vmem_limit_bytes=16 << 20),
        name="finish",
    )(near, other, far_terms, basis)


def solution(mesh):
    placed = (
        P("long", None, None),
        P(None, "long"),
        P(None, "long"),
        P("long", None),
        P(None, ("row", "long")),
        P(("row", "long")),
        P(None, ("row", "long")),
        P(("row", "long"), None),
        P("long", None, None),
    )
    return jax.shard_map(
        shards, mesh=mesh, in_specs=placed, out_specs=P("long", None, None), check_vma=False
    )
```

```python
import functools

import jax
import jax.numpy as jnp
from jax import lax
from jax.experimental import pallas as pl
from jax.experimental.pallas import tpu as pltpu
from jax.sharding import PartitionSpec as P

NEARC = 2
LANES = 128
ROWS = 16

soften = 0.25

VMEM = pl.BlockSpec(memory_space=pltpu.VMEM)
SMEM = pl.BlockSpec(memory_space=pltpu.SMEM)
HBM = pl.BlockSpec(memory_space=pltpu.HBM)
ANY = pl.BlockSpec(memory_space=pl.ANY)


def lane_gather(table, index):
    length = table.shape[1]
    lane = index & (LANES - 1)
    chunk = index // LANES
    found = jnp.zeros(index.shape, table.dtype)
    for piece_id in range(-(-length // LANES)):
        piece = table[:, piece_id * LANES : min(length, (piece_id + 1) * LANES)]
        missing = LANES - piece.shape[1]
        if missing:
            piece = jnp.concatenate([piece, jnp.zeros((1, missing), table.dtype)], axis=1)
        picked = jnp.take_along_axis(jnp.broadcast_to(piece, index.shape), lane, axis=1)
        found = jnp.where(chunk == piece_id, picked, found)
    return found


def split_three(value):
    high = value.astype(jnp.bfloat16).astype(jnp.float32)
    rest = value - high
    middle = rest.astype(jnp.bfloat16).astype(jnp.float32)
    return [high, middle, rest - middle]


def coeffs_kernel(
    slip_hbm, basis_hbm, pairs_hbm, count_ref, pay_hbm, slip_ref, basis_ref, pairs_ref, sent_ref, sems, out_sems
):
    clusters = slip_hbm.shape[0]
    rhs_count = slip_ref.shape[0]
    rank_size = basis_ref.shape[0]
    mine = lax.axis_index("row") % clusters
    copies = [
        pltpu.make_async_copy(slip_hbm.at[mine], slip_ref, sems.at[0]),
        pltpu.make_async_copy(basis_hbm.at[mine], basis_ref, sems.at[1]),
        pltpu.make_async_copy(pairs_hbm, pairs_ref, sems.at[2]),
    ]
    for copy in copies:
        copy.start()
    half = rhs_count // 2
    copies[2].wait()
    first = pairs_ref[0:1, :]
    kind = (first - lax.axis_index("long") * clusters) * (NEARC + 1) + pairs_ref[1:2, :] - first
    kinds = lax.broadcasted_iota(jnp.int32, (half, kind.shape[1]), 0)
    live = lax.broadcasted_iota(jnp.int32, kinds.shape, 1) < count_ref[0]
    low = jnp.sum(jnp.where(live & (kinds == kind), 1.0, 0.0), axis=1, keepdims=True)
    high = jnp.sum(jnp.where(live & (kinds + half == kind), 1.0, 0.0), axis=1, keepdims=True)
    copies[0].wait()
    copies[1].wait()
    coeffs = lax.dot_general(
        slip_ref[...].astype(jnp.bfloat16),
        basis_ref[...],
        (((1,), (1,)), ((), ())),
        preferred_element_type=jnp.float32,
    )
    counts = [jnp.broadcast_to(value, (half, rank_size)) for value in (low, high)]
    pay = jnp.concatenate([coeffs[0:half], coeffs[half:]] + counts, axis=1).astype(jnp.bfloat16)
    for target in range(sent_ref.shape[0]):
        sent_ref[target] = pay
    parts = pay_hbm.shape[0] // sent_ref.shape[0]
    sends = [
        pltpu.make_async_copy(
            sent_ref, pay_hbm.at[pl.ds(part * sent_ref.shape[0], sent_ref.shape[0])], out_sems.at[part]
        )
        for part in range(parts)
    ]
    for send in sends:
        send.start()
    for send in sends:
        send.wait()


def geometry_kernel(
    slip_ref, vertices_ref, triangles_ref, map_ref, after_ref, xs_ref, halo_ref, geom_ref
):
    clusters, rhs_count, unknowns = slip_ref.shape
    xs_ref[...] = slip_ref[...].astype(jnp.bfloat16)
    long_index = lax.axis_index("long")

    size = map_ref.shape[1]
    half = size // LANES
    slot_map = map_ref[...]
    index = jnp.concatenate(
        [slot_map[:, part * LANES : (part + 1) * LANES] for part in range(half)], axis=0
    )
    vertex_base = long_index * vertices_ref.shape[1]
    corners = []
    for corner_id in range(3):
        vertex = lane_gather(triangles_ref[corner_id : corner_id + 1, :], index) - vertex_base
        corners.append(
            [lane_gather(vertices_ref[axis_id : axis_id + 1, :], vertex) for axis_id in range(3)]
        )
    one, two, three = corners
    centre = [(one[a] + two[a] + three[a]) / 3.0 for a in range(3)]
    edge_one = [two[a] - one[a] for a in range(3)]
    edge_two = [three[a] - one[a] for a in range(3)]
    normal = [
        edge_one[1] * edge_two[2] - edge_one[2] * edge_two[1],
        edge_one[2] * edge_two[0] - edge_one[0] * edge_two[2],
        edge_one[0] * edge_two[1] - edge_one[1] * edge_two[0],
    ]
    area = 0.5 * jnp.sqrt(normal[0] * normal[0] + normal[1] * normal[1] + normal[2] * normal[2])
    geometry = []
    for value in centre + [area]:
        geometry.append(
            jnp.concatenate(
                [value[part * clusters : (part + 1) * clusters] for part in range(half)], axis=1
            )
        )
    for cluster in range(clusters):
        geom_ref[cluster] = jnp.concatenate(
            [whole[cluster : cluster + 1, :] for whole in geometry], axis=0
        )

    upward = lax.axis_index("row") % 2 == 0
    start = jnp.where(upward, clusters - NEARC, 0)
    pieces = [piece for whole in geometry for piece in split_three(whole)]
    for turn in range(NEARC):
        last = clusters - NEARC + turn
        rows = [
            jnp.where(upward, piece[last : last + 1, :], piece[turn : turn + 1, :])
            for piece in pieces
        ]
        rows.append(jnp.zeros((rhs_count - len(rows), size), jnp.float32))
        halo_ref[turn, :, 0:unknowns] = xs_ref[start + turn]
        halo_ref[turn, :, unknowns : unknowns + size] = jnp.concatenate(rows, axis=0).astype(
            jnp.bfloat16
        )


def window_kernel(xs_ref, geom_ref, halo_ref, slip_ref, place_ref):
    clusters, rhs_count, unknowns = xs_ref.shape
    size = geom_ref.shape[2]
    slots = clusters + NEARC
    odd = lax.axis_index("row") % 2

    def place_of(cluster):
        return (cluster + NEARC * (1 - odd) + slots) % slots

    for cluster in range(clusters):
        slip_ref[place_of(cluster)] = xs_ref[cluster]
        place_ref[place_of(cluster)] = geom_ref[cluster]
    for turn in range(NEARC):
        at = place_of(clusters + turn)
        slip_ref[at] = halo_ref[turn, :, 0:unknowns]
        pieces = halo_ref[turn, :, unknowns : unknowns + size].astype(jnp.float32)
        place_ref[at] = jnp.concatenate(
            [
                (pieces[3 * p + 2 : 3 * p + 3] + pieces[3 * p + 1 : 3 * p + 2])
                + pieces[3 * p : 3 * p + 1]
                for p in range(4)
            ],
            axis=0,
        )


def near_kernel(
    slip_ref, place_ref, pay_ref, after_ref, out_ref, cols_ref, even_ref, odd_ref, *, long_count, clusters
):
    slots, rhs_count, unknowns = slip_ref.shape
    size = place_ref.shape[2]
    long_index = lax.axis_index("long")
    before = jnp.maximum(long_index - 1, 0)
    totals = [jnp.zeros(pay_ref.shape[1:], jnp.float32) for _ in range(2)]
    for row in range(pay_ref.shape[0] // long_count):
        for source, owner in enumerate((long_index, before)):
            totals[source] += pay_ref[row * long_count + owner].astype(jnp.float32)
    even = lax.axis_index("row") % 2 == 0
    half = pay_ref.shape[1]
    rank_size = pay_ref.shape[2] // 4
    group = lax.broadcasted_iota(jnp.int32, (half, LANES), 1) // rank_size
    kinds = lax.broadcasted_iota(jnp.int32, (half, LANES), 0) + jnp.where(group == 3, half, 0)
    kinds = jnp.where(group < 2, -1, kinds)
    lane_id = lax.broadcasted_iota(jnp.int32, (half, LANES), 1)
    kinds = jnp.where(lane_id % rank_size == 0, kinds, -1)

    def count_of(place, u):
        both = []
        for cluster in (u, clusters - NEARC + u):
            reach = place - u - NEARC
            lower = cluster + jnp.minimum(reach, 0)
            inside = lower >= 0
            kind = jnp.where(inside, lower, lower + clusters) * (NEARC + 1) + jnp.abs(reach)
            source = jnp.where(inside, totals[0], totals[1])
            both.append(jnp.where(kinds == kind, source, 0.0))
        picked = jnp.sum(jnp.where(even, both[0], both[1]), axis=0, keepdims=True)
        return jnp.sum(picked, axis=1, keepdims=True)

    out_ref[...] = jnp.zeros(out_ref.shape, jnp.float32)
    for place in range(slots):
        rows = jnp.concatenate([place_ref[place], jnp.zeros((4, size), jnp.float32)], axis=0)
        cols_ref[place] = rows.T
    right = [[place_ref[NEARC + u, p : p + 1, :] for p in range(4)] for u in range(NEARC)]
    parts = [(0, 0), (1, 1), (2, 2), (0, 1), (0, 2), (1, 2)]

    def fill(place, targets, block_ref):
        for step in range(size // ROWS):
            here = pl.ds(step * ROWS, ROWS)
            column = cols_ref[place, here, :]
            left = [jnp.broadcast_to(column[:, p : p + 1], (ROWS, size)) for p in range(4)]
            for u in targets:
                offset = [left[p] - right[u][p] for p in range(3)]
                radius_sq = offset[0] * offset[0] + offset[1] * offset[1] + offset[2] * offset[2]
                inverse = lax.rsqrt(radius_sq + soften)
                flat = (left[3] * right[u][3]) * inverse
                cubed = flat * (inverse * inverse)
                scaled = [offset[p] * cubed for p in range(3)]
                for part_id, (i, j) in enumerate(parts):
                    term = offset[i] * scaled[j]
                    if i == j:
                        term = term + flat
                    block_ref[u, part_id, here, :] = term.astype(jnp.bfloat16)

    def apply(place, targets, block_ref):
        slip = slip_ref[place]
        pieces = [slip[:, p * size : (p + 1) * size] for p in range(3)]
        for u in targets:
            count = count_of(place, u)
            sums = [
                jnp.dot(pieces[p], block_ref[u, p], preferred_element_type=jnp.float32)
                for p in range(3)
            ]
            for part_id in range(3, 6):
                i, j = parts[part_id]
                both = jnp.dot(
                    jnp.concatenate([pieces[j], pieces[i]], axis=0),
                    block_ref[u, part_id],
                    preferred_element_type=jnp.float32,
                )
                sums[i] = sums[i] + both[0:rhs_count]
                sums[j] = sums[j] + both[rhs_count : 2 * rhs_count]
            for p in range(3):
                out_ref[u, :, p * size : (p + 1) * size] += count * sums[p]

    every = list(range(NEARC))
    fill(0, [0], even_ref)
    for u in range(1, NEARC):
        even_ref[u] = jnp.zeros(even_ref.shape[1:], jnp.bfloat16)

    def two_places(turn, carry):
        place = 2 * turn
        fill(place + 1, every, odd_ref)
        apply(place, every, even_ref)
        fill(place + 2, every, even_ref)
        apply(place + 1, every, odd_ref)
        return carry

    lax.fori_loop(0, (slots - 2) // 2, two_places, 0)
    fill(slots - 1, [NEARC - 1], odd_ref)
    apply(slots - 2, every, even_ref)
    apply(slots - 1, [NEARC - 1], odd_ref)


def coupling_kernel(
    coupling_ref, pairs_ref, after_ref, to_second_ref, to_first_ref, list_ref, *, clusters, long_count
):
    owner, group = pairs_ref[...] // clusters, pairs_ref[...] % clusters
    list_ref[...] = jnp.concatenate([group * long_count + owner, owner, group], axis=0)
    pair_count, rank_size, _ = coupling_ref.shape
    groups = LANES // rank_size
    for pair_id in range(pair_count):
        here = pl.ds(pair_id * rank_size, rank_size)
        coupling = coupling_ref[pair_id].astype(jnp.float32)
        for out_ref, value in ((to_second_ref, coupling), (to_first_ref, coupling.T)):
            out_ref[here, :] = jnp.concatenate([value] * groups, axis=1).astype(jnp.bfloat16)


def far_kernel(
    pairs_ref, coeff_ref, to_second_ref, to_first_ref, out_hbm, done_ref, sent_ref, sems, *total_refs, clusters
):
    done_ref[...] = jnp.zeros(done_ref.shape, jnp.float32)
    long_count, rhs_count, _ = total_refs[0].shape
    pair_count = pairs_ref.shape[1]
    rank_size = LANES // clusters
    group_id = lax.broadcasted_iota(jnp.int32, (rhs_count, LANES), 1) // rank_size
    for total_ref in total_refs:
        total_ref[...] = jnp.zeros(total_ref.shape, jnp.float32)

    def coeff_of(at, group):
        whole = coeff_ref[at]
        whole = whole.astype(jnp.float32)
        low = pltpu.roll(whole, rank_size * group, 1) if group else whole
        high = pltpu.roll(whole, (rank_size * (group - 1)) % LANES, 1) if group != 1 else whole
        both = jnp.concatenate([low, high], axis=0)
        return jnp.where(group_id == group, both, 0.0)

    results = []
    for begin in range(0, pair_count, clusters):
        pair_ids = range(begin, min(begin + clusters, pair_count))
        depth = len(pair_ids) * rank_size
        here = pl.ds(begin * rank_size, depth)
        for source, target, matrix_ref in ((0, 1, to_second_ref), (1, 0, to_first_ref)):
            coeffs = jnp.concatenate(
                [coeff_of(pairs_ref[source, f], f - begin) for f in pair_ids], axis=0
            ).astype(jnp.bfloat16)
            value = jnp.dot(
                coeffs[:, 0:depth], matrix_ref[here, :], preferred_element_type=jnp.float32
            )
            for turn, f in enumerate(pair_ids):
                results.append(
                    (target, f, value[turn * rhs_count : (turn + 1) * rhs_count])
                )
    for turn, (target, f, value) in enumerate(results):
        total_ref = total_refs[turn % len(total_refs)]
        owner, group = pairs_ref[2 + target, f], pairs_ref[4 + target, f]
        total_ref[owner] += jnp.where(group_id == group, value, 0.0)
    total = total_refs[0][...]
    for total_ref in total_refs[1:]:
        total = total + total_ref[...]
    sent_ref[...] = total.astype(jnp.bfloat16)
    copies = [
        pltpu.make_async_copy(
            sent_ref, out_hbm.at[pl.ds(copy_id * long_count, long_count)], sems.at[copy_id]
        )
        for copy_id in range(out_hbm.shape[0] // long_count)
    ]
    for copy in copies:
        copy.start()
    for copy in copies:
        copy.wait()


def finish_kernel(own_ref, other_ref, far_ref, basis_ref, out_hbm, sent_ref, sems):
    clusters, rank_size, unknowns = basis_ref.shape
    total = jnp.sum(far_ref[...].astype(jnp.float32), axis=0)
    group_id = lax.broadcasted_iota(jnp.int32, total.shape, 1) // rank_size
    flat_basis = basis_ref[...].reshape(clusters * rank_size, unknowns)
    even = lax.axis_index("row") % 2 == 0
    copies = []
    for cluster in range(clusters):
        u = cluster % NEARC
        here = even if cluster < NEARC else jnp.logical_not(even)
        near = jnp.where(here, own_ref[u], other_ref[u])
        picked = jnp.where(group_id == cluster, total, 0.0).astype(jnp.bfloat16)
        result = jnp.dot(picked, flat_basis, preferred_element_type=jnp.float32)
        sent_ref[cluster] = result + near
        copies.append(
            pltpu.make_async_copy(sent_ref.at[cluster], out_hbm.at[cluster], sems.at[cluster])
        )
        copies[-1].start()
    for copy in copies:
        copy.wait()


def shards(slip, vertices, triangles, elem_map, near_pairs, near_count, far_pairs, far_coef, basis):
    clusters, rhs_count, unknowns = slip.shape
    rank_size = basis.shape[1]
    size = elem_map.shape[1]
    row_count = lax.axis_size("row")
    long_count = lax.axis_size("long")
    devices = row_count * long_count
    coupling = far_coef.reshape(-1, rank_size, rank_size)
    slots = clusters + NEARC

    pay = pl.pallas_call(
        coeffs_kernel,
        out_shape=jax.ShapeDtypeStruct((devices, rhs_count // 2, LANES), jnp.bfloat16),
        in_specs=[HBM] * 3 + [SMEM],
        out_specs=HBM,
        scratch_shapes=[
            pltpu.VMEM(slip.shape[1:], slip.dtype),
            pltpu.VMEM(basis.shape[1:], basis.dtype),
            pltpu.VMEM(near_pairs.shape, near_pairs.dtype),
            pltpu.VMEM((long_count, rhs_count // 2, LANES), jnp.bfloat16),
            pltpu.SemaphoreType.DMA((3,)),
            pltpu.SemaphoreType.DMA((row_count,)),
        ],
        compiler_params=pltpu.CompilerParams(vmem_limit_bytes=16 << 20),
        name="coeffs",
    )(
        *[
            pltpu.with_memory_space_constraint(array, pltpu.HBM)
            for array in (slip, basis, near_pairs)
        ],
        near_count,
    )
    everyone = lax.all_to_all(pay, ("row", "long"), 0, 0, tiled=True)

    xs, to_neighbour, geometry = pl.pallas_call(
        geometry_kernel,
        out_shape=[
            jax.ShapeDtypeStruct(slip.shape, jnp.bfloat16),
            jax.ShapeDtypeStruct((NEARC, rhs_count, unknowns + size), jnp.bfloat16),
            jax.ShapeDtypeStruct((clusters, 4, size), jnp.float32),
        ],
        in_specs=[VMEM] * 4 + [ANY],
        out_specs=[VMEM] * 3,
        compiler_params=pltpu.CompilerParams(vmem_limit_bytes=16 << 20),
        cost_estimate=pl.CostEstimate(
            flops=2_000_000, bytes_accessed=1_000_000, transcendentals=1_000
        ),
        name="geometry",
    )(slip, vertices, triangles, elem_map, pay)
    route = []
    for row in range(row_count):
        step = 1 if row % 2 == 0 else -1
        for owner in range(long_count):
            if 0 <= owner - step < long_count:
                route.append((row * long_count + owner - step, row * long_count + owner))
    halo = lax.ppermute(to_neighbour, ("row", "long"), route)

    window, places = pl.pallas_call(
        window_kernel,
        out_shape=[
            jax.ShapeDtypeStruct((slots, rhs_count, unknowns), jnp.bfloat16),
            jax.ShapeDtypeStruct((slots, 4, size), jnp.float32),
        ],
        in_specs=[VMEM] * 3,
        out_specs=[VMEM] * 2,
        compiler_params=pltpu.CompilerParams(vmem_limit_bytes=16 << 20),
        cost_estimate=pl.CostEstimate(flops=1000, bytes_accessed=1000, transcendentals=0),
        name="window",
    )(xs, geometry, halo)

    to_second, to_first, pair_list = pl.pallas_call(
        functools.partial(coupling_kernel, clusters=clusters, long_count=long_count),
        out_shape=[jax.ShapeDtypeStruct((coupling.shape[0] * rank_size, LANES), jnp.bfloat16)] * 2
        + [jax.ShapeDtypeStruct((6,) + far_pairs.shape[1:], far_pairs.dtype)],
        in_specs=[VMEM, VMEM, ANY],
        out_specs=[VMEM] * 3,
        compiler_params=pltpu.CompilerParams(vmem_limit_bytes=16 << 20),
        cost_estimate=pl.CostEstimate(flops=1000, bytes_accessed=1000, transcendentals=0),
        name="coupling",
    )(coupling, far_pairs, pay)
    far, far_done = pl.pallas_call(
        functools.partial(far_kernel, clusters=clusters),
        out_shape=[
            jax.ShapeDtypeStruct((devices, rhs_count, clusters * rank_size), jnp.bfloat16),
            jax.ShapeDtypeStruct((8, LANES), jnp.float32),
        ],
        in_specs=[SMEM, VMEM, VMEM, VMEM],
        out_specs=[HBM, VMEM],
        scratch_shapes=[
            pltpu.VMEM((long_count, rhs_count, clusters * rank_size), jnp.bfloat16),
            pltpu.SemaphoreType.DMA((row_count,)),
        ]
        + [pltpu.VMEM((long_count, rhs_count, clusters * rank_size), jnp.float32)] * 4,
        compiler_params=pltpu.CompilerParams(vmem_limit_bytes=16 << 20),
        name="far",
    )(pair_list, everyone, to_second, to_first)
    far_terms = lax.all_to_all(far, ("row", "long"), 0, 0, tiled=True)

    near = pl.pallas_call(
        functools.partial(near_kernel, long_count=long_count, clusters=clusters),
        out_shape=jax.ShapeDtypeStruct((NEARC, rhs_count, unknowns), jnp.float32),
        in_specs=[VMEM] * 3 + [ANY],
        out_specs=VMEM,
        scratch_shapes=[
            pltpu.VMEM((slots, size, 8), jnp.float32),
            pltpu.VMEM((NEARC, 6, size, size), jnp.bfloat16),
            pltpu.VMEM((NEARC, 6, size, size), jnp.bfloat16),
        ],
        compiler_params=pltpu.CompilerParams(vmem_limit_bytes=24 << 20),
        cost_estimate=pl.CostEstimate(
            flops=1_000_000_000, bytes_accessed=1_000_000, transcendentals=660_000
        ),
        name="near",
    )(window, places, everyone, far_done)
    partner = [(row, row ^ 1) for row in range(row_count)]
    other = lax.ppermute(near, "row", partner)

    return pl.pallas_call(
        finish_kernel,
        out_shape=jax.ShapeDtypeStruct(slip.shape, jnp.float32),
        in_specs=[VMEM] * 4,
        out_specs=HBM,
        scratch_shapes=[
            pltpu.VMEM(slip.shape, jnp.float32),
            pltpu.SemaphoreType.DMA((clusters,)),
        ],
        compiler_params=pltpu.CompilerParams(vmem_limit_bytes=16 << 20),
        name="finish",
    )(near, other, far_terms, basis)


def solution(mesh):
    placed = (
        P("long", None, None),
        P(None, "long"),
        P(None, "long"),
        P("long", None),
        P(None, ("row", "long")),
        P(("row", "long")),
        P(None, ("row", "long")),
        P(("row", "long"), None),
        P("long", None, None),
    )
    return jax.shard_map(
        shards, mesh=mesh, in_specs=placed, out_specs=P("long", None, None), check_vma=False
    )
```

```python
import functools

import jax
import jax.numpy as jnp
from jax import lax
from jax.experimental import pallas as pl
from jax.experimental.pallas import tpu as pltpu
from jax.sharding import PartitionSpec as P

NEARC = 2
LANES = 128
ROWS = 16

soften = 0.25

VMEM = pl.BlockSpec(memory_space=pltpu.VMEM)
SMEM = pl.BlockSpec(memory_space=pltpu.SMEM)
HBM = pl.BlockSpec(memory_space=pltpu.HBM)
ANY = pl.BlockSpec(memory_space=pl.ANY)
SMALL = pl.CostEstimate(flops=1000, bytes_accessed=1000, transcendentals=0)


def first_place(row_count, long_count):
    return row_count // 2 * long_count - 1


def same_core(row_count, long_count):
    total = row_count // 2 * long_count
    order = [(place + first_place(row_count, long_count)) % total for place in range(total)]
    return [
        [(2 * (at // long_count) + core) * long_count + at % long_count for at in order]
        for core in range(2)
    ]


def place_in_core(row, owner, row_count, long_count):
    total = row_count // 2 * long_count
    return (row * long_count + owner + total - first_place(row_count, long_count)) % total


def lane_gather(table, index):
    length = table.shape[1]
    lane = index & (LANES - 1)
    chunk = index // LANES
    found = jnp.zeros(index.shape, table.dtype)
    for piece_id in range(-(-length // LANES)):
        piece = table[:, piece_id * LANES : min(length, (piece_id + 1) * LANES)]
        missing = LANES - piece.shape[1]
        if missing:
            piece = jnp.concatenate([piece, jnp.zeros((1, missing), table.dtype)], axis=1)
        picked = jnp.take_along_axis(jnp.broadcast_to(piece, index.shape), lane, axis=1)
        found = jnp.where(chunk == piece_id, picked, found)
    return found


def split_three(value):
    high = value.astype(jnp.bfloat16).astype(jnp.float32)
    rest = value - high
    middle = rest.astype(jnp.bfloat16).astype(jnp.float32)
    return [high, middle, rest - middle]


def coeffs_kernel(
    slip_hbm, basis_hbm, pairs_hbm, count_ref, pay_hbm, slip_ref, basis_ref, pairs_ref, sent_ref, sems, out_sems
):
    clusters = slip_hbm.shape[0]
    share, rhs_count, _ = slip_ref.shape
    rank_size = basis_ref.shape[1]
    begin = (lax.axis_index("row") // 2) % (clusters // share) * share
    copies = [
        pltpu.make_async_copy(slip_hbm.at[pl.ds(begin, share)], slip_ref, sems.at[0]),
        pltpu.make_async_copy(basis_hbm.at[pl.ds(begin, share)], basis_ref, sems.at[1]),
        pltpu.make_async_copy(pairs_hbm, pairs_ref, sems.at[2]),
    ]
    for copy in copies:
        copy.start()
    copies[2].wait()
    first = pairs_ref[0:1, :]
    kind = (first - lax.axis_index("long") * clusters) * (NEARC + 1) + pairs_ref[1:2, :] - first
    kinds = lax.broadcasted_iota(jnp.int32, (rhs_count, kind.shape[1]), 0)
    live = lax.broadcasted_iota(jnp.int32, kinds.shape, 1) < count_ref[0]
    counts = jnp.sum(jnp.where(live & (kinds == kind), 1.0, 0.0), axis=1, keepdims=True)
    copies[0].wait()
    copies[1].wait()
    coeffs = [
        lax.dot_general(
            slip_ref[turn].astype(jnp.bfloat16),
            basis_ref[turn],
            (((1,), (1,)), ((), ())),
            preferred_element_type=jnp.float32,
        )
        for turn in range(share)
    ]
    counts = jnp.broadcast_to(counts, (rhs_count, LANES - share * rank_size))
    pay = jnp.concatenate(coeffs + [counts], axis=1).astype(jnp.bfloat16)
    for target in range(sent_ref.shape[0]):
        sent_ref[target] = pay
    parts = pay_hbm.shape[0] // sent_ref.shape[0]
    sends = [
        pltpu.make_async_copy(
            sent_ref, pay_hbm.at[pl.ds(part * sent_ref.shape[0], sent_ref.shape[0])], out_sems.at[part]
        )
        for part in range(parts)
    ]
    for send in sends:
        send.start()
    for send in sends:
        send.wait()


def geometry_kernel(
    slip_ref, vertices_ref, triangles_ref, map_ref, after_ref, xs_ref, halo_ref, geom_ref
):
    clusters, rhs_count, unknowns = slip_ref.shape
    xs_ref[...] = slip_ref[...].astype(jnp.bfloat16)
    long_index = lax.axis_index("long")

    size = map_ref.shape[1]
    half = size // LANES
    slot_map = map_ref[...]
    index = jnp.concatenate(
        [slot_map[:, part * LANES : (part + 1) * LANES] for part in range(half)], axis=0
    )
    vertex_base = long_index * vertices_ref.shape[1]
    corners = []
    for corner_id in range(3):
        vertex = lane_gather(triangles_ref[corner_id : corner_id + 1, :], index) - vertex_base
        corners.append(
            [lane_gather(vertices_ref[axis_id : axis_id + 1, :], vertex) for axis_id in range(3)]
        )
    one, two, three = corners
    centre = [(one[a] + two[a] + three[a]) / 3.0 for a in range(3)]
    edge_one = [two[a] - one[a] for a in range(3)]
    edge_two = [three[a] - one[a] for a in range(3)]
    normal = [
        edge_one[1] * edge_two[2] - edge_one[2] * edge_two[1],
        edge_one[2] * edge_two[0] - edge_one[0] * edge_two[2],
        edge_one[0] * edge_two[1] - edge_one[1] * edge_two[0],
    ]
    area = 0.5 * jnp.sqrt(normal[0] * normal[0] + normal[1] * normal[1] + normal[2] * normal[2])
    geometry = []
    for value in centre + [area]:
        geometry.append(
            jnp.concatenate(
                [value[part * clusters : (part + 1) * clusters] for part in range(half)], axis=1
            )
        )
    for cluster in range(clusters):
        geom_ref[cluster] = jnp.concatenate(
            [whole[cluster : cluster + 1, :] for whole in geometry], axis=0
        )

    upward = lax.axis_index("row") % 2 == 0
    start = jnp.where(upward, clusters - NEARC, 0)
    pieces = [piece for whole in geometry for piece in split_three(whole)]
    for turn in range(NEARC):
        last = clusters - NEARC + turn
        rows = [
            jnp.where(upward, piece[last : last + 1, :], piece[turn : turn + 1, :])
            for piece in pieces
        ]
        rows.append(jnp.zeros((rhs_count - len(rows), size), jnp.float32))
        halo_ref[turn, :, 0:unknowns] = xs_ref[start + turn]
        halo_ref[turn, :, unknowns : unknowns + size] = jnp.concatenate(rows, axis=0).astype(
            jnp.bfloat16
        )


def window_kernel(xs_ref, geom_ref, halo_ref, slip_ref, place_ref):
    clusters, rhs_count, unknowns = xs_ref.shape
    size = geom_ref.shape[2]
    slots = clusters + NEARC
    odd = lax.axis_index("row") % 2

    def place_of(cluster):
        return (cluster + NEARC * (1 - odd) + slots) % slots

    for cluster in range(clusters):
        slip_ref[place_of(cluster)] = xs_ref[cluster]
        place_ref[place_of(cluster)] = geom_ref[cluster]
    for turn in range(NEARC):
        at = place_of(clusters + turn)
        slip_ref[at] = halo_ref[turn, :, 0:unknowns]
        pieces = halo_ref[turn, :, unknowns : unknowns + size].astype(jnp.float32)
        place_ref[at] = jnp.concatenate(
            [
                (pieces[3 * p + 2 : 3 * p + 3] + pieces[3 * p + 1 : 3 * p + 2])
                + pieces[3 * p : 3 * p + 1]
                for p in range(4)
            ],
            axis=0,
        )


def totals_kernel(pay_ref, out_ref, *, long_count):
    row_count = 2 * pay_ref.shape[0] // long_count
    long_index = lax.axis_index("long")
    totals = [jnp.zeros(pay_ref.shape[1:], jnp.float32) for _ in range(2)]
    for row in range(row_count // 2):
        for source, owner in enumerate((long_index, jnp.maximum(long_index - 1, 0))):
            at = place_in_core(row, owner, row_count, long_count)
            totals[source] += pay_ref[at].astype(jnp.float32)
    lane_id = lax.broadcasted_iota(jnp.int32, out_ref.shape, 1)
    out_ref[...] = jnp.where(lane_id < 3 * LANES // 4, totals[0], totals[1])


def near_kernel(
    slip_ref, place_ref, mine_ref, theirs_ref, after_ref, out_ref, cols_ref, even_ref, odd_ref, *, clusters
):
    slots, rhs_count, unknowns = slip_ref.shape
    size = place_ref.shape[2]
    totals = mine_ref[...] + theirs_ref[...]
    even = lax.axis_index("row") % 2 == 0
    kinds = lax.broadcasted_iota(jnp.int32, totals.shape, 0)
    lane_id = lax.broadcasted_iota(jnp.int32, totals.shape, 1)

    def count_of(place, u):
        both = []
        for cluster in (u, clusters - NEARC + u):
            reach = place - u - NEARC
            lower = cluster + jnp.minimum(reach, 0)
            inside = lower >= 0
            kind = jnp.where(inside, lower, lower + clusters) * (NEARC + 1) + jnp.abs(reach)
            lane = jnp.where(inside, LANES // 2, 3 * LANES // 4)
            both.append(jnp.where((kinds == kind) & (lane_id == lane), totals, 0.0))
        picked = jnp.sum(jnp.where(even, both[0], both[1]), axis=0, keepdims=True)
        return jnp.sum(picked, axis=1, keepdims=True)

    out_ref[...] = jnp.zeros(out_ref.shape, jnp.float32)
    for place in range(slots):
        rows = jnp.concatenate([place_ref[place], jnp.zeros((4, size), jnp.float32)], axis=0)
        cols_ref[place] = rows.T
    right = [[place_ref[NEARC + u, p : p + 1, :] for p in range(4)] for u in range(NEARC)]
    parts = [(0, 0), (1, 1), (2, 2), (0, 1), (0, 2), (1, 2)]

    def fill(place, targets, block_ref):
        for step in range(size // ROWS):
            here = pl.ds(step * ROWS, ROWS)
            column = cols_ref[place, here, :]
            left = [jnp.broadcast_to(column[:, p : p + 1], (ROWS, size)) for p in range(4)]
            for u in targets:
                offset = [left[p] - right[u][p] for p in range(3)]
                radius_sq = offset[0] * offset[0] + offset[1] * offset[1] + offset[2] * offset[2]
                inverse = lax.rsqrt(radius_sq + soften)
                flat = (left[3] * right[u][3]) * inverse
                cubed = flat * (inverse * inverse)
                scaled = [offset[p] * cubed for p in range(3)]
                for part_id, (i, j) in enumerate(parts):
                    term = offset[i] * scaled[j]
                    if i == j:
                        term = term + flat
                    block_ref[u, part_id, here, :] = term.astype(jnp.bfloat16)

    def apply(place, targets, block_ref):
        slip = slip_ref[place]
        pieces = [slip[:, p * size : (p + 1) * size] for p in range(3)]
        for u in targets:
            count = count_of(place, u)
            sums = [
                jnp.dot(pieces[p], block_ref[u, p], preferred_element_type=jnp.float32)
                for p in range(3)
            ]
            for part_id in range(3, 6):
                i, j = parts[part_id]
                both = jnp.dot(
                    jnp.concatenate([pieces[j], pieces[i]], axis=0),
                    block_ref[u, part_id],
                    preferred_element_type=jnp.float32,
                )
                sums[i] = sums[i] + both[0:rhs_count]
                sums[j] = sums[j] + both[rhs_count : 2 * rhs_count]
            for p in range(3):
                out_ref[u, :, p * size : (p + 1) * size] += count * sums[p]

    every = list(range(NEARC))
    fill(0, [0], even_ref)
    for u in range(1, NEARC):
        even_ref[u] = jnp.zeros(even_ref.shape[1:], jnp.bfloat16)

    def two_places(turn, carry):
        place = 2 * turn
        fill(place + 1, every, odd_ref)
        apply(place, every, even_ref)
        fill(place + 2, every, even_ref)
        apply(place + 1, every, odd_ref)
        return carry

    lax.fori_loop(0, (slots - 2) // 2, two_places, 0)
    fill(slots - 1, [NEARC - 1], odd_ref)
    apply(slots - 2, every, even_ref)
    apply(slots - 1, [NEARC - 1], odd_ref)


def coupling_kernel(
    coupling_ref, pairs_ref, after_ref, to_second_ref, to_first_ref, list_ref, *, clusters, long_count, row_count
):
    share = clusters // 2
    owner, group = pairs_ref[...] // clusters, pairs_ref[...] % clusters
    at = place_in_core(group // share, owner, row_count, long_count) * share + group % share
    list_ref[...] = jnp.concatenate([at, owner, group], axis=0)
    pair_count, rank_size, _ = coupling_ref.shape
    groups = LANES // rank_size
    for pair_id in range(pair_count):
        here = pl.ds(pair_id * rank_size, rank_size)
        coupling = coupling_ref[pair_id].astype(jnp.float32)
        for out_ref, value in ((to_second_ref, coupling), (to_first_ref, coupling.T)):
            out_ref[here, :] = jnp.concatenate([value] * groups, axis=1).astype(jnp.bfloat16)


def far_kernel(
    pairs_ref, coeff_ref, to_second_ref, to_first_ref, out_hbm, done_ref, sent_ref, sems, moved_ref, *total_refs, clusters
):
    done_ref[...] = jnp.zeros(done_ref.shape, jnp.float32)
    long_count, rhs_count, _ = total_refs[0].shape
    row_count = out_hbm.shape[0] // long_count
    pair_count = pairs_ref.shape[1]
    rank_size = LANES // clusters
    group_id = lax.broadcasted_iota(jnp.int32, (rhs_count, LANES), 1) // rank_size
    for total_ref in total_refs:
        total_ref[...] = jnp.zeros(total_ref.shape, jnp.float32)

    share = clusters // 2
    for at in range(coeff_ref.shape[0]):
        whole = coeff_ref[at].astype(jnp.float32)
        for turn in range(share):
            moved_ref[at * share + turn] = (
                pltpu.roll(whole, LANES - rank_size * turn, 1) if turn else whole
            )

    def coeff_of(at, group):
        whole = moved_ref[at]
        both = pltpu.roll(whole, rank_size * group, 1) if group else whole
        return jnp.where(group_id == group, both, 0.0)

    results = []
    for begin in range(0, pair_count, clusters):
        pair_ids = range(begin, min(begin + clusters, pair_count))
        depth = len(pair_ids) * rank_size
        here = pl.ds(begin * rank_size, depth)
        for source, target, matrix_ref in ((0, 1, to_second_ref), (1, 0, to_first_ref)):
            coeffs = jnp.concatenate(
                [coeff_of(pairs_ref[source, f], f - begin) for f in pair_ids], axis=0
            ).astype(jnp.bfloat16)
            value = jnp.dot(
                coeffs[:, 0:depth], matrix_ref[here, :], preferred_element_type=jnp.float32
            )
            for turn, f in enumerate(pair_ids):
                results.append(
                    (target, f, value[turn * rhs_count : (turn + 1) * rhs_count])
                )
    for turn, (target, f, value) in enumerate(results):
        total_ref = total_refs[turn % len(total_refs)]
        owner, group = pairs_ref[2 + target, f], pairs_ref[4 + target, f]
        total_ref[owner] += jnp.where(group_id == group, value, 0.0)
    total = total_refs[0][...]
    for total_ref in total_refs[1:]:
        total = total + total_ref[...]
    sent_ref[...] = total.astype(jnp.bfloat16)
    copies = [
        pltpu.make_async_copy(
            sent_ref, out_hbm.at[pl.ds(copy_id * long_count, long_count)], sems.at[copy_id]
        )
        for copy_id in range(out_hbm.shape[0] // long_count)
    ]
    for copy in copies:
        copy.start()
    for copy in copies:
        copy.wait()


def finish_kernel(own_ref, other_ref, far_ref, basis_ref, out_hbm, sent_ref, sems):
    clusters, rank_size, unknowns = basis_ref.shape
    total = jnp.sum(far_ref[...].astype(jnp.float32), axis=0)
    group_id = lax.broadcasted_iota(jnp.int32, total.shape, 1) // rank_size
    flat_basis = basis_ref[...].reshape(clusters * rank_size, unknowns)
    even = lax.axis_index("row") % 2 == 0
    copies = []
    for cluster in range(clusters):
        u = cluster % NEARC
        here = even if cluster < NEARC else jnp.logical_not(even)
        near = jnp.where(here, own_ref[u], other_ref[u])
        picked = jnp.where(group_id == cluster, total, 0.0).astype(jnp.bfloat16)
        result = jnp.dot(picked, flat_basis, preferred_element_type=jnp.float32)
        sent_ref[cluster] = result + near
        copies.append(
            pltpu.make_async_copy(sent_ref.at[cluster], out_hbm.at[cluster], sems.at[cluster])
        )
        copies[-1].start()
    for copy in copies:
        copy.wait()


def shards(slip, vertices, triangles, elem_map, near_pairs, near_count, far_pairs, far_coef, basis):
    clusters, rhs_count, unknowns = slip.shape
    rank_size = basis.shape[1]
    size = elem_map.shape[1]
    row_count = lax.axis_size("row")
    long_count = lax.axis_size("long")
    devices = row_count * long_count
    share = clusters // 2
    coupling = far_coef.reshape(-1, rank_size, rank_size)
    slots = clusters + NEARC

    pay = pl.pallas_call(
        coeffs_kernel,
        out_shape=jax.ShapeDtypeStruct((devices // 2, rhs_count, LANES), jnp.bfloat16),
        in_specs=[HBM] * 3 + [SMEM],
        out_specs=HBM,
        scratch_shapes=[
            pltpu.VMEM((share,) + slip.shape[1:], slip.dtype),
            pltpu.VMEM((share,) + basis.shape[1:], basis.dtype),
            pltpu.VMEM(near_pairs.shape, near_pairs.dtype),
            pltpu.VMEM((long_count, rhs_count, LANES), jnp.bfloat16),
            pltpu.SemaphoreType.DMA((3,)),
            pltpu.SemaphoreType.DMA((row_count // 2,)),
        ],
        compiler_params=pltpu.CompilerParams(vmem_limit_bytes=16 << 20),
        name="coeffs",
    )(
        *[
            pltpu.with_memory_space_constraint(array, pltpu.HBM)
            for array in (slip, basis, near_pairs)
        ],
        near_count,
    )
    everyone = lax.all_to_all(
        pay, ("row", "long"), 0, 0, axis_index_groups=same_core(row_count, long_count), tiled=True
    )

    xs, to_neighbour, geometry = pl.pallas_call(
        geometry_kernel,
        out_shape=[
            jax.ShapeDtypeStruct(slip.shape, jnp.bfloat16),
            jax.ShapeDtypeStruct((NEARC, rhs_count, unknowns + size), jnp.bfloat16),
            jax.ShapeDtypeStruct((clusters, 4, size), jnp.float32),
        ],
        in_specs=[VMEM] * 4 + [ANY],
        out_specs=[VMEM] * 3,
        compiler_params=pltpu.CompilerParams(vmem_limit_bytes=16 << 20),
        cost_estimate=pl.CostEstimate(
            flops=2_000_000, bytes_accessed=1_000_000, transcendentals=1_000
        ),
        name="geometry",
    )(slip, vertices, triangles, elem_map, pay)
    route = []
    for row in range(row_count):
        step = 1 if row % 2 == 0 else -1
        for owner in range(long_count):
            if 0 <= owner - step < long_count:
                route.append((row * long_count + owner - step, row * long_count + owner))
    halo = lax.ppermute(to_neighbour, ("row", "long"), route)

    window, places = pl.pallas_call(
        window_kernel,
        out_shape=[
            jax.ShapeDtypeStruct((slots, rhs_count, unknowns), jnp.bfloat16),
            jax.ShapeDtypeStruct((slots, 4, size), jnp.float32),
        ],
        in_specs=[VMEM] * 3,
        out_specs=[VMEM] * 2,
        compiler_params=pltpu.CompilerParams(vmem_limit_bytes=16 << 20),
        cost_estimate=pl.CostEstimate(flops=1000, bytes_accessed=1000, transcendentals=0),
        name="window",
    )(xs, geometry, halo)

    to_second, to_first, pair_list = pl.pallas_call(
        functools.partial(
            coupling_kernel, clusters=clusters, long_count=long_count, row_count=row_count
        ),
        out_shape=[jax.ShapeDtypeStruct((coupling.shape[0] * rank_size, LANES), jnp.bfloat16)] * 2
        + [jax.ShapeDtypeStruct((6,) + far_pairs.shape[1:], far_pairs.dtype)],
        in_specs=[VMEM, VMEM, ANY],
        out_specs=[VMEM] * 3,
        compiler_params=pltpu.CompilerParams(vmem_limit_bytes=16 << 20),
        cost_estimate=pl.CostEstimate(flops=1000, bytes_accessed=1000, transcendentals=0),
        name="coupling",
    )(coupling, far_pairs, pay)
    far, far_done = pl.pallas_call(
        functools.partial(far_kernel, clusters=clusters),
        out_shape=[
            jax.ShapeDtypeStruct((devices, rhs_count, clusters * rank_size), jnp.bfloat16),
            jax.ShapeDtypeStruct((8, LANES), jnp.float32),
        ],
        in_specs=[SMEM, VMEM, VMEM, VMEM],
        out_specs=[HBM, VMEM],
        scratch_shapes=[
            pltpu.VMEM((long_count, rhs_count, clusters * rank_size), jnp.bfloat16),
            pltpu.SemaphoreType.DMA((row_count,)),
            pltpu.VMEM((devices // 2 * share, rhs_count, LANES), jnp.float32),
        ]
        + [pltpu.VMEM((long_count, rhs_count, clusters * rank_size), jnp.float32)] * 4,
        compiler_params=pltpu.CompilerParams(vmem_limit_bytes=16 << 20),
        name="far",
    )(pair_list, everyone, to_second, to_first)
    far_terms = lax.all_to_all(far, ("row", "long"), 0, 0, tiled=True)

    totals = pl.pallas_call(
        functools.partial(totals_kernel, long_count=long_count),
        out_shape=jax.ShapeDtypeStruct((rhs_count, LANES), jnp.float32),
        in_specs=[VMEM],
        out_specs=VMEM,
        compiler_params=pltpu.CompilerParams(vmem_limit_bytes=16 << 20),
        cost_estimate=SMALL,
        name="totals",
    )(everyone)
    partner = [(row, row ^ 1) for row in range(row_count)]
    totals_other = lax.ppermute(totals, "row", partner)

    near = pl.pallas_call(
        functools.partial(near_kernel, clusters=clusters),
        out_shape=jax.ShapeDtypeStruct((NEARC, rhs_count, unknowns), jnp.float32),
        in_specs=[VMEM] * 4 + [ANY],
        out_specs=VMEM,
        scratch_shapes=[
            pltpu.VMEM((slots, size, 8), jnp.float32),
            pltpu.VMEM((NEARC, 6, size, size), jnp.bfloat16),
            pltpu.VMEM((NEARC, 6, size, size), jnp.bfloat16),
        ],
        compiler_params=pltpu.CompilerParams(vmem_limit_bytes=24 << 20),
        cost_estimate=pl.CostEstimate(
            flops=1_000_000_000, bytes_accessed=1_000_000, transcendentals=660_000
        ),
        name="near",
    )(window, places, totals, totals_other, far_done)
    other = lax.ppermute(near, "row", partner)

    return pl.pallas_call(
        finish_kernel,
        out_shape=jax.ShapeDtypeStruct(slip.shape, jnp.float32),
        in_specs=[VMEM] * 4,
        out_specs=HBM,
        scratch_shapes=[
            pltpu.VMEM(slip.shape, jnp.float32),
            pltpu.SemaphoreType.DMA((clusters,)),
        ],
        compiler_params=pltpu.CompilerParams(vmem_limit_bytes=16 << 20),
        name="finish",
    )(near, other, far_terms, basis)


def solution(mesh):
    placed = (
        P("long", None, None),
        P(None, "long"),
        P(None, "long"),
        P("long", None),
        P(None, ("row", "long")),
        P(("row", "long")),
        P(None, ("row", "long")),
        P(("row", "long"), None),
        P("long", None, None),
    )
    return jax.shard_map(
        shards, mesh=mesh, in_specs=placed, out_specs=P("long", None, None), check_vma=False
    )
```

```python
import functools

import jax
import jax.numpy as jnp
from jax import lax
from jax.experimental import pallas as pl
from jax.experimental.pallas import tpu as pltpu
from jax.sharding import PartitionSpec as P

NEARC = 2
LANES = 128
ROWS = 16

soften = 0.25

VMEM = pl.BlockSpec(memory_space=pltpu.VMEM)
SMEM = pl.BlockSpec(memory_space=pltpu.SMEM)
HBM = pl.BlockSpec(memory_space=pltpu.HBM)
ANY = pl.BlockSpec(memory_space=pl.ANY)


def lane_gather(table, index):
    length = table.shape[1]
    lane = index & (LANES - 1)
    chunk = index // LANES
    found = jnp.zeros(index.shape, table.dtype)
    for piece_id in range(-(-length // LANES)):
        piece = table[:, piece_id * LANES : min(length, (piece_id + 1) * LANES)]
        missing = LANES - piece.shape[1]
        if missing:
            piece = jnp.concatenate([piece, jnp.zeros((1, missing), table.dtype)], axis=1)
        picked = jnp.take_along_axis(jnp.broadcast_to(piece, index.shape), lane, axis=1)
        found = jnp.where(chunk == piece_id, picked, found)
    return found


def split_three(value):
    high = value.astype(jnp.bfloat16).astype(jnp.float32)
    rest = value - high
    middle = rest.astype(jnp.bfloat16).astype(jnp.float32)
    return [high, middle, rest - middle]


def coeffs_kernel(
    slip_hbm, basis_hbm, pairs_hbm, count_ref, pay_hbm, slip_ref, basis_ref, pairs_ref, sent_ref, sems, out_sems
):
    clusters = slip_hbm.shape[0]
    rhs_count = slip_ref.shape[0]
    rank_size = basis_ref.shape[0]
    mine = lax.axis_index("row") % clusters
    copies = [
        pltpu.make_async_copy(slip_hbm.at[mine], slip_ref, sems.at[0]),
        pltpu.make_async_copy(basis_hbm.at[mine], basis_ref, sems.at[1]),
        pltpu.make_async_copy(pairs_hbm, pairs_ref, sems.at[2]),
    ]
    for copy in copies:
        copy.start()
    half = rhs_count // 2
    copies[2].wait()
    first = pairs_ref[0:1, :]
    kind = (first - lax.axis_index("long") * clusters) * (NEARC + 1) + pairs_ref[1:2, :] - first
    kinds = lax.broadcasted_iota(jnp.int32, (half, kind.shape[1]), 0)
    live = lax.broadcasted_iota(jnp.int32, kinds.shape, 1) < count_ref[0]
    low = jnp.sum(jnp.where(live & (kinds == kind), 1.0, 0.0), axis=1, keepdims=True)
    high = jnp.sum(jnp.where(live & (kinds + half == kind), 1.0, 0.0), axis=1, keepdims=True)
    copies[0].wait()
    copies[1].wait()
    coeffs = lax.dot_general(
        slip_ref[...].astype(jnp.bfloat16),
        basis_ref[...],
        (((1,), (1,)), ((), ())),
        preferred_element_type=jnp.float32,
    )
    counts = [jnp.broadcast_to(value, (half, rank_size)) for value in (low, high)]
    pay = jnp.concatenate([coeffs[0:half], coeffs[half:]] + counts, axis=1).astype(jnp.bfloat16)
    for target in range(sent_ref.shape[0]):
        sent_ref[target] = pay
    parts = pay_hbm.shape[0] // sent_ref.shape[0]
    sends = [
        pltpu.make_async_copy(
            sent_ref, pay_hbm.at[pl.ds(part * sent_ref.shape[0], sent_ref.shape[0])], out_sems.at[part]
        )
        for part in range(parts)
    ]
    for send in sends:
        send.start()
    for send in sends:
        send.wait()


def geometry_kernel(
    slip_ref, vertices_ref, triangles_ref, map_ref, after_ref, xs_ref, halo_ref, geom_ref
):
    clusters, rhs_count, unknowns = slip_ref.shape
    xs_ref[...] = slip_ref[...].astype(jnp.bfloat16)
    long_index = lax.axis_index("long")

    size = map_ref.shape[1]
    half = size // LANES
    slot_map = map_ref[...]
    index = jnp.concatenate(
        [slot_map[:, part * LANES : (part + 1) * LANES] for part in range(half)], axis=0
    )
    vertex_base = long_index * vertices_ref.shape[1]
    corners = []
    for corner_id in range(3):
        vertex = lane_gather(triangles_ref[corner_id : corner_id + 1, :], index) - vertex_base
        corners.append(
            [lane_gather(vertices_ref[axis_id : axis_id + 1, :], vertex) for axis_id in range(3)]
        )
    one, two, three = corners
    centre = [(one[a] + two[a] + three[a]) / 3.0 for a in range(3)]
    edge_one = [two[a] - one[a] for a in range(3)]
    edge_two = [three[a] - one[a] for a in range(3)]
    normal = [
        edge_one[1] * edge_two[2] - edge_one[2] * edge_two[1],
        edge_one[2] * edge_two[0] - edge_one[0] * edge_two[2],
        edge_one[0] * edge_two[1] - edge_one[1] * edge_two[0],
    ]
    area = 0.5 * jnp.sqrt(normal[0] * normal[0] + normal[1] * normal[1] + normal[2] * normal[2])
    geometry = []
    for value in centre + [area]:
        geometry.append(
            jnp.concatenate(
                [value[part * clusters : (part + 1) * clusters] for part in range(half)], axis=1
            )
        )
    for cluster in range(clusters):
        geom_ref[cluster] = jnp.concatenate(
            [whole[cluster : cluster + 1, :] for whole in geometry], axis=0
        )

    upward = lax.axis_index("row") % 2 == 0
    start = jnp.where(upward, clusters - NEARC, 0)
    pieces = [piece for whole in geometry for piece in split_three(whole)]
    for turn in range(NEARC):
        last = clusters - NEARC + turn
        rows = [
            jnp.where(upward, piece[last : last + 1, :], piece[turn : turn + 1, :])
            for piece in pieces
        ]
        rows.append(jnp.zeros((rhs_count - len(rows), size), jnp.float32))
        halo_ref[turn, :, 0:unknowns] = xs_ref[start + turn]
        halo_ref[turn, :, unknowns : unknowns + size] = jnp.concatenate(rows, axis=0).astype(
            jnp.bfloat16
        )


def window_kernel(xs_ref, geom_ref, halo_ref, slip_ref, place_ref):
    clusters, rhs_count, unknowns = xs_ref.shape
    size = geom_ref.shape[2]
    slots = clusters + NEARC
    odd = lax.axis_index("row") % 2

    def place_of(cluster):
        return (cluster + NEARC * (1 - odd) + slots) % slots

    for cluster in range(clusters):
        slip_ref[place_of(cluster)] = xs_ref[cluster]
        place_ref[place_of(cluster)] = geom_ref[cluster]
    for turn in range(NEARC):
        at = place_of(clusters + turn)
        slip_ref[at] = halo_ref[turn, :, 0:unknowns]
        pieces = halo_ref[turn, :, unknowns : unknowns + size].astype(jnp.float32)
        place_ref[at] = jnp.concatenate(
            [
                (pieces[3 * p + 2 : 3 * p + 3] + pieces[3 * p + 1 : 3 * p + 2])
                + pieces[3 * p : 3 * p + 1]
                for p in range(4)
            ],
            axis=0,
        )


def near_kernel(
    slip_ref, place_ref, pay_ref, after_ref, out_ref, cols_ref, even_ref, odd_ref, *, long_count, clusters
):
    slots, rhs_count, unknowns = slip_ref.shape
    size = place_ref.shape[2]
    long_index = lax.axis_index("long")
    before = jnp.maximum(long_index - 1, 0)
    totals = [jnp.zeros(pay_ref.shape[1:], jnp.float32) for _ in range(2)]
    for row in range(pay_ref.shape[0] // long_count):
        for source, owner in enumerate((long_index, before)):
            totals[source] += pay_ref[row * long_count + owner].astype(jnp.float32)
    even = lax.axis_index("row") % 2 == 0
    half = pay_ref.shape[1]
    rank_size = pay_ref.shape[2] // 4
    group = lax.broadcasted_iota(jnp.int32, (half, LANES), 1) // rank_size
    kinds = lax.broadcasted_iota(jnp.int32, (half, LANES), 0) + jnp.where(group == 3, half, 0)
    kinds = jnp.where(group < 2, -1, kinds)
    lane_id = lax.broadcasted_iota(jnp.int32, (half, LANES), 1)
    kinds = jnp.where(lane_id % rank_size == 0, kinds, -1)

    def count_of(place, u):
        both = []
        for cluster in (u, clusters - NEARC + u):
            reach = place - u - NEARC
            lower = cluster + jnp.minimum(reach, 0)
            inside = lower >= 0
            kind = jnp.where(inside, lower, lower + clusters) * (NEARC + 1) + jnp.abs(reach)
            source = jnp.where(inside, totals[0], totals[1])
            both.append(jnp.where(kinds == kind, source, 0.0))
        picked = jnp.sum(jnp.where(even, both[0], both[1]), axis=0, keepdims=True)
        return jnp.sum(picked, axis=1, keepdims=True)

    out_ref[...] = jnp.zeros(out_ref.shape, jnp.float32)
    for place in range(slots):
        rows = jnp.concatenate([place_ref[place], jnp.zeros((4, size), jnp.float32)], axis=0)
        cols_ref[place] = rows.T
    right = [[place_ref[NEARC + u, p : p + 1, :] for p in range(4)] for u in range(NEARC)]
    parts = [(0, 0), (1, 1), (2, 2), (0, 1), (0, 2), (1, 2)]

    def fill(place, targets, block_ref):
        for step in range(size // ROWS):
            here = pl.ds(step * ROWS, ROWS)
            column = cols_ref[place, here, :]
            left = [jnp.broadcast_to(column[:, p : p + 1], (ROWS, size)) for p in range(4)]
            for u in targets:
                offset = [left[p] - right[u][p] for p in range(3)]
                radius_sq = offset[0] * offset[0] + offset[1] * offset[1] + offset[2] * offset[2]
                inverse = lax.rsqrt(radius_sq + soften)
                flat = (left[3] * right[u][3]) * inverse
                cubed = flat * (inverse * inverse)
                scaled = [offset[p] * cubed for p in range(3)]
                for part_id, (i, j) in enumerate(parts):
                    term = offset[i] * scaled[j]
                    if i == j:
                        term = term + flat
                    block_ref[u, part_id, here, :] = term.astype(jnp.bfloat16)

    def apply(place, targets, block_ref):
        slip = slip_ref[place]
        pieces = [slip[:, p * size : (p + 1) * size] for p in range(3)]
        for u in targets:
            count = count_of(place, u)
            sums = [
                jnp.dot(pieces[p], block_ref[u, p], preferred_element_type=jnp.float32)
                for p in range(3)
            ]
            for part_id in range(3, 6):
                i, j = parts[part_id]
                both = jnp.dot(
                    jnp.concatenate([pieces[j], pieces[i]], axis=0),
                    block_ref[u, part_id],
                    preferred_element_type=jnp.float32,
                )
                sums[i] = sums[i] + both[0:rhs_count]
                sums[j] = sums[j] + both[rhs_count : 2 * rhs_count]
            for p in range(3):
                out_ref[u, :, p * size : (p + 1) * size] += count * sums[p]

    every = list(range(NEARC))
    fill(0, [0], even_ref)
    for u in range(1, NEARC):
        even_ref[u] = jnp.zeros(even_ref.shape[1:], jnp.bfloat16)

    def two_places(turn, carry):
        place = 2 * turn
        fill(place + 1, every, odd_ref)
        apply(place, every, even_ref)
        fill(place + 2, every, even_ref)
        apply(place + 1, every, odd_ref)
        return carry

    lax.fori_loop(0, (slots - 2) // 2, two_places, 0)
    fill(slots - 1, [NEARC - 1], odd_ref)
    apply(slots - 2, every, even_ref)
    apply(slots - 1, [NEARC - 1], odd_ref)


def coupling_kernel(
    coupling_ref, pairs_ref, after_ref, to_second_ref, to_first_ref, list_ref, *, clusters, long_count
):
    owner, group = pairs_ref[...] // clusters, pairs_ref[...] % clusters
    list_ref[...] = jnp.concatenate([group * long_count + owner, owner, group], axis=0)
    pair_count, rank_size, _ = coupling_ref.shape
    groups = LANES // rank_size
    for pair_id in range(pair_count):
        here = pl.ds(pair_id * rank_size, rank_size)
        coupling = coupling_ref[pair_id].astype(jnp.float32)
        for out_ref, value in ((to_second_ref, coupling), (to_first_ref, coupling.T)):
            out_ref[here, :] = jnp.concatenate([value] * groups, axis=1).astype(jnp.bfloat16)


def far_kernel(
    list_ref, coeff_ref, to_second_ref, to_first_ref, out_hbm, done_ref, pairs_ref, moved_ref, sent_ref, sems,
    *total_refs, clusters
):
    fetch = pltpu.make_async_copy(list_ref, pairs_ref, sems.at[0])
    fetch.start()
    done_ref[...] = jnp.zeros(done_ref.shape, jnp.float32)
    long_count, rhs_count, _ = total_refs[0].shape
    pair_count = pairs_ref.shape[1]
    rank_size = LANES // clusters
    group_id = lax.broadcasted_iota(jnp.int32, (rhs_count, LANES), 1) // rank_size
    for total_ref in total_refs:
        total_ref[...] = jnp.zeros(total_ref.shape, jnp.float32)
    for at in range(coeff_ref.shape[0]):
        whole = coeff_ref[at].astype(jnp.float32)
        moved_ref[at] = jnp.concatenate([whole, pltpu.roll(whole, LANES - rank_size, 1)], axis=0)
    fetch.wait()

    def coeff_of(at, group):
        whole = moved_ref[at]
        both = pltpu.roll(whole, rank_size * group, 1) if group else whole
        return jnp.where(group_id == group, both, 0.0)

    results = []
    for begin in range(0, pair_count, clusters):
        pair_ids = range(begin, min(begin + clusters, pair_count))
        depth = len(pair_ids) * rank_size
        here = pl.ds(begin * rank_size, depth)
        for source, target, matrix_ref in ((0, 1, to_second_ref), (1, 0, to_first_ref)):
            coeffs = jnp.concatenate(
                [coeff_of(pairs_ref[source, f], f - begin) for f in pair_ids], axis=0
            ).astype(jnp.bfloat16)
            value = jnp.dot(
                coeffs[:, 0:depth], matrix_ref[here, :], preferred_element_type=jnp.float32
            )
            for turn, f in enumerate(pair_ids):
                results.append(
                    (target, f, value[turn * rhs_count : (turn + 1) * rhs_count])
                )
    for turn, (target, f, value) in enumerate(results):
        total_ref = total_refs[turn % len(total_refs)]
        owner, group = pairs_ref[2 + target, f], pairs_ref[4 + target, f]
        total_ref[owner] += jnp.where(group_id == group, value, 0.0)
    total = total_refs[0][...]
    for total_ref in total_refs[1:]:
        total = total + total_ref[...]
    sent_ref[...] = total.astype(jnp.bfloat16)
    copies = [
        pltpu.make_async_copy(
            sent_ref, out_hbm.at[pl.ds(copy_id * long_count, long_count)], sems.at[copy_id]
        )
        for copy_id in range(out_hbm.shape[0] // long_count)
    ]
    for copy in copies:
        copy.start()
    for copy in copies:
        copy.wait()


def gather_near_kernel(own_ref, other_ref, out_ref):
    even = lax.axis_index("row") % 2 == 0
    for cluster in range(out_ref.shape[0]):
        u = cluster % NEARC
        here = even if cluster < NEARC else jnp.logical_not(even)
        out_ref[cluster] = jnp.where(here, own_ref[u], other_ref[u])


def finish_kernel(near_ref, far_ref, basis_ref, out_hbm, sent_ref, sems):
    clusters, rank_size, unknowns = basis_ref.shape
    rhs_count = near_ref.shape[1]
    total = jnp.sum(far_ref[...].astype(jnp.float32), axis=0)
    group_id = lax.broadcasted_iota(jnp.int32, total.shape, 1) // rank_size
    flat_basis = basis_ref[...].reshape(clusters * rank_size, unknowns)
    picked = [jnp.where(group_id == cluster, total, 0.0) for cluster in range(clusters)]
    result = jnp.dot(
        jnp.concatenate(picked, axis=0).astype(jnp.bfloat16),
        flat_basis,
        preferred_element_type=jnp.float32,
    )
    copies = []
    for cluster in range(clusters):
        far = result[cluster * rhs_count : (cluster + 1) * rhs_count]
        sent_ref[cluster] = far + near_ref[cluster]
        copies.append(
            pltpu.make_async_copy(sent_ref.at[cluster], out_hbm.at[cluster], sems.at[cluster])
        )
        copies[-1].start()
    for copy in copies:
        copy.wait()


def shards(slip, vertices, triangles, elem_map, near_pairs, near_count, far_pairs, far_coef, basis):
    clusters, rhs_count, unknowns = slip.shape
    rank_size = basis.shape[1]
    size = elem_map.shape[1]
    row_count = lax.axis_size("row")
    long_count = lax.axis_size("long")
    devices = row_count * long_count
    coupling = far_coef.reshape(-1, rank_size, rank_size)
    slots = clusters + NEARC

    pay = pl.pallas_call(
        coeffs_kernel,
        out_shape=jax.ShapeDtypeStruct((devices, rhs_count // 2, LANES), jnp.bfloat16),
        in_specs=[HBM] * 3 + [SMEM],
        out_specs=HBM,
        scratch_shapes=[
            pltpu.VMEM(slip.shape[1:], slip.dtype),
            pltpu.VMEM(basis.shape[1:], basis.dtype),
            pltpu.VMEM(near_pairs.shape, near_pairs.dtype),
            pltpu.VMEM((long_count, rhs_count // 2, LANES), jnp.bfloat16),
            pltpu.SemaphoreType.DMA((3,)),
            pltpu.SemaphoreType.DMA((row_count,)),
        ],
        compiler_params=pltpu.CompilerParams(vmem_limit_bytes=16 << 20),
        name="coeffs",
    )(
        *[
            pltpu.with_memory_space_constraint(array, pltpu.HBM)
            for array in (slip, basis, near_pairs)
        ],
        near_count,
    )
    everyone = lax.all_to_all(pay, ("row", "long"), 0, 0, tiled=True)

    xs, to_neighbour, geometry = pl.pallas_call(
        geometry_kernel,
        out_shape=[
            jax.ShapeDtypeStruct(slip.shape, jnp.bfloat16),
            jax.ShapeDtypeStruct((NEARC, rhs_count, unknowns + size), jnp.bfloat16),
            jax.ShapeDtypeStruct((clusters, 4, size), jnp.float32),
        ],
        in_specs=[VMEM] * 4 + [ANY],
        out_specs=[VMEM] * 3,
        compiler_params=pltpu.CompilerParams(vmem_limit_bytes=16 << 20),
        cost_estimate=pl.CostEstimate(
            flops=2_000_000, bytes_accessed=1_000_000, transcendentals=1_000
        ),
        name="geometry",
    )(slip, vertices, triangles, elem_map, pay)
    route = []
    for row in range(row_count):
        step = 1 if row % 2 == 0 else -1
        for owner in range(long_count):
            if 0 <= owner - step < long_count:
                route.append((row * long_count + owner - step, row * long_count + owner))
    halo = lax.ppermute(to_neighbour, ("row", "long"), route)

    window, places = pl.pallas_call(
        window_kernel,
        out_shape=[
            jax.ShapeDtypeStruct((slots, rhs_count, unknowns), jnp.bfloat16),
            jax.ShapeDtypeStruct((slots, 4, size), jnp.float32),
        ],
        in_specs=[VMEM] * 3,
        out_specs=[VMEM] * 2,
        compiler_params=pltpu.CompilerParams(vmem_limit_bytes=16 << 20),
        cost_estimate=pl.CostEstimate(flops=1000, bytes_accessed=1000, transcendentals=0),
        name="window",
    )(xs, geometry, halo)

    to_second, to_first, pair_list = pl.pallas_call(
        functools.partial(coupling_kernel, clusters=clusters, long_count=long_count),
        out_shape=[jax.ShapeDtypeStruct((coupling.shape[0] * rank_size, LANES), jnp.bfloat16)] * 2
        + [jax.ShapeDtypeStruct((6,) + far_pairs.shape[1:], far_pairs.dtype)],
        in_specs=[VMEM, VMEM, ANY],
        out_specs=[VMEM] * 3,
        compiler_params=pltpu.CompilerParams(vmem_limit_bytes=16 << 20),
        cost_estimate=pl.CostEstimate(flops=1000, bytes_accessed=1000, transcendentals=0),
        name="coupling",
    )(coupling, far_pairs, pay)
    far, far_done = pl.pallas_call(
        functools.partial(far_kernel, clusters=clusters),
        out_shape=[
            jax.ShapeDtypeStruct((devices, rhs_count, clusters * rank_size), jnp.bfloat16),
            jax.ShapeDtypeStruct((8, LANES), jnp.float32),
        ],
        in_specs=[VMEM] * 4,
        out_specs=[HBM, VMEM],
        scratch_shapes=[
            pltpu.SMEM((6,) + far_pairs.shape[1:], far_pairs.dtype),
            pltpu.VMEM((devices, rhs_count, LANES), jnp.float32),
            pltpu.VMEM((long_count, rhs_count, clusters * rank_size), jnp.bfloat16),
            pltpu.SemaphoreType.DMA((row_count,)),
        ]
        + [pltpu.VMEM((long_count, rhs_count, clusters * rank_size), jnp.float32)] * 4,
        compiler_params=pltpu.CompilerParams(vmem_limit_bytes=16 << 20),
        name="far",
    )(pair_list, everyone, to_second, to_first)
    far_terms = lax.all_to_all(far, ("row", "long"), 0, 0, tiled=True)

    near = pl.pallas_call(
        functools.partial(near_kernel, long_count=long_count, clusters=clusters),
        out_shape=jax.ShapeDtypeStruct((NEARC, rhs_count, unknowns), jnp.float32),
        in_specs=[VMEM] * 3 + [ANY],
        out_specs=VMEM,
        scratch_shapes=[
            pltpu.VMEM((slots, size, 8), jnp.float32),
            pltpu.VMEM((NEARC, 6, size, size), jnp.bfloat16),
            pltpu.VMEM((NEARC, 6, size, size), jnp.bfloat16),
        ],
        compiler_params=pltpu.CompilerParams(vmem_limit_bytes=24 << 20),
        cost_estimate=pl.CostEstimate(
            flops=1_000_000_000, bytes_accessed=1_000_000, transcendentals=660_000
        ),
        name="near",
    )(window, places, everyone, far_done)
    partner = [(row, row ^ 1) for row in range(row_count)]
    other = lax.ppermute(near, "row", partner)

    near_field = pl.pallas_call(
        gather_near_kernel,
        out_shape=jax.ShapeDtypeStruct(slip.shape, jnp.float32),
        in_specs=[VMEM] * 2,
        out_specs=VMEM,
        compiler_params=pltpu.CompilerParams(vmem_limit_bytes=16 << 20),
        cost_estimate=pl.CostEstimate(flops=1000, bytes_accessed=1000, transcendentals=0),
        name="gather_near",
    )(near, other)

    return pl.pallas_call(
        finish_kernel,
        out_shape=jax.ShapeDtypeStruct(slip.shape, jnp.float32),
        in_specs=[VMEM] * 3,
        out_specs=HBM,
        scratch_shapes=[
            pltpu.VMEM(slip.shape, jnp.float32),
            pltpu.SemaphoreType.DMA((clusters,)),
        ],
        compiler_params=pltpu.CompilerParams(vmem_limit_bytes=16 << 20),
        name="finish",
    )(near_field, far_terms, basis)


def solution(mesh):
    placed = (
        P("long", None, None),
        P(None, "long"),
        P(None, "long"),
        P("long", None),
        P(None, ("row", "long")),
        P(("row", "long")),
        P(None, ("row", "long")),
        P(("row", "long"), None),
        P("long", None, None),
    )
    return jax.shard_map(
        shards, mesh=mesh, in_specs=placed, out_specs=P("long", None, None), check_vma=False
    )
```

```python
import functools

import jax
import jax.numpy as jnp
from jax import lax
from jax.experimental import pallas as pl
from jax.experimental.pallas import tpu as pltpu
from jax.sharding import PartitionSpec as P

NEARC = 2
LANES = 128
ROWS = 16

soften = 0.25

VMEM = pl.BlockSpec(memory_space=pltpu.VMEM)
SMEM = pl.BlockSpec(memory_space=pltpu.SMEM)
HBM = pl.BlockSpec(memory_space=pltpu.HBM)
ANY = pl.BlockSpec(memory_space=pl.ANY)


def lane_gather(table, index):
    length = table.shape[1]
    lane = index & (LANES - 1)
    chunk = index // LANES
    found = jnp.zeros(index.shape, table.dtype)
    for piece_id in range(-(-length // LANES)):
        piece = table[:, piece_id * LANES : min(length, (piece_id + 1) * LANES)]
        missing = LANES - piece.shape[1]
        if missing:
            piece = jnp.concatenate([piece, jnp.zeros((1, missing), table.dtype)], axis=1)
        picked = jnp.take_along_axis(jnp.broadcast_to(piece, index.shape), lane, axis=1)
        found = jnp.where(chunk == piece_id, picked, found)
    return found


def split_three(value):
    high = value.astype(jnp.bfloat16).astype(jnp.float32)
    rest = value - high
    middle = rest.astype(jnp.bfloat16).astype(jnp.float32)
    return [high, middle, rest - middle]


def coeffs_kernel(
    slip_hbm, basis_hbm, pairs_hbm, count_ref, room_ref, pay_ref, slip_ref, basis_ref, pairs_ref, sems
):
    clusters = slip_hbm.shape[0]
    rhs_count = slip_ref.shape[0]
    rank_size = basis_ref.shape[0]
    mine = lax.axis_index("row") % clusters
    copies = [
        pltpu.make_async_copy(slip_hbm.at[mine], slip_ref, sems.at[0]),
        pltpu.make_async_copy(basis_hbm.at[mine], basis_ref, sems.at[1]),
        pltpu.make_async_copy(pairs_hbm, pairs_ref, sems.at[2]),
    ]
    for copy in copies:
        copy.start()
    half = rhs_count // 2
    copies[2].wait()
    first = pairs_ref[0:1, :]
    kind = (first - lax.axis_index("long") * clusters) * (NEARC + 1) + pairs_ref[1:2, :] - first
    kinds = lax.broadcasted_iota(jnp.int32, (half, kind.shape[1]), 0)
    live = lax.broadcasted_iota(jnp.int32, kinds.shape, 1) < count_ref[0]
    low = jnp.sum(jnp.where(live & (kinds == kind), 1.0, 0.0), axis=1, keepdims=True)
    high = jnp.sum(jnp.where(live & (kinds + half == kind), 1.0, 0.0), axis=1, keepdims=True)
    copies[0].wait()
    copies[1].wait()
    coeffs = lax.dot_general(
        slip_ref[...].astype(jnp.bfloat16),
        basis_ref[...],
        (((1,), (1,)), ((), ())),
        preferred_element_type=jnp.float32,
    )
    counts = [jnp.broadcast_to(value, (half, rank_size)) for value in (low, high)]
    pay = jnp.concatenate([coeffs[0:half], coeffs[half:]] + counts, axis=1).astype(jnp.bfloat16)
    for target in range(pay_ref.shape[0]):
        pay_ref[target] = pay


def geometry_kernel(
    slip_ref, vertices_ref, triangles_ref, map_ref, after_ref, xs_ref, halo_ref, geom_ref
):
    clusters, rhs_count, unknowns = slip_ref.shape
    xs_ref[...] = slip_ref[...].astype(jnp.bfloat16)
    long_index = lax.axis_index("long")

    size = map_ref.shape[1]
    half = size // LANES
    slot_map = map_ref[...]
    index = jnp.concatenate(
        [slot_map[:, part * LANES : (part + 1) * LANES] for part in range(half)], axis=0
    )
    vertex_base = long_index * vertices_ref.shape[1]
    corners = []
    for corner_id in range(3):
        vertex = lane_gather(triangles_ref[corner_id : corner_id + 1, :], index) - vertex_base
        corners.append(
            [lane_gather(vertices_ref[axis_id : axis_id + 1, :], vertex) for axis_id in range(3)]
        )
    one, two, three = corners
    centre = [(one[a] + two[a] + three[a]) / 3.0 for a in range(3)]
    edge_one = [two[a] - one[a] for a in range(3)]
    edge_two = [three[a] - one[a] for a in range(3)]
    normal = [
        edge_one[1] * edge_two[2] - edge_one[2] * edge_two[1],
        edge_one[2] * edge_two[0] - edge_one[0] * edge_two[2],
        edge_one[0] * edge_two[1] - edge_one[1] * edge_two[0],
    ]
    area = 0.5 * jnp.sqrt(normal[0] * normal[0] + normal[1] * normal[1] + normal[2] * normal[2])
    geometry = []
    for value in centre + [area]:
        geometry.append(
            jnp.concatenate(
                [value[part * clusters : (part + 1) * clusters] for part in range(half)], axis=1
            )
        )
    for cluster in range(clusters):
        geom_ref[cluster] = jnp.concatenate(
            [whole[cluster : cluster + 1, :] for whole in geometry], axis=0
        )

    upward = lax.axis_index("row") % 2 == 0
    start = jnp.where(upward, clusters - NEARC, 0)
    pieces = [piece for whole in geometry for piece in split_three(whole)]
    for turn in range(NEARC):
        last = clusters - NEARC + turn
        rows = [
            jnp.where(upward, piece[last : last + 1, :], piece[turn : turn + 1, :])
            for piece in pieces
        ]
        rows.append(jnp.zeros((rhs_count - len(rows), size), jnp.float32))
        halo_ref[turn, :, 0:unknowns] = xs_ref[start + turn]
        halo_ref[turn, :, unknowns : unknowns + size] = jnp.concatenate(rows, axis=0).astype(
            jnp.bfloat16
        )


def window_kernel(xs_ref, geom_ref, halo_ref, slip_ref, place_ref):
    clusters, rhs_count, unknowns = xs_ref.shape
    size = geom_ref.shape[2]
    slots = clusters + NEARC
    odd = lax.axis_index("row") % 2

    def place_of(cluster):
        return (cluster + NEARC * (1 - odd) + slots) % slots

    for cluster in range(clusters):
        slip_ref[place_of(cluster)] = xs_ref[cluster]
        place_ref[place_of(cluster)] = geom_ref[cluster]
    for turn in range(NEARC):
        at = place_of(clusters + turn)
        slip_ref[at] = halo_ref[turn, :, 0:unknowns]
        pieces = halo_ref[turn, :, unknowns : unknowns + size].astype(jnp.float32)
        place_ref[at] = jnp.concatenate(
            [
                (pieces[3 * p + 2 : 3 * p + 3] + pieces[3 * p + 1 : 3 * p + 2])
                + pieces[3 * p : 3 * p + 1]
                for p in range(4)
            ],
            axis=0,
        )


def near_kernel(
    slip_ref, place_ref, pay_ref, after_ref, out_ref, cols_ref, even_ref, odd_ref, *, long_count, clusters
):
    slots, rhs_count, unknowns = slip_ref.shape
    size = place_ref.shape[2]
    long_index = lax.axis_index("long")
    before = jnp.maximum(long_index - 1, 0)
    totals = [jnp.zeros(pay_ref.shape[1:], jnp.float32) for _ in range(2)]
    for row in range(pay_ref.shape[0] // long_count):
        for source, owner in enumerate((long_index, before)):
            totals[source] += pay_ref[row * long_count + owner].astype(jnp.float32)
    even = lax.axis_index("row") % 2 == 0
    half = pay_ref.shape[1]
    rank_size = pay_ref.shape[2] // 4
    group = lax.broadcasted_iota(jnp.int32, (half, LANES), 1) // rank_size
    kinds = lax.broadcasted_iota(jnp.int32, (half, LANES), 0) + jnp.where(group == 3, half, 0)
    kinds = jnp.where(group < 2, -1, kinds)
    lane_id = lax.broadcasted_iota(jnp.int32, (half, LANES), 1)
    kinds = jnp.where(lane_id % rank_size == 0, kinds, -1)

    def count_of(place, u):
        both = []
        for cluster in (u, clusters - NEARC + u):
            reach = place - u - NEARC
            lower = cluster + jnp.minimum(reach, 0)
            inside = lower >= 0
            kind = jnp.where(inside, lower, lower + clusters) * (NEARC + 1) + jnp.abs(reach)
            source = jnp.where(inside, totals[0], totals[1])
            both.append(jnp.where(kinds == kind, source, 0.0))
        picked = jnp.sum(jnp.where(even, both[0], both[1]), axis=0, keepdims=True)
        return jnp.sum(picked, axis=1, keepdims=True)

    out_ref[...] = jnp.zeros(out_ref.shape, jnp.float32)
    for place in range(slots):
        rows = jnp.concatenate([place_ref[place], jnp.zeros((4, size), jnp.float32)], axis=0)
        cols_ref[place] = rows.T
    right = [[place_ref[NEARC + u, p : p + 1, :] for p in range(4)] for u in range(NEARC)]
    parts = [(0, 0), (1, 1), (2, 2), (0, 1), (0, 2), (1, 2)]

    def fill(place, targets, block_ref):
        for step in range(size // ROWS):
            here = pl.ds(step * ROWS, ROWS)
            column = cols_ref[place, here, :]
            left = [jnp.broadcast_to(column[:, p : p + 1], (ROWS, size)) for p in range(4)]
            for u in targets:
                offset = [left[p] - right[u][p] for p in range(3)]
                radius_sq = offset[0] * offset[0] + offset[1] * offset[1] + offset[2] * offset[2]
                inverse = lax.rsqrt(radius_sq + soften)
                flat = (left[3] * right[u][3]) * inverse
                cubed = flat * (inverse * inverse)
                scaled = [offset[p] * cubed for p in range(3)]
                for part_id, (i, j) in enumerate(parts):
                    term = offset[i] * scaled[j]
                    if i == j:
                        term = term + flat
                    block_ref[u, part_id, here, :] = term.astype(jnp.bfloat16)

    def apply(place, targets, block_ref):
        slip = slip_ref[place]
        pieces = [slip[:, p * size : (p + 1) * size] for p in range(3)]
        for u in targets:
            count = count_of(place, u)
            sums = [
                jnp.dot(pieces[p], block_ref[u, p], preferred_element_type=jnp.float32)
                for p in range(3)
            ]
            for part_id in range(3, 6):
                i, j = parts[part_id]
                both = jnp.dot(
                    jnp.concatenate([pieces[j], pieces[i]], axis=0),
                    block_ref[u, part_id],
                    preferred_element_type=jnp.float32,
                )
                sums[i] = sums[i] + both[0:rhs_count]
                sums[j] = sums[j] + both[rhs_count : 2 * rhs_count]
            for p in range(3):
                out_ref[u, :, p * size : (p + 1) * size] += count * sums[p]

    every = list(range(NEARC))
    fill(0, [0], even_ref)
    for u in range(1, NEARC):
        even_ref[u] = jnp.zeros(even_ref.shape[1:], jnp.bfloat16)

    def two_places(turn, carry):
        place = 2 * turn
        fill(place + 1, every, odd_ref)
        apply(place, every, even_ref)
        fill(place + 2, every, even_ref)
        apply(place + 1, every, odd_ref)
        return carry

    lax.fori_loop(0, (slots - 2) // 2, two_places, 0)
    fill(slots - 1, [NEARC - 1], odd_ref)
    apply(slots - 2, every, even_ref)
    apply(slots - 1, [NEARC - 1], odd_ref)


def coupling_kernel(
    coupling_ref, pairs_ref, after_ref, to_second_ref, to_first_ref, list_ref, room_ref, *, clusters, long_count
):
    room_ref[...] = jnp.zeros(room_ref.shape, room_ref.dtype)
    owner, group = pairs_ref[...] // clusters, pairs_ref[...] % clusters
    list_ref[...] = jnp.concatenate([group * long_count + owner, owner, group], axis=0)
    pair_count, rank_size, _ = coupling_ref.shape
    groups = LANES // rank_size
    for pair_id in range(pair_count):
        here = pl.ds(pair_id * rank_size, rank_size)
        coupling = coupling_ref[pair_id].astype(jnp.float32)
        for out_ref, value in ((to_second_ref, coupling), (to_first_ref, coupling.T)):
            out_ref[here, :] = jnp.concatenate([value] * groups, axis=1).astype(jnp.bfloat16)


def far_kernel(
    list_ref, coeff_ref, to_second_ref, to_first_ref, room_ref, out_ref, done_ref, pairs_ref, moved_ref, sems,
    *total_refs, clusters
):
    fetch = pltpu.make_async_copy(list_ref, pairs_ref, sems.at[0])
    fetch.start()
    done_ref[...] = jnp.zeros(done_ref.shape, jnp.float32)
    long_count, rhs_count, _ = total_refs[0].shape
    pair_count = pairs_ref.shape[1]
    rank_size = LANES // clusters
    group_id = lax.broadcasted_iota(jnp.int32, (rhs_count, LANES), 1) // rank_size
    for total_ref in total_refs:
        total_ref[...] = jnp.zeros(total_ref.shape, jnp.float32)
    for at in range(coeff_ref.shape[0]):
        whole = coeff_ref[at].astype(jnp.float32)
        moved_ref[at] = jnp.concatenate([whole, pltpu.roll(whole, LANES - rank_size, 1)], axis=0)
    fetch.wait()

    def coeff_of(at, group):
        whole = moved_ref[at]
        both = pltpu.roll(whole, rank_size * group, 1) if group else whole
        return jnp.where(group_id == group, both, 0.0)

    results = []
    for begin in range(0, pair_count, clusters):
        pair_ids = range(begin, min(begin + clusters, pair_count))
        depth = len(pair_ids) * rank_size
        here = pl.ds(begin * rank_size, depth)
        for source, target, matrix_ref in ((0, 1, to_second_ref), (1, 0, to_first_ref)):
            coeffs = jnp.concatenate(
                [coeff_of(pairs_ref[source, f], f - begin) for f in pair_ids], axis=0
            ).astype(jnp.bfloat16)
            value = jnp.dot(
                coeffs[:, 0:depth], matrix_ref[here, :], preferred_element_type=jnp.float32
            )
            for turn, f in enumerate(pair_ids):
                results.append(
                    (target, f, value[turn * rhs_count : (turn + 1) * rhs_count])
                )
    for turn, (target, f, value) in enumerate(results):
        total_ref = total_refs[turn % len(total_refs)]
        owner, group = pairs_ref[2 + target, f], pairs_ref[4 + target, f]
        total_ref[owner] += jnp.where(group_id == group, value, 0.0)
    total = total_refs[0][...]
    for total_ref in total_refs[1:]:
        total = total + total_ref[...]
    sent = total.astype(jnp.bfloat16)
    for copy_id in range(out_ref.shape[0] // long_count):
        out_ref[copy_id * long_count : (copy_id + 1) * long_count] = sent


def gather_near_kernel(own_ref, other_ref, out_ref):
    even = lax.axis_index("row") % 2 == 0
    for cluster in range(out_ref.shape[0]):
        u = cluster % NEARC
        here = even if cluster < NEARC else jnp.logical_not(even)
        out_ref[cluster] = jnp.where(here, own_ref[u], other_ref[u])


def finish_kernel(near_ref, far_ref, basis_ref, out_hbm, sent_ref, sems):
    clusters, rank_size, unknowns = basis_ref.shape
    rhs_count = near_ref.shape[1]
    total = jnp.sum(far_ref[...].astype(jnp.float32), axis=0)
    group_id = lax.broadcasted_iota(jnp.int32, total.shape, 1) // rank_size
    flat_basis = basis_ref[...].reshape(clusters * rank_size, unknowns)
    picked = [jnp.where(group_id == cluster, total, 0.0) for cluster in range(clusters)]
    result = jnp.dot(
        jnp.concatenate(picked, axis=0).astype(jnp.bfloat16),
        flat_basis,
        preferred_element_type=jnp.float32,
    )
    copies = []
    for cluster in range(clusters):
        far = result[cluster * rhs_count : (cluster + 1) * rhs_count]
        sent_ref[cluster] = far + near_ref[cluster]
        copies.append(
            pltpu.make_async_copy(sent_ref.at[cluster], out_hbm.at[cluster], sems.at[cluster])
        )
        copies[-1].start()
    for copy in copies:
        copy.wait()


def shards(slip, vertices, triangles, elem_map, near_pairs, near_count, far_pairs, far_coef, basis):
    clusters, rhs_count, unknowns = slip.shape
    rank_size = basis.shape[1]
    size = elem_map.shape[1]
    row_count = lax.axis_size("row")
    long_count = lax.axis_size("long")
    devices = row_count * long_count
    coupling = far_coef.reshape(-1, rank_size, rank_size)
    slots = clusters + NEARC

    pay = pl.pallas_call(
        coeffs_kernel,
        out_shape=jax.ShapeDtypeStruct((devices, rhs_count // 2, LANES), jnp.bfloat16),
        in_specs=[HBM] * 3 + [SMEM, VMEM],
        out_specs=VMEM,
        input_output_aliases={4: 0},
        scratch_shapes=[
            pltpu.VMEM(slip.shape[1:], slip.dtype),
            pltpu.VMEM(basis.shape[1:], basis.dtype),
            pltpu.VMEM(near_pairs.shape, near_pairs.dtype),
            pltpu.SemaphoreType.DMA((3,)),
        ],
        compiler_params=pltpu.CompilerParams(vmem_limit_bytes=16 << 20),
        name="coeffs",
    )(
        *[
            pltpu.with_memory_space_constraint(array, pltpu.HBM)
            for array in (slip, basis, near_pairs)
        ],
        near_count,
        pltpu.with_memory_space_constraint(
            jnp.zeros((devices, rhs_count // 2, LANES), jnp.bfloat16), pltpu.VMEM
        ),
    )
    everyone = lax.all_to_all(pay, ("row", "long"), 0, 0, tiled=True)

    xs, to_neighbour, geometry = pl.pallas_call(
        geometry_kernel,
        out_shape=[
            jax.ShapeDtypeStruct(slip.shape, jnp.bfloat16),
            jax.ShapeDtypeStruct((NEARC, rhs_count, unknowns + size), jnp.bfloat16),
            jax.ShapeDtypeStruct((clusters, 4, size), jnp.float32),
        ],
        in_specs=[VMEM] * 4 + [ANY],
        out_specs=[VMEM] * 3,
        compiler_params=pltpu.CompilerParams(vmem_limit_bytes=16 << 20),
        cost_estimate=pl.CostEstimate(
            flops=2_000_000, bytes_accessed=1_000_000, transcendentals=1_000
        ),
        name="geometry",
    )(slip, vertices, triangles, elem_map, pay)
    route = []
    for row in range(row_count):
        step = 1 if row % 2 == 0 else -1
        for owner in range(long_count):
            if 0 <= owner - step < long_count:
                route.append((row * long_count + owner - step, row * long_count + owner))
    halo = lax.ppermute(to_neighbour, ("row", "long"), route)

    window, places = pl.pallas_call(
        window_kernel,
        out_shape=[
            jax.ShapeDtypeStruct((slots, rhs_count, unknowns), jnp.bfloat16),
            jax.ShapeDtypeStruct((slots, 4, size), jnp.float32),
        ],
        in_specs=[VMEM] * 3,
        out_specs=[VMEM] * 2,
        compiler_params=pltpu.CompilerParams(vmem_limit_bytes=16 << 20),
        cost_estimate=pl.CostEstimate(flops=1000, bytes_accessed=1000, transcendentals=0),
        name="window",
    )(xs, geometry, halo)

    to_second, to_first, pair_list, room = pl.pallas_call(
        functools.partial(coupling_kernel, clusters=clusters, long_count=long_count),
        out_shape=[jax.ShapeDtypeStruct((coupling.shape[0] * rank_size, LANES), jnp.bfloat16)] * 2
        + [
            jax.ShapeDtypeStruct((6,) + far_pairs.shape[1:], far_pairs.dtype),
            jax.ShapeDtypeStruct((devices, rhs_count, clusters * rank_size), jnp.bfloat16),
        ],
        in_specs=[VMEM, VMEM, ANY],
        out_specs=[VMEM] * 4,
        compiler_params=pltpu.CompilerParams(vmem_limit_bytes=16 << 20),
        cost_estimate=pl.CostEstimate(flops=1000, bytes_accessed=1000, transcendentals=0),
        name="coupling",
    )(coupling, far_pairs, pay)
    far, far_done = pl.pallas_call(
        functools.partial(far_kernel, clusters=clusters),
        out_shape=[
            jax.ShapeDtypeStruct((devices, rhs_count, clusters * rank_size), jnp.bfloat16),
            jax.ShapeDtypeStruct((8, LANES), jnp.float32),
        ],
        in_specs=[VMEM] * 5,
        out_specs=[VMEM] * 2,
        input_output_aliases={4: 0},
        scratch_shapes=[
            pltpu.SMEM((6,) + far_pairs.shape[1:], far_pairs.dtype),
            pltpu.VMEM((devices, rhs_count, LANES), jnp.float32),
            pltpu.SemaphoreType.DMA((1,)),
        ]
        + [pltpu.VMEM((long_count, rhs_count, clusters * rank_size), jnp.float32)] * 4,
        compiler_params=pltpu.CompilerParams(vmem_limit_bytes=16 << 20),
        name="far",
    )(pair_list, everyone, to_second, to_first, pltpu.with_memory_space_constraint(room, pltpu.VMEM))
    far_terms = lax.all_to_all(far, ("row", "long"), 0, 0, tiled=True)

    near = pl.pallas_call(
        functools.partial(near_kernel, long_count=long_count, clusters=clusters),
        out_shape=jax.ShapeDtypeStruct((NEARC, rhs_count, unknowns), jnp.float32),
        in_specs=[VMEM] * 3 + [ANY],
        out_specs=VMEM,
        scratch_shapes=[
            pltpu.VMEM((slots, size, 8), jnp.float32),
            pltpu.VMEM((NEARC, 6, size, size), jnp.bfloat16),
            pltpu.VMEM((NEARC, 6, size, size), jnp.bfloat16),
        ],
        compiler_params=pltpu.CompilerParams(vmem_limit_bytes=24 << 20),
        cost_estimate=pl.CostEstimate(
            flops=1_000_000_000, bytes_accessed=1_000_000, transcendentals=660_000
        ),
        name="near",
    )(window, places, everyone, far_done)
    partner = [(row, row ^ 1) for row in range(row_count)]
    other = lax.ppermute(near, "row", partner)

    near_field = pl.pallas_call(
        gather_near_kernel,
        out_shape=jax.ShapeDtypeStruct(slip.shape, jnp.float32),
        in_specs=[VMEM] * 2,
        out_specs=VMEM,
        compiler_params=pltpu.CompilerParams(vmem_limit_bytes=16 << 20),
        cost_estimate=pl.CostEstimate(flops=1000, bytes_accessed=1000, transcendentals=0),
        name="gather_near",
    )(near, other)

    return pl.pallas_call(
        finish_kernel,
        out_shape=jax.ShapeDtypeStruct(slip.shape, jnp.float32),
        in_specs=[VMEM] * 3,
        out_specs=HBM,
        scratch_shapes=[
            pltpu.VMEM(slip.shape, jnp.float32),
            pltpu.SemaphoreType.DMA((clusters,)),
        ],
        compiler_params=pltpu.CompilerParams(vmem_limit_bytes=16 << 20),
        name="finish",
    )(near_field, far_terms, basis)


def solution(mesh):
    placed = (
        P("long", None, None),
        P(None, "long"),
        P(None, "long"),
        P("long", None),
        P(None, ("row", "long")),
        P(("row", "long")),
        P(None, ("row", "long")),
        P(("row", "long"), None),
        P("long", None, None),
    )
    return jax.shard_map(
        shards, mesh=mesh, in_specs=placed, out_specs=P("long", None, None), check_vma=False
    )
```

```python
import functools

import jax
import jax.numpy as jnp
from jax import lax
from jax.experimental import pallas as pl
from jax.experimental.pallas import tpu as pltpu
from jax.sharding import PartitionSpec as P

NEARC = 2
LANES = 128
ROWS = 16

soften = 0.25

VMEM = pl.BlockSpec(memory_space=pltpu.VMEM)
SMEM = pl.BlockSpec(memory_space=pltpu.SMEM)
HBM = pl.BlockSpec(memory_space=pltpu.HBM)
ANY = pl.BlockSpec(memory_space=pl.ANY)


def lane_gather(table, index):
    length = table.shape[1]
    lane = index & (LANES - 1)
    chunk = index // LANES
    found = jnp.zeros(index.shape, table.dtype)
    for piece_id in range(-(-length // LANES)):
        piece = table[:, piece_id * LANES : min(length, (piece_id + 1) * LANES)]
        missing = LANES - piece.shape[1]
        if missing:
            piece = jnp.concatenate([piece, jnp.zeros((1, missing), table.dtype)], axis=1)
        picked = jnp.take_along_axis(jnp.broadcast_to(piece, index.shape), lane, axis=1)
        found = jnp.where(chunk == piece_id, picked, found)
    return found


def split_three(value):
    high = value.astype(jnp.bfloat16).astype(jnp.float32)
    rest = value - high
    middle = rest.astype(jnp.bfloat16).astype(jnp.float32)
    return [high, middle, rest - middle]


def coeffs_kernel(
    slip_hbm, basis_hbm, pairs_hbm, count_ref, pay_hbm, slip_ref, basis_ref, pairs_ref, sent_ref, sems, out_sems
):
    clusters = slip_hbm.shape[0]
    rhs_count = slip_ref.shape[0]
    rank_size = basis_ref.shape[0]
    mine = lax.axis_index("row") % clusters
    copies = [
        pltpu.make_async_copy(slip_hbm.at[mine], slip_ref, sems.at[0]),
        pltpu.make_async_copy(basis_hbm.at[mine], basis_ref, sems.at[1]),
        pltpu.make_async_copy(pairs_hbm, pairs_ref, sems.at[2]),
    ]
    for copy in copies:
        copy.start()
    half = rhs_count // 2
    copies[2].wait()
    first = pairs_ref[0:1, :]
    kind = (first - lax.axis_index("long") * clusters) * (NEARC + 1) + pairs_ref[1:2, :] - first
    kinds = lax.broadcasted_iota(jnp.int32, (half, kind.shape[1]), 0)
    live = lax.broadcasted_iota(jnp.int32, kinds.shape, 1) < count_ref[0]
    low = jnp.sum(jnp.where(live & (kinds == kind), 1.0, 0.0), axis=1, keepdims=True)
    high = jnp.sum(jnp.where(live & (kinds + half == kind), 1.0, 0.0), axis=1, keepdims=True)
    copies[0].wait()
    copies[1].wait()
    coeffs = lax.dot_general(
        slip_ref[...].astype(jnp.bfloat16),
        basis_ref[...],
        (((1,), (1,)), ((), ())),
        preferred_element_type=jnp.float32,
    )
    counts = [jnp.broadcast_to(value, (half, rank_size)) for value in (low, high)]
    pay = jnp.concatenate([coeffs[0:half], coeffs[half:]] + counts, axis=1).astype(jnp.bfloat16)
    for target in range(sent_ref.shape[0]):
        sent_ref[target] = pay
    parts = pay_hbm.shape[0] // sent_ref.shape[0]
    sends = [
        pltpu.make_async_copy(
            sent_ref, pay_hbm.at[pl.ds(part * sent_ref.shape[0], sent_ref.shape[0])], out_sems.at[part]
        )
        for part in range(parts)
    ]
    for send in sends:
        send.start()
    for send in sends:
        send.wait()


def geometry_kernel(
    slip_ref, vertices_ref, triangles_ref, map_ref, after_ref, xs_ref, halo_ref, geom_ref
):
    clusters, rhs_count, unknowns = slip_ref.shape
    xs_ref[...] = slip_ref[...].astype(jnp.bfloat16)
    long_index = lax.axis_index("long")

    size = map_ref.shape[1]
    half = size // LANES
    slot_map = map_ref[...]
    index = jnp.concatenate(
        [slot_map[:, part * LANES : (part + 1) * LANES] for part in range(half)], axis=0
    )
    vertex_base = long_index * vertices_ref.shape[1]
    corners = []
    for corner_id in range(3):
        vertex = lane_gather(triangles_ref[corner_id : corner_id + 1, :], index) - vertex_base
        corners.append(
            [lane_gather(vertices_ref[axis_id : axis_id + 1, :], vertex) for axis_id in range(3)]
        )
    one, two, three = corners
    centre = [(one[a] + two[a] + three[a]) / 3.0 for a in range(3)]
    edge_one = [two[a] - one[a] for a in range(3)]
    edge_two = [three[a] - one[a] for a in range(3)]
    normal = [
        edge_one[1] * edge_two[2] - edge_one[2] * edge_two[1],
        edge_one[2] * edge_two[0] - edge_one[0] * edge_two[2],
        edge_one[0] * edge_two[1] - edge_one[1] * edge_two[0],
    ]
    area = 0.5 * jnp.sqrt(normal[0] * normal[0] + normal[1] * normal[1] + normal[2] * normal[2])
    geometry = []
    for value in centre + [area]:
        geometry.append(
            jnp.concatenate(
                [value[part * clusters : (part + 1) * clusters] for part in range(half)], axis=1
            )
        )
    for cluster in range(clusters):
        geom_ref[cluster] = jnp.concatenate(
            [whole[cluster : cluster + 1, :] for whole in geometry], axis=0
        )

    upward = lax.axis_index("row") % 2 == 0
    start = jnp.where(upward, clusters - NEARC, 0)
    pieces = [piece for whole in geometry for piece in split_three(whole)]
    for turn in range(NEARC):
        last = clusters - NEARC + turn
        rows = [
            jnp.where(upward, piece[last : last + 1, :], piece[turn : turn + 1, :])
            for piece in pieces
        ]
        rows.append(jnp.zeros((rhs_count - len(rows), size), jnp.float32))
        halo_ref[turn, :, 0:unknowns] = xs_ref[start + turn]
        halo_ref[turn, :, unknowns : unknowns + size] = jnp.concatenate(rows, axis=0).astype(
            jnp.bfloat16
        )


def window_kernel(xs_ref, geom_ref, halo_ref, slip_ref, place_ref):
    clusters, rhs_count, unknowns = xs_ref.shape
    size = geom_ref.shape[2]
    slots = clusters + NEARC
    odd = lax.axis_index("row") % 2

    def place_of(cluster):
        return (cluster + NEARC * (1 - odd) + slots) % slots

    for cluster in range(clusters):
        slip_ref[place_of(cluster)] = xs_ref[cluster]
        place_ref[place_of(cluster)] = geom_ref[cluster]
    for turn in range(NEARC):
        at = place_of(clusters + turn)
        slip_ref[at] = halo_ref[turn, :, 0:unknowns]
        pieces = halo_ref[turn, :, unknowns : unknowns + size].astype(jnp.float32)
        place_ref[at] = jnp.concatenate(
            [
                (pieces[3 * p + 2 : 3 * p + 3] + pieces[3 * p + 1 : 3 * p + 2])
                + pieces[3 * p : 3 * p + 1]
                for p in range(4)
            ],
            axis=0,
        )


def near_kernel(
    slip_ref, place_ref, pay_ref, after_ref, out_ref, cols_ref, even_ref, odd_ref, *, long_count, clusters
):
    slots, rhs_count, unknowns = slip_ref.shape
    size = place_ref.shape[2]
    long_index = lax.axis_index("long")
    before = jnp.maximum(long_index - 1, 0)
    totals = [jnp.zeros(pay_ref.shape[1:], jnp.float32) for _ in range(2)]
    for row in range(pay_ref.shape[0] // long_count):
        for source, owner in enumerate((long_index, before)):
            totals[source] += pay_ref[row * long_count + owner].astype(jnp.float32)
    even = lax.axis_index("row") % 2 == 0
    half = pay_ref.shape[1]
    rank_size = pay_ref.shape[2] // 4
    group = lax.broadcasted_iota(jnp.int32, (half, LANES), 1) // rank_size
    kinds = lax.broadcasted_iota(jnp.int32, (half, LANES), 0) + jnp.where(group == 3, half, 0)
    kinds = jnp.where(group < 2, -1, kinds)
    lane_id = lax.broadcasted_iota(jnp.int32, (half, LANES), 1)
    kinds = jnp.where(lane_id % rank_size == 0, kinds, -1)

    def count_of(place, u):
        both = []
        for cluster in (u, clusters - NEARC + u):
            reach = place - u - NEARC
            lower = cluster + jnp.minimum(reach, 0)
            inside = lower >= 0
            kind = jnp.where(inside, lower, lower + clusters) * (NEARC + 1) + jnp.abs(reach)
            source = jnp.where(inside, totals[0], totals[1])
            both.append(jnp.where(kinds == kind, source, 0.0))
        picked = jnp.sum(jnp.where(even, both[0], both[1]), axis=0, keepdims=True)
        return jnp.sum(picked, axis=1, keepdims=True)

    out_ref[...] = jnp.zeros(out_ref.shape, jnp.float32)
    for place in range(slots):
        rows = jnp.concatenate([place_ref[place], jnp.zeros((4, size), jnp.float32)], axis=0)
        cols_ref[place] = rows.T
    right = [[place_ref[NEARC + u, p : p + 1, :] for p in range(4)] for u in range(NEARC)]
    parts = [(0, 0), (1, 1), (2, 2), (0, 1), (0, 2), (1, 2)]

    def fill(place, targets, block_ref):
        for step in range(size // ROWS):
            here = pl.ds(step * ROWS, ROWS)
            column = cols_ref[place, here, :]
            left = [jnp.broadcast_to(column[:, p : p + 1], (ROWS, size)) for p in range(4)]
            for u in targets:
                offset = [left[p] - right[u][p] for p in range(3)]
                radius_sq = offset[0] * offset[0] + offset[1] * offset[1] + offset[2] * offset[2]
                inverse = lax.rsqrt(radius_sq + soften)
                flat = (left[3] * right[u][3]) * inverse
                cubed = flat * (inverse * inverse)
                scaled = [offset[p] * cubed for p in range(3)]
                for part_id, (i, j) in enumerate(parts):
                    term = offset[i] * scaled[j]
                    if i == j:
                        term = term + flat
                    block_ref[u, part_id, here, :] = term.astype(jnp.bfloat16)

    def apply(place, targets, block_ref):
        slip = slip_ref[place]
        pieces = [slip[:, p * size : (p + 1) * size] for p in range(3)]
        for u in targets:
            count = count_of(place, u)
            sums = [
                jnp.dot(pieces[p], block_ref[u, p], preferred_element_type=jnp.float32)
                for p in range(3)
            ]
            for part_id in range(3, 6):
                i, j = parts[part_id]
                both = jnp.dot(
                    jnp.concatenate([pieces[j], pieces[i]], axis=0),
                    block_ref[u, part_id],
                    preferred_element_type=jnp.float32,
                )
                sums[i] = sums[i] + both[0:rhs_count]
                sums[j] = sums[j] + both[rhs_count : 2 * rhs_count]
            for p in range(3):
                out_ref[u, :, p * size : (p + 1) * size] += count * sums[p]

    every = list(range(NEARC))
    fill(0, [0], even_ref)
    for u in range(1, NEARC):
        even_ref[u] = jnp.zeros(even_ref.shape[1:], jnp.bfloat16)

    def two_places(turn, carry):
        place = 2 * turn
        fill(place + 1, every, odd_ref)
        apply(place, every, even_ref)
        fill(place + 2, every, even_ref)
        apply(place + 1, every, odd_ref)
        return carry

    lax.fori_loop(0, (slots - 2) // 2, two_places, 0)
    fill(slots - 1, [NEARC - 1], odd_ref)
    apply(slots - 2, every, even_ref)
    apply(slots - 1, [NEARC - 1], odd_ref)


def coupling_kernel(
    coupling_ref, pairs_ref, after_ref, to_second_ref, to_first_ref, list_ref, *, clusters, long_count
):
    owner, group = pairs_ref[...] // clusters, pairs_ref[...] % clusters
    list_ref[...] = jnp.concatenate([group * long_count + owner, owner, group], axis=0)
    pair_count, rank_size, _ = coupling_ref.shape
    groups = LANES // rank_size
    for pair_id in range(pair_count):
        here = pl.ds(pair_id * rank_size, rank_size)
        coupling = coupling_ref[pair_id].astype(jnp.float32)
        for out_ref, value in ((to_second_ref, coupling), (to_first_ref, coupling.T)):
            out_ref[here, :] = jnp.concatenate([value] * groups, axis=1).astype(jnp.bfloat16)


def far_kernel(
    list_ref, coeff_ref, to_second_ref, to_first_ref, out_hbm, done_ref, pairs_ref, moved_ref, sent_ref, sems,
    *total_refs, clusters
):
    fetch = pltpu.make_async_copy(list_ref, pairs_ref, sems.at[0])
    fetch.start()
    done_ref[...] = jnp.zeros(done_ref.shape, jnp.float32)
    long_count, rhs_count, _ = total_refs[0].shape
    pair_count = pairs_ref.shape[1]
    rank_size = LANES // clusters
    group_id = lax.broadcasted_iota(jnp.int32, (rhs_count, LANES), 1) // rank_size
    for total_ref in total_refs:
        total_ref[...] = jnp.zeros(total_ref.shape, jnp.float32)
    for at in range(coeff_ref.shape[0]):
        whole = coeff_ref[at].astype(jnp.float32)
        moved_ref[at] = jnp.concatenate([whole, pltpu.roll(whole, LANES - rank_size, 1)], axis=0)
    fetch.wait()

    def coeff_of(at, group):
        whole = moved_ref[at]
        both = pltpu.roll(whole, rank_size * group, 1) if group else whole
        return jnp.where(group_id == group, both, 0.0)

    results = []
    for begin in range(0, pair_count, clusters):
        pair_ids = range(begin, min(begin + clusters, pair_count))
        depth = len(pair_ids) * rank_size
        here = pl.ds(begin * rank_size, depth)
        for source, target, matrix_ref in ((0, 1, to_second_ref), (1, 0, to_first_ref)):
            coeffs = jnp.concatenate(
                [coeff_of(pairs_ref[source, f], f - begin) for f in pair_ids], axis=0
            ).astype(jnp.bfloat16)
            value = jnp.dot(
                coeffs[:, 0:depth], matrix_ref[here, :], preferred_element_type=jnp.float32
            )
            for turn, f in enumerate(pair_ids):
                results.append(
                    (target, f, value[turn * rhs_count : (turn + 1) * rhs_count])
                )
    for turn, (target, f, value) in enumerate(results):
        total_ref = total_refs[turn % len(total_refs)]
        owner, group = pairs_ref[2 + target, f], pairs_ref[4 + target, f]
        total_ref[owner] += jnp.where(group_id == group, value, 0.0)
    total = total_refs[0][...]
    for total_ref in total_refs[1:]:
        total = total + total_ref[...]
    sent_ref[...] = total.astype(jnp.bfloat16)
    copies = [
        pltpu.make_async_copy(
            sent_ref, out_hbm.at[pl.ds(copy_id * long_count, long_count)], sems.at[copy_id]
        )
        for copy_id in range(out_hbm.shape[0] // long_count)
    ]
    for copy in copies:
        copy.start()
    for copy in copies:
        copy.wait()


def gather_near_kernel(own_ref, other_ref, out_ref):
    even = lax.axis_index("row") % 2 == 0
    for cluster in range(out_ref.shape[0]):
        u = cluster % NEARC
        here = even if cluster < NEARC else jnp.logical_not(even)
        out_ref[cluster] = jnp.where(here, own_ref[u], other_ref[u])


def finish_kernel(near_ref, far_ref, basis_ref, out_hbm, sent_ref, sems):
    clusters, rank_size, unknowns = basis_ref.shape
    rhs_count = near_ref.shape[1]
    total = jnp.sum(far_ref[...].astype(jnp.float32), axis=0)
    group_id = lax.broadcasted_iota(jnp.int32, total.shape, 1) // rank_size
    flat_basis = basis_ref[...].reshape(clusters * rank_size, unknowns)
    picked = [jnp.where(group_id == cluster, total, 0.0) for cluster in range(clusters)]
    result = jnp.dot(
        jnp.concatenate(picked, axis=0).astype(jnp.bfloat16),
        flat_basis,
        preferred_element_type=jnp.float32,
    )
    copies = []
    for cluster in range(clusters):
        far = result[cluster * rhs_count : (cluster + 1) * rhs_count]
        sent_ref[cluster] = far + near_ref[cluster]
        copies.append(
            pltpu.make_async_copy(sent_ref.at[cluster], out_hbm.at[cluster], sems.at[cluster])
        )
        copies[-1].start()
    for copy in copies:
        copy.wait()


def shards(slip, vertices, triangles, elem_map, near_pairs, near_count, far_pairs, far_coef, basis):
    clusters, rhs_count, unknowns = slip.shape
    rank_size = basis.shape[1]
    size = elem_map.shape[1]
    row_count = lax.axis_size("row")
    long_count = lax.axis_size("long")
    devices = row_count * long_count
    coupling = far_coef.reshape(-1, rank_size, rank_size)
    slots = clusters + NEARC

    pay = pl.pallas_call(
        coeffs_kernel,
        out_shape=jax.ShapeDtypeStruct((devices, rhs_count // 2, LANES), jnp.bfloat16),
        in_specs=[HBM] * 3 + [SMEM],
        out_specs=HBM,
        scratch_shapes=[
            pltpu.VMEM(slip.shape[1:], slip.dtype),
            pltpu.VMEM(basis.shape[1:], basis.dtype),
            pltpu.VMEM(near_pairs.shape, near_pairs.dtype),
            pltpu.VMEM((long_count, rhs_count // 2, LANES), jnp.bfloat16),
            pltpu.SemaphoreType.DMA((3,)),
            pltpu.SemaphoreType.DMA((row_count,)),
        ],
        compiler_params=pltpu.CompilerParams(vmem_limit_bytes=16 << 20),
        name="coeffs",
    )(
        *[
            pltpu.with_memory_space_constraint(array, pltpu.HBM)
            for array in (slip, basis, near_pairs)
        ],
        near_count,
    )
    everyone = lax.all_to_all(pay, ("row", "long"), 0, 0, tiled=True)

    xs, to_neighbour, geometry = pl.pallas_call(
        geometry_kernel,
        out_shape=[
            jax.ShapeDtypeStruct(slip.shape, jnp.bfloat16),
            jax.ShapeDtypeStruct((NEARC, rhs_count, unknowns + size), jnp.bfloat16),
            jax.ShapeDtypeStruct((clusters, 4, size), jnp.float32),
        ],
        in_specs=[VMEM] * 4 + [ANY],
        out_specs=[VMEM] * 3,
        compiler_params=pltpu.CompilerParams(vmem_limit_bytes=16 << 20),
        cost_estimate=pl.CostEstimate(
            flops=2_000_000, bytes_accessed=1_000_000, transcendentals=1_000
        ),
        name="geometry",
    )(slip, vertices, triangles, elem_map, pay)
    route = []
    for row in range(row_count):
        step = 1 if row % 2 == 0 else -1
        for owner in range(long_count):
            if 0 <= owner - step < long_count:
                route.append((row * long_count + owner - step, row * long_count + owner))
    halo = lax.ppermute(to_neighbour, ("row", "long"), route)

    window, places = pl.pallas_call(
        window_kernel,
        out_shape=[
            jax.ShapeDtypeStruct((slots, rhs_count, unknowns), jnp.bfloat16),
            jax.ShapeDtypeStruct((slots, 4, size), jnp.float32),
        ],
        in_specs=[VMEM] * 3,
        out_specs=[VMEM] * 2,
        compiler_params=pltpu.CompilerParams(vmem_limit_bytes=16 << 20),
        cost_estimate=pl.CostEstimate(flops=1000, bytes_accessed=1000, transcendentals=0),
        name="window",
    )(xs, geometry, halo)

    to_second, to_first, pair_list = pl.pallas_call(
        functools.partial(coupling_kernel, clusters=clusters, long_count=long_count),
        out_shape=[jax.ShapeDtypeStruct((coupling.shape[0] * rank_size, LANES), jnp.bfloat16)] * 2
        + [jax.ShapeDtypeStruct((6,) + far_pairs.shape[1:], far_pairs.dtype)],
        in_specs=[VMEM, VMEM, ANY],
        out_specs=[VMEM] * 3,
        compiler_params=pltpu.CompilerParams(vmem_limit_bytes=16 << 20),
        cost_estimate=pl.CostEstimate(flops=1000, bytes_accessed=1000, transcendentals=0),
        name="coupling",
    )(coupling, far_pairs, pay)
    far, far_done = pl.pallas_call(
        functools.partial(far_kernel, clusters=clusters),
        out_shape=[
            jax.ShapeDtypeStruct((devices, rhs_count, clusters * rank_size), jnp.bfloat16),
            jax.ShapeDtypeStruct((8, LANES), jnp.float32),
        ],
        in_specs=[VMEM] * 4,
        out_specs=[HBM, VMEM],
        scratch_shapes=[
            pltpu.SMEM((6,) + far_pairs.shape[1:], far_pairs.dtype),
            pltpu.VMEM((devices, rhs_count, LANES), jnp.float32),
            pltpu.VMEM((long_count, rhs_count, clusters * rank_size), jnp.bfloat16),
            pltpu.SemaphoreType.DMA((row_count,)),
        ]
        + [pltpu.VMEM((long_count, rhs_count, clusters * rank_size), jnp.float32)] * 4,
        compiler_params=pltpu.CompilerParams(vmem_limit_bytes=16 << 20),
        name="far",
    )(pair_list, everyone, to_second, to_first)
    rows = list(range(0, row_count, 2)) + list(range(1, row_count, 2))
    order = [[row * long_count + owner for row in rows for owner in range(long_count)]]
    far_terms = lax.all_to_all(far, ("row", "long"), 0, 0, axis_index_groups=order, tiled=True)

    near = pl.pallas_call(
        functools.partial(near_kernel, long_count=long_count, clusters=clusters),
        out_shape=jax.ShapeDtypeStruct((NEARC, rhs_count, unknowns), jnp.float32),
        in_specs=[VMEM] * 3 + [ANY],
        out_specs=VMEM,
        scratch_shapes=[
            pltpu.VMEM((slots, size, 8), jnp.float32),
            pltpu.VMEM((NEARC, 6, size, size), jnp.bfloat16),
            pltpu.VMEM((NEARC, 6, size, size), jnp.bfloat16),
        ],
        compiler_params=pltpu.CompilerParams(vmem_limit_bytes=24 << 20),
        cost_estimate=pl.CostEstimate(
            flops=1_000_000_000, bytes_accessed=1_000_000, transcendentals=660_000
        ),
        name="near",
    )(window, places, everyone, far_done)
    partner = [(row, row ^ 1) for row in range(row_count)]
    other = lax.ppermute(near, "row", partner)

    near_field = pl.pallas_call(
        gather_near_kernel,
        out_shape=jax.ShapeDtypeStruct(slip.shape, jnp.float32),
        in_specs=[VMEM] * 2,
        out_specs=VMEM,
        compiler_params=pltpu.CompilerParams(vmem_limit_bytes=16 << 20),
        cost_estimate=pl.CostEstimate(flops=1000, bytes_accessed=1000, transcendentals=0),
        name="gather_near",
    )(near, other)

    return pl.pallas_call(
        finish_kernel,
        out_shape=jax.ShapeDtypeStruct(slip.shape, jnp.float32),
        in_specs=[VMEM] * 3,
        out_specs=HBM,
        scratch_shapes=[
            pltpu.VMEM(slip.shape, jnp.float32),
            pltpu.SemaphoreType.DMA((clusters,)),
        ],
        compiler_params=pltpu.CompilerParams(vmem_limit_bytes=16 << 20),
        name="finish",
    )(near_field, far_terms, basis)


def solution(mesh):
    placed = (
        P("long", None, None),
        P(None, "long"),
        P(None, "long"),
        P("long", None),
        P(None, ("row", "long")),
        P(("row", "long")),
        P(None, ("row", "long")),
        P(("row", "long"), None),
        P("long", None, None),
    )
    return jax.shard_map(
        shards, mesh=mesh, in_specs=placed, out_specs=P("long", None, None), check_vma=False
    )
```

```python
import functools

import jax
import jax.numpy as jnp
from jax import lax
from jax.experimental import pallas as pl
from jax.experimental.pallas import tpu as pltpu
from jax.sharding import PartitionSpec as P

NEARC = 2
LANES = 128
ROWS = 16

soften = 0.25

VMEM = pl.BlockSpec(memory_space=pltpu.VMEM)
SMEM = pl.BlockSpec(memory_space=pltpu.SMEM)
HBM = pl.BlockSpec(memory_space=pltpu.HBM)
ANY = pl.BlockSpec(memory_space=pl.ANY)


def lane_gather(table, index):
    length = table.shape[1]
    lane = index & (LANES - 1)
    chunk = index // LANES
    found = jnp.zeros(index.shape, table.dtype)
    for piece_id in range(-(-length // LANES)):
        piece = table[:, piece_id * LANES : min(length, (piece_id + 1) * LANES)]
        missing = LANES - piece.shape[1]
        if missing:
            piece = jnp.concatenate([piece, jnp.zeros((1, missing), table.dtype)], axis=1)
        picked = jnp.take_along_axis(jnp.broadcast_to(piece, index.shape), lane, axis=1)
        found = jnp.where(chunk == piece_id, picked, found)
    return found


def split_three(value):
    high = value.astype(jnp.bfloat16).astype(jnp.float32)
    rest = value - high
    middle = rest.astype(jnp.bfloat16).astype(jnp.float32)
    return [high, middle, rest - middle]


def coeffs_kernel(
    slip_hbm, basis_hbm, pairs_hbm, count_ref, pay_hbm, slip_ref, basis_ref, pairs_ref, sent_ref, sems, out_sems
):
    clusters = slip_hbm.shape[0]
    rhs_count = slip_ref.shape[0]
    rank_size = basis_ref.shape[0]
    mine = lax.axis_index("row") % clusters
    copies = [
        pltpu.make_async_copy(slip_hbm.at[mine], slip_ref, sems.at[0]),
        pltpu.make_async_copy(basis_hbm.at[mine], basis_ref, sems.at[1]),
        pltpu.make_async_copy(pairs_hbm, pairs_ref, sems.at[2]),
    ]
    for copy in copies:
        copy.start()
    half = rhs_count // 2
    copies[2].wait()
    first = pairs_ref[0:1, :]
    kind = (first - lax.axis_index("long") * clusters) * (NEARC + 1) + pairs_ref[1:2, :] - first
    kinds = lax.broadcasted_iota(jnp.int32, (half, kind.shape[1]), 0)
    live = lax.broadcasted_iota(jnp.int32, kinds.shape, 1) < count_ref[0]
    low = jnp.sum(jnp.where(live & (kinds == kind), 1.0, 0.0), axis=1, keepdims=True)
    high = jnp.sum(jnp.where(live & (kinds + half == kind), 1.0, 0.0), axis=1, keepdims=True)
    copies[0].wait()
    copies[1].wait()
    coeffs = lax.dot_general(
        slip_ref[...].astype(jnp.bfloat16),
        basis_ref[...],
        (((1,), (1,)), ((), ())),
        preferred_element_type=jnp.float32,
    )
    counts = [jnp.broadcast_to(value, (half, rank_size)) for value in (low, high)]
    pay = jnp.concatenate([coeffs[0:half], coeffs[half:]] + counts, axis=1).astype(jnp.bfloat16)
    for target in range(sent_ref.shape[0]):
        sent_ref[target] = pay
    parts = pay_hbm.shape[0] // sent_ref.shape[0]
    sends = [
        pltpu.make_async_copy(
            sent_ref, pay_hbm.at[pl.ds(part * sent_ref.shape[0], sent_ref.shape[0])], out_sems.at[part]
        )
        for part in range(parts)
    ]
    for send in sends:
        send.start()
    for send in sends:
        send.wait()


def geometry_kernel(
    slip_ref, vertices_ref, triangles_ref, map_ref, after_ref, xs_ref, halo_ref, geom_ref
):
    clusters, rhs_count, unknowns = slip_ref.shape
    xs_ref[...] = slip_ref[...].astype(jnp.bfloat16)
    long_index = lax.axis_index("long")

    size = map_ref.shape[1]
    half = size // LANES
    slot_map = map_ref[...]
    index = jnp.concatenate(
        [slot_map[:, part * LANES : (part + 1) * LANES] for part in range(half)], axis=0
    )
    vertex_base = long_index * vertices_ref.shape[1]
    corners = []
    for corner_id in range(3):
        vertex = lane_gather(triangles_ref[corner_id : corner_id + 1, :], index) - vertex_base
        corners.append(
            [lane_gather(vertices_ref[axis_id : axis_id + 1, :], vertex) for axis_id in range(3)]
        )
    one, two, three = corners
    centre = [(one[a] + two[a] + three[a]) / 3.0 for a in range(3)]
    edge_one = [two[a] - one[a] for a in range(3)]
    edge_two = [three[a] - one[a] for a in range(3)]
    normal = [
        edge_one[1] * edge_two[2] - edge_one[2] * edge_two[1],
        edge_one[2] * edge_two[0] - edge_one[0] * edge_two[2],
        edge_one[0] * edge_two[1] - edge_one[1] * edge_two[0],
    ]
    area = 0.5 * jnp.sqrt(normal[0] * normal[0] + normal[1] * normal[1] + normal[2] * normal[2])
    geometry = []
    for value in centre + [area]:
        geometry.append(
            jnp.concatenate(
                [value[part * clusters : (part + 1) * clusters] for part in range(half)], axis=1
            )
        )
    for cluster in range(clusters):
        geom_ref[cluster] = jnp.concatenate(
            [whole[cluster : cluster + 1, :] for whole in geometry], axis=0
        )

    upward = lax.axis_index("row") % 2 == 0
    start = jnp.where(upward, clusters - NEARC, 0)
    pieces = [piece for whole in geometry for piece in split_three(whole)]
    for turn in range(NEARC):
        last = clusters - NEARC + turn
        rows = [
            jnp.where(upward, piece[last : last + 1, :], piece[turn : turn + 1, :])
            for piece in pieces
        ]
        rows.append(jnp.zeros((rhs_count - len(rows), size), jnp.float32))
        halo_ref[turn, :, 0:unknowns] = xs_ref[start + turn]
        halo_ref[turn, :, unknowns : unknowns + size] = jnp.concatenate(rows, axis=0).astype(
            jnp.bfloat16
        )


def window_kernel(xs_ref, geom_ref, halo_ref, slip_ref, place_ref):
    clusters, rhs_count, unknowns = xs_ref.shape
    size = geom_ref.shape[2]
    slots = clusters + NEARC
    odd = lax.axis_index("row") % 2

    def place_of(cluster):
        return (cluster + NEARC * (1 - odd) + slots) % slots

    for cluster in range(clusters):
        slip_ref[place_of(cluster)] = xs_ref[cluster]
        place_ref[place_of(cluster)] = geom_ref[cluster]
    for turn in range(NEARC):
        at = place_of(clusters + turn)
        slip_ref[at] = halo_ref[turn, :, 0:unknowns]
        pieces = halo_ref[turn, :, unknowns : unknowns + size].astype(jnp.float32)
        place_ref[at] = jnp.concatenate(
            [
                (pieces[3 * p + 2 : 3 * p + 3] + pieces[3 * p + 1 : 3 * p + 2])
                + pieces[3 * p : 3 * p + 1]
                for p in range(4)
            ],
            axis=0,
        )


def near_kernel(
    slip_ref, place_ref, pay_ref, after_ref, out_ref, cols_ref, even_ref, odd_ref, *, long_count, clusters
):
    slots, rhs_count, unknowns = slip_ref.shape
    size = place_ref.shape[2]
    long_index = lax.axis_index("long")
    before = jnp.maximum(long_index - 1, 0)
    totals = [jnp.zeros(pay_ref.shape[1:], jnp.float32) for _ in range(2)]
    for row in range(pay_ref.shape[0] // long_count):
        for source, owner in enumerate((long_index, before)):
            totals[source] += pay_ref[row * long_count + owner].astype(jnp.float32)
    even = lax.axis_index("row") % 2 == 0
    half = pay_ref.shape[1]
    rank_size = pay_ref.shape[2] // 4
    group = lax.broadcasted_iota(jnp.int32, (half, LANES), 1) // rank_size
    kinds = lax.broadcasted_iota(jnp.int32, (half, LANES), 0) + jnp.where(group == 3, half, 0)
    kinds = jnp.where(group < 2, -1, kinds)
    lane_id = lax.broadcasted_iota(jnp.int32, (half, LANES), 1)
    kinds = jnp.where(lane_id % rank_size == 0, kinds, -1)

    def count_of(place, u):
        both = []
        for cluster in (u, clusters - NEARC + u):
            reach = place - u - NEARC
            lower = cluster + jnp.minimum(reach, 0)
            inside = lower >= 0
            kind = jnp.where(inside, lower, lower + clusters) * (NEARC + 1) + jnp.abs(reach)
            source = jnp.where(inside, totals[0], totals[1])
            both.append(jnp.where(kinds == kind, source, 0.0))
        picked = jnp.sum(jnp.where(even, both[0], both[1]), axis=0, keepdims=True)
        return jnp.sum(picked, axis=1, keepdims=True)

    out_ref[...] = jnp.zeros(out_ref.shape, jnp.float32)
    for place in range(slots):
        rows = jnp.concatenate([place_ref[place], jnp.zeros((4, size), jnp.float32)], axis=0)
        cols_ref[place] = rows.T
    right = [[place_ref[NEARC + u, p : p + 1, :] for p in range(4)] for u in range(NEARC)]
    parts = [(0, 0), (1, 1), (2, 2), (0, 1), (0, 2), (1, 2)]

    def fill(place, targets, block_ref):
        for step in range(size // ROWS):
            here = pl.ds(step * ROWS, ROWS)
            column = cols_ref[place, here, :]
            left = [jnp.broadcast_to(column[:, p : p + 1], (ROWS, size)) for p in range(4)]
            for u in targets:
                offset = [left[p] - right[u][p] for p in range(3)]
                radius_sq = offset[0] * offset[0] + offset[1] * offset[1] + offset[2] * offset[2]
                inverse = lax.rsqrt(radius_sq + soften)
                flat = (left[3] * right[u][3]) * inverse
                cubed = flat * (inverse * inverse)
                scaled = [offset[p] * cubed for p in range(3)]
                for part_id, (i, j) in enumerate(parts):
                    term = offset[i] * scaled[j]
                    if i == j:
                        term = term + flat
                    block_ref[u, part_id, here, :] = term.astype(jnp.bfloat16)

    def apply(place, targets, block_ref):
        slip = slip_ref[place]
        pieces = [slip[:, p * size : (p + 1) * size] for p in range(3)]
        for u in targets:
            count = count_of(place, u)
            sums = [
                jnp.dot(pieces[p], block_ref[u, p], preferred_element_type=jnp.float32)
                for p in range(3)
            ]
            for part_id in range(3, 6):
                i, j = parts[part_id]
                both = jnp.dot(
                    jnp.concatenate([pieces[j], pieces[i]], axis=0),
                    block_ref[u, part_id],
                    preferred_element_type=jnp.float32,
                )
                sums[i] = sums[i] + both[0:rhs_count]
                sums[j] = sums[j] + both[rhs_count : 2 * rhs_count]
            for p in range(3):
                out_ref[u, :, p * size : (p + 1) * size] += count * sums[p]

    every = list(range(NEARC))
    fill(0, [0], even_ref)
    for u in range(1, NEARC):
        even_ref[u] = jnp.zeros(even_ref.shape[1:], jnp.bfloat16)

    def two_places(turn, carry):
        place = 2 * turn
        fill(place + 1, every, odd_ref)
        apply(place, every, even_ref)
        fill(place + 2, every, even_ref)
        apply(place + 1, every, odd_ref)
        return carry

    lax.fori_loop(0, (slots - 2) // 2, two_places, 0)
    fill(slots - 1, [NEARC - 1], odd_ref)
    apply(slots - 2, every, even_ref)
    apply(slots - 1, [NEARC - 1], odd_ref)


def coupling_kernel(
    coupling_ref, pairs_ref, after_ref, to_second_ref, to_first_ref, list_ref, *, clusters, long_count
):
    owner, group = pairs_ref[...] // clusters, pairs_ref[...] % clusters
    list_ref[...] = jnp.concatenate([group * long_count + owner, owner, group], axis=0)
    pair_count, rank_size, _ = coupling_ref.shape
    groups = LANES // rank_size
    for pair_id in range(pair_count):
        here = pl.ds(pair_id * rank_size, rank_size)
        coupling = coupling_ref[pair_id].astype(jnp.float32)
        for out_ref, value in ((to_second_ref, coupling), (to_first_ref, coupling.T)):
            out_ref[here, :] = jnp.concatenate([value] * groups, axis=1).astype(jnp.bfloat16)


def far_kernel(
    list_ref, coeff_ref, to_second_ref, to_first_ref, out_hbm, done_ref, pairs_ref, moved_ref, sent_ref, sems,
    *total_refs, clusters
):
    fetch = pltpu.make_async_copy(list_ref, pairs_ref, sems.at[0])
    fetch.start()
    done_ref[...] = jnp.zeros(done_ref.shape, jnp.float32)
    long_count, rhs_count, _ = total_refs[0].shape
    pair_count = pairs_ref.shape[1]
    rank_size = LANES // clusters
    group_id = lax.broadcasted_iota(jnp.int32, (rhs_count, LANES), 1) // rank_size
    for total_ref in total_refs:
        total_ref[...] = jnp.zeros(total_ref.shape, jnp.float32)
    for at in range(coeff_ref.shape[0]):
        whole = coeff_ref[at].astype(jnp.float32)
        moved_ref[at] = jnp.concatenate([whole, pltpu.roll(whole, LANES - rank_size, 1)], axis=0)
    fetch.wait()

    def coeff_of(at, group):
        whole = moved_ref[at]
        both = pltpu.roll(whole, rank_size * group, 1) if group else whole
        return jnp.where(group_id == group, both, 0.0)

    results = []
    for begin in range(0, pair_count, clusters):
        pair_ids = range(begin, min(begin + clusters, pair_count))
        depth = len(pair_ids) * rank_size
        here = pl.ds(begin * rank_size, depth)
        for source, target, matrix_ref in ((0, 1, to_second_ref), (1, 0, to_first_ref)):
            coeffs = jnp.concatenate(
                [coeff_of(pairs_ref[source, f], f - begin) for f in pair_ids], axis=0
            ).astype(jnp.bfloat16)
            value = jnp.dot(
                coeffs[:, 0:depth], matrix_ref[here, :], preferred_element_type=jnp.float32
            )
            for turn, f in enumerate(pair_ids):
                results.append(
                    (target, f, value[turn * rhs_count : (turn + 1) * rhs_count])
                )
    for turn, (target, f, value) in enumerate(results):
        total_ref = total_refs[turn % len(total_refs)]
        owner, group = pairs_ref[2 + target, f], pairs_ref[4 + target, f]
        total_ref[owner] += jnp.where(group_id == group, value, 0.0)
    total = total_refs[0][...]
    for total_ref in total_refs[1:]:
        total = total + total_ref[...]
    for owner in range(long_count):
        sent_ref[long_count - 1 - owner] = total[owner].astype(jnp.bfloat16)
    copies = [
        pltpu.make_async_copy(
            sent_ref, out_hbm.at[pl.ds(copy_id * long_count, long_count)], sems.at[copy_id]
        )
        for copy_id in range(out_hbm.shape[0] // long_count)
    ]
    for copy in copies:
        copy.start()
    for copy in copies:
        copy.wait()


def gather_near_kernel(own_ref, other_ref, out_ref):
    even = lax.axis_index("row") % 2 == 0
    for cluster in range(out_ref.shape[0]):
        u = cluster % NEARC
        here = even if cluster < NEARC else jnp.logical_not(even)
        out_ref[cluster] = jnp.where(here, own_ref[u], other_ref[u])


def finish_kernel(near_ref, far_ref, basis_ref, out_hbm, sent_ref, sems):
    clusters, rank_size, unknowns = basis_ref.shape
    rhs_count = near_ref.shape[1]
    total = jnp.sum(far_ref[...].astype(jnp.float32), axis=0)
    group_id = lax.broadcasted_iota(jnp.int32, total.shape, 1) // rank_size
    flat_basis = basis_ref[...].reshape(clusters * rank_size, unknowns)
    picked = [jnp.where(group_id == cluster, total, 0.0) for cluster in range(clusters)]
    result = jnp.dot(
        jnp.concatenate(picked, axis=0).astype(jnp.bfloat16),
        flat_basis,
        preferred_element_type=jnp.float32,
    )
    copies = []
    for cluster in range(clusters):
        far = result[cluster * rhs_count : (cluster + 1) * rhs_count]
        sent_ref[cluster] = far + near_ref[cluster]
        copies.append(
            pltpu.make_async_copy(sent_ref.at[cluster], out_hbm.at[cluster], sems.at[cluster])
        )
        copies[-1].start()
    for copy in copies:
        copy.wait()


def shards(slip, vertices, triangles, elem_map, near_pairs, near_count, far_pairs, far_coef, basis):
    clusters, rhs_count, unknowns = slip.shape
    rank_size = basis.shape[1]
    size = elem_map.shape[1]
    row_count = lax.axis_size("row")
    long_count = lax.axis_size("long")
    devices = row_count * long_count
    coupling = far_coef.reshape(-1, rank_size, rank_size)
    slots = clusters + NEARC

    pay = pl.pallas_call(
        coeffs_kernel,
        out_shape=jax.ShapeDtypeStruct((devices, rhs_count // 2, LANES), jnp.bfloat16),
        in_specs=[HBM] * 3 + [SMEM],
        out_specs=HBM,
        scratch_shapes=[
            pltpu.VMEM(slip.shape[1:], slip.dtype),
            pltpu.VMEM(basis.shape[1:], basis.dtype),
            pltpu.VMEM(near_pairs.shape, near_pairs.dtype),
            pltpu.VMEM((long_count, rhs_count // 2, LANES), jnp.bfloat16),
            pltpu.SemaphoreType.DMA((3,)),
            pltpu.SemaphoreType.DMA((row_count,)),
        ],
        compiler_params=pltpu.CompilerParams(vmem_limit_bytes=16 << 20),
        name="coeffs",
    )(
        *[
            pltpu.with_memory_space_constraint(array, pltpu.HBM)
            for array in (slip, basis, near_pairs)
        ],
        near_count,
    )
    everyone = lax.all_to_all(pay, ("row", "long"), 0, 0, tiled=True)

    xs, to_neighbour, geometry = pl.pallas_call(
        geometry_kernel,
        out_shape=[
            jax.ShapeDtypeStruct(slip.shape, jnp.bfloat16),
            jax.ShapeDtypeStruct((NEARC, rhs_count, unknowns + size), jnp.bfloat16),
            jax.ShapeDtypeStruct((clusters, 4, size), jnp.float32),
        ],
        in_specs=[VMEM] * 4 + [ANY],
        out_specs=[VMEM] * 3,
        compiler_params=pltpu.CompilerParams(vmem_limit_bytes=16 << 20),
        cost_estimate=pl.CostEstimate(
            flops=2_000_000, bytes_accessed=1_000_000, transcendentals=1_000
        ),
        name="geometry",
    )(slip, vertices, triangles, elem_map, pay)
    route = []
    for row in range(row_count):
        step = 1 if row % 2 == 0 else -1
        for owner in range(long_count):
            if 0 <= owner - step < long_count:
                route.append((row * long_count + owner - step, row * long_count + owner))
    halo = lax.ppermute(to_neighbour, ("row", "long"), route)

    window, places = pl.pallas_call(
        window_kernel,
        out_shape=[
            jax.ShapeDtypeStruct((slots, rhs_count, unknowns), jnp.bfloat16),
            jax.ShapeDtypeStruct((slots, 4, size), jnp.float32),
        ],
        in_specs=[VMEM] * 3,
        out_specs=[VMEM] * 2,
        compiler_params=pltpu.CompilerParams(vmem_limit_bytes=16 << 20),
        cost_estimate=pl.CostEstimate(flops=1000, bytes_accessed=1000, transcendentals=0),
        name="window",
    )(xs, geometry, halo)

    to_second, to_first, pair_list = pl.pallas_call(
        functools.partial(coupling_kernel, clusters=clusters, long_count=long_count),
        out_shape=[jax.ShapeDtypeStruct((coupling.shape[0] * rank_size, LANES), jnp.bfloat16)] * 2
        + [jax.ShapeDtypeStruct((6,) + far_pairs.shape[1:], far_pairs.dtype)],
        in_specs=[VMEM, VMEM, ANY],
        out_specs=[VMEM] * 3,
        compiler_params=pltpu.CompilerParams(vmem_limit_bytes=16 << 20),
        cost_estimate=pl.CostEstimate(flops=1000, bytes_accessed=1000, transcendentals=0),
        name="coupling",
    )(coupling, far_pairs, pay)
    far, far_done = pl.pallas_call(
        functools.partial(far_kernel, clusters=clusters),
        out_shape=[
            jax.ShapeDtypeStruct((devices, rhs_count, clusters * rank_size), jnp.bfloat16),
            jax.ShapeDtypeStruct((8, LANES), jnp.float32),
        ],
        in_specs=[VMEM] * 4,
        out_specs=[HBM, VMEM],
        scratch_shapes=[
            pltpu.SMEM((6,) + far_pairs.shape[1:], far_pairs.dtype),
            pltpu.VMEM((devices, rhs_count, LANES), jnp.float32),
            pltpu.VMEM((long_count, rhs_count, clusters * rank_size), jnp.bfloat16),
            pltpu.SemaphoreType.DMA((row_count,)),
        ]
        + [pltpu.VMEM((long_count, rhs_count, clusters * rank_size), jnp.float32)] * 4,
        compiler_params=pltpu.CompilerParams(vmem_limit_bytes=16 << 20),
        name="far",
    )(pair_list, everyone, to_second, to_first)
    order = [list(reversed(range(devices)))]
    far_terms = lax.all_to_all(far, ("row", "long"), 0, 0, axis_index_groups=order, tiled=True)

    near = pl.pallas_call(
        functools.partial(near_kernel, long_count=long_count, clusters=clusters),
        out_shape=jax.ShapeDtypeStruct((NEARC, rhs_count, unknowns), jnp.float32),
        in_specs=[VMEM] * 3 + [ANY],
        out_specs=VMEM,
        scratch_shapes=[
            pltpu.VMEM((slots, size, 8), jnp.float32),
            pltpu.VMEM((NEARC, 6, size, size), jnp.bfloat16),
            pltpu.VMEM((NEARC, 6, size, size), jnp.bfloat16),
        ],
        compiler_params=pltpu.CompilerParams(vmem_limit_bytes=24 << 20),
        cost_estimate=pl.CostEstimate(
            flops=1_000_000_000, bytes_accessed=1_000_000, transcendentals=660_000
        ),
        name="near",
    )(window, places, everyone, far_done)
    partner = [(row, row ^ 1) for row in range(row_count)]
    other = lax.ppermute(near, "row", partner)

    near_field = pl.pallas_call(
        gather_near_kernel,
        out_shape=jax.ShapeDtypeStruct(slip.shape, jnp.float32),
        in_specs=[VMEM] * 2,
        out_specs=VMEM,
        compiler_params=pltpu.CompilerParams(vmem_limit_bytes=16 << 20),
        cost_estimate=pl.CostEstimate(flops=1000, bytes_accessed=1000, transcendentals=0),
        name="gather_near",
    )(near, other)

    return pl.pallas_call(
        finish_kernel,
        out_shape=jax.ShapeDtypeStruct(slip.shape, jnp.float32),
        in_specs=[VMEM] * 3,
        out_specs=HBM,
        scratch_shapes=[
            pltpu.VMEM(slip.shape, jnp.float32),
            pltpu.SemaphoreType.DMA((clusters,)),
        ],
        compiler_params=pltpu.CompilerParams(vmem_limit_bytes=16 << 20),
        name="finish",
    )(near_field, far_terms, basis)


def solution(mesh):
    placed = (
        P("long", None, None),
        P(None, "long"),
        P(None, "long"),
        P("long", None),
        P(None, ("row", "long")),
        P(("row", "long")),
        P(None, ("row", "long")),
        P(("row", "long"), None),
        P("long", None, None),
    )
    return jax.shard_map(
        shards, mesh=mesh, in_specs=placed, out_specs=P("long", None, None), check_vma=False
    )
```

```python
import functools

import jax
import jax.numpy as jnp
from jax import lax
from jax.experimental import pallas as pl
from jax.experimental.pallas import tpu as pltpu
from jax.sharding import PartitionSpec as P

NEARC = 2
LANES = 128
ROWS = 16

soften = 0.25

VMEM = pl.BlockSpec(memory_space=pltpu.VMEM)
SMEM = pl.BlockSpec(memory_space=pltpu.SMEM)
HBM = pl.BlockSpec(memory_space=pltpu.HBM)
ANY = pl.BlockSpec(memory_space=pl.ANY)


def everyone_sends(chunks, row_count, long_count):
    rows = [(row + row_count // 2) % row_count for row in range(row_count)]
    order = [[row * long_count + owner for row in rows for owner in range(long_count)]]
    return lax.all_to_all(chunks, ("row", "long"), 0, 0, axis_index_groups=order, tiled=True)


def lane_gather(table, index):
    length = table.shape[1]
    lane = index & (LANES - 1)
    chunk = index // LANES
    found = jnp.zeros(index.shape, table.dtype)
    for piece_id in range(-(-length // LANES)):
        piece = table[:, piece_id * LANES : min(length, (piece_id + 1) * LANES)]
        missing = LANES - piece.shape[1]
        if missing:
            piece = jnp.concatenate([piece, jnp.zeros((1, missing), table.dtype)], axis=1)
        picked = jnp.take_along_axis(jnp.broadcast_to(piece, index.shape), lane, axis=1)
        found = jnp.where(chunk == piece_id, picked, found)
    return found


def split_three(value):
    high = value.astype(jnp.bfloat16).astype(jnp.float32)
    rest = value - high
    middle = rest.astype(jnp.bfloat16).astype(jnp.float32)
    return [high, middle, rest - middle]


def coeffs_kernel(
    slip_hbm, basis_hbm, pairs_hbm, count_ref, pay_hbm, slip_ref, basis_ref, pairs_ref, sent_ref, sems, out_sems
):
    clusters = slip_hbm.shape[0]
    rhs_count = slip_ref.shape[0]
    rank_size = basis_ref.shape[0]
    mine = lax.axis_index("row") % clusters
    copies = [
        pltpu.make_async_copy(slip_hbm.at[mine], slip_ref, sems.at[0]),
        pltpu.make_async_copy(basis_hbm.at[mine], basis_ref, sems.at[1]),
        pltpu.make_async_copy(pairs_hbm, pairs_ref, sems.at[2]),
    ]
    for copy in copies:
        copy.start()
    half = rhs_count // 2
    copies[2].wait()
    first = pairs_ref[0:1, :]
    kind = (first - lax.axis_index("long") * clusters) * (NEARC + 1) + pairs_ref[1:2, :] - first
    kinds = lax.broadcasted_iota(jnp.int32, (half, kind.shape[1]), 0)
    live = lax.broadcasted_iota(jnp.int32, kinds.shape, 1) < count_ref[0]
    low = jnp.sum(jnp.where(live & (kinds == kind), 1.0, 0.0), axis=1, keepdims=True)
    high = jnp.sum(jnp.where(live & (kinds + half == kind), 1.0, 0.0), axis=1, keepdims=True)
    copies[0].wait()
    copies[1].wait()
    coeffs = lax.dot_general(
        slip_ref[...].astype(jnp.bfloat16),
        basis_ref[...],
        (((1,), (1,)), ((), ())),
        preferred_element_type=jnp.float32,
    )
    counts = [jnp.broadcast_to(value, (half, rank_size)) for value in (low, high)]
    pay = jnp.concatenate([coeffs[0:half], coeffs[half:]] + counts, axis=1).astype(jnp.bfloat16)
    for target in range(sent_ref.shape[0]):
        sent_ref[target] = pay
    parts = pay_hbm.shape[0] // sent_ref.shape[0]
    sends = [
        pltpu.make_async_copy(
            sent_ref, pay_hbm.at[pl.ds(part * sent_ref.shape[0], sent_ref.shape[0])], out_sems.at[part]
        )
        for part in range(parts)
    ]
    for send in sends:
        send.start()
    for send in sends:
        send.wait()


def geometry_kernel(
    slip_ref, vertices_ref, triangles_ref, map_ref, after_ref, xs_ref, halo_ref, geom_ref
):
    clusters, rhs_count, unknowns = slip_ref.shape
    xs_ref[...] = slip_ref[...].astype(jnp.bfloat16)
    long_index = lax.axis_index("long")

    size = map_ref.shape[1]
    half = size // LANES
    slot_map = map_ref[...]
    index = jnp.concatenate(
        [slot_map[:, part * LANES : (part + 1) * LANES] for part in range(half)], axis=0
    )
    vertex_base = long_index * vertices_ref.shape[1]
    corners = []
    for corner_id in range(3):
        vertex = lane_gather(triangles_ref[corner_id : corner_id + 1, :], index) - vertex_base
        corners.append(
            [lane_gather(vertices_ref[axis_id : axis_id + 1, :], vertex) for axis_id in range(3)]
        )
    one, two, three = corners
    centre = [(one[a] + two[a] + three[a]) / 3.0 for a in range(3)]
    edge_one = [two[a] - one[a] for a in range(3)]
    edge_two = [three[a] - one[a] for a in range(3)]
    normal = [
        edge_one[1] * edge_two[2] - edge_one[2] * edge_two[1],
        edge_one[2] * edge_two[0] - edge_one[0] * edge_two[2],
        edge_one[0] * edge_two[1] - edge_one[1] * edge_two[0],
    ]
    area = 0.5 * jnp.sqrt(normal[0] * normal[0] + normal[1] * normal[1] + normal[2] * normal[2])
    geometry = []
    for value in centre + [area]:
        geometry.append(
            jnp.concatenate(
                [value[part * clusters : (part + 1) * clusters] for part in range(half)], axis=1
            )
        )
    for cluster in range(clusters):
        geom_ref[cluster] = jnp.concatenate(
            [whole[cluster : cluster + 1, :] for whole in geometry], axis=0
        )

    upward = lax.axis_index("row") % 2 == 0
    start = jnp.where(upward, clusters - NEARC, 0)
    pieces = [piece for whole in geometry for piece in split_three(whole)]
    for turn in range(NEARC):
        last = clusters - NEARC + turn
        rows = [
            jnp.where(upward, piece[last : last + 1, :], piece[turn : turn + 1, :])
            for piece in pieces
        ]
        rows.append(jnp.zeros((rhs_count - len(rows), size), jnp.float32))
        halo_ref[turn, :, 0:unknowns] = xs_ref[start + turn]
        halo_ref[turn, :, unknowns : unknowns + size] = jnp.concatenate(rows, axis=0).astype(
            jnp.bfloat16
        )


def window_kernel(xs_ref, geom_ref, halo_ref, slip_ref, place_ref):
    clusters, rhs_count, unknowns = xs_ref.shape
    size = geom_ref.shape[2]
    slots = clusters + NEARC
    odd = lax.axis_index("row") % 2

    def place_of(cluster):
        return (cluster + NEARC * (1 - odd) + slots) % slots

    for cluster in range(clusters):
        slip_ref[place_of(cluster)] = xs_ref[cluster]
        place_ref[place_of(cluster)] = geom_ref[cluster]
    for turn in range(NEARC):
        at = place_of(clusters + turn)
        slip_ref[at] = halo_ref[turn, :, 0:unknowns]
        pieces = halo_ref[turn, :, unknowns : unknowns + size].astype(jnp.float32)
        place_ref[at] = jnp.concatenate(
            [
                (pieces[3 * p + 2 : 3 * p + 3] + pieces[3 * p + 1 : 3 * p + 2])
                + pieces[3 * p : 3 * p + 1]
                for p in range(4)
            ],
            axis=0,
        )


def near_kernel(
    slip_ref, place_ref, pay_ref, after_ref, out_ref, cols_ref, even_ref, odd_ref, *, long_count, clusters
):
    slots, rhs_count, unknowns = slip_ref.shape
    size = place_ref.shape[2]
    long_index = lax.axis_index("long")
    before = jnp.maximum(long_index - 1, 0)
    totals = [jnp.zeros(pay_ref.shape[1:], jnp.float32) for _ in range(2)]
    for row in range(pay_ref.shape[0] // long_count):
        for source, owner in enumerate((long_index, before)):
            totals[source] += pay_ref[row * long_count + owner].astype(jnp.float32)
    even = lax.axis_index("row") % 2 == 0
    half = pay_ref.shape[1]
    rank_size = pay_ref.shape[2] // 4
    group = lax.broadcasted_iota(jnp.int32, (half, LANES), 1) // rank_size
    kinds = lax.broadcasted_iota(jnp.int32, (half, LANES), 0) + jnp.where(group == 3, half, 0)
    kinds = jnp.where(group < 2, -1, kinds)
    lane_id = lax.broadcasted_iota(jnp.int32, (half, LANES), 1)
    kinds = jnp.where(lane_id % rank_size == 0, kinds, -1)

    def count_of(place, u):
        both = []
        for cluster in (u, clusters - NEARC + u):
            reach = place - u - NEARC
            lower = cluster + jnp.minimum(reach, 0)
            inside = lower >= 0
            kind = jnp.where(inside, lower, lower + clusters) * (NEARC + 1) + jnp.abs(reach)
            source = jnp.where(inside, totals[0], totals[1])
            both.append(jnp.where(kinds == kind, source, 0.0))
        picked = jnp.sum(jnp.where(even, both[0], both[1]), axis=0, keepdims=True)
        return jnp.sum(picked, axis=1, keepdims=True)

    out_ref[...] = jnp.zeros(out_ref.shape, jnp.float32)
    for place in range(slots):
        rows = jnp.concatenate([place_ref[place], jnp.zeros((4, size), jnp.float32)], axis=0)
        cols_ref[place] = rows.T
    right = [[place_ref[NEARC + u, p : p + 1, :] for p in range(4)] for u in range(NEARC)]
    parts = [(0, 0), (1, 1), (2, 2), (0, 1), (0, 2), (1, 2)]

    def fill(place, targets, block_ref):
        for step in range(size // ROWS):
            here = pl.ds(step * ROWS, ROWS)
            column = cols_ref[place, here, :]
            left = [jnp.broadcast_to(column[:, p : p + 1], (ROWS, size)) for p in range(4)]
            for u in targets:
                offset = [left[p] - right[u][p] for p in range(3)]
                radius_sq = offset[0] * offset[0] + offset[1] * offset[1] + offset[2] * offset[2]
                inverse = lax.rsqrt(radius_sq + soften)
                flat = (left[3] * right[u][3]) * inverse
                cubed = flat * (inverse * inverse)
                scaled = [offset[p] * cubed for p in range(3)]
                for part_id, (i, j) in enumerate(parts):
                    term = offset[i] * scaled[j]
                    if i == j:
                        term = term + flat
                    block_ref[u, part_id, here, :] = term.astype(jnp.bfloat16)

    def apply(place, targets, block_ref):
        slip = slip_ref[place]
        pieces = [slip[:, p * size : (p + 1) * size] for p in range(3)]
        for u in targets:
            count = count_of(place, u)
            sums = [
                jnp.dot(pieces[p], block_ref[u, p], preferred_element_type=jnp.float32)
                for p in range(3)
            ]
            for part_id in range(3, 6):
                i, j = parts[part_id]
                both = jnp.dot(
                    jnp.concatenate([pieces[j], pieces[i]], axis=0),
                    block_ref[u, part_id],
                    preferred_element_type=jnp.float32,
                )
                sums[i] = sums[i] + both[0:rhs_count]
                sums[j] = sums[j] + both[rhs_count : 2 * rhs_count]
            for p in range(3):
                out_ref[u, :, p * size : (p + 1) * size] += count * sums[p]

    every = list(range(NEARC))
    fill(0, [0], even_ref)
    for u in range(1, NEARC):
        even_ref[u] = jnp.zeros(even_ref.shape[1:], jnp.bfloat16)

    def two_places(turn, carry):
        place = 2 * turn
        fill(place + 1, every, odd_ref)
        apply(place, every, even_ref)
        fill(place + 2, every, even_ref)
        apply(place + 1, every, odd_ref)
        return carry

    lax.fori_loop(0, (slots - 2) // 2, two_places, 0)
    fill(slots - 1, [NEARC - 1], odd_ref)
    apply(slots - 2, every, even_ref)
    apply(slots - 1, [NEARC - 1], odd_ref)


def coupling_kernel(
    coupling_ref, pairs_ref, after_ref, to_second_ref, to_first_ref, list_ref, *, clusters, long_count, row_count
):
    owner, group = pairs_ref[...] // clusters, pairs_ref[...] % clusters
    at = (group + row_count // 2) % row_count * long_count + owner
    list_ref[...] = jnp.concatenate([at, owner, group], axis=0)
    pair_count, rank_size, _ = coupling_ref.shape
    groups = LANES // rank_size
    for pair_id in range(pair_count):
        here = pl.ds(pair_id * rank_size, rank_size)
        coupling = coupling_ref[pair_id].astype(jnp.float32)
        for out_ref, value in ((to_second_ref, coupling), (to_first_ref, coupling.T)):
            out_ref[here, :] = jnp.concatenate([value] * groups, axis=1).astype(jnp.bfloat16)


def far_kernel(
    list_ref, coeff_ref, to_second_ref, to_first_ref, out_hbm, done_ref, pairs_ref, moved_ref, sent_ref, sems,
    *total_refs, clusters
):
    fetch = pltpu.make_async_copy(list_ref, pairs_ref, sems.at[0])
    fetch.start()
    done_ref[...] = jnp.zeros(done_ref.shape, jnp.float32)
    long_count, rhs_count, _ = total_refs[0].shape
    pair_count = pairs_ref.shape[1]
    rank_size = LANES // clusters
    group_id = lax.broadcasted_iota(jnp.int32, (rhs_count, LANES), 1) // rank_size
    for total_ref in total_refs:
        total_ref[...] = jnp.zeros(total_ref.shape, jnp.float32)
    for at in range(coeff_ref.shape[0]):
        whole = coeff_ref[at].astype(jnp.float32)
        moved_ref[at] = jnp.concatenate([whole, pltpu.roll(whole, LANES - rank_size, 1)], axis=0)
    fetch.wait()

    def coeff_of(at, group):
        whole = moved_ref[at]
        both = pltpu.roll(whole, rank_size * group, 1) if group else whole
        return jnp.where(group_id == group, both, 0.0)

    results = []
    for begin in range(0, pair_count, clusters):
        pair_ids = range(begin, min(begin + clusters, pair_count))
        depth = len(pair_ids) * rank_size
        here = pl.ds(begin * rank_size, depth)
        for source, target, matrix_ref in ((0, 1, to_second_ref), (1, 0, to_first_ref)):
            coeffs = jnp.concatenate(
                [coeff_of(pairs_ref[source, f], f - begin) for f in pair_ids], axis=0
            ).astype(jnp.bfloat16)
            value = jnp.dot(
                coeffs[:, 0:depth], matrix_ref[here, :], preferred_element_type=jnp.float32
            )
            for turn, f in enumerate(pair_ids):
                results.append(
                    (target, f, value[turn * rhs_count : (turn + 1) * rhs_count])
                )
    for turn, (target, f, value) in enumerate(results):
        total_ref = total_refs[turn % len(total_refs)]
        owner, group = pairs_ref[2 + target, f], pairs_ref[4 + target, f]
        total_ref[owner] += jnp.where(group_id == group, value, 0.0)
    total = total_refs[0][...]
    for total_ref in total_refs[1:]:
        total = total + total_ref[...]
    sent_ref[...] = total.astype(jnp.bfloat16)
    copies = [
        pltpu.make_async_copy(
            sent_ref, out_hbm.at[pl.ds(copy_id * long_count, long_count)], sems.at[copy_id]
        )
        for copy_id in range(out_hbm.shape[0] // long_count)
    ]
    for copy in copies:
        copy.start()
    for copy in copies:
        copy.wait()


def gather_near_kernel(own_ref, other_ref, out_ref):
    even = lax.axis_index("row") % 2 == 0
    for cluster in range(out_ref.shape[0]):
        u = cluster % NEARC
        here = even if cluster < NEARC else jnp.logical_not(even)
        out_ref[cluster] = jnp.where(here, own_ref[u], other_ref[u])


def finish_kernel(near_ref, far_ref, basis_ref, out_hbm, sent_ref, sems):
    clusters, rank_size, unknowns = basis_ref.shape
    rhs_count = near_ref.shape[1]
    total = jnp.sum(far_ref[...].astype(jnp.float32), axis=0)
    group_id = lax.broadcasted_iota(jnp.int32, total.shape, 1) // rank_size
    flat_basis = basis_ref[...].reshape(clusters * rank_size, unknowns)
    picked = [jnp.where(group_id == cluster, total, 0.0) for cluster in range(clusters)]
    result = jnp.dot(
        jnp.concatenate(picked, axis=0).astype(jnp.bfloat16),
        flat_basis,
        preferred_element_type=jnp.float32,
    )
    copies = []
    for cluster in range(clusters):
        far = result[cluster * rhs_count : (cluster + 1) * rhs_count]
        sent_ref[cluster] = far + near_ref[cluster]
        copies.append(
            pltpu.make_async_copy(sent_ref.at[cluster], out_hbm.at[cluster], sems.at[cluster])
        )
        copies[-1].start()
    for copy in copies:
        copy.wait()


def shards(slip, vertices, triangles, elem_map, near_pairs, near_count, far_pairs, far_coef, basis):
    clusters, rhs_count, unknowns = slip.shape
    rank_size = basis.shape[1]
    size = elem_map.shape[1]
    row_count = lax.axis_size("row")
    long_count = lax.axis_size("long")
    devices = row_count * long_count
    coupling = far_coef.reshape(-1, rank_size, rank_size)
    slots = clusters + NEARC

    pay = pl.pallas_call(
        coeffs_kernel,
        out_shape=jax.ShapeDtypeStruct((devices, rhs_count // 2, LANES), jnp.bfloat16),
        in_specs=[HBM] * 3 + [SMEM],
        out_specs=HBM,
        scratch_shapes=[
            pltpu.VMEM(slip.shape[1:], slip.dtype),
            pltpu.VMEM(basis.shape[1:], basis.dtype),
            pltpu.VMEM(near_pairs.shape, near_pairs.dtype),
            pltpu.VMEM((long_count, rhs_count // 2, LANES), jnp.bfloat16),
            pltpu.SemaphoreType.DMA((3,)),
            pltpu.SemaphoreType.DMA((row_count,)),
        ],
        compiler_params=pltpu.CompilerParams(vmem_limit_bytes=16 << 20),
        name="coeffs",
    )(
        *[
            pltpu.with_memory_space_constraint(array, pltpu.HBM)
            for array in (slip, basis, near_pairs)
        ],
        near_count,
    )
    everyone = everyone_sends(pay, row_count, long_count)

    xs, to_neighbour, geometry = pl.pallas_call(
        geometry_kernel,
        out_shape=[
            jax.ShapeDtypeStruct(slip.shape, jnp.bfloat16),
            jax.ShapeDtypeStruct((NEARC, rhs_count, unknowns + size), jnp.bfloat16),
            jax.ShapeDtypeStruct((clusters, 4, size), jnp.float32),
        ],
        in_specs=[VMEM] * 4 + [ANY],
        out_specs=[VMEM] * 3,
        compiler_params=pltpu.CompilerParams(vmem_limit_bytes=16 << 20),
        cost_estimate=pl.CostEstimate(
            flops=2_000_000, bytes_accessed=1_000_000, transcendentals=1_000
        ),
        name="geometry",
    )(slip, vertices, triangles, elem_map, pay)
    route = []
    for row in range(row_count):
        step = 1 if row % 2 == 0 else -1
        for owner in range(long_count):
            if 0 <= owner - step < long_count:
                route.append((row * long_count + owner - step, row * long_count + owner))
    halo = lax.ppermute(to_neighbour, ("row", "long"), route)

    window, places = pl.pallas_call(
        window_kernel,
        out_shape=[
            jax.ShapeDtypeStruct((slots, rhs_count, unknowns), jnp.bfloat16),
            jax.ShapeDtypeStruct((slots, 4, size), jnp.float32),
        ],
        in_specs=[VMEM] * 3,
        out_specs=[VMEM] * 2,
        compiler_params=pltpu.CompilerParams(vmem_limit_bytes=16 << 20),
        cost_estimate=pl.CostEstimate(flops=1000, bytes_accessed=1000, transcendentals=0),
        name="window",
    )(xs, geometry, halo)

    to_second, to_first, pair_list = pl.pallas_call(
        functools.partial(
            coupling_kernel, clusters=clusters, long_count=long_count, row_count=row_count
        ),
        out_shape=[jax.ShapeDtypeStruct((coupling.shape[0] * rank_size, LANES), jnp.bfloat16)] * 2
        + [jax.ShapeDtypeStruct((6,) + far_pairs.shape[1:], far_pairs.dtype)],
        in_specs=[VMEM, VMEM, ANY],
        out_specs=[VMEM] * 3,
        compiler_params=pltpu.CompilerParams(vmem_limit_bytes=16 << 20),
        cost_estimate=pl.CostEstimate(flops=1000, bytes_accessed=1000, transcendentals=0),
        name="coupling",
    )(coupling, far_pairs, pay)
    far, far_done = pl.pallas_call(
        functools.partial(far_kernel, clusters=clusters),
        out_shape=[
            jax.ShapeDtypeStruct((devices, rhs_count, clusters * rank_size), jnp.bfloat16),
            jax.ShapeDtypeStruct((8, LANES), jnp.float32),
        ],
        in_specs=[VMEM] * 4,
        out_specs=[HBM, VMEM],
        scratch_shapes=[
            pltpu.SMEM((6,) + far_pairs.shape[1:], far_pairs.dtype),
            pltpu.VMEM((devices, rhs_count, LANES), jnp.float32),
            pltpu.VMEM((long_count, rhs_count, clusters * rank_size), jnp.bfloat16),
            pltpu.SemaphoreType.DMA((row_count,)),
        ]
        + [pltpu.VMEM((long_count, rhs_count, clusters * rank_size), jnp.float32)] * 4,
        compiler_params=pltpu.CompilerParams(vmem_limit_bytes=16 << 20),
        name="far",
    )(pair_list, everyone, to_second, to_first)
    far_terms = everyone_sends(far, row_count, long_count)

    near = pl.pallas_call(
        functools.partial(near_kernel, long_count=long_count, clusters=clusters),
        out_shape=jax.ShapeDtypeStruct((NEARC, rhs_count, unknowns), jnp.float32),
        in_specs=[VMEM] * 3 + [ANY],
        out_specs=VMEM,
        scratch_shapes=[
            pltpu.VMEM((slots, size, 8), jnp.float32),
            pltpu.VMEM((NEARC, 6, size, size), jnp.bfloat16),
            pltpu.VMEM((NEARC, 6, size, size), jnp.bfloat16),
        ],
        compiler_params=pltpu.CompilerParams(vmem_limit_bytes=24 << 20),
        cost_estimate=pl.CostEstimate(
            flops=1_000_000_000, bytes_accessed=1_000_000, transcendentals=660_000
        ),
        name="near",
    )(window, places, everyone, far_done)
    partner = [(row, row ^ 1) for row in range(row_count)]
    other = lax.ppermute(near, "row", partner)

    near_field = pl.pallas_call(
        gather_near_kernel,
        out_shape=jax.ShapeDtypeStruct(slip.shape, jnp.float32),
        in_specs=[VMEM] * 2,
        out_specs=VMEM,
        compiler_params=pltpu.CompilerParams(vmem_limit_bytes=16 << 20),
        cost_estimate=pl.CostEstimate(flops=1000, bytes_accessed=1000, transcendentals=0),
        name="gather_near",
    )(near, other)

    return pl.pallas_call(
        finish_kernel,
        out_shape=jax.ShapeDtypeStruct(slip.shape, jnp.float32),
        in_specs=[VMEM] * 3,
        out_specs=HBM,
        scratch_shapes=[
            pltpu.VMEM(slip.shape, jnp.float32),
            pltpu.SemaphoreType.DMA((clusters,)),
        ],
        compiler_params=pltpu.CompilerParams(vmem_limit_bytes=16 << 20),
        name="finish",
    )(near_field, far_terms, basis)


def solution(mesh):
    placed = (
        P("long", None, None),
        P(None, "long"),
        P(None, "long"),
        P("long", None),
        P(None, ("row", "long")),
        P(("row", "long")),
        P(None, ("row", "long")),
        P(("row", "long"), None),
        P("long", None, None),
    )
    return jax.shard_map(
        shards, mesh=mesh, in_specs=placed, out_specs=P("long", None, None), check_vma=False
    )
```

```python
import functools

import jax
import jax.numpy as jnp
from jax import lax
from jax.experimental import pallas as pl
from jax.experimental.pallas import tpu as pltpu
from jax.sharding import PartitionSpec as P

NEARC = 2
LANES = 128
ROWS = 16

soften = 0.25

VMEM = pl.BlockSpec(memory_space=pltpu.VMEM)
SMEM = pl.BlockSpec(memory_space=pltpu.SMEM)
HBM = pl.BlockSpec(memory_space=pltpu.HBM)
ANY = pl.BlockSpec(memory_space=pl.ANY)


def lane_gather(table, index):
    length = table.shape[1]
    lane = index & (LANES - 1)
    chunk = index // LANES
    found = jnp.zeros(index.shape, table.dtype)
    for piece_id in range(-(-length // LANES)):
        piece = table[:, piece_id * LANES : min(length, (piece_id + 1) * LANES)]
        missing = LANES - piece.shape[1]
        if missing:
            piece = jnp.concatenate([piece, jnp.zeros((1, missing), table.dtype)], axis=1)
        picked = jnp.take_along_axis(jnp.broadcast_to(piece, index.shape), lane, axis=1)
        found = jnp.where(chunk == piece_id, picked, found)
    return found


def split_three(value):
    high = value.astype(jnp.bfloat16).astype(jnp.float32)
    rest = value - high
    middle = rest.astype(jnp.bfloat16).astype(jnp.float32)
    return [high, middle, rest - middle]


def coeffs_kernel(
    slip_hbm, basis_hbm, pairs_hbm, count_ref, pay_hbm, slip_ref, basis_ref, pairs_ref, sent_ref, sems, out_sems
):
    clusters = slip_hbm.shape[0]
    rhs_count = slip_ref.shape[0]
    rank_size = basis_ref.shape[0]
    mine = lax.axis_index("row") % clusters
    copies = [
        pltpu.make_async_copy(slip_hbm.at[mine], slip_ref, sems.at[0]),
        pltpu.make_async_copy(basis_hbm.at[mine], basis_ref, sems.at[1]),
        pltpu.make_async_copy(pairs_hbm, pairs_ref, sems.at[2]),
    ]
    for copy in copies:
        copy.start()
    half = rhs_count // 2
    copies[2].wait()
    first = pairs_ref[0:1, :]
    kind = (first - lax.axis_index("long") * clusters) * (NEARC + 1) + pairs_ref[1:2, :] - first
    kinds = lax.broadcasted_iota(jnp.int32, (half, kind.shape[1]), 0)
    live = lax.broadcasted_iota(jnp.int32, kinds.shape, 1) < count_ref[0]
    low = jnp.sum(jnp.where(live & (kinds == kind), 1.0, 0.0), axis=1, keepdims=True)
    high = jnp.sum(jnp.where(live & (kinds + half == kind), 1.0, 0.0), axis=1, keepdims=True)
    copies[0].wait()
    copies[1].wait()
    coeffs = lax.dot_general(
        slip_ref[...].astype(jnp.bfloat16),
        basis_ref[...],
        (((1,), (1,)), ((), ())),
        preferred_element_type=jnp.float32,
    )
    counts = [jnp.broadcast_to(value, (half, rank_size)) for value in (low, high)]
    pay = jnp.concatenate([coeffs[0:half], coeffs[half:]] + counts, axis=1).astype(jnp.bfloat16)
    for target in range(sent_ref.shape[0]):
        sent_ref[target] = pay
    parts = pay_hbm.shape[0] // sent_ref.shape[0]
    sends = [
        pltpu.make_async_copy(
            sent_ref, pay_hbm.at[pl.ds(part * sent_ref.shape[0], sent_ref.shape[0])], out_sems.at[part]
        )
        for part in range(parts)
    ]
    for send in sends:
        send.start()
    for send in sends:
        send.wait()


def geometry_kernel(
    slip_ref, vertices_ref, triangles_ref, map_ref, after_ref, xs_ref, halo_ref, geom_ref
):
    clusters, rhs_count, unknowns = slip_ref.shape
    xs_ref[...] = slip_ref[...].astype(jnp.bfloat16)
    long_index = lax.axis_index("long")

    size = map_ref.shape[1]
    half = size // LANES
    slot_map = map_ref[...]
    index = jnp.concatenate(
        [slot_map[:, part * LANES : (part + 1) * LANES] for part in range(half)], axis=0
    )
    vertex_base = long_index * vertices_ref.shape[1]
    corners = []
    for corner_id in range(3):
        vertex = lane_gather(triangles_ref[corner_id : corner_id + 1, :], index) - vertex_base
        corners.append(
            [lane_gather(vertices_ref[axis_id : axis_id + 1, :], vertex) for axis_id in range(3)]
        )
    one, two, three = corners
    centre = [(one[a] + two[a] + three[a]) / 3.0 for a in range(3)]
    edge_one = [two[a] - one[a] for a in range(3)]
    edge_two = [three[a] - one[a] for a in range(3)]
    normal = [
        edge_one[1] * edge_two[2] - edge_one[2] * edge_two[1],
        edge_one[2] * edge_two[0] - edge_one[0] * edge_two[2],
        edge_one[0] * edge_two[1] - edge_one[1] * edge_two[0],
    ]
    area = 0.5 * jnp.sqrt(normal[0] * normal[0] + normal[1] * normal[1] + normal[2] * normal[2])
    geometry = []
    for value in centre + [area]:
        geometry.append(
            jnp.concatenate(
                [value[part * clusters : (part + 1) * clusters] for part in range(half)], axis=1
            )
        )
    for cluster in range(clusters):
        geom_ref[cluster] = jnp.concatenate(
            [whole[cluster : cluster + 1, :] for whole in geometry], axis=0
        )

    upward = lax.axis_index("row") % 2 == 0
    start = jnp.where(upward, clusters - NEARC, 0)
    pieces = [piece for whole in geometry for piece in split_three(whole)]
    for turn in range(NEARC):
        last = clusters - NEARC + turn
        rows = [
            jnp.where(upward, piece[last : last + 1, :], piece[turn : turn + 1, :])
            for piece in pieces
        ]
        rows.append(jnp.zeros((rhs_count - len(rows), size), jnp.float32))
        halo_ref[turn, :, 0:unknowns] = xs_ref[start + turn]
        halo_ref[turn, :, unknowns : unknowns + size] = jnp.concatenate(rows, axis=0).astype(
            jnp.bfloat16
        )


def window_kernel(xs_ref, geom_ref, halo_ref, slip_ref, place_ref):
    clusters, rhs_count, unknowns = xs_ref.shape
    size = geom_ref.shape[2]
    slots = clusters + NEARC
    odd = lax.axis_index("row") % 2

    def place_of(cluster):
        return (cluster + NEARC * (1 - odd) + slots) % slots

    for cluster in range(clusters):
        slip_ref[place_of(cluster)] = xs_ref[cluster]
        place_ref[place_of(cluster)] = geom_ref[cluster]
    for turn in range(NEARC):
        at = place_of(clusters + turn)
        slip_ref[at] = halo_ref[turn, :, 0:unknowns]
        pieces = halo_ref[turn, :, unknowns : unknowns + size].astype(jnp.float32)
        place_ref[at] = jnp.concatenate(
            [
                (pieces[3 * p + 2 : 3 * p + 3] + pieces[3 * p + 1 : 3 * p + 2])
                + pieces[3 * p : 3 * p + 1]
                for p in range(4)
            ],
            axis=0,
        )


def near_kernel(
    slip_ref, place_ref, pay_ref, after_ref, out_ref, cols_ref, even_ref, odd_ref, *, long_count, clusters
):
    slots, rhs_count, unknowns = slip_ref.shape
    size = place_ref.shape[2]
    long_index = lax.axis_index("long")
    before = jnp.maximum(long_index - 1, 0)
    totals = [jnp.zeros(pay_ref.shape[1:], jnp.float32) for _ in range(2)]
    for row in range(pay_ref.shape[0] // long_count):
        for source, owner in enumerate((long_index, before)):
            totals[source] += pay_ref[row * long_count + owner].astype(jnp.float32)
    even = lax.axis_index("row") % 2 == 0
    half = pay_ref.shape[1]
    rank_size = pay_ref.shape[2] // 4
    group = lax.broadcasted_iota(jnp.int32, (half, LANES), 1) // rank_size
    kinds = lax.broadcasted_iota(jnp.int32, (half, LANES), 0) + jnp.where(group == 3, half, 0)
    kinds = jnp.where(group < 2, -1, kinds)
    lane_id = lax.broadcasted_iota(jnp.int32, (half, LANES), 1)
    kinds = jnp.where(lane_id % rank_size == 0, kinds, -1)

    def count_of(place, u):
        both = []
        for cluster in (u, clusters - NEARC + u):
            reach = place - u - NEARC
            lower = cluster + jnp.minimum(reach, 0)
            inside = lower >= 0
            kind = jnp.where(inside, lower, lower + clusters) * (NEARC + 1) + jnp.abs(reach)
            source = jnp.where(inside, totals[0], totals[1])
            both.append(jnp.where(kinds == kind, source, 0.0))
        picked = jnp.sum(jnp.where(even, both[0], both[1]), axis=0, keepdims=True)
        return jnp.sum(picked, axis=1, keepdims=True)

    out_ref[...] = jnp.zeros(out_ref.shape, jnp.float32)
    for place in range(slots):
        rows = jnp.concatenate([place_ref[place], jnp.zeros((4, size), jnp.float32)], axis=0)
        cols_ref[place] = rows.T
    right = [[place_ref[NEARC + u, p : p + 1, :] for p in range(4)] for u in range(NEARC)]
    parts = [(0, 0), (1, 1), (2, 2), (0, 1), (0, 2), (1, 2)]

    def fill(place, targets, block_ref):
        for step in range(size // ROWS):
            here = pl.ds(step * ROWS, ROWS)
            column = cols_ref[place, here, :]
            left = [jnp.broadcast_to(column[:, p : p + 1], (ROWS, size)) for p in range(4)]
            for u in targets:
                offset = [left[p] - right[u][p] for p in range(3)]
                radius_sq = offset[0] * offset[0] + offset[1] * offset[1] + offset[2] * offset[2]
                inverse = lax.rsqrt(radius_sq + soften)
                flat = (left[3] * right[u][3]) * inverse
                cubed = flat * (inverse * inverse)
                scaled = [offset[p] * cubed for p in range(3)]
                for part_id, (i, j) in enumerate(parts):
                    term = offset[i] * scaled[j]
                    if i == j:
                        term = term + flat
                    block_ref[u, part_id, here, :] = term.astype(jnp.bfloat16)

    def apply(place, targets, block_ref):
        slip = slip_ref[place]
        pieces = [slip[:, p * size : (p + 1) * size] for p in range(3)]
        for u in targets:
            count = count_of(place, u)
            sums = [
                jnp.dot(pieces[p], block_ref[u, p], preferred_element_type=jnp.float32)
                for p in range(3)
            ]
            for part_id in range(3, 6):
                i, j = parts[part_id]
                both = jnp.dot(
                    jnp.concatenate([pieces[j], pieces[i]], axis=0),
                    block_ref[u, part_id],
                    preferred_element_type=jnp.float32,
                )
                sums[i] = sums[i] + both[0:rhs_count]
                sums[j] = sums[j] + both[rhs_count : 2 * rhs_count]
            for p in range(3):
                out_ref[u, :, p * size : (p + 1) * size] += count * sums[p]

    every = list(range(NEARC))
    fill(0, [0], even_ref)
    for u in range(1, NEARC):
        even_ref[u] = jnp.zeros(even_ref.shape[1:], jnp.bfloat16)

    def two_places(turn, carry):
        place = 2 * turn
        fill(place + 1, every, odd_ref)
        apply(place, every, even_ref)
        fill(place + 2, every, even_ref)
        apply(place + 1, every, odd_ref)
        return carry

    lax.fori_loop(0, (slots - 2) // 2, two_places, 0)
    fill(slots - 1, [NEARC - 1], odd_ref)
    apply(slots - 2, every, even_ref)
    apply(slots - 1, [NEARC - 1], odd_ref)


def coupling_kernel(
    coupling_ref, pairs_ref, after_ref, to_second_ref, to_first_ref, list_ref, *, clusters, long_count
):
    owner, group = pairs_ref[...] // clusters, pairs_ref[...] % clusters
    list_ref[...] = jnp.concatenate([group * long_count + owner, owner, group], axis=0)
    pair_count, rank_size, _ = coupling_ref.shape
    groups = LANES // rank_size
    for pair_id in range(pair_count):
        here = pl.ds(pair_id * rank_size, rank_size)
        coupling = coupling_ref[pair_id].astype(jnp.float32)
        for out_ref, value in ((to_second_ref, coupling), (to_first_ref, coupling.T)):
            out_ref[here, :] = jnp.concatenate([value] * groups, axis=1).astype(jnp.bfloat16)


def far_kernel(
    list_ref, coeff_ref, to_second_ref, to_first_ref, out_hbm, done_ref, pairs_ref, moved_ref, sent_ref, sems,
    *total_refs, clusters
):
    fetch = pltpu.make_async_copy(list_ref, pairs_ref, sems.at[0])
    fetch.start()
    done_ref[...] = jnp.zeros(done_ref.shape, jnp.float32)
    long_count, rhs_count, _ = total_refs[0].shape
    pair_count = pairs_ref.shape[1]
    rank_size = LANES // clusters
    group_id = lax.broadcasted_iota(jnp.int32, (rhs_count, LANES), 1) // rank_size
    for total_ref in total_refs:
        total_ref[...] = jnp.zeros(total_ref.shape, jnp.float32)
    for at in range(coeff_ref.shape[0]):
        whole = coeff_ref[at].astype(jnp.float32)
        moved_ref[at] = jnp.concatenate([whole, pltpu.roll(whole, LANES - rank_size, 1)], axis=0)
    fetch.wait()

    def coeff_of(at, group):
        whole = moved_ref[at]
        both = pltpu.roll(whole, rank_size * group, 1) if group else whole
        return jnp.where(group_id == group, both, 0.0)

    results = []
    for begin in range(0, pair_count, clusters):
        pair_ids = range(begin, min(begin + clusters, pair_count))
        depth = len(pair_ids) * rank_size
        here = pl.ds(begin * rank_size, depth)
        for source, target, matrix_ref in ((0, 1, to_second_ref), (1, 0, to_first_ref)):
            coeffs = jnp.concatenate(
                [coeff_of(pairs_ref[source, f], f - begin) for f in pair_ids], axis=0
            ).astype(jnp.bfloat16)
            value = jnp.dot(
                coeffs[:, 0:depth], matrix_ref[here, :], preferred_element_type=jnp.float32
            )
            for turn, f in enumerate(pair_ids):
                results.append(
                    (target, f, value[turn * rhs_count : (turn + 1) * rhs_count])
                )
    for turn, (target, f, value) in enumerate(results):
        total_ref = total_refs[turn % len(total_refs)]
        owner, group = pairs_ref[2 + target, f], pairs_ref[4 + target, f]
        total_ref[owner] += jnp.where(group_id == group, value, 0.0)
    total = total_refs[0][...]
    for total_ref in total_refs[1:]:
        total = total + total_ref[...]
    sent_ref[...] = total.astype(jnp.bfloat16)
    copies = [
        pltpu.make_async_copy(
            sent_ref, out_hbm.at[pl.ds(copy_id * long_count, long_count)], sems.at[copy_id]
        )
        for copy_id in range(out_hbm.shape[0] // long_count)
    ]
    for copy in copies:
        copy.start()
    for copy in copies:
        copy.wait()


def gather_near_kernel(own_ref, other_ref, out_ref):
    even = lax.axis_index("row") % 2 == 0
    for cluster in range(out_ref.shape[0]):
        u = cluster % NEARC
        here = even if cluster < NEARC else jnp.logical_not(even)
        out_ref[cluster] = jnp.where(here, own_ref[u], other_ref[u])


def finish_kernel(near_ref, far_ref, basis_ref, out_hbm, sent_ref, sems):
    clusters, rank_size, unknowns = basis_ref.shape
    rhs_count = near_ref.shape[1]
    total = jnp.sum(far_ref[...].astype(jnp.float32), axis=0)
    group_id = lax.broadcasted_iota(jnp.int32, total.shape, 1) // rank_size
    flat_basis = basis_ref[...].reshape(clusters * rank_size, unknowns)
    picked = [jnp.where(group_id == cluster, total, 0.0) for cluster in range(clusters)]
    result = jnp.dot(
        jnp.concatenate(picked, axis=0).astype(jnp.bfloat16),
        flat_basis,
        preferred_element_type=jnp.float32,
    )
    copies = []
    for cluster in range(clusters):
        far = result[cluster * rhs_count : (cluster + 1) * rhs_count]
        sent_ref[cluster] = far + near_ref[cluster]
        copies.append(
            pltpu.make_async_copy(sent_ref.at[cluster], out_hbm.at[cluster], sems.at[cluster])
        )
        copies[-1].start()
    for copy in copies:
        copy.wait()


def shards(slip, vertices, triangles, elem_map, near_pairs, near_count, far_pairs, far_coef, basis):
    clusters, rhs_count, unknowns = slip.shape
    rank_size = basis.shape[1]
    size = elem_map.shape[1]
    row_count = lax.axis_size("row")
    long_count = lax.axis_size("long")
    devices = row_count * long_count
    coupling = far_coef.reshape(-1, rank_size, rank_size)
    slots = clusters + NEARC

    pay = pl.pallas_call(
        coeffs_kernel,
        out_shape=jax.ShapeDtypeStruct((devices, rhs_count // 2, LANES), jnp.bfloat16),
        in_specs=[HBM] * 3 + [SMEM],
        out_specs=HBM,
        scratch_shapes=[
            pltpu.VMEM(slip.shape[1:], slip.dtype),
            pltpu.VMEM(basis.shape[1:], basis.dtype),
            pltpu.VMEM(near_pairs.shape, near_pairs.dtype),
            pltpu.VMEM((long_count, rhs_count // 2, LANES), jnp.bfloat16),
            pltpu.SemaphoreType.DMA((3,)),
            pltpu.SemaphoreType.DMA((row_count,)),
        ],
        compiler_params=pltpu.CompilerParams(vmem_limit_bytes=16 << 20),
        name="coeffs",
    )(
        *[
            pltpu.with_memory_space_constraint(array, pltpu.HBM)
            for array in (slip, basis, near_pairs)
        ],
        near_count,
    )
    everyone = lax.all_to_all(pay, ("row", "long"), 0, 0, tiled=True)

    slip_later, pay = lax.optimization_barrier((slip, pay))
    xs, to_neighbour, geometry = pl.pallas_call(
        geometry_kernel,
        out_shape=[
            jax.ShapeDtypeStruct(slip.shape, jnp.bfloat16),
            jax.ShapeDtypeStruct((NEARC, rhs_count, unknowns + size), jnp.bfloat16),
            jax.ShapeDtypeStruct((clusters, 4, size), jnp.float32),
        ],
        in_specs=[VMEM] * 4 + [ANY],
        out_specs=[VMEM] * 3,
        compiler_params=pltpu.CompilerParams(vmem_limit_bytes=16 << 20),
        cost_estimate=pl.CostEstimate(
            flops=2_000_000, bytes_accessed=1_000_000, transcendentals=1_000
        ),
        name="geometry",
    )(slip_later, vertices, triangles, elem_map, pay)
    route = []
    for row in range(row_count):
        step = 1 if row % 2 == 0 else -1
        for owner in range(long_count):
            if 0 <= owner - step < long_count:
                route.append((row * long_count + owner - step, row * long_count + owner))
    halo = lax.ppermute(to_neighbour, ("row", "long"), route)

    window, places = pl.pallas_call(
        window_kernel,
        out_shape=[
            jax.ShapeDtypeStruct((slots, rhs_count, unknowns), jnp.bfloat16),
            jax.ShapeDtypeStruct((slots, 4, size), jnp.float32),
        ],
        in_specs=[VMEM] * 3,
        out_specs=[VMEM] * 2,
        compiler_params=pltpu.CompilerParams(vmem_limit_bytes=16 << 20),
        cost_estimate=pl.CostEstimate(flops=1000, bytes_accessed=1000, transcendentals=0),
        name="window",
    )(xs, geometry, halo)

    to_second, to_first, pair_list = pl.pallas_call(
        functools.partial(coupling_kernel, clusters=clusters, long_count=long_count),
        out_shape=[jax.ShapeDtypeStruct((coupling.shape[0] * rank_size, LANES), jnp.bfloat16)] * 2
        + [jax.ShapeDtypeStruct((6,) + far_pairs.shape[1:], far_pairs.dtype)],
        in_specs=[VMEM, VMEM, ANY],
        out_specs=[VMEM] * 3,
        compiler_params=pltpu.CompilerParams(vmem_limit_bytes=16 << 20),
        cost_estimate=pl.CostEstimate(flops=1000, bytes_accessed=1000, transcendentals=0),
        name="coupling",
    )(coupling, far_pairs, pay)
    far, far_done = pl.pallas_call(
        functools.partial(far_kernel, clusters=clusters),
        out_shape=[
            jax.ShapeDtypeStruct((devices, rhs_count, clusters * rank_size), jnp.bfloat16),
            jax.ShapeDtypeStruct((8, LANES), jnp.float32),
        ],
        in_specs=[VMEM] * 4,
        out_specs=[HBM, VMEM],
        scratch_shapes=[
            pltpu.SMEM((6,) + far_pairs.shape[1:], far_pairs.dtype),
            pltpu.VMEM((devices, rhs_count, LANES), jnp.float32),
            pltpu.VMEM((long_count, rhs_count, clusters * rank_size), jnp.bfloat16),
            pltpu.SemaphoreType.DMA((row_count,)),
        ]
        + [pltpu.VMEM((long_count, rhs_count, clusters * rank_size), jnp.float32)] * 4,
        compiler_params=pltpu.CompilerParams(vmem_limit_bytes=16 << 20),
        name="far",
    )(pair_list, everyone, to_second, to_first)
    far_terms = lax.all_to_all(far, ("row", "long"), 0, 0, tiled=True)

    near = pl.pallas_call(
        functools.partial(near_kernel, long_count=long_count, clusters=clusters),
        out_shape=jax.ShapeDtypeStruct((NEARC, rhs_count, unknowns), jnp.float32),
        in_specs=[VMEM] * 3 + [ANY],
        out_specs=VMEM,
        scratch_shapes=[
            pltpu.VMEM((slots, size, 8), jnp.float32),
            pltpu.VMEM((NEARC, 6, size, size), jnp.bfloat16),
            pltpu.VMEM((NEARC, 6, size, size), jnp.bfloat16),
        ],
        compiler_params=pltpu.CompilerParams(vmem_limit_bytes=24 << 20),
        cost_estimate=pl.CostEstimate(
            flops=1_000_000_000, bytes_accessed=1_000_000, transcendentals=660_000
        ),
        name="near",
    )(window, places, everyone, far_done)
    partner = [(row, row ^ 1) for row in range(row_count)]
    other = lax.ppermute(near, "row", partner)

    near_field = pl.pallas_call(
        gather_near_kernel,
        out_shape=jax.ShapeDtypeStruct(slip.shape, jnp.float32),
        in_specs=[VMEM] * 2,
        out_specs=VMEM,
        compiler_params=pltpu.CompilerParams(vmem_limit_bytes=16 << 20),
        cost_estimate=pl.CostEstimate(flops=1000, bytes_accessed=1000, transcendentals=0),
        name="gather_near",
    )(near, other)

    return pl.pallas_call(
        finish_kernel,
        out_shape=jax.ShapeDtypeStruct(slip.shape, jnp.float32),
        in_specs=[VMEM] * 3,
        out_specs=HBM,
        scratch_shapes=[
            pltpu.VMEM(slip.shape, jnp.float32),
            pltpu.SemaphoreType.DMA((clusters,)),
        ],
        compiler_params=pltpu.CompilerParams(vmem_limit_bytes=16 << 20),
        name="finish",
    )(near_field, far_terms, basis)


def solution(mesh):
    placed = (
        P("long", None, None),
        P(None, "long"),
        P(None, "long"),
        P("long", None),
        P(None, ("row", "long")),
        P(("row", "long")),
        P(None, ("row", "long")),
        P(("row", "long"), None),
        P("long", None, None),
    )
    return jax.shard_map(
        shards, mesh=mesh, in_specs=placed, out_specs=P("long", None, None), check_vma=False
    )
```

```python
import functools

import jax
import jax.numpy as jnp
from jax import lax
from jax.experimental import pallas as pl
from jax.experimental.pallas import tpu as pltpu
from jax.sharding import PartitionSpec as P

NEARC = 2
LANES = 128
ROWS = 16

soften = 0.25

VMEM = pl.BlockSpec(memory_space=pltpu.VMEM)
SMEM = pl.BlockSpec(memory_space=pltpu.SMEM)
HBM = pl.BlockSpec(memory_space=pltpu.HBM)
ANY = pl.BlockSpec(memory_space=pl.ANY)


def lane_gather(table, index):
    length = table.shape[1]
    lane = index & (LANES - 1)
    chunk = index // LANES
    found = jnp.zeros(index.shape, table.dtype)
    for piece_id in range(-(-length // LANES)):
        piece = table[:, piece_id * LANES : min(length, (piece_id + 1) * LANES)]
        missing = LANES - piece.shape[1]
        if missing:
            piece = jnp.concatenate([piece, jnp.zeros((1, missing), table.dtype)], axis=1)
        picked = jnp.take_along_axis(jnp.broadcast_to(piece, index.shape), lane, axis=1)
        found = jnp.where(chunk == piece_id, picked, found)
    return found


def split_three(value):
    high = value.astype(jnp.bfloat16).astype(jnp.float32)
    rest = value - high
    middle = rest.astype(jnp.bfloat16).astype(jnp.float32)
    return [high, middle, rest - middle]


def coeffs_kernel(
    slip_hbm, basis_hbm, pairs_hbm, count_ref, pay_hbm, slip_ref, basis_ref, pairs_ref, sent_ref, sems, out_sems
):
    clusters = slip_hbm.shape[0]
    rhs_count = slip_ref.shape[0]
    rank_size = basis_ref.shape[0]
    mine = lax.axis_index("row") % clusters
    copies = [
        pltpu.make_async_copy(slip_hbm.at[mine], slip_ref, sems.at[0]),
        pltpu.make_async_copy(basis_hbm.at[mine], basis_ref, sems.at[1]),
        pltpu.make_async_copy(pairs_hbm, pairs_ref, sems.at[2]),
    ]
    for copy in copies:
        copy.start()
    half = rhs_count // 2
    copies[2].wait()
    first = pairs_ref[0:1, :]
    kind = (first - lax.axis_index("long") * clusters) * (NEARC + 1) + pairs_ref[1:2, :] - first
    kinds = lax.broadcasted_iota(jnp.int32, (half, kind.shape[1]), 0)
    live = lax.broadcasted_iota(jnp.int32, kinds.shape, 1) < count_ref[0]
    low = jnp.sum(jnp.where(live & (kinds == kind), 1.0, 0.0), axis=1, keepdims=True)
    high = jnp.sum(jnp.where(live & (kinds + half == kind), 1.0, 0.0), axis=1, keepdims=True)
    copies[0].wait()
    copies[1].wait()
    coeffs = lax.dot_general(
        slip_ref[...].astype(jnp.bfloat16),
        basis_ref[...],
        (((1,), (1,)), ((), ())),
        preferred_element_type=jnp.float32,
    )
    counts = [jnp.broadcast_to(value, (half, rank_size)) for value in (low, high)]
    pay = jnp.concatenate([coeffs[0:half], coeffs[half:]] + counts, axis=1).astype(jnp.bfloat16)
    for target in range(sent_ref.shape[0]):
        sent_ref[target] = pay
    parts = pay_hbm.shape[0] // sent_ref.shape[0]
    sends = [
        pltpu.make_async_copy(
            sent_ref, pay_hbm.at[pl.ds(part * sent_ref.shape[0], sent_ref.shape[0])], out_sems.at[part]
        )
        for part in range(parts)
    ]
    for send in sends:
        send.start()
    for send in sends:
        send.wait()


def geometry_kernel(
    slip_hbm, vertices_ref, triangles_ref, map_ref, after_ref, xs_ref, halo_ref, geom_ref, slip_ref, sem
):
    clusters, rhs_count, unknowns = slip_hbm.shape
    fetch = pltpu.make_async_copy(slip_hbm, slip_ref, sem)
    fetch.start()
    long_index = lax.axis_index("long")

    size = map_ref.shape[1]
    half = size // LANES
    slot_map = map_ref[...]
    index = jnp.concatenate(
        [slot_map[:, part * LANES : (part + 1) * LANES] for part in range(half)], axis=0
    )
    vertex_base = long_index * vertices_ref.shape[1]
    corners = []
    for corner_id in range(3):
        vertex = lane_gather(triangles_ref[corner_id : corner_id + 1, :], index) - vertex_base
        corners.append(
            [lane_gather(vertices_ref[axis_id : axis_id + 1, :], vertex) for axis_id in range(3)]
        )
    one, two, three = corners
    centre = [(one[a] + two[a] + three[a]) / 3.0 for a in range(3)]
    edge_one = [two[a] - one[a] for a in range(3)]
    edge_two = [three[a] - one[a] for a in range(3)]
    normal = [
        edge_one[1] * edge_two[2] - edge_one[2] * edge_two[1],
        edge_one[2] * edge_two[0] - edge_one[0] * edge_two[2],
        edge_one[0] * edge_two[1] - edge_one[1] * edge_two[0],
    ]
    area = 0.5 * jnp.sqrt(normal[0] * normal[0] + normal[1] * normal[1] + normal[2] * normal[2])
    geometry = []
    for value in centre + [area]:
        geometry.append(
            jnp.concatenate(
                [value[part * clusters : (part + 1) * clusters] for part in range(half)], axis=1
            )
        )
    for cluster in range(clusters):
        geom_ref[cluster] = jnp.concatenate(
            [whole[cluster : cluster + 1, :] for whole in geometry], axis=0
        )

    fetch.wait()
    xs_ref[...] = slip_ref[...].astype(jnp.bfloat16)
    upward = lax.axis_index("row") % 2 == 0
    start = jnp.where(upward, clusters - NEARC, 0)
    pieces = [piece for whole in geometry for piece in split_three(whole)]
    for turn in range(NEARC):
        last = clusters - NEARC + turn
        rows = [
            jnp.where(upward, piece[last : last + 1, :], piece[turn : turn + 1, :])
            for piece in pieces
        ]
        rows.append(jnp.zeros((rhs_count - len(rows), size), jnp.float32))
        halo_ref[turn, :, 0:unknowns] = xs_ref[start + turn]
        halo_ref[turn, :, unknowns : unknowns + size] = jnp.concatenate(rows, axis=0).astype(
            jnp.bfloat16
        )


def window_kernel(xs_ref, geom_ref, halo_ref, slip_ref, place_ref):
    clusters, rhs_count, unknowns = xs_ref.shape
    size = geom_ref.shape[2]
    slots = clusters + NEARC
    odd = lax.axis_index("row") % 2

    def place_of(cluster):
        return (cluster + NEARC * (1 - odd) + slots) % slots

    for cluster in range(clusters):
        slip_ref[place_of(cluster)] = xs_ref[cluster]
        place_ref[place_of(cluster)] = geom_ref[cluster]
    for turn in range(NEARC):
        at = place_of(clusters + turn)
        slip_ref[at] = halo_ref[turn, :, 0:unknowns]
        pieces = halo_ref[turn, :, unknowns : unknowns + size].astype(jnp.float32)
        place_ref[at] = jnp.concatenate(
            [
                (pieces[3 * p + 2 : 3 * p + 3] + pieces[3 * p + 1 : 3 * p + 2])
                + pieces[3 * p : 3 * p + 1]
                for p in range(4)
            ],
            axis=0,
        )


def near_kernel(
    slip_ref, place_ref, pay_ref, after_ref, out_ref, cols_ref, even_ref, odd_ref, *, long_count, clusters
):
    slots, rhs_count, unknowns = slip_ref.shape
    size = place_ref.shape[2]
    long_index = lax.axis_index("long")
    before = jnp.maximum(long_index - 1, 0)
    totals = [jnp.zeros(pay_ref.shape[1:], jnp.float32) for _ in range(2)]
    for row in range(pay_ref.shape[0] // long_count):
        for source, owner in enumerate((long_index, before)):
            totals[source] += pay_ref[row * long_count + owner].astype(jnp.float32)
    even = lax.axis_index("row") % 2 == 0
    half = pay_ref.shape[1]
    rank_size = pay_ref.shape[2] // 4
    group = lax.broadcasted_iota(jnp.int32, (half, LANES), 1) // rank_size
    kinds = lax.broadcasted_iota(jnp.int32, (half, LANES), 0) + jnp.where(group == 3, half, 0)
    kinds = jnp.where(group < 2, -1, kinds)
    lane_id = lax.broadcasted_iota(jnp.int32, (half, LANES), 1)
    kinds = jnp.where(lane_id % rank_size == 0, kinds, -1)

    def count_of(place, u):
        both = []
        for cluster in (u, clusters - NEARC + u):
            reach = place - u - NEARC
            lower = cluster + jnp.minimum(reach, 0)
            inside = lower >= 0
            kind = jnp.where(inside, lower, lower + clusters) * (NEARC + 1) + jnp.abs(reach)
            source = jnp.where(inside, totals[0], totals[1])
            both.append(jnp.where(kinds == kind, source, 0.0))
        picked = jnp.sum(jnp.where(even, both[0], both[1]), axis=0, keepdims=True)
        return jnp.sum(picked, axis=1, keepdims=True)

    out_ref[...] = jnp.zeros(out_ref.shape, jnp.float32)
    for place in range(slots):
        rows = jnp.concatenate([place_ref[place], jnp.zeros((4, size), jnp.float32)], axis=0)
        cols_ref[place] = rows.T
    right = [[place_ref[NEARC + u, p : p + 1, :] for p in range(4)] for u in range(NEARC)]
    parts = [(0, 0), (1, 1), (2, 2), (0, 1), (0, 2), (1, 2)]

    def fill(place, targets, block_ref):
        for step in range(size // ROWS):
            here = pl.ds(step * ROWS, ROWS)
            column = cols_ref[place, here, :]
            left = [jnp.broadcast_to(column[:, p : p + 1], (ROWS, size)) for p in range(4)]
            for u in targets:
                offset = [left[p] - right[u][p] for p in range(3)]
                radius_sq = offset[0] * offset[0] + offset[1] * offset[1] + offset[2] * offset[2]
                inverse = lax.rsqrt(radius_sq + soften)
                flat = (left[3] * right[u][3]) * inverse
                cubed = flat * (inverse * inverse)
                scaled = [offset[p] * cubed for p in range(3)]
                for part_id, (i, j) in enumerate(parts):
                    term = offset[i] * scaled[j]
                    if i == j:
                        term = term + flat
                    block_ref[u, part_id, here, :] = term.astype(jnp.bfloat16)

    def apply(place, targets, block_ref):
        slip = slip_ref[place]
        pieces = [slip[:, p * size : (p + 1) * size] for p in range(3)]
        for u in targets:
            count = count_of(place, u)
            sums = [
                jnp.dot(pieces[p], block_ref[u, p], preferred_element_type=jnp.float32)
                for p in range(3)
            ]
            for part_id in range(3, 6):
                i, j = parts[part_id]
                both = jnp.dot(
                    jnp.concatenate([pieces[j], pieces[i]], axis=0),
                    block_ref[u, part_id],
                    preferred_element_type=jnp.float32,
                )
                sums[i] = sums[i] + both[0:rhs_count]
                sums[j] = sums[j] + both[rhs_count : 2 * rhs_count]
            for p in range(3):
                out_ref[u, :, p * size : (p + 1) * size] += count * sums[p]

    every = list(range(NEARC))
    fill(0, [0], even_ref)
    for u in range(1, NEARC):
        even_ref[u] = jnp.zeros(even_ref.shape[1:], jnp.bfloat16)

    def two_places(turn, carry):
        place = 2 * turn
        fill(place + 1, every, odd_ref)
        apply(place, every, even_ref)
        fill(place + 2, every, even_ref)
        apply(place + 1, every, odd_ref)
        return carry

    lax.fori_loop(0, (slots - 2) // 2, two_places, 0)
    fill(slots - 1, [NEARC - 1], odd_ref)
    apply(slots - 2, every, even_ref)
    apply(slots - 1, [NEARC - 1], odd_ref)


def coupling_kernel(
    coupling_ref, pairs_ref, after_ref, to_second_ref, to_first_ref, list_ref, *, clusters, long_count
):
    owner, group = pairs_ref[...] // clusters, pairs_ref[...] % clusters
    list_ref[...] = jnp.concatenate([group * long_count + owner, owner, group], axis=0)
    pair_count, rank_size, _ = coupling_ref.shape
    groups = LANES // rank_size
    for pair_id in range(pair_count):
        here = pl.ds(pair_id * rank_size, rank_size)
        coupling = coupling_ref[pair_id].astype(jnp.float32)
        for out_ref, value in ((to_second_ref, coupling), (to_first_ref, coupling.T)):
            out_ref[here, :] = jnp.concatenate([value] * groups, axis=1).astype(jnp.bfloat16)


def far_kernel(
    list_ref, coeff_ref, to_second_ref, to_first_ref, out_hbm, done_ref, pairs_ref, moved_ref, sent_ref, sems,
    *total_refs, clusters
):
    fetch = pltpu.make_async_copy(list_ref, pairs_ref, sems.at[0])
    fetch.start()
    done_ref[...] = jnp.zeros(done_ref.shape, jnp.float32)
    long_count, rhs_count, _ = total_refs[0].shape
    pair_count = pairs_ref.shape[1]
    rank_size = LANES // clusters
    group_id = lax.broadcasted_iota(jnp.int32, (rhs_count, LANES), 1) // rank_size
    for total_ref in total_refs:
        total_ref[...] = jnp.zeros(total_ref.shape, jnp.float32)
    for at in range(coeff_ref.shape[0]):
        whole = coeff_ref[at].astype(jnp.float32)
        moved_ref[at] = jnp.concatenate([whole, pltpu.roll(whole, LANES - rank_size, 1)], axis=0)
    fetch.wait()

    def coeff_of(at, group):
        whole = moved_ref[at]
        both = pltpu.roll(whole, rank_size * group, 1) if group else whole
        return jnp.where(group_id == group, both, 0.0)

    results = []
    for begin in range(0, pair_count, clusters):
        pair_ids = range(begin, min(begin + clusters, pair_count))
        depth = len(pair_ids) * rank_size
        here = pl.ds(begin * rank_size, depth)
        for source, target, matrix_ref in ((0, 1, to_second_ref), (1, 0, to_first_ref)):
            coeffs = jnp.concatenate(
                [coeff_of(pairs_ref[source, f], f - begin) for f in pair_ids], axis=0
            ).astype(jnp.bfloat16)
            value = jnp.dot(
                coeffs[:, 0:depth], matrix_ref[here, :], preferred_element_type=jnp.float32
            )
            for turn, f in enumerate(pair_ids):
                results.append(
                    (target, f, value[turn * rhs_count : (turn + 1) * rhs_count])
                )
    for turn, (target, f, value) in enumerate(results):
        total_ref = total_refs[turn % len(total_refs)]
        owner, group = pairs_ref[2 + target, f], pairs_ref[4 + target, f]
        total_ref[owner] += jnp.where(group_id == group, value, 0.0)
    total = total_refs[0][...]
    for total_ref in total_refs[1:]:
        total = total + total_ref[...]
    sent_ref[...] = total.astype(jnp.bfloat16)
    copies = [
        pltpu.make_async_copy(
            sent_ref, out_hbm.at[pl.ds(copy_id * long_count, long_count)], sems.at[copy_id]
        )
        for copy_id in range(out_hbm.shape[0] // long_count)
    ]
    for copy in copies:
        copy.start()
    for copy in copies:
        copy.wait()


def gather_near_kernel(own_ref, other_ref, out_ref):
    even = lax.axis_index("row") % 2 == 0
    for cluster in range(out_ref.shape[0]):
        u = cluster % NEARC
        here = even if cluster < NEARC else jnp.logical_not(even)
        out_ref[cluster] = jnp.where(here, own_ref[u], other_ref[u])


def finish_kernel(near_ref, far_ref, basis_ref, out_hbm, sent_ref, sems):
    clusters, rank_size, unknowns = basis_ref.shape
    rhs_count = near_ref.shape[1]
    total = jnp.sum(far_ref[...].astype(jnp.float32), axis=0)
    group_id = lax.broadcasted_iota(jnp.int32, total.shape, 1) // rank_size
    flat_basis = basis_ref[...].reshape(clusters * rank_size, unknowns)
    picked = [jnp.where(group_id == cluster, total, 0.0) for cluster in range(clusters)]
    result = jnp.dot(
        jnp.concatenate(picked, axis=0).astype(jnp.bfloat16),
        flat_basis,
        preferred_element_type=jnp.float32,
    )
    copies = []
    for cluster in range(clusters):
        far = result[cluster * rhs_count : (cluster + 1) * rhs_count]
        sent_ref[cluster] = far + near_ref[cluster]
        copies.append(
            pltpu.make_async_copy(sent_ref.at[cluster], out_hbm.at[cluster], sems.at[cluster])
        )
        copies[-1].start()
    for copy in copies:
        copy.wait()


def shards(slip, vertices, triangles, elem_map, near_pairs, near_count, far_pairs, far_coef, basis):
    clusters, rhs_count, unknowns = slip.shape
    rank_size = basis.shape[1]
    size = elem_map.shape[1]
    row_count = lax.axis_size("row")
    long_count = lax.axis_size("long")
    devices = row_count * long_count
    coupling = far_coef.reshape(-1, rank_size, rank_size)
    slots = clusters + NEARC

    pay = pl.pallas_call(
        coeffs_kernel,
        out_shape=jax.ShapeDtypeStruct((devices, rhs_count // 2, LANES), jnp.bfloat16),
        in_specs=[HBM] * 3 + [SMEM],
        out_specs=HBM,
        scratch_shapes=[
            pltpu.VMEM(slip.shape[1:], slip.dtype),
            pltpu.VMEM(basis.shape[1:], basis.dtype),
            pltpu.VMEM(near_pairs.shape, near_pairs.dtype),
            pltpu.VMEM((long_count, rhs_count // 2, LANES), jnp.bfloat16),
            pltpu.SemaphoreType.DMA((3,)),
            pltpu.SemaphoreType.DMA((row_count,)),
        ],
        compiler_params=pltpu.CompilerParams(vmem_limit_bytes=16 << 20),
        name="coeffs",
    )(
        *[
            pltpu.with_memory_space_constraint(array, pltpu.HBM)
            for array in (slip, basis, near_pairs)
        ],
        near_count,
    )
    everyone = lax.all_to_all(pay, ("row", "long"), 0, 0, tiled=True)

    xs, to_neighbour, geometry = pl.pallas_call(
        geometry_kernel,
        out_shape=[
            jax.ShapeDtypeStruct(slip.shape, jnp.bfloat16),
            jax.ShapeDtypeStruct((NEARC, rhs_count, unknowns + size), jnp.bfloat16),
            jax.ShapeDtypeStruct((clusters, 4, size), jnp.float32),
        ],
        in_specs=[HBM] + [VMEM] * 3 + [ANY],
        out_specs=[VMEM] * 3,
        scratch_shapes=[pltpu.VMEM(slip.shape, slip.dtype), pltpu.SemaphoreType.DMA],
        compiler_params=pltpu.CompilerParams(vmem_limit_bytes=16 << 20),
        cost_estimate=pl.CostEstimate(
            flops=2_000_000, bytes_accessed=1_000_000, transcendentals=1_000
        ),
        name="geometry",
    )(
        pltpu.with_memory_space_constraint(slip, pltpu.HBM), vertices, triangles, elem_map, pay
    )
    route = []
    for row in range(row_count):
        step = 1 if row % 2 == 0 else -1
        for owner in range(long_count):
            if 0 <= owner - step < long_count:
                route.append((row * long_count + owner - step, row * long_count + owner))
    halo = lax.ppermute(to_neighbour, ("row", "long"), route)

    window, places = pl.pallas_call(
        window_kernel,
        out_shape=[
            jax.ShapeDtypeStruct((slots, rhs_count, unknowns), jnp.bfloat16),
            jax.ShapeDtypeStruct((slots, 4, size), jnp.float32),
        ],
        in_specs=[VMEM] * 3,
        out_specs=[VMEM] * 2,
        compiler_params=pltpu.CompilerParams(vmem_limit_bytes=16 << 20),
        cost_estimate=pl.CostEstimate(flops=1000, bytes_accessed=1000, transcendentals=0),
        name="window",
    )(xs, geometry, halo)

    to_second, to_first, pair_list = pl.pallas_call(
        functools.partial(coupling_kernel, clusters=clusters, long_count=long_count),
        out_shape=[jax.ShapeDtypeStruct((coupling.shape[0] * rank_size, LANES), jnp.bfloat16)] * 2
        + [jax.ShapeDtypeStruct((6,) + far_pairs.shape[1:], far_pairs.dtype)],
        in_specs=[VMEM, VMEM, ANY],
        out_specs=[VMEM] * 3,
        compiler_params=pltpu.CompilerParams(vmem_limit_bytes=16 << 20),
        cost_estimate=pl.CostEstimate(flops=1000, bytes_accessed=1000, transcendentals=0),
        name="coupling",
    )(coupling, far_pairs, pay)
    far, far_done = pl.pallas_call(
        functools.partial(far_kernel, clusters=clusters),
        out_shape=[
            jax.ShapeDtypeStruct((devices, rhs_count, clusters * rank_size), jnp.bfloat16),
            jax.ShapeDtypeStruct((8, LANES), jnp.float32),
        ],
        in_specs=[VMEM] * 4,
        out_specs=[HBM, VMEM],
        scratch_shapes=[
            pltpu.SMEM((6,) + far_pairs.shape[1:], far_pairs.dtype),
            pltpu.VMEM((devices, rhs_count, LANES), jnp.float32),
            pltpu.VMEM((long_count, rhs_count, clusters * rank_size), jnp.bfloat16),
            pltpu.SemaphoreType.DMA((row_count,)),
        ]
        + [pltpu.VMEM((long_count, rhs_count, clusters * rank_size), jnp.float32)] * 4,
        compiler_params=pltpu.CompilerParams(vmem_limit_bytes=16 << 20),
        name="far",
    )(pair_list, everyone, to_second, to_first)
    far_terms = lax.all_to_all(far, ("row", "long"), 0, 0, tiled=True)

    near = pl.pallas_call(
        functools.partial(near_kernel, long_count=long_count, clusters=clusters),
        out_shape=jax.ShapeDtypeStruct((NEARC, rhs_count, unknowns), jnp.float32),
        in_specs=[VMEM] * 3 + [ANY],
        out_specs=VMEM,
        scratch_shapes=[
            pltpu.VMEM((slots, size, 8), jnp.float32),
            pltpu.VMEM((NEARC, 6, size, size), jnp.bfloat16),
            pltpu.VMEM((NEARC, 6, size, size), jnp.bfloat16),
        ],
        compiler_params=pltpu.CompilerParams(vmem_limit_bytes=24 << 20),
        cost_estimate=pl.CostEstimate(
            flops=1_000_000_000, bytes_accessed=1_000_000, transcendentals=660_000
        ),
        name="near",
    )(window, places, everyone, far_done)
    partner = [(row, row ^ 1) for row in range(row_count)]
    other = lax.ppermute(near, "row", partner)

    near_field = pl.pallas_call(
        gather_near_kernel,
        out_shape=jax.ShapeDtypeStruct(slip.shape, jnp.float32),
        in_specs=[VMEM] * 2,
        out_specs=VMEM,
        compiler_params=pltpu.CompilerParams(vmem_limit_bytes=16 << 20),
        cost_estimate=pl.CostEstimate(flops=1000, bytes_accessed=1000, transcendentals=0),
        name="gather_near",
    )(near, other)

    return pl.pallas_call(
        finish_kernel,
        out_shape=jax.ShapeDtypeStruct(slip.shape, jnp.float32),
        in_specs=[VMEM] * 3,
        out_specs=HBM,
        scratch_shapes=[
            pltpu.VMEM(slip.shape, jnp.float32),
            pltpu.SemaphoreType.DMA((clusters,)),
        ],
        compiler_params=pltpu.CompilerParams(vmem_limit_bytes=16 << 20),
        name="finish",
    )(near_field, far_terms, basis)


def solution(mesh):
    placed = (
        P("long", None, None),
        P(None, "long"),
        P(None, "long"),
        P("long", None),
        P(None, ("row", "long")),
        P(("row", "long")),
        P(None, ("row", "long")),
        P(("row", "long"), None),
        P("long", None, None),
    )
    return jax.shard_map(
        shards, mesh=mesh, in_specs=placed, out_specs=P("long", None, None), check_vma=False
    )
```

```python
import functools

import jax
import jax.numpy as jnp
from jax import lax
from jax.experimental import pallas as pl
from jax.experimental.pallas import tpu as pltpu
from jax.sharding import PartitionSpec as P

NEARC = 2
LANES = 128
ROWS = 16

soften = 0.25

VMEM = pl.BlockSpec(memory_space=pltpu.VMEM)
SMEM = pl.BlockSpec(memory_space=pltpu.SMEM)
HBM = pl.BlockSpec(memory_space=pltpu.HBM)
ANY = pl.BlockSpec(memory_space=pl.ANY)


def lane_gather(table, index):
    length = table.shape[1]
    lane = index & (LANES - 1)
    chunk = index // LANES
    found = jnp.zeros(index.shape, table.dtype)
    for piece_id in range(-(-length // LANES)):
        piece = table[:, piece_id * LANES : min(length, (piece_id + 1) * LANES)]
        missing = LANES - piece.shape[1]
        if missing:
            piece = jnp.concatenate([piece, jnp.zeros((1, missing), table.dtype)], axis=1)
        picked = jnp.take_along_axis(jnp.broadcast_to(piece, index.shape), lane, axis=1)
        found = jnp.where(chunk == piece_id, picked, found)
    return found


def split_three(value):
    high = value.astype(jnp.bfloat16).astype(jnp.float32)
    rest = value - high
    middle = rest.astype(jnp.bfloat16).astype(jnp.float32)
    return [high, middle, rest - middle]


def coeffs_kernel(
    slip_hbm, basis_hbm, pairs_ref, count_ref, pay_hbm, slip_ref, basis_ref, sent_ref, sems, out_sems
):
    clusters = slip_hbm.shape[0]
    rhs_count = slip_ref.shape[0]
    rank_size = basis_ref.shape[0]
    mine = lax.axis_index("row") % clusters
    copies = [
        pltpu.make_async_copy(slip_hbm.at[mine], slip_ref, sems.at[0]),
        pltpu.make_async_copy(basis_hbm.at[mine], basis_ref, sems.at[1]),
    ]
    for copy in copies:
        copy.start()
    half = rhs_count // 2
    first = pairs_ref[0:1, :]
    kind = (first - lax.axis_index("long") * clusters) * (NEARC + 1) + pairs_ref[1:2, :] - first
    kinds = lax.broadcasted_iota(jnp.int32, (half, kind.shape[1]), 0)
    live = lax.broadcasted_iota(jnp.int32, kinds.shape, 1) < count_ref[0]
    low = jnp.sum(jnp.where(live & (kinds == kind), 1.0, 0.0), axis=1, keepdims=True)
    high = jnp.sum(jnp.where(live & (kinds + half == kind), 1.0, 0.0), axis=1, keepdims=True)
    copies[0].wait()
    copies[1].wait()
    coeffs = lax.dot_general(
        slip_ref[...].astype(jnp.bfloat16),
        basis_ref[...],
        (((1,), (1,)), ((), ())),
        preferred_element_type=jnp.float32,
    )
    counts = [jnp.broadcast_to(value, (half, rank_size)) for value in (low, high)]
    pay = jnp.concatenate([coeffs[0:half], coeffs[half:]] + counts, axis=1).astype(jnp.bfloat16)
    for target in range(sent_ref.shape[0]):
        sent_ref[target] = pay
    parts = pay_hbm.shape[0] // sent_ref.shape[0]
    sends = [
        pltpu.make_async_copy(
            sent_ref, pay_hbm.at[pl.ds(part * sent_ref.shape[0], sent_ref.shape[0])], out_sems.at[part]
        )
        for part in range(parts)
    ]
    for send in sends:
        send.start()
    for send in sends:
        send.wait()


def geometry_kernel(
    slip_ref, vertices_ref, triangles_ref, map_ref, after_ref, xs_ref, halo_ref, geom_ref
):
    clusters, rhs_count, unknowns = slip_ref.shape
    xs_ref[...] = slip_ref[...].astype(jnp.bfloat16)
    long_index = lax.axis_index("long")

    size = map_ref.shape[1]
    half = size // LANES
    slot_map = map_ref[...]
    index = jnp.concatenate(
        [slot_map[:, part * LANES : (part + 1) * LANES] for part in range(half)], axis=0
    )
    vertex_base = long_index * vertices_ref.shape[1]
    corners = []
    for corner_id in range(3):
        vertex = lane_gather(triangles_ref[corner_id : corner_id + 1, :], index) - vertex_base
        corners.append(
            [lane_gather(vertices_ref[axis_id : axis_id + 1, :], vertex) for axis_id in range(3)]
        )
    one, two, three = corners
    centre = [(one[a] + two[a] + three[a]) / 3.0 for a in range(3)]
    edge_one = [two[a] - one[a] for a in range(3)]
    edge_two = [three[a] - one[a] for a in range(3)]
    normal = [
        edge_one[1] * edge_two[2] - edge_one[2] * edge_two[1],
        edge_one[2] * edge_two[0] - edge_one[0] * edge_two[2],
        edge_one[0] * edge_two[1] - edge_one[1] * edge_two[0],
    ]
    area = 0.5 * jnp.sqrt(normal[0] * normal[0] + normal[1] * normal[1] + normal[2] * normal[2])
    geometry = []
    for value in centre + [area]:
        geometry.append(
            jnp.concatenate(
                [value[part * clusters : (part + 1) * clusters] for part in range(half)], axis=1
            )
        )
    for cluster in range(clusters):
        geom_ref[cluster] = jnp.concatenate(
            [whole[cluster : cluster + 1, :] for whole in geometry], axis=0
        )

    upward = lax.axis_index("row") % 2 == 0
    start = jnp.where(upward, clusters - NEARC, 0)
    pieces = [piece for whole in geometry for piece in split_three(whole)]
    for turn in range(NEARC):
        last = clusters - NEARC + turn
        rows = [
            jnp.where(upward, piece[last : last + 1, :], piece[turn : turn + 1, :])
            for piece in pieces
        ]
        rows.append(jnp.zeros((rhs_count - len(rows), size), jnp.float32))
        halo_ref[turn, :, 0:unknowns] = xs_ref[start + turn]
        halo_ref[turn, :, unknowns : unknowns + size] = jnp.concatenate(rows, axis=0).astype(
            jnp.bfloat16
        )


def window_kernel(xs_ref, geom_ref, halo_ref, slip_ref, place_ref):
    clusters, rhs_count, unknowns = xs_ref.shape
    size = geom_ref.shape[2]
    slots = clusters + NEARC
    odd = lax.axis_index("row") % 2

    def place_of(cluster):
        return (cluster + NEARC * (1 - odd) + slots) % slots

    for cluster in range(clusters):
        slip_ref[place_of(cluster)] = xs_ref[cluster]
        place_ref[place_of(cluster)] = geom_ref[cluster]
    for turn in range(NEARC):
        at = place_of(clusters + turn)
        slip_ref[at] = halo_ref[turn, :, 0:unknowns]
        pieces = halo_ref[turn, :, unknowns : unknowns + size].astype(jnp.float32)
        place_ref[at] = jnp.concatenate(
            [
                (pieces[3 * p + 2 : 3 * p + 3] + pieces[3 * p + 1 : 3 * p + 2])
                + pieces[3 * p : 3 * p + 1]
                for p in range(4)
            ],
            axis=0,
        )


def near_kernel(
    slip_ref, place_ref, pay_ref, after_ref, out_ref, cols_ref, even_ref, odd_ref, *, long_count, clusters
):
    slots, rhs_count, unknowns = slip_ref.shape
    size = place_ref.shape[2]
    long_index = lax.axis_index("long")
    before = jnp.maximum(long_index - 1, 0)
    totals = [jnp.zeros(pay_ref.shape[1:], jnp.float32) for _ in range(2)]
    for row in range(pay_ref.shape[0] // long_count):
        for source, owner in enumerate((long_index, before)):
            totals[source] += pay_ref[row * long_count + owner].astype(jnp.float32)
    even = lax.axis_index("row") % 2 == 0
    half = pay_ref.shape[1]
    rank_size = pay_ref.shape[2] // 4
    group = lax.broadcasted_iota(jnp.int32, (half, LANES), 1) // rank_size
    kinds = lax.broadcasted_iota(jnp.int32, (half, LANES), 0) + jnp.where(group == 3, half, 0)
    kinds = jnp.where(group < 2, -1, kinds)
    lane_id = lax.broadcasted_iota(jnp.int32, (half, LANES), 1)
    kinds = jnp.where(lane_id % rank_size == 0, kinds, -1)

    def count_of(place, u):
        both = []
        for cluster in (u, clusters - NEARC + u):
            reach = place - u - NEARC
            lower = cluster + jnp.minimum(reach, 0)
            inside = lower >= 0
            kind = jnp.where(inside, lower, lower + clusters) * (NEARC + 1) + jnp.abs(reach)
            source = jnp.where(inside, totals[0], totals[1])
            both.append(jnp.where(kinds == kind, source, 0.0))
        picked = jnp.sum(jnp.where(even, both[0], both[1]), axis=0, keepdims=True)
        return jnp.sum(picked, axis=1, keepdims=True)

    out_ref[...] = jnp.zeros(out_ref.shape, jnp.float32)
    for place in range(slots):
        rows = jnp.concatenate([place_ref[place], jnp.zeros((4, size), jnp.float32)], axis=0)
        cols_ref[place] = rows.T
    right = [[place_ref[NEARC + u, p : p + 1, :] for p in range(4)] for u in range(NEARC)]
    parts = [(0, 0), (1, 1), (2, 2), (0, 1), (0, 2), (1, 2)]

    def fill(place, targets, block_ref):
        for step in range(size // ROWS):
            here = pl.ds(step * ROWS, ROWS)
            column = cols_ref[place, here, :]
            left = [jnp.broadcast_to(column[:, p : p + 1], (ROWS, size)) for p in range(4)]
            for u in targets:
                offset = [left[p] - right[u][p] for p in range(3)]
                radius_sq = offset[0] * offset[0] + offset[1] * offset[1] + offset[2] * offset[2]
                inverse = lax.rsqrt(radius_sq + soften)
                flat = (left[3] * right[u][3]) * inverse
                cubed = flat * (inverse * inverse)
                scaled = [offset[p] * cubed for p in range(3)]
                for part_id, (i, j) in enumerate(parts):
                    term = offset[i] * scaled[j]
                    if i == j:
                        term = term + flat
                    block_ref[u, part_id, here, :] = term.astype(jnp.bfloat16)

    def apply(place, targets, block_ref):
        slip = slip_ref[place]
        pieces = [slip[:, p * size : (p + 1) * size] for p in range(3)]
        for u in targets:
            count = count_of(place, u)
            sums = [
                jnp.dot(pieces[p], block_ref[u, p], preferred_element_type=jnp.float32)
                for p in range(3)
            ]
            for part_id in range(3, 6):
                i, j = parts[part_id]
                both = jnp.dot(
                    jnp.concatenate([pieces[j], pieces[i]], axis=0),
                    block_ref[u, part_id],
                    preferred_element_type=jnp.float32,
                )
                sums[i] = sums[i] + both[0:rhs_count]
                sums[j] = sums[j] + both[rhs_count : 2 * rhs_count]
            for p in range(3):
                out_ref[u, :, p * size : (p + 1) * size] += count * sums[p]

    every = list(range(NEARC))
    fill(0, [0], even_ref)
    for u in range(1, NEARC):
        even_ref[u] = jnp.zeros(even_ref.shape[1:], jnp.bfloat16)

    def two_places(turn, carry):
        place = 2 * turn
        fill(place + 1, every, odd_ref)
        apply(place, every, even_ref)
        fill(place + 2, every, even_ref)
        apply(place + 1, every, odd_ref)
        return carry

    lax.fori_loop(0, (slots - 2) // 2, two_places, 0)
    fill(slots - 1, [NEARC - 1], odd_ref)
    apply(slots - 2, every, even_ref)
    apply(slots - 1, [NEARC - 1], odd_ref)


def coupling_kernel(
    coupling_ref, pairs_ref, after_ref, to_second_ref, to_first_ref, list_ref, *, clusters, long_count
):
    owner, group = pairs_ref[...] // clusters, pairs_ref[...] % clusters
    list_ref[...] = jnp.concatenate([group * long_count + owner, owner, group], axis=0)
    pair_count, rank_size, _ = coupling_ref.shape
    groups = LANES // rank_size
    for pair_id in range(pair_count):
        here = pl.ds(pair_id * rank_size, rank_size)
        coupling = coupling_ref[pair_id].astype(jnp.float32)
        for out_ref, value in ((to_second_ref, coupling), (to_first_ref, coupling.T)):
            out_ref[here, :] = jnp.concatenate([value] * groups, axis=1).astype(jnp.bfloat16)


def far_kernel(
    list_ref, coeff_ref, to_second_ref, to_first_ref, out_hbm, done_ref, pairs_ref, moved_ref, sent_ref, sems,
    *total_refs, clusters
):
    fetch = pltpu.make_async_copy(list_ref, pairs_ref, sems.at[0])
    fetch.start()
    done_ref[...] = jnp.zeros(done_ref.shape, jnp.float32)
    long_count, rhs_count, _ = total_refs[0].shape
    pair_count = pairs_ref.shape[1]
    rank_size = LANES // clusters
    group_id = lax.broadcasted_iota(jnp.int32, (rhs_count, LANES), 1) // rank_size
    for total_ref in total_refs:
        total_ref[...] = jnp.zeros(total_ref.shape, jnp.float32)
    for at in range(coeff_ref.shape[0]):
        whole = coeff_ref[at].astype(jnp.float32)
        moved_ref[at] = jnp.concatenate([whole, pltpu.roll(whole, LANES - rank_size, 1)], axis=0)
    fetch.wait()

    def coeff_of(at, group):
        whole = moved_ref[at]
        both = pltpu.roll(whole, rank_size * group, 1) if group else whole
        return jnp.where(group_id == group, both, 0.0)

    results = []
    for begin in range(0, pair_count, clusters):
        pair_ids = range(begin, min(begin + clusters, pair_count))
        depth = len(pair_ids) * rank_size
        here = pl.ds(begin * rank_size, depth)
        for source, target, matrix_ref in ((0, 1, to_second_ref), (1, 0, to_first_ref)):
            coeffs = jnp.concatenate(
                [coeff_of(pairs_ref[source, f], f - begin) for f in pair_ids], axis=0
            ).astype(jnp.bfloat16)
            value = jnp.dot(
                coeffs[:, 0:depth], matrix_ref[here, :], preferred_element_type=jnp.float32
            )
            for turn, f in enumerate(pair_ids):
                results.append(
                    (target, f, value[turn * rhs_count : (turn + 1) * rhs_count])
                )
    for turn, (target, f, value) in enumerate(results):
        total_ref = total_refs[turn % len(total_refs)]
        owner, group = pairs_ref[2 + target, f], pairs_ref[4 + target, f]
        total_ref[owner] += jnp.where(group_id == group, value, 0.0)
    total = total_refs[0][...]
    for total_ref in total_refs[1:]:
        total = total + total_ref[...]
    sent_ref[...] = total.astype(jnp.bfloat16)
    copies = [
        pltpu.make_async_copy(
            sent_ref, out_hbm.at[pl.ds(copy_id * long_count, long_count)], sems.at[copy_id]
        )
        for copy_id in range(out_hbm.shape[0] // long_count)
    ]
    for copy in copies:
        copy.start()
    for copy in copies:
        copy.wait()


def gather_near_kernel(own_ref, other_ref, out_ref):
    even = lax.axis_index("row") % 2 == 0
    for cluster in range(out_ref.shape[0]):
        u = cluster % NEARC
        here = even if cluster < NEARC else jnp.logical_not(even)
        out_ref[cluster] = jnp.where(here, own_ref[u], other_ref[u])


def finish_kernel(near_ref, far_ref, basis_ref, out_hbm, sent_ref, sems):
    clusters, rank_size, unknowns = basis_ref.shape
    rhs_count = near_ref.shape[1]
    total = jnp.sum(far_ref[...].astype(jnp.float32), axis=0)
    group_id = lax.broadcasted_iota(jnp.int32, total.shape, 1) // rank_size
    flat_basis = basis_ref[...].reshape(clusters * rank_size, unknowns)
    picked = [jnp.where(group_id == cluster, total, 0.0) for cluster in range(clusters)]
    result = jnp.dot(
        jnp.concatenate(picked, axis=0).astype(jnp.bfloat16),
        flat_basis,
        preferred_element_type=jnp.float32,
    )
    copies = []
    for cluster in range(clusters):
        far = result[cluster * rhs_count : (cluster + 1) * rhs_count]
        sent_ref[cluster] = far + near_ref[cluster]
        copies.append(
            pltpu.make_async_copy(sent_ref.at[cluster], out_hbm.at[cluster], sems.at[cluster])
        )
        copies[-1].start()
    for copy in copies:
        copy.wait()


def shards(slip, vertices, triangles, elem_map, near_pairs, near_count, far_pairs, far_coef, basis):
    clusters, rhs_count, unknowns = slip.shape
    rank_size = basis.shape[1]
    size = elem_map.shape[1]
    row_count = lax.axis_size("row")
    long_count = lax.axis_size("long")
    devices = row_count * long_count
    coupling = far_coef.reshape(-1, rank_size, rank_size)
    slots = clusters + NEARC

    pay = pl.pallas_call(
        coeffs_kernel,
        out_shape=jax.ShapeDtypeStruct((devices, rhs_count // 2, LANES), jnp.bfloat16),
        in_specs=[HBM] * 2 + [VMEM, SMEM],
        out_specs=HBM,
        scratch_shapes=[
            pltpu.VMEM(slip.shape[1:], slip.dtype),
            pltpu.VMEM(basis.shape[1:], basis.dtype),
            pltpu.VMEM((long_count, rhs_count // 2, LANES), jnp.bfloat16),
            pltpu.SemaphoreType.DMA((2,)),
            pltpu.SemaphoreType.DMA((row_count,)),
        ],
        compiler_params=pltpu.CompilerParams(vmem_limit_bytes=16 << 20),
        name="coeffs",
    )(
        *[
            pltpu.with_memory_space_constraint(array, pltpu.HBM)
            for array in (slip, basis)
        ],
        near_pairs,
        near_count,
    )
    everyone = lax.all_to_all(pay, ("row", "long"), 0, 0, tiled=True)

    xs, to_neighbour, geometry = pl.pallas_call(
        geometry_kernel,
        out_shape=[
            jax.ShapeDtypeStruct(slip.shape, jnp.bfloat16),
            jax.ShapeDtypeStruct((NEARC, rhs_count, unknowns + size), jnp.bfloat16),
            jax.ShapeDtypeStruct((clusters, 4, size), jnp.float32),
        ],
        in_specs=[VMEM] * 4 + [ANY],
        out_specs=[VMEM] * 3,
        compiler_params=pltpu.CompilerParams(vmem_limit_bytes=16 << 20),
        cost_estimate=pl.CostEstimate(
            flops=2_000_000, bytes_accessed=1_000_000, transcendentals=1_000
        ),
        name="geometry",
    )(slip, vertices, triangles, elem_map, pay)
    route = []
    for row in range(row_count):
        step = 1 if row % 2 == 0 else -1
        for owner in range(long_count):
            if 0 <= owner - step < long_count:
                route.append((row * long_count + owner - step, row * long_count + owner))
    halo = lax.ppermute(to_neighbour, ("row", "long"), route)

    window, places = pl.pallas_call(
        window_kernel,
        out_shape=[
            jax.ShapeDtypeStruct((slots, rhs_count, unknowns), jnp.bfloat16),
            jax.ShapeDtypeStruct((slots, 4, size), jnp.float32),
        ],
        in_specs=[VMEM] * 3,
        out_specs=[VMEM] * 2,
        compiler_params=pltpu.CompilerParams(vmem_limit_bytes=16 << 20),
        cost_estimate=pl.CostEstimate(flops=1000, bytes_accessed=1000, transcendentals=0),
        name="window",
    )(xs, geometry, halo)

    to_second, to_first, pair_list = pl.pallas_call(
        functools.partial(coupling_kernel, clusters=clusters, long_count=long_count),
        out_shape=[jax.ShapeDtypeStruct((coupling.shape[0] * rank_size, LANES), jnp.bfloat16)] * 2
        + [jax.ShapeDtypeStruct((6,) + far_pairs.shape[1:], far_pairs.dtype)],
        in_specs=[VMEM, VMEM, ANY],
        out_specs=[VMEM] * 3,
        compiler_params=pltpu.CompilerParams(vmem_limit_bytes=16 << 20),
        cost_estimate=pl.CostEstimate(flops=1000, bytes_accessed=1000, transcendentals=0),
        name="coupling",
    )(coupling, far_pairs, pay)
    far, far_done = pl.pallas_call(
        functools.partial(far_kernel, clusters=clusters),
        out_shape=[
            jax.ShapeDtypeStruct((devices, rhs_count, clusters * rank_size), jnp.bfloat16),
            jax.ShapeDtypeStruct((8, LANES), jnp.float32),
        ],
        in_specs=[VMEM] * 4,
        out_specs=[HBM, VMEM],
        scratch_shapes=[
            pltpu.SMEM((6,) + far_pairs.shape[1:], far_pairs.dtype),
            pltpu.VMEM((devices, rhs_count, LANES), jnp.float32),
            pltpu.VMEM((long_count, rhs_count, clusters * rank_size), jnp.bfloat16),
            pltpu.SemaphoreType.DMA((row_count,)),
        ]
        + [pltpu.VMEM((long_count, rhs_count, clusters * rank_size), jnp.float32)] * 4,
        compiler_params=pltpu.CompilerParams(vmem_limit_bytes=16 << 20),
        name="far",
    )(pair_list, everyone, to_second, to_first)
    far_terms = lax.all_to_all(far, ("row", "long"), 0, 0, tiled=True)

    near = pl.pallas_call(
        functools.partial(near_kernel, long_count=long_count, clusters=clusters),
        out_shape=jax.ShapeDtypeStruct((NEARC, rhs_count, unknowns), jnp.float32),
        in_specs=[VMEM] * 3 + [ANY],
        out_specs=VMEM,
        scratch_shapes=[
            pltpu.VMEM((slots, size, 8), jnp.float32),
            pltpu.VMEM((NEARC, 6, size, size), jnp.bfloat16),
            pltpu.VMEM((NEARC, 6, size, size), jnp.bfloat16),
        ],
        compiler_params=pltpu.CompilerParams(vmem_limit_bytes=24 << 20),
        cost_estimate=pl.CostEstimate(
            flops=1_000_000_000, bytes_accessed=1_000_000, transcendentals=660_000
        ),
        name="near",
    )(window, places, everyone, far_done)
    partner = [(row, row ^ 1) for row in range(row_count)]
    other = lax.ppermute(near, "row", partner)

    near_field = pl.pallas_call(
        gather_near_kernel,
        out_shape=jax.ShapeDtypeStruct(slip.shape, jnp.float32),
        in_specs=[VMEM] * 2,
        out_specs=VMEM,
        compiler_params=pltpu.CompilerParams(vmem_limit_bytes=16 << 20),
        cost_estimate=pl.CostEstimate(flops=1000, bytes_accessed=1000, transcendentals=0),
        name="gather_near",
    )(near, other)

    return pl.pallas_call(
        finish_kernel,
        out_shape=jax.ShapeDtypeStruct(slip.shape, jnp.float32),
        in_specs=[VMEM] * 3,
        out_specs=HBM,
        scratch_shapes=[
            pltpu.VMEM(slip.shape, jnp.float32),
            pltpu.SemaphoreType.DMA((clusters,)),
        ],
        compiler_params=pltpu.CompilerParams(vmem_limit_bytes=16 << 20),
        name="finish",
    )(near_field, far_terms, basis)


def solution(mesh):
    placed = (
        P("long", None, None),
        P(None, "long"),
        P(None, "long"),
        P("long", None),
        P(None, ("row", "long")),
        P(("row", "long")),
        P(None, ("row", "long")),
        P(("row", "long"), None),
        P("long", None, None),
    )
    return jax.shard_map(
        shards, mesh=mesh, in_specs=placed, out_specs=P("long", None, None), check_vma=False
    )
```
